32 devices in a mesh: dp: 8 (over y, x, core), fsdp: 4 (over z).
Axes of the slice: x: 2, y: 2, z: 4, core: 2. Of those that a mesh axis runs over, the one named last changes fastest.
Arguments:
- decoder_in: bfloat16 [64, 128, 768], P(('dp', 'fsdp')), may hold values from -12 to 12
- encoder_out: bfloat16 [64, 512, 768], P(('dp', 'fsdp')), may hold values from -12 to 12
- self_query: bfloat16 [768, 768], P(('dp', 'fsdp')), may hold values from -0.02734375 to 0.02734375
- self_key: bfloat16 [768, 768], P(('dp', 'fsdp')), may hold values from -0.21875 to 0.21875
- self_value: bfloat16 [768, 768], P(('dp', 'fsdp')), may hold values from -0.21875 to 0.21875
- self_output: bfloat16 [768, 768], P(('dp', 'fsdp')), may hold values from -0.625 to 0.625
- cross_query: bfloat16 [768, 768], P(('dp', 'fsdp')), may hold values from -0.02734375 to 0.02734375
- cross_key: bfloat16 [768, 768], P(('dp', 'fsdp')), may hold values from -0.21875 to 0.21875
- cross_value: bfloat16 [768, 768], P(('dp', 'fsdp')), may hold values from -0.21875 to 0.21875
- cross_output: bfloat16 [768, 768], P(('dp', 'fsdp')), may hold values from -1.25 to 1.25
- hidden_in: bfloat16 [768, 3072], P(('dp', 'fsdp')), may hold values from -0.21875 to 0.21875
- hidden_out: bfloat16 [3072, 768], P(('dp', 'fsdp')), may hold values from -0.109375 to 0.109375
- norm_gains: bfloat16 [3, 768], P(None, ('dp', 'fsdp')), may hold values from 0.099609375 to 1.8984375
- bias_table: bfloat16 [32, 12], replicated, may hold values from -6 to 6
- target_lengths: int32 [64], P(('dp', 'fsdp')), may hold values from 64 to 128, as said below
- source_lengths: int32 [64], P(('dp', 'fsdp')), may hold values from 256 to 512, as said below
- example_counts: int32 [32], P(('dp', 'fsdp')), may hold values from 1 to 2, as said below
- cotangent: bfloat16 [64, 128, 768], P(('dp', 'fsdp')), may hold values from -12 to 12
Outputs:
- layer_out: bfloat16 [64, 128, 768], P(('dp', 'fsdp'))
- grad_decoder: float32 [64, 128, 768], P(('dp', 'fsdp'))
- grad_encoder: float32 [64, 512, 768], P(('dp', 'fsdp'))
- grad_self_query: float32 [768, 768], P(('dp', 'fsdp'))
- grad_self_key: float32 [768, 768], P(('dp', 'fsdp'))
- grad_self_value: float32 [768, 768], P(('dp', 'fsdp'))
- grad_self_output: float32 [768, 768], P(('dp', 'fsdp'))
- grad_cross_query: float32 [768, 768], P(('dp', 'fsdp'))
- grad_cross_key: float32 [768, 768], P(('dp', 'fsdp'))
- grad_cross_value: float32 [768, 768], P(('dp', 'fsdp'))
- grad_cross_output: float32 [768, 768], P(('dp', 'fsdp'))
- grad_hidden_in: float32 [768, 3072], P(('dp', 'fsdp'))
- grad_hidden_out: float32 [3072, 768], P(('dp', 'fsdp'))
- grad_gains: float32 [3, 768], P(None, ('dp', 'fsdp'))
- grad_table: float32 [32, 12], replicated
The draws below stay inside these ranges and needn't reach their ends.
Inputs may be any that keep to these rules, and one draw needn't show every extreme that they name: `target_lengths`: every example's target length is at most 128 and some example's equals 128. `source_lengths`: every example's encoder length is at most 512 and some example's equals 512. `example_counts`: A device's present examples are its first slots; some device holds 2.
All inputs are finite; a program needn't handle non-finite values.
Results may differ from the reference program's by a relative error of at most 0.019.
Values may be sent and summed in bfloat16 or wider, within the bound.
A program may use at most 192 MiB of HBM per device.

```python
import jax
import jax.numpy as jnp
from jax import lax

D = 768
H = 12
DH = 64
FF = 3072
NB = 32
EX_DEV = 2
TGT = 128
ENC = 512
NDEV = 32
EXAMPLES = 64


def full_lengths(key, count, longest):
    first, second = jax.random.split(key)
    values = jax.random.randint(first, (count,), longest // 2, longest + 1, dtype=jnp.int32)
    chosen = jax.random.randint(second, (), 0, count, dtype=jnp.int32)
    return values.at[chosen].set(longest)


def draw_target_lengths(key, part):
    key = jax.random.fold_in(key, 12)
    return full_lengths(key, EXAMPLES, TGT)


def draw_source_lengths(key, part):
    key = jax.random.fold_in(key, 13)
    return full_lengths(key, EXAMPLES, ENC)


def draw_example_counts(key, part):
    key = jax.random.fold_in(key, 11)
    first, second = jax.random.split(key)
    counts = jax.random.randint(first, (NDEV,), max(1, EX_DEV // 2), EX_DEV + 1, dtype=jnp.int32)
    chosen = jax.random.randint(second, (), 0, NDEV, dtype=jnp.int32)
    return counts.at[chosen].set(EX_DEV)


def with_spikes(entries, stream_key, source, target, parts, factor):
    owner, partner = [(jnp.arange(entries.shape[position]) // (entries.shape[position] // parts)).reshape([-1 if axis == position else 1 for axis in range(entries.ndim)]) for position in (source, target)]
    chosen = jax.random.permutation(stream_key, parts)[partner]
    strong = (owner == chosen) | (owner == (partner + parts // 2) % parts)
    return jnp.where(strong, factor * entries, entries)


def levels(own_key, shape, cuts, low, high):
    factor_of = 1.0
    for position, blocks in cuts:
        draws = jax.random.uniform(jax.random.fold_in(jax.random.fold_in(own_key, 6), position), (blocks,), jnp.float32, low / len(cuts), high / len(cuts))
        factor_of = factor_of * jnp.repeat(jnp.exp(draws), shape[position] // blocks).reshape((-1,) + (1,) * (len(shape) - 1 - position))
    return factor_of


def normal_values(stream_key, dims, scale, reach, shards=(), held_as=jnp.bfloat16):
    entries = scale * jax.random.normal(stream_key, dims, jnp.float32)
    if shards:
        entries = entries * levels(stream_key, dims, shards, -0.22, 0.18)
    return jnp.clip(entries, -reach, reach).astype(held_as)


def heavy_noise(key, extent, deviation, bound, cuts, heavy, held_as=jnp.bfloat16):
    values = deviation * jax.random.normal(key, extent, jnp.float32)
    if cuts:
        values = values * levels(key, extent, cuts, -0.22, 0.18)
    return jnp.clip(with_spikes(values, jax.random.fold_in(key, 3), *heavy), -bound, bound).astype(held_as)


def setup_inputs(seed: int = 0) -> dict:
    streams_of = jax.random.split(jax.random.key(seed), 19)
    decoder_in = heavy_noise(streams_of[0], (EXAMPLES, TGT, D), 1.0, 12.0, ((0, 32),), (0, 2, 32, 2.75))
    encoder_out = heavy_noise(streams_of[1], (EXAMPLES, ENC, D), 1.0, 12.0, ((0, 32),), (0, 2, 32, 2.75))
    self_query = normal_values(streams_of[2], (D, D), (64 * D) ** -0.5, 0.02734375, ((0, 32),))
    self_key = normal_values(streams_of[3], (D, D), D ** -0.5, 0.21875, ((0, 32),))
    self_value = normal_values(streams_of[4], (D, D), D ** -0.5, 0.21875, ((0, 32),))
    self_output = normal_values(streams_of[5], (D, D), (D // 8) ** -0.5, 0.625, ((0, 32),))
    cross_query = normal_values(streams_of[6], (D, D), (64 * D) ** -0.5, 0.02734375, ((0, 32),))
    cross_key = normal_values(streams_of[7], (D, D), D ** -0.5, 0.21875, ((0, 32),))
    cross_value = normal_values(streams_of[8], (D, D), D ** -0.5, 0.21875, ((0, 32),))
    cross_output = normal_values(streams_of[9], (D, D), (D // 32) ** -0.5, 1.25, ((0, 32),))
    hidden_in = normal_values(streams_of[10], (D, FF), D ** -0.5, 0.21875, ((0, 32),))
    hidden_out = normal_values(streams_of[11], (FF, D), FF ** -0.5, 0.109375, ((0, 32),))
    norm_gains = jnp.clip(1.0 + 0.18 * jax.random.normal(streams_of[12], (3, D), jnp.float32), 0.099609375, 1.8984375).astype(jnp.bfloat16)
    bias_table = normal_values(streams_of[13], (NB, H), 1.0, 6.0)
    target_lengths = draw_target_lengths(jax.random.fold_in(streams_of[18], 71), 0)
    source_lengths = draw_source_lengths(jax.random.fold_in(streams_of[18], 71), 0)
    example_counts = draw_example_counts(jax.random.fold_in(streams_of[18], 71), 0)
    cotangent = heavy_noise(streams_of[17], (EXAMPLES, TGT, D), 1.0, 12.0, ((0, 32),), (0, 2, 32, 2.75))
    return dict(decoder_in=decoder_in, encoder_out=encoder_out, self_query=self_query, self_key=self_key, self_value=self_value, self_output=self_output, cross_query=cross_query, cross_key=cross_key, cross_value=cross_value, cross_output=cross_output, hidden_in=hidden_in, hidden_out=hidden_out, norm_gains=norm_gains, bias_table=bias_table, target_lengths=target_lengths, source_lengths=source_lengths, example_counts=example_counts, cotangent=cotangent)


eps = 1e-06
thresholds = [19, 21, 24, 27, 31, 35, 40, 46, 52, 59, 67, 77, 87, 99, 113]
highest = lax.Precision.HIGHEST

@jax.custom_vjp
def low(v):
    return lax.optimization_barrier(v.astype(jnp.bfloat16)).astype(jnp.float32)

@jax.custom_vjp
def low_back(v):
    return v

def low_keep(v):
    return (low(v), None)

def low_pass(kept, grad):
    return (grad,)

def back_keep(v):
    return (v, None)

def back_low(kept, grad):
    return (low(grad),)
low.defvjp(low_keep, low_pass)
low_back.defvjp(back_keep, back_low)

def rounded_both(v):
    return low(low_back(v))

def normalize(v, gain):
    return v * lax.rsqrt(lax.optimization_barrier(jnp.mean(v * v, axis=-1, keepdims=True)) + eps) * gain

def project(v, weight):
    return jnp.einsum('etd,df->etf', v, weight, precision=highest)

def buckets(length):
    place = jnp.arange(length, dtype=jnp.int32)
    distance = jnp.maximum(place[:, None] - place[None, :], 0)
    level = jnp.minimum(distance, 16)
    for edge in thresholds:
        level = level + (distance >= edge).astype(jnp.int32)
    return level

def attend(query, key, value, bias, mask):
    scores = jnp.einsum('lhd,shd->hls', query.reshape(query.shape[0], H, DH), key.reshape(key.shape[0], H, DH), precision=highest) + bias
    scores = low_back(jnp.where(mask[None], scores, -1e+30))
    top = lax.optimization_barrier(jnp.max(scores, axis=-1, keepdims=True))
    expo = jnp.exp(scores - top)
    probs = expo / lax.optimization_barrier(jnp.sum(expo, axis=-1, keepdims=True))
    mixed = jnp.einsum('hls,shd->lhd', low(probs), value.reshape(value.shape[0], H, DH), precision=highest)
    return mixed.reshape(mixed.shape[0], H * DH)

def layer(decoder, encoder, w_query, w_key, w_value, w_out, x_query, x_key, x_value, x_out, w_up, w_down, gains, table, target_lengths, source_lengths, live):
    level = buckets(TGT)
    bias = jnp.transpose(table[level], (2, 0, 1))
    place = jnp.arange(TGT, dtype=jnp.int32)
    source_place = jnp.arange(ENC, dtype=jnp.int32)
    causal = place[None, :] <= place[:, None]
    first = low(normalize(decoder, gains[0]))
    query = rounded_both(project(first, w_query))
    key = rounded_both(project(first, w_key))
    value = rounded_both(project(first, w_value))

    def self_one(item):
        one_q, one_k, one_v, length = item
        mask = causal & (place[None, :] < length)
        return attend(one_q, one_k, one_v, bias, mask)
    mixed = rounded_both(lax.map(jax.checkpoint(self_one), (query, key, value, target_lengths)))
    after_self = decoder + low_back(project(mixed, w_out))
    second = low(normalize(after_self, gains[1]))
    cross_q = rounded_both(project(second, x_query))
    cross_k = rounded_both(project(encoder, x_key))
    cross_v = rounded_both(project(encoder, x_value))

    def cross_one(item):
        one_q, one_k, one_v, length = item
        mask = jnp.broadcast_to(source_place[None, :] < length, (TGT, ENC))
        return attend(one_q, one_k, one_v, jnp.float32(0.0), mask)
    crossed = rounded_both(lax.map(jax.checkpoint(cross_one), (cross_q, cross_k, cross_v, source_lengths)))
    after_cross = after_self + low_back(project(crossed, x_out))
    third = low(normalize(after_cross, gains[2]))
    inner = low_back(project(third, w_up))
    active = low(jax.nn.gelu(inner))
    result = after_cross + low_back(project(active, w_down))
    return result * live[:, :, None]

def reference(decoder_in, encoder_out, self_query, self_key, self_value, self_output, cross_query, cross_key, cross_value, cross_output, hidden_in, hidden_out, norm_gains, bias_table, target_lengths, source_lengths, example_counts, cotangent):
    slots = jnp.arange(EXAMPLES, dtype=jnp.int32)
    owner = slots // EX_DEV
    present = slots % EX_DEV < example_counts[owner]
    place = jnp.arange(TGT, dtype=jnp.int32)
    live = (present[:, None] & (place[None, :] < target_lengths[:, None])).astype(jnp.float32)
    floats = [item.astype(jnp.float32) for item in (decoder_in, encoder_out, self_query, self_key, self_value, self_output, cross_query, cross_key, cross_value, cross_output, hidden_in, hidden_out, norm_gains, bias_table)]

    def forward(*params):
        return layer(*params, target_lengths, source_lengths, live)
    result, pullback = jax.vjp(forward, *floats)
    grads = pullback(cotangent.astype(jnp.float32))
    return (result.astype(jnp.bfloat16), grads[0], grads[1], grads[2], grads[3], grads[4], grads[5], grads[6], grads[7], grads[8], grads[9], grads[10], grads[11], grads[12], grads[13])
```

```python
import functools

import jax
import jax.numpy as jnp
from jax import lax
from jax.experimental import pallas as pl
from jax.experimental.pallas import tpu as pltpu
from jax.sharding import PartitionSpec as P

H = 12
AXES = ("dp", "fsdp")
MESH = pl.DeviceIdType.MESH
BF = jnp.bfloat16
F32 = jnp.float32


eps = 1e-06
thresholds = [19, 21, 24, 27, 31, 35, 40, 46, 52, 59, 67, 77, 87, 99, 113]


def normalize(v, gain):
    return v * lax.rsqrt(jnp.mean(v * v, axis=-1, keepdims=True) + eps) * gain


def norm_grad(v, gain, grad):
    _, pullback = jax.vjp(normalize, v, gain)
    return pullback(grad)


def gelu_grad(v, grad):
    _, pullback = jax.vjp(jax.nn.gelu, v)
    return pullback(grad)[0]


def project(v, weight):
    return jnp.einsum("btd,df->btf", v, weight, preferred_element_type=jnp.float32)


def project_back(grad, weight):
    return jnp.einsum("btf,df->btd", grad, weight, preferred_element_type=jnp.float32)


def outer_sum(v, grad):
    return jnp.einsum("btd,btf->df", v, grad, preferred_element_type=jnp.float32)


def split_heads(v):
    return v.reshape(v.shape[0], v.shape[1], H, v.shape[2] // H)


def join_heads(v):
    return v.reshape(v.shape[0], v.shape[1], v.shape[2] * v.shape[3])


def buckets(length):
    place = jnp.arange(length, dtype=jnp.int32)
    distance = jnp.maximum(place[:, None] - place[None, :], 0)
    level = jnp.minimum(distance, 16)
    for edge in thresholds:
        level = level + (distance >= edge).astype(jnp.int32)
    return level


def scores_of(query, key, bias, mask):
    scores = jnp.einsum("blhd,bshd->bhls", query, key, preferred_element_type=jnp.float32) + bias
    return jnp.where(mask, scores, -1e30)


def attention_forward(query, key, value, bias, mask):
    scores = scores_of(query, key, bias, mask)
    top = jnp.max(scores, axis=-1, keepdims=True)
    expo = jnp.exp(scores - top)
    total = jnp.sum(expo, axis=-1, keepdims=True)
    probs = (expo / total).astype(jnp.bfloat16)
    mixed = jnp.einsum("bhls,bshd->blhd", probs, value, preferred_element_type=jnp.float32)
    return (join_heads(mixed).astype(jnp.bfloat16), top + jnp.log(total))


def attention_backward(query, key, value, bias, mask, logsum, d_out):
    probs = jnp.exp(scores_of(query, key, bias, mask) - logsum)
    d_probs = jnp.einsum("blhd,bshd->bhls", d_out, value, preferred_element_type=jnp.float32)
    delta = jnp.sum(d_probs * probs, axis=-1, keepdims=True)
    d_scores = (probs * (d_probs - delta)).astype(jnp.bfloat16)
    d_query = jnp.einsum(
        "bhls,bshd->blhd", d_scores, key, preferred_element_type=jnp.float32
    ).astype(jnp.bfloat16)
    d_key = jnp.einsum(
        "bhls,blhd->bshd", d_scores, query, preferred_element_type=jnp.float32
    ).astype(jnp.bfloat16)
    d_value = jnp.einsum(
        "bhls,blhd->bshd", probs.astype(jnp.bfloat16), d_out, preferred_element_type=jnp.float32
    ).astype(jnp.bfloat16)
    return (join_heads(d_query), join_heads(d_key), join_heads(d_value), d_scores)


class Place:
    def __init__(self):
        d = lax.axis_index("dp")
        self.z = lax.axis_index("fsdp")
        self.c = lax.rem(d, 2)
        self.x = lax.rem(lax.div(d, 2), 2)
        self.y = lax.div(d, 4)

    def dev(self, y, x, c, z):
        return ((y * 2 + x) * 2 + c, z)

    @property
    def core(self):
        return self.dev(self.y, self.x, 1 - self.c, self.z)

    @property
    def xn(self):
        return self.dev(self.y, 1 - self.x, self.c, self.z)

    @property
    def yn(self):
        return self.dev(1 - self.y, self.x, self.c, self.z)

    def zn(self, step):
        return self.dev(self.y, self.x, self.c, lax.rem(self.z + step, 4))

    def enter(self):
        bar = pltpu.get_barrier_semaphore()
        others = [self.core, self.xn, self.yn] + [self.zn(s) for s in (1, 2, 3)]
        for other in others:
            pl.semaphore_signal(bar, inc=1, device_id=other, device_id_type=MESH)
        pl.semaphore_wait(bar, len(others))


def rcopy(src, dst, sems, index, device):
    send, recv = sems
    return pltpu.make_async_remote_copy(
        src_ref=src,
        dst_ref=dst,
        send_sem=send.at[index],
        recv_sem=recv.at[index],
        device_id=device,
        device_id_type=MESH,
    )


class Small:
    def __init__(self, here, buf, sems):
        self.here, self.buf, self.sems = here, buf, sems

    def pair(self, stage):
        h = self.here
        return rcopy(
            self.buf.at[2 * stage], self.buf.at[2 * stage + 1], self.sems, stage,
            (h.core, h.xn, h.yn)[stage],
        )

    def start(self, stage):
        if stage < 3:
            self.pair(stage).start()
        else:
            for s in (1, 2, 3):
                self.last(s).start()

    def last(self, s):
        return rcopy(self.buf.at[6], self.buf.at[6 + s], self.sems, 2 + s, self.here.zn(s))

    def finish(self, stage):
        b = self.buf
        if stage < 3:
            self.pair(stage).wait()
            b[2 * stage + 2] = b[2 * stage] + b[2 * stage + 1]
        else:
            for s in (1, 2, 3):
                self.last(s).wait()

    def total(self):
        b = self.buf
        return b[6] + b[7] + b[8] + b[9]


class Gather:
    def __init__(self, here, sq, up, down, zland, zsems, sems):
        self.here, self.sq, self.up, self.down = here, sq, up, down
        self.zland, self.zsems, self.sems = zland, zsems, sems

    def blk(self, u, y, x, c):
        if u < 8:
            return self.sq.at[u, y, x, c]
        if u < 12:
            return self.up.at[u - 8, y, x, c]
        return self.down.at[y, x, c, u - 12]

    def blks(self, u, c):
        if u < 8:
            return self.sq.at[u, :, :, c]
        if u < 12:
            return self.up.at[u - 8, :, :, c]
        return self.down.at[:, :, c, u - 12]

    def zcopy(self, k, s):
        h = self.here
        if k < 6:
            ref = self.zland.at[k, h.z]
        else:
            ref = self.down.at[h.y, h.x, h.c, h.z]
        return rcopy(ref, ref, self.zsems, (k, s - 1), h.zn(s))

    def z_start(self, k):
        if k > 6:
            return
        for s in (1, 2, 3):
            self.zcopy(k, s).start()

    def z_finish(self, k):
        h = self.here
        if k <= 6:
            for s in (1, 2, 3):
                self.zcopy(k, s).wait_recv()
        if k < 6:
            slabs = self.zland[k].astype(F32)
            for half in (0, 1):
                rows = jnp.concatenate(
                    [slabs[z, 24 * half : 24 * half + 24] for z in range(4)], axis=0
                ).astype(BF)
                u = 2 * k + half
                if u < 8:
                    self.sq[u, h.y, h.x, h.c] = rows
                else:
                    self.up[u - 8, h.y, h.x, h.c] = rows
        for u in (2 * k, 2 * k + 1):
            self.first(u).start()
            self.second(u).start()

    def nbrs(self, u):
        h = self.here
        return (h.yn, h.xn) if u % 2 == 0 else (h.xn, h.yn)

    def own(self, u):
        h = self.here
        return self.blk(u, h.y, h.x, h.c)

    def got(self, u):
        h = self.here
        return self.blk(u, 1 - h.y, h.x, h.c) if u % 2 == 0 else self.blk(u, h.y, 1 - h.x, h.c)

    def first(self, u):
        return rcopy(self.own(u), self.own(u), self.sems, (u, 0), self.nbrs(u)[0])

    def second(self, u):
        return rcopy(self.own(u), self.own(u), self.sems, (u, 1), self.nbrs(u)[1])

    def third(self, u):
        return rcopy(self.got(u), self.got(u), self.sems, (u, 2), self.nbrs(u)[1])

    def cross(self, u):
        ref = self.blks(u, self.here.c)
        return rcopy(ref, ref, self.sems, (u, 3), self.here.core)

    def mid(self, k):
        for u in (2 * k, 2 * k + 1):
            self.first(u).wait_recv()
            self.third(u).start()

    def core(self, k):
        for u in (2 * k, 2 * k + 1):
            self.second(u).wait_recv()
            self.third(u).wait_recv()
            self.cross(u).start()

    def done(self, k):
        for u in (2 * k, 2 * k + 1):
            self.cross(u).wait_recv()

    def drain(self):
        for k in range(7):
            for s in (1, 2, 3):
                self.zcopy(k, s).wait_send()
        for u in range(16):
            self.first(u).wait_send()
            self.second(u).wait_send()
            self.third(u).wait_send()
            self.cross(u).wait_send()


def gather_kernel(*refs):
    squares, up_in, down_in, gain_in = refs[:8], refs[8], refs[9], refs[10]
    sq, up, down, gain_out = refs[11:15]
    zland, small, zs, zr, ss, sr, ms, mr = refs[15:]
    here = Place()
    for k in range(4):
        zland[k, here.z] = jnp.concatenate(
            [squares[2 * k][...].astype(F32), squares[2 * k + 1][...].astype(F32)], axis=0
        ).astype(BF)
    for k in range(2):
        zland[4 + k, here.z] = jnp.concatenate(
            [up_in[:, 768 * n : 768 * n + 768].astype(F32) for n in (2 * k, 2 * k + 1)], axis=0
        ).astype(BF)
    down[here.y, here.x, here.c, here.z] = down_in[...]
    small[0] = gain_in[...]
    here.enter()
    g = Gather(here, sq, up, down, zland, (zs, zr), (ss, sr))
    m = Small(here, small, (ms, mr))
    g.z_start(0)
    g.z_start(1)
    g.z_start(2)
    m.start(0)
    for t in range(8 + 3):
        if t < 8:
            g.z_finish(t)
            if t + 3 < 8:
                g.z_start(t + 3)
        if t < 4:
            m.finish(t)
            if t < 3:
                m.start(t + 1)
        if 0 <= t - 1 < 8:
            g.mid(t - 1)
        if 0 <= t - 2 < 8:
            g.core(t - 2)
        if 0 <= t - 3 < 8:
            g.done(t - 3)
    g.drain()
    gain_out[...] = m.total()


VM = pl.BlockSpec(memory_space=pltpu.VMEM)


def gather_call(squares, up, down, gains):
    return pl.pallas_call(
        gather_kernel,
        out_shape=(
            jax.ShapeDtypeStruct((8, 2, 2, 2, 96, 768), BF),
            jax.ShapeDtypeStruct((4, 2, 2, 2, 96, 768), BF),
            jax.ShapeDtypeStruct((2, 2, 2, 4, 96, 768), BF),
            jax.ShapeDtypeStruct((8, 768), F32),
        ),
        in_specs=[VM] * 11,
        out_specs=(VM,) * 4,
        scratch_shapes=[
            pltpu.VMEM((6, 4, 48, 768), BF),
            pltpu.VMEM((10, 8, 768), F32),
            pltpu.SemaphoreType.DMA((7, 3)),
            pltpu.SemaphoreType.DMA((7, 3)),
            pltpu.SemaphoreType.DMA((16, 4)),
            pltpu.SemaphoreType.DMA((16, 4)),
            pltpu.SemaphoreType.DMA((6,)),
            pltpu.SemaphoreType.DMA((6,)),
        ],
        compiler_params=pltpu.CompilerParams(
            collective_id=0, has_side_effects=True, vmem_limit_bytes=50 * 2**20
        ),
        name="gather",
    )(*squares, up, down, gains)


class Scatter:
    def __init__(self, here, gsq, gup, gdown, rc, s1, r1, r2, zsend, zland, sems, zsems):
        self.here, self.gsq, self.gup, self.gdown = here, gsq, gup, gdown
        self.rc, self.s1, self.r1, self.r2 = rc, s1, r1, r2
        self.zsend, self.zland, self.sems, self.zsems = zsend, zland, sems, zsems

    def blks(self, u, c):
        if u < 8:
            return self.gsq.at[u, :, :, c]
        if u < 12:
            return self.gup.at[u - 8, :, :, c]
        return self.gdown.at[:, :, c, u - 12]

    def cross(self, u):
        return rcopy(
            self.blks(u, 1 - self.here.c), self.rc.at[u], self.sems, (u, 0), self.here.core
        )

    def first(self, u):
        h = self.here
        if u % 2 == 0:
            src, device = self.s1.at[u, :, 1 - h.x], h.xn
        else:
            src, device = self.s1.at[u, 1 - h.y], h.yn
        return rcopy(src, self.r1.at[u], self.sems, (u, 1), device)

    def second(self, u):
        h = self.here
        if u % 2 == 0:
            src, device = self.r1.at[u, 1 - h.y], h.yn
        else:
            src, device = self.r1.at[u, 1 - h.x], h.xn
        return rcopy(src, self.r2.at[u], self.sems, (u, 2), device)

    def start(self, k):
        for u in (2 * k, 2 * k + 1):
            self.cross(u).start()

    def one(self, k):
        h = self.here
        for u in (2 * k, 2 * k + 1):
            self.cross(u).wait_recv()
            self.s1[u] = (self.blks(u, h.c)[...].astype(F32) + self.rc[u].astype(F32)).astype(BF)
            self.first(u).start()

    def two(self, k):
        h = self.here
        for u in (2 * k, 2 * k + 1):
            self.first(u).wait_recv()
            mine = self.s1[u, :, h.x] if u % 2 == 0 else self.s1[u, h.y]
            self.r1[u] = (mine.astype(F32) + self.r1[u].astype(F32)).astype(BF)
            self.second(u).start()

    def three(self, k):
        h = self.here
        sums = []
        for u in (2 * k, 2 * k + 1):
            self.second(u).wait_recv()
            at = h.y if u % 2 == 0 else h.x
            sums.append(self.r1[u, at].astype(F32) + self.r2[u].astype(F32))
        if k < 6:
            for z in range(4):
                self.zsend[k, z] = jnp.concatenate(
                    [item[24 * z : 24 * z + 24] for item in sums], axis=0
                ).astype(BF)
        else:
            for half in (0, 1):
                for part in (0, 1):
                    self.zsend[6 + part, 2 * (k - 6) + half] = sums[half][
                        48 * part : 48 * part + 48
                    ].astype(BF)
        if k < 6:
            self.z_start(k)
        if k == 7:
            self.z_start(6)
            self.z_start(7)

    def zcopy(self, k, s):
        h = self.here
        return rcopy(
            self.zsend.at[k, lax.rem(h.z + s, 4)], self.zland.at[k, s - 1], self.zsems,
            (k, s - 1), h.zn(s),
        )

    def z_start(self, k):
        for s in (1, 2, 3):
            self.zcopy(k, s).start()

    def last(self, k):
        h = self.here
        for s in (1, 2, 3):
            self.zcopy(k, s).wait_recv()
        total = self.zsend[k, h.z].astype(F32)
        for s in (1, 2, 3):
            total = total + self.zland[k, s - 1].astype(F32)
        return total

    def drain(self):
        for u in range(16):
            self.cross(u).wait_send()
            self.first(u).wait_send()
            self.second(u).wait_send()
        for k in range(8):
            for s in (1, 2, 3):
                self.zcopy(k, s).wait_send()


ORDER = (6, 7, 4, 5, 3, 2, 1, 0)


def scatter_kernel(*refs):
    gsq, gup, gdown, small_in = refs[:4]
    outs, up_out, down_out, small_out = refs[4:12], refs[12], refs[13], refs[14]
    rc, s1, r1, r2, zsend, zland, small, ss, sr, zs, zr, ms, mr = refs[15:]
    here = Place()
    small[0] = small_in[...]
    here.enter()
    r = Scatter(here, gsq, gup, gdown, rc, s1, r1, r2, zsend, zland, (ss, sr), (zs, zr))
    m = Small(here, small, (ms, mr))
    m.start(0)
    r.start(ORDER[0])
    r.start(ORDER[1])

    def finish(k):
        total = r.last(k)
        if k < 4:
            outs[2 * k][...] = total[:24]
            outs[2 * k + 1][...] = total[24:]
        elif k < 6:
            up_out[:, 1536 * (k - 4) : 1536 * (k - 4) + 768] = total[:24]
            up_out[:, 1536 * (k - 4) + 768 : 1536 * (k - 4) + 1536] = total[24:]
        else:
            down_out[48 * (k - 6) : 48 * (k - 6) + 48, :] = total

    for t in range(8 + 4):
        if t + 2 < 8:
            r.start(ORDER[t + 2])
        if t < 8:
            r.one(ORDER[t])
        if 0 <= t - 1 < 8:
            r.two(ORDER[t - 1])
        if 0 <= t - 2 < 8:
            r.three(ORDER[t - 2])
        if t < 4:
            m.finish(t)
            if t < 3:
                m.start(t + 1)
        if 0 <= t - 4 < 8:
            finish(ORDER[t - 4])
    r.drain()
    small_out[...] = m.total()


def scatter_call(gsq, gup, gdown, small):
    return pl.pallas_call(
        scatter_kernel,
        out_shape=(jax.ShapeDtypeStruct((24, 768), F32),) * 8
        + (
            jax.ShapeDtypeStruct((24, 3072), F32),
            jax.ShapeDtypeStruct((96, 768), F32),
            jax.ShapeDtypeStruct((8, 768), F32),
        ),
        in_specs=[VM] * 4,
        out_specs=(VM,) * 11,
        scratch_shapes=[
            pltpu.VMEM((16, 2, 2, 96, 768), BF),
            pltpu.VMEM((16, 2, 2, 96, 768), BF),
            pltpu.VMEM((16, 2, 96, 768), BF),
            pltpu.VMEM((16, 96, 768), BF),
            pltpu.VMEM((8, 4, 48, 768), BF),
            pltpu.VMEM((8, 3, 48, 768), BF),
            pltpu.VMEM((10, 8, 768), F32),
            pltpu.SemaphoreType.DMA((16, 3)),
            pltpu.SemaphoreType.DMA((16, 3)),
            pltpu.SemaphoreType.DMA((8, 3)),
            pltpu.SemaphoreType.DMA((8, 3)),
            pltpu.SemaphoreType.DMA((6,)),
            pltpu.SemaphoreType.DMA((6,)),
        ],
        compiler_params=pltpu.CompilerParams(
            collective_id=1, has_side_effects=True, vmem_limit_bytes=60 * 2**20
        ),
        name="scatter",
    )(gsq, gup, gdown, small)


def gather_all(by_kernel, squares, hidden_in, hidden_out, norm_gains):
    if not by_kernel:
        gathered = [lax.all_gather(item, AXES, axis=0, tiled=True) for item in squares]
        up = lax.all_gather(hidden_in, AXES, axis=0, tiled=True)
        down = lax.all_gather(hidden_out, AXES, axis=0, tiled=True)
        gains = lax.all_gather(norm_gains, AXES, axis=1, tiled=True)
        return (gathered, up, down, gains.astype(F32))
    rows, width = squares[0].shape
    index = lax.axis_index("dp") * 4 + lax.axis_index("fsdp")
    spread = lax.dynamic_update_slice(
        jnp.zeros((8, width), F32), norm_gains.astype(F32), (0, index * norm_gains.shape[1])
    )
    sq, up, down, gains = gather_call(squares, hidden_in, hidden_out, spread)
    gathered = [sq[m].reshape(width, width) for m in range(8)]
    up = jnp.transpose(up.reshape(4, width, width), (1, 0, 2)).reshape(width, 4 * width)
    return (gathered, up, down.reshape(4 * width, width), gains[:3])


def scatter_all(by_kernel, squares, up, down, gain_terms, table_term):
    if not by_kernel:
        sums = [
            lax.psum_scatter(item, AXES, scatter_dimension=0, tiled=True)
            for item in (*squares, up, down)
        ]
        gains = lax.psum_scatter(gain_terms, AXES, scatter_dimension=1, tiled=True)
        return (*sums, gains, lax.psum(table_term, AXES))
    width = squares[0].shape[0]
    gsq = jnp.stack([item.astype(BF) for item in squares]).reshape(8, 2, 2, 2, 96, width)
    gup = jnp.transpose(up.astype(BF).reshape(width, 4, width), (1, 0, 2))
    gup = gup.reshape(4, 2, 2, 2, 96, width)
    gdown = down.astype(BF).reshape(2, 2, 2, 4, 96, width)
    flat = jnp.pad(table_term.reshape(1, -1), ((0, 0), (0, width - table_term.size)))
    small = jnp.concatenate([gain_terms, flat, jnp.zeros((4, width), F32)], axis=0)
    *sums, small = scatter_call(gsq, gup, gdown, small)
    index = lax.axis_index("dp") * 4 + lax.axis_index("fsdp")
    gains = lax.dynamic_slice(small, (0, index * 24), (3, 24))
    table = small[3, : table_term.size].reshape(table_term.shape)
    return (*sums, gains, table)


def local(
    by_kernel,
    decoder_in,
    encoder_out,
    self_query,
    self_key,
    self_value,
    self_output,
    cross_query,
    cross_key,
    cross_value,
    cross_output,
    hidden_in,
    hidden_out,
    norm_gains,
    bias_table,
    target_lengths,
    source_lengths,
    example_counts,
    cotangent,
):
    squares, w_up, w_down, gains = gather_all(
        by_kernel,
        (
            self_query,
            self_key,
            self_value,
            self_output,
            cross_query,
            cross_key,
            cross_value,
            cross_output,
        ),
        hidden_in,
        hidden_out,
        norm_gains,
    )
    w_query, w_key, w_value, w_out, x_query, x_key, x_value, x_out = squares
    slots = jnp.arange(decoder_in.shape[0], dtype=jnp.int32)
    length = decoder_in.shape[1]
    source = encoder_out.shape[1]
    place = jnp.arange(length, dtype=jnp.int32)
    source_place = jnp.arange(source, dtype=jnp.int32)
    live = (
        (slots < example_counts[0])[:, None] & (place[None, :] < target_lengths[:, None])
    ).astype(jnp.float32)[:, :, None]
    self_mask = (place[None, :] <= place[:, None])[None, None] & (
        place[None, None, None, :] < target_lengths[:, None, None, None]
    )
    cross_mask = source_place[None, None, None, :] < source_lengths[:, None, None, None]
    onehot = (
        buckets(length)[:, :, None] == jnp.arange(bias_table.shape[0], dtype=jnp.int32)
    ).astype(jnp.bfloat16)
    bias = jnp.einsum("lsn,nh->hls", onehot, bias_table, preferred_element_type=jnp.float32)
    inputs = decoder_in.astype(jnp.float32)
    first = normalize(inputs, gains[0]).astype(jnp.bfloat16)
    query = project(first, w_query).astype(jnp.bfloat16)
    key = project(first, w_key).astype(jnp.bfloat16)
    value = project(first, w_value).astype(jnp.bfloat16)
    mixed, logsum_self = attention_forward(
        split_heads(query), split_heads(key), split_heads(value), bias, self_mask
    )
    after_self = inputs + project(mixed, w_out)
    second = normalize(after_self, gains[1]).astype(jnp.bfloat16)
    cross_q = project(second, x_query).astype(jnp.bfloat16)
    cross_k = project(encoder_out, x_key).astype(jnp.bfloat16)
    cross_v = project(encoder_out, x_value).astype(jnp.bfloat16)
    crossed, logsum_cross = attention_forward(
        split_heads(cross_q), split_heads(cross_k), split_heads(cross_v), 0.0, cross_mask
    )
    after_cross = after_self + project(crossed, x_out)
    third = normalize(after_cross, gains[2]).astype(jnp.bfloat16)
    inner = project(third, w_up)
    active = jax.nn.gelu(inner).astype(jnp.bfloat16)
    result = after_cross + project(active, w_down)
    layer_out = (result * live).astype(jnp.bfloat16)
    d_result = cotangent.astype(jnp.float32) * live
    d_branch = d_result.astype(jnp.bfloat16)
    grad_down = outer_sum(active, d_branch)
    d_inner = gelu_grad(inner, project_back(d_branch, w_down)).astype(jnp.bfloat16)
    grad_up = outer_sum(third, d_inner)
    d_cross, gain_three = norm_grad(after_cross, gains[2], project_back(d_inner, w_up))
    d_cross = d_cross + d_result
    d_branch = d_cross.astype(jnp.bfloat16)
    grad_x_out = outer_sum(crossed, d_branch)
    d_crossed = project_back(d_branch, x_out).astype(jnp.bfloat16)
    dq_cross, dk_cross, dv_cross, unused = attention_backward(
        split_heads(cross_q),
        split_heads(cross_k),
        split_heads(cross_v),
        0.0,
        cross_mask,
        logsum_cross,
        split_heads(d_crossed),
    )
    grad_x_query = outer_sum(second, dq_cross)
    grad_x_key = outer_sum(encoder_out, dk_cross)
    grad_x_value = outer_sum(encoder_out, dv_cross)
    grad_encoder = project_back(dk_cross, x_key) + project_back(dv_cross, x_value)
    d_self, gain_two = norm_grad(after_self, gains[1], project_back(dq_cross, x_query))
    d_self = d_self + d_cross
    d_branch = d_self.astype(jnp.bfloat16)
    grad_w_out = outer_sum(mixed, d_branch)
    d_mixed = project_back(d_branch, w_out).astype(jnp.bfloat16)
    dq_self, dk_self, dv_self, d_scores = attention_backward(
        split_heads(query),
        split_heads(key),
        split_heads(value),
        bias,
        self_mask,
        logsum_self,
        split_heads(d_mixed),
    )
    d_bias = jnp.sum(d_scores, axis=0, dtype=jnp.float32)
    table_term = jnp.einsum(
        "hls,lsn->nh", d_bias, onehot.astype(jnp.float32), precision=lax.Precision.HIGHEST
    )
    grad_w_query = outer_sum(first, dq_self)
    grad_w_key = outer_sum(first, dk_self)
    grad_w_value = outer_sum(first, dv_self)
    d_first = (
        project_back(dq_self, w_query)
        + project_back(dk_self, w_key)
        + project_back(dv_self, w_value)
    )
    d_inputs, gain_one = norm_grad(inputs, gains[0], d_first)
    grad_decoder = d_inputs + d_self
    gain_terms = jnp.stack([gain_one, gain_two, gain_three], axis=0)
    sums = scatter_all(
        by_kernel,
        (
            grad_w_query,
            grad_w_key,
            grad_w_value,
            grad_w_out,
            grad_x_query,
            grad_x_key,
            grad_x_value,
            grad_x_out,
        ),
        grad_up,
        grad_down,
        gain_terms,
        table_term,
    )
    return (layer_out, grad_decoder, grad_encoder, *sums)


def solution(mesh):
    rows = P(AXES, None)
    slots = P(AXES, None, None)
    flat = P(AXES)
    gains = P(None, AXES)
    by_kernel = mesh.shape["dp"] == 8 and mesh.shape["fsdp"] == 4
    return jax.shard_map(
        functools.partial(local, by_kernel),
        mesh=mesh,
        in_specs=(slots, slots) + (rows,) * 10 + (gains, P(), flat, flat, flat, slots),
        out_specs=(slots, slots, slots) + (rows,) * 10 + (gains, P()),
        check_vma=False,
    )
```

```python
import functools

import jax
import jax.numpy as jnp
from jax import lax
from jax.experimental import pallas as pl
from jax.experimental.pallas import tpu as pltpu
from jax.sharding import PartitionSpec as P

H = 12
AXES = ("dp", "fsdp")
MESH = pl.DeviceIdType.MESH
BF = jnp.bfloat16
F32 = jnp.float32


eps = 1e-06
thresholds = [19, 21, 24, 27, 31, 35, 40, 46, 52, 59, 67, 77, 87, 99, 113]


def normalize(v, gain):
    return v * lax.rsqrt(jnp.mean(v * v, axis=-1, keepdims=True) + eps) * gain


def norm_grad(v, gain, grad):
    _, pullback = jax.vjp(normalize, v, gain)
    return pullback(grad)


def gelu_grad(v, grad):
    _, pullback = jax.vjp(jax.nn.gelu, v)
    return pullback(grad)[0]


def project(v, weight):
    return jnp.einsum("btd,df->btf", v, weight, preferred_element_type=jnp.float32)


def project_back(grad, weight):
    return jnp.einsum("btf,df->btd", grad, weight, preferred_element_type=jnp.float32)


def outer_sum(v, grad):
    return jnp.einsum("btd,btf->df", v, grad, preferred_element_type=jnp.float32)


def split_heads(v):
    return v.reshape(v.shape[0], v.shape[1], H, v.shape[2] // H)


def join_heads(v):
    return v.reshape(v.shape[0], v.shape[1], v.shape[2] * v.shape[3])


def flat_rows(items):
    return tuple((item.reshape(-1) for item in items))


def unflat_rows(items, widths):
    return tuple((item.reshape(-1, width) for item, width in zip(items, widths)))


def buckets(length):
    place = jnp.arange(length, dtype=jnp.int32)
    distance = jnp.maximum(place[:, None] - place[None, :], 0)
    level = jnp.minimum(distance, 16)
    for edge in thresholds:
        level = level + (distance >= edge).astype(jnp.int32)
    return level


def scores_of(query, key, bias, mask):
    scores = jnp.einsum("blhd,bshd->bhls", query, key, preferred_element_type=jnp.float32) + bias
    return jnp.where(mask, scores, -1e30)


def attention_forward(query, key, value, bias, mask):
    scores = scores_of(query, key, bias, mask)
    top = jnp.max(scores, axis=-1, keepdims=True)
    expo = jnp.exp(scores - top)
    total = jnp.sum(expo, axis=-1, keepdims=True)
    probs = (expo / total).astype(jnp.bfloat16)
    mixed = jnp.einsum("bhls,bshd->blhd", probs, value, preferred_element_type=jnp.float32)
    return (join_heads(mixed).astype(jnp.bfloat16), top + jnp.log(total))


def attention_backward(query, key, value, bias, mask, logsum, d_out):
    probs = jnp.exp(scores_of(query, key, bias, mask) - logsum)
    d_probs = jnp.einsum("blhd,bshd->bhls", d_out, value, preferred_element_type=jnp.float32)
    delta = jnp.sum(d_probs * probs, axis=-1, keepdims=True)
    d_scores = (probs * (d_probs - delta)).astype(jnp.bfloat16)
    d_query = jnp.einsum(
        "bhls,bshd->blhd", d_scores, key, preferred_element_type=jnp.float32
    ).astype(jnp.bfloat16)
    d_key = jnp.einsum(
        "bhls,blhd->bshd", d_scores, query, preferred_element_type=jnp.float32
    ).astype(jnp.bfloat16)
    d_value = jnp.einsum(
        "bhls,blhd->bshd", probs.astype(jnp.bfloat16), d_out, preferred_element_type=jnp.float32
    ).astype(jnp.bfloat16)
    return (join_heads(d_query), join_heads(d_key), join_heads(d_value), d_scores)


class Place:
    def __init__(self):
        d = lax.axis_index("dp")
        self.z = lax.axis_index("fsdp")
        self.c = lax.rem(d, 2)
        self.x = lax.rem(lax.div(d, 2), 2)
        self.y = lax.div(d, 4)

    def dev(self, y, x, c, z):
        return ((y * 2 + x) * 2 + c, z)

    @property
    def core(self):
        return self.dev(self.y, self.x, 1 - self.c, self.z)

    @property
    def xn(self):
        return self.dev(self.y, 1 - self.x, self.c, self.z)

    @property
    def yn(self):
        return self.dev(1 - self.y, self.x, self.c, self.z)

    def zn(self, step):
        return self.dev(self.y, self.x, self.c, lax.rem(self.z + step, 4))

    def enter(self):
        bar = pltpu.get_barrier_semaphore()
        others = [self.core, self.xn, self.yn] + [self.zn(s) for s in (1, 2, 3)]
        for other in others:
            pl.semaphore_signal(bar, inc=1, device_id=other, device_id_type=MESH)
        pl.semaphore_wait(bar, len(others))


def rcopy(src, dst, sems, index, device):
    send, recv = sems
    return pltpu.make_async_remote_copy(
        src_ref=src,
        dst_ref=dst,
        send_sem=send.at[index],
        recv_sem=recv.at[index],
        device_id=device,
        device_id_type=MESH,
    )


class Small:
    def __init__(self, here, buf, sems):
        self.here, self.buf, self.sems = here, buf, sems

    def pair(self, stage):
        h = self.here
        return rcopy(
            self.buf.at[2 * stage], self.buf.at[2 * stage + 1], self.sems, stage,
            (h.core, h.xn, h.yn)[stage],
        )

    def start(self, stage):
        if stage < 3:
            self.pair(stage).start()
        else:
            for s in (1, 2, 3):
                self.last(s).start()

    def last(self, s):
        return rcopy(self.buf.at[6], self.buf.at[6 + s], self.sems, 2 + s, self.here.zn(s))

    def finish(self, stage):
        b = self.buf
        if stage < 3:
            self.pair(stage).wait()
            b[2 * stage + 2] = b[2 * stage] + b[2 * stage + 1]
        else:
            for s in (1, 2, 3):
                self.last(s).wait()

    def total(self):
        b = self.buf
        return b[6] + b[7] + b[8] + b[9]


class Gather:
    def __init__(self, here, sq, up, down, zland, zsems, sems):
        self.here, self.sq, self.up, self.down = here, sq, up, down
        self.zland, self.zsems, self.sems = zland, zsems, sems

    def blk(self, u, y, x, c):
        if u < 8:
            return self.sq.at[u, y, x, c]
        if u < 12:
            return self.up.at[u - 8, y, x, c]
        return self.down.at[y, x, c, u - 12]

    def blks(self, u, c):
        if u < 8:
            return self.sq.at[u, :, :, c]
        if u < 12:
            return self.up.at[u - 8, :, :, c]
        return self.down.at[:, :, c, u - 12]

    def zcopy(self, k, s):
        h = self.here
        if k < 6:
            ref = self.zland.at[k, h.z]
        else:
            ref = self.down.at[h.y, h.x, h.c, h.z]
        return rcopy(ref, ref, self.zsems, (k, s - 1), h.zn(s))

    def z_start(self, k):
        if k > 6:
            return
        for s in (1, 2, 3):
            self.zcopy(k, s).start()

    def z_finish(self, k):
        h = self.here
        if k <= 6:
            for s in (1, 2, 3):
                self.zcopy(k, s).wait_recv()
        if k < 6:
            slabs = self.zland[k].astype(F32)
            for half in (0, 1):
                rows = jnp.concatenate(
                    [slabs[z, 24 * half : 24 * half + 24] for z in range(4)], axis=0
                ).astype(BF)
                u = 2 * k + half
                if u < 8:
                    self.sq[u, h.y, h.x, h.c] = rows
                else:
                    self.up[u - 8, h.y, h.x, h.c] = rows
        for u in (2 * k, 2 * k + 1):
            self.first(u).start()
            self.second(u).start()

    def nbrs(self, u):
        h = self.here
        return (h.yn, h.xn) if u % 2 == 0 else (h.xn, h.yn)

    def own(self, u):
        h = self.here
        return self.blk(u, h.y, h.x, h.c)

    def got(self, u):
        h = self.here
        return self.blk(u, 1 - h.y, h.x, h.c) if u % 2 == 0 else self.blk(u, h.y, 1 - h.x, h.c)

    def first(self, u):
        return rcopy(self.own(u), self.own(u), self.sems, (u, 0), self.nbrs(u)[0])

    def second(self, u):
        return rcopy(self.own(u), self.own(u), self.sems, (u, 1), self.nbrs(u)[1])

    def third(self, u):
        return rcopy(self.got(u), self.got(u), self.sems, (u, 2), self.nbrs(u)[1])

    def cross(self, u):
        ref = self.blks(u, self.here.c)
        return rcopy(ref, ref, self.sems, (u, 3), self.here.core)

    def mid(self, k):
        for u in (2 * k, 2 * k + 1):
            self.first(u).wait_recv()
            self.third(u).start()

    def core(self, k):
        for u in (2 * k, 2 * k + 1):
            self.second(u).wait_recv()
            self.third(u).wait_recv()
            self.cross(u).start()

    def done(self, k):
        for u in (2 * k, 2 * k + 1):
            self.cross(u).wait_recv()

    def drain(self):
        for k in range(7):
            for s in (1, 2, 3):
                self.zcopy(k, s).wait_send()
        for u in range(16):
            self.first(u).wait_send()
            self.second(u).wait_send()
            self.third(u).wait_send()
            self.cross(u).wait_send()


class Scatter:
    def __init__(self, here, gsq, gup, gdown, rc, s1, r1, r2, zsend, zland, sems, zsems):
        self.here, self.gsq, self.gup, self.gdown = here, gsq, gup, gdown
        self.rc, self.s1, self.r1, self.r2 = rc, s1, r1, r2
        self.zsend, self.zland, self.sems, self.zsems = zsend, zland, sems, zsems

    def blks(self, u, c):
        if u < 8:
            return self.gsq.at[u, :, :, c]
        if u < 12:
            return self.gup.at[u - 8, :, :, c]
        return self.gdown.at[:, :, c, u - 12]

    def cross(self, u):
        return rcopy(
            self.blks(u, 1 - self.here.c), self.rc.at[u], self.sems, (u, 0), self.here.core
        )

    def first(self, u):
        h = self.here
        if u % 2 == 0:
            src, device = self.s1.at[u, :, 1 - h.x], h.xn
        else:
            src, device = self.s1.at[u, 1 - h.y], h.yn
        return rcopy(src, self.r1.at[u], self.sems, (u, 1), device)

    def second(self, u):
        h = self.here
        if u % 2 == 0:
            src, device = self.r1.at[u, 1 - h.y], h.yn
        else:
            src, device = self.r1.at[u, 1 - h.x], h.xn
        return rcopy(src, self.r2.at[u], self.sems, (u, 2), device)

    def start(self, k):
        for u in (2 * k, 2 * k + 1):
            self.cross(u).start()

    def one(self, k):
        h = self.here
        for u in (2 * k, 2 * k + 1):
            self.cross(u).wait_recv()
            self.s1[u] = (self.blks(u, h.c)[...].astype(F32) + self.rc[u].astype(F32)).astype(BF)
            self.first(u).start()

    def two(self, k):
        h = self.here
        for u in (2 * k, 2 * k + 1):
            self.first(u).wait_recv()
            mine = self.s1[u, :, h.x] if u % 2 == 0 else self.s1[u, h.y]
            self.r1[u] = (mine.astype(F32) + self.r1[u].astype(F32)).astype(BF)
            self.second(u).start()

    def three(self, k):
        h = self.here
        sums = []
        for u in (2 * k, 2 * k + 1):
            self.second(u).wait_recv()
            at = h.y if u % 2 == 0 else h.x
            sums.append(self.r1[u, at].astype(F32) + self.r2[u].astype(F32))
        if k < 6:
            for z in range(4):
                self.zsend[k, z] = jnp.concatenate(
                    [item[24 * z : 24 * z + 24] for item in sums], axis=0
                ).astype(BF)
        else:
            for half in (0, 1):
                for part in (0, 1):
                    self.zsend[6 + part, 2 * (k - 6) + half] = sums[half][
                        48 * part : 48 * part + 48
                    ].astype(BF)
        if k < 6:
            self.z_start(k)
        if k == 7:
            self.z_start(6)
            self.z_start(7)

    def zcopy(self, k, s):
        h = self.here
        return rcopy(
            self.zsend.at[k, lax.rem(h.z + s, 4)], self.zland.at[k, s - 1], self.zsems,
            (k, s - 1), h.zn(s),
        )

    def z_start(self, k):
        for s in (1, 2, 3):
            self.zcopy(k, s).start()

    def last(self, k):
        h = self.here
        for s in (1, 2, 3):
            self.zcopy(k, s).wait_recv()
        total = self.zsend[k, h.z].astype(F32)
        for s in (1, 2, 3):
            total = total + self.zland[k, s - 1].astype(F32)
        return total

    def drain(self):
        for u in range(16):
            self.cross(u).wait_send()
            self.first(u).wait_send()
            self.second(u).wait_send()
        for k in range(8):
            for s in (1, 2, 3):
                self.zcopy(k, s).wait_send()


def mm(a, b):
    return lax.dot_general(a, b, (((1,), (0,)), ((), ())), preferred_element_type=F32)


def mt(a, b):
    return lax.dot_general(a, b, (((1,), (1,)), ((), ())), preferred_element_type=F32)


def tm(a, b):
    return lax.dot_general(a, b, (((0,), (0,)), ((), ())), preferred_element_type=F32)


def iota(shape, axis):
    return lax.broadcasted_iota(jnp.int32, shape, axis)


def lanes(hp):
    return pl.ds(pl.multiple_of(hp * 128, 128), 128)


def both(q):
    low = iota(q.shape, 1) < 64
    zero = jnp.zeros_like(q)
    return jnp.concatenate([jnp.where(low, q, zero), jnp.where(low, zero, q)], axis=0)


def merge(pair):
    rows = pair.shape[0] // 2
    low = iota((rows, 128), 1) < 64
    return jnp.where(low, pair[:rows], pair[rows:]).astype(BF)


def probs(key, query, bias, mask):
    scores = mt(key, query)
    if bias is not None:
        scores = scores + bias.astype(F32)
    scores = jnp.where(mask, scores, -1e30)
    expo = jnp.exp(scores - jnp.max(scores, axis=0, keepdims=True))
    return expo * (1.0 / jnp.sum(expo, axis=0, keepdims=True))


def rms(v):
    return lax.rsqrt(jnp.mean(v * v, axis=-1, keepdims=True) + eps)


def norm_back(v, gain, grad):
    r = rms(v)
    scaled = grad * gain
    inner = jnp.mean(scaled * v, axis=-1, keepdims=True)
    return r * scaled - v * (r * r * r * inner), jnp.sum(grad * v * r, axis=0, keepdims=True)


def gelu_both(v):
    c = 0.7978845608028654
    square = v * v
    t = jnp.tanh(c * v * (1.0 + 0.044715 * square))
    half = 0.5 * (1.0 + t)
    slope = half + 0.5 * v * (1.0 - t * t) * (c * (1.0 + 3 * 0.044715 * square))
    return v * half, slope


class FusedScatter(Scatter):
    def __init__(self, here, up, down, gup, gdown, rc, r1, r2, zsend, zland, sems, zsems):
        self.here, self.up, self.down, self.gup, self.gdown = here, up, down, gup, gdown
        self.rc, self.r1, self.r2 = rc, r1, r2
        self.zsend, self.zland, self.sems, self.zsems = zsend, zland, sems, zsems

    def blks(self, u, c):
        if u < 4:
            return self.up.at[u, :, :, c]
        if u < 8:
            return self.down.at[:, :, c, u - 4]
        if u < 12:
            return self.gup.at[u - 8, :, :, c]
        return self.gdown.at[:, :, c, u - 12]

    def put(self, u, y, cols, value):
        value = value.astype(BF).reshape(2, 2, 96, 256)
        if u < 4:
            self.up[u, y, :, :, :, cols] = value
        else:
            self.down[y, :, :, u - 4, :, cols] = value

    def cross(self, u):
        return rcopy(
            self.blks(u, 1 - self.here.c), self.rc.at[u % 8], self.sems, (u, 0), self.here.core
        )

    def sub(self, u, y, x):
        h = self.here
        if u < 4:
            return self.up.at[u, y, x, h.c]
        if u < 8:
            return self.down.at[y, x, h.c, u - 4]
        if u < 12:
            return self.gup.at[u - 8, y, x, h.c]
        return self.gdown.at[y, x, h.c, u - 12]

    def first(self, u):
        h = self.here
        every = slice(None)
        if u % 2 == 0:
            src, device = self.sub(u, every, 1 - h.x), h.xn
        else:
            src, device = self.sub(u, 1 - h.y, every), h.yn
        return rcopy(src, self.r1.at[u], self.sems, (u, 1), device)

    def one(self, k):
        h = self.here
        for u in (2 * k, 2 * k + 1):
            self.cross(u).wait_recv()
            mine = self.blks(u, h.c)
            mine[...] = (mine[...].astype(F32) + self.rc[u % 8].astype(F32)).astype(BF)
            self.first(u).start()

    def two(self, k):
        h = self.here
        every = slice(None)
        for u in (2 * k, 2 * k + 1):
            self.first(u).wait_recv()
            mine = self.sub(u, every, h.x) if u % 2 == 0 else self.sub(u, h.y, every)
            self.r1[u] = (mine[...].astype(F32) + self.r1[u].astype(F32)).astype(BF)
            self.second(u).start()


def layer_kernel(*refs):
    squares, up_in, down_in, gain_in, table_in = refs[:8], refs[8], refs[9], refs[10], refs[11]
    tlen, slen, count, x_in, cot, enc = refs[12:18]
    layer_out, g_dec, g_enc, g_sq, g_up, g_down, g_gain, g_table = refs[18:26]
    (
        sq, up, down, gup, gdown, rc, r1, r2, zland, zland2, small, small2,
        bias, h1, h2, h3, q1, k1, v1, o1, q2, o2, k2, v2, g, gp, x1, x2, stage,
        zs, zr, ss, sr, ms, mr, rzs, rzr, rss, rsr, m2s, m2r, out_sem, credit,
    ) = refs[26:]
    here = Place()
    index = (here.y * 4 + here.x * 2 + here.c) * 4 + here.z
    for k in range(4):
        zland[k, here.z] = jnp.concatenate(
            [squares[2 * k][...].astype(F32), squares[2 * k + 1][...].astype(F32)], axis=0
        ).astype(BF)
    for k in range(2):
        zland[4 + k, here.z] = jnp.concatenate(
            [up_in[:, 768 * n : 768 * n + 768].astype(F32) for n in (2 * k, 2 * k + 1)], axis=0
        ).astype(BF)
    down[here.y, here.x, here.c, here.z] = down_in[...]
    spot = (iota((24, 768), 1) == iota((24, 768), 0) + 24 * index).astype(BF)
    small[0] = jnp.zeros((8, 768), F32)
    small[0, 0:3] = mm(gain_in[...], spot)
    here.enter()
    ga = Gather(here, sq, up, down, zland, (zs, zr), (ss, sr))
    m = Small(here, small, (ms, mr))
    rs = FusedScatter(
        here, up, down, gup, gdown, rc, r1, r2, zland, zland2, (rss, rsr), (rzs, rzr)
    )
    m2 = Small(here, small2, (m2s, m2r))

    def tick(t):
        if t < 8:
            ga.z_finish(t)
            if t + 3 < 8:
                ga.z_start(t + 3)
        if t < 4:
            m.finish(t)
            if t < 3:
                m.start(t + 1)
        if 0 <= t - 1 < 8:
            ga.mid(t - 1)
        if 0 <= t - 2 < 8:
            ga.core(t - 2)
        if 0 <= t - 3 < 8:
            ga.done(t - 3)

    def weight(u):
        return sq[u].reshape(768, 768)

    def columns(u, n):
        return sq[u, :, :, :, :, 256 * n : 256 * n + 256].reshape(768, 256)

    ga.z_start(0)
    ga.z_start(1)
    ga.z_start(2)
    m.start(0)

    def bucket_hot(rows_are_buckets):
        shape = (32, 128) if rows_are_buckets else (128, 32)
        distance = iota(shape, 1 if rows_are_buckets else 0)
        level = jnp.minimum(distance, 16)
        for edge in thresholds:
            level = level + (distance >= edge).astype(jnp.int32)
        return level == iota(shape, 0 if rows_are_buckets else 1)

    by_distance = tm(table_in[...], bucket_hot(True).astype(BF))
    for head in range(12):
        row = jnp.broadcast_to(by_distance[head : head + 1, :], (128, 128))
        bias[head // 2, :, 128 * (head % 2) : 128 * (head % 2) + 128] = pltpu.roll(
            row, 0, 1, stride=1, stride_axis=0
        ).astype(BF)

    key_place, target_place = iota((128, 256), 0), iota((128, 256), 1) & 127
    causal = key_place <= target_place
    source_place = iota((512, 256), 0)

    def self_mask(ex):
        return causal & (key_place < tlen[ex])

    def cross_mask(ex):
        return source_place < slen[ex]

    row_place = iota((256, 1), 0)
    live = (
        ((row_place < 128) & (row_place < tlen[0]) & (0 < count[0]))
        | ((row_place >= 128) & (row_place - 128 < tlen[1]) & (1 < count[0]))
    ).astype(F32)

    for t in range(4):
        tick(t)
    gains = m.total()
    gain = [gains[i : i + 1, :] for i in range(3)]

    first = x_in[...].astype(F32)
    h1[...] = (first * rms(first) * gain[0]).astype(BF)
    for n in range(3):
        cols = slice(256 * n, 256 * n + 256)
        q1[:, cols] = mm(h1[...], columns(0, n)).astype(BF)
        k1[:, cols] = mm(h1[...], columns(1, n)).astype(BF)
    tick(4)
    for n in range(3):
        cols = slice(256 * n, 256 * n + 256)
        v1[:, cols] = mm(h1[...], columns(2, n)).astype(BF)

    def self_forward(hp, carry):
        for ex in range(2):
            rows = slice(128 * ex, 128 * ex + 128)
            query = both(q1[rows, lanes(hp)])
            p = probs(k1[rows, lanes(hp)], query, bias[hp], self_mask(ex)).astype(BF)
            o1[rows, lanes(hp)] = merge(tm(p, v1[rows, lanes(hp)]))
        return carry

    lax.fori_loop(0, 6, self_forward, 0)
    tick(5)
    x1[...] = x_in[...].astype(F32) + mm(o1[...], weight(3))
    h2[...] = (x1[...] * rms(x1[...]) * gain[1]).astype(BF)

    def encode(r, carry):
        rows = pl.ds(pl.multiple_of(r * 256, 256), 256)
        for n in range(3):
            cols = slice(256 * n, 256 * n + 256)
            k2[rows, cols] = mm(enc[rows, :], columns(4, n)).astype(BF)
            v2[rows, cols] = mm(enc[rows, :], columns(5, n)).astype(BF)
        return carry

    lax.fori_loop(0, 4, encode, 0)
    tick(6)
    for n in range(3):
        cols = slice(256 * n, 256 * n + 256)
        q2[:, cols] = mm(h2[...], columns(6, n)).astype(BF)

    def cross_forward(hp, carry):
        for ex in range(2):
            rows = slice(128 * ex, 128 * ex + 128)
            keys = slice(512 * ex, 512 * ex + 512)
            query = both(q2[rows, lanes(hp)])
            p = probs(k2[keys, lanes(hp)], query, None, cross_mask(ex)).astype(BF)
            o2[rows, lanes(hp)] = merge(tm(p, v2[keys, lanes(hp)]))
        return carry

    lax.fori_loop(0, 3, cross_forward, 0)
    tick(7)
    lax.fori_loop(3, 6, cross_forward, 0)
    x2[...] = x1[...] + mm(o2[...], weight(7))
    h3[...] = (x2[...] * rms(x2[...]) * gain[2]).astype(BF)
    tick(8)
    def hidden(n, carry):
        for part in range(3):
            lo = 256 * part
            a = mm(h3[...], up[n, :, :, :, :, lo : lo + 256].reshape(768, 256))
            active, slope = gelu_both(a)
            cols = pl.ds(pl.multiple_of(768 * n + lo, 256), 256)
            g[:, cols] = active.astype(BF)
            gp[:, cols] = slope.astype(BF)
        return carry

    lax.fori_loop(0, 4, hidden, 0)
    tick(9)

    def keep_gain(i, term):
        for j in range(6):
            small2[0, 6 * i + j : 6 * i + j + 1, :] = term[:, 128 * j : 128 * j + 128]

    def df(cols=slice(None)):
        return (cot[:, cols].astype(F32) * live).astype(BF)

    def wide(e):
        return pl.ds(pl.multiple_of(768 * e, 256), 768)

    def grad_down(e, carry):
        turned = g[:, wide(e)].T
        for n in range(3):
            cols = slice(256 * n, 256 * n + 256)
            grad = mm(turned, df(cols)).astype(BF)
            gdown[lax.div(e, 2), lax.rem(e, 2), :, :, :, cols] = grad.reshape(2, 4, 96, 256)
        return carry

    lax.fori_loop(0, 4, grad_down, 0)
    rs.start(6)
    rs.start(7)
    tick(10)

    def down_block(e):
        return down[lax.div(e, 2), lax.rem(e, 2)].reshape(768, 768)

    def inner_grad(e, carry):
        dg = mt(df(), down_block(e))
        gp[:, wide(e)] = (dg * gp[:, wide(e)].astype(F32)).astype(BF)
        return carry

    lax.fori_loop(0, 2, inner_grad, 0)
    rs.one(6)
    lax.fori_loop(2, 4, inner_grad, 0)
    rs.one(7)

    def grad_up(n, carry):
        turned = h3[...].T
        for part in range(3):
            cols = slice(256 * part, 256 * part + 256)
            source = pl.ds(pl.multiple_of(768 * n + 256 * part, 256), 256)
            grad = mm(turned, gp[:, source]).astype(BF)
            gup[n, :, :, :, :, cols] = grad.reshape(2, 2, 2, 96, 256)
        return carry

    lax.fori_loop(0, 2, grad_up, 0)
    rs.start(4)
    lax.fori_loop(2, 4, grad_up, 0)
    rs.start(5)
    stage[0] = x2[...]

    def result(e, carry):
        stage[0] += mm(g[:, wide(e)], down_block(e))
        return carry

    lax.fori_loop(0, 4, result, 0)
    layer_out[...] = (stage[0] * live).astype(BF)
    rs.one(4)
    stage[0] = jnp.zeros((256, 768), F32)

    def inner_back(n, carry):
        stage[0] += mt(gp[:, wide(n)], up[n].reshape(768, 768))
        return carry

    lax.fori_loop(0, 4, inner_back, 0)
    d_norm, gain_three = norm_back(x2[...], gain[2], stage[0])
    keep_gain(2, gain_three)
    x2[...] = cot[...].astype(F32) * live + d_norm
    rs.one(5)
    pl.semaphore_signal(credit, inc=1, device_id=here.core, device_id_type=MESH)
    rs.two(6)
    ga.drain()

    def put_grads(value, rows, pairs):
        def half_rows(y, carry):
            turned = value[:, pl.ds(pl.multiple_of(384 * y, 128), 384)].T
            for u, ref in pairs:
                for n in range(3):
                    cols = slice(256 * n, 256 * n + 256)
                    rs.put(u, y, cols, mm(turned, ref[:, cols]))
            return carry

        lax.fori_loop(0, 2, half_rows, 0)

    h3[...] = x2[...].astype(BF)
    put_grads(o2, 256, ((7, h3),))
    rs.two(7)
    o2[...] = mt(h3[...], weight(7)).astype(BF)

    def cross_backward(hp, carry):
        for ex in range(2):
            rows = slice(128 * ex, 128 * ex + 128)
            keys = slice(512 * ex, 512 * ex + 512)
            query, d_out = both(q2[rows, lanes(hp)]), both(o2[rows, lanes(hp)])
            key, value = k2[keys, lanes(hp)], v2[keys, lanes(hp)]
            p = probs(key, query, None, cross_mask(ex))
            dp = mt(value, d_out)
            delta = jnp.sum(dp * p, axis=0, keepdims=True)
            ds = (p * (dp - delta)).astype(BF)
            q2[rows, lanes(hp)] = merge(tm(ds, key))
            k2[keys, lanes(hp)] = mm(ds, query).astype(BF)
            v2[keys, lanes(hp)] = mm(p.astype(BF), d_out).astype(BF)
        return carry

    lax.fori_loop(0, 2, cross_backward, 0)
    rs.two(4)
    rs.three(6)
    rs.three(7)
    lax.fori_loop(2, 4, cross_backward, 0)
    rs.two(5)
    rs.three(4)
    lax.fori_loop(4, 6, cross_backward, 0)
    put_grads(h2, 256, ((6, q2),))
    pl.semaphore_wait(credit, 1)
    rs.start(3)
    rs.three(5)
    put_grads(enc, 1024, ((4, k2), (5, v2)))
    rs.start(2)

    def finish(k):
        total = rs.last(k)
        if k < 4:
            g_sq[2 * k] = total[:24]
            g_sq[2 * k + 1] = total[24:]
        elif k < 6:
            g_up[:, 1536 * (k - 4) : 1536 * (k - 4) + 768] = total[:24]
            g_up[:, 1536 * (k - 4) + 768 : 1536 * (k - 4) + 1536] = total[24:]
        else:
            g_down[48 * (k - 6) : 48 * (k - 6) + 48, :] = total

    rs.one(3)
    finish(6)
    finish(7)
    d_norm, gain_two = norm_back(x1[...], gain[1], mt(q2[...], weight(6)))
    keep_gain(1, gain_two)
    x2[...] = x2[...] + d_norm
    rs.one(2)
    rs.two(3)
    finish(4)

    h3[...] = x2[...].astype(BF)
    put_grads(o1, 256, ((3, h3),))
    o1[...] = mt(h3[...], weight(3)).astype(BF)
    rs.two(2)
    turn = (iota((128, 256), 0) + (iota((128, 256), 1) & 127) == 127).astype(BF)

    def self_backward(hp, carry):
        scores = []
        for ex in range(2):
            rows = slice(128 * ex, 128 * ex + 128)
            query, d_out = both(q1[rows, lanes(hp)]), both(o1[rows, lanes(hp)])
            key, value = k1[rows, lanes(hp)], v1[rows, lanes(hp)]
            p = probs(key, query, bias[hp], self_mask(ex))
            dp = mt(value, d_out)
            delta = jnp.sum(dp * p, axis=0, keepdims=True)
            ds = (p * (dp - delta)).astype(BF)
            q1[rows, lanes(hp)] = merge(tm(ds, key))
            k1[rows, lanes(hp)] = mm(ds, query).astype(BF)
            v1[rows, lanes(hp)] = mm(p.astype(BF), d_out).astype(BF)
            scores.append(ds)
        pair = mm(turn, jnp.concatenate(scores, axis=0))
        for head in range(2):
            skew = pltpu.roll(pair[:, 128 * head : 128 * head + 128], 0, 1, stride=1, stride_axis=0)
            small2[0, pl.ds(18 + 2 * hp + head, 1), :] = jnp.sum(skew, axis=0, keepdims=True)
        return carry

    lax.fori_loop(0, 3, self_backward, 0)
    rs.three(3)
    lax.fori_loop(3, 6, self_backward, 0)
    finish(5)
    put_grads(h1, 256, ((2, v1), (0, q1), (1, k1)))
    rs.start(1)
    rs.start(0)
    rs.three(2)
    stage[0] = jnp.zeros((256, 768), F32)

    def first_back(y, carry):
        cols = pl.ds(pl.multiple_of(384 * y, 128), 384)
        for u, ref in ((0, q1), (1, k1), (2, v1)):
            stage[0, :, cols] += mt(ref[...], sq[u, y].reshape(384, 768))
        return carry

    lax.fori_loop(0, 2, first_back, 0)
    rs.one(1)
    d_norm, gain_one = norm_back(x_in[...].astype(F32), gain[0], stage[0])
    g_dec[...] = x2[...] + d_norm
    keep_gain(0, gain_one)
    small2[0, 30:32, :] = jnp.zeros((2, 128), F32)
    m2.start(0)
    rs.one(0)
    finish(3)
    rs.two(1)
    m2.finish(0)
    m2.start(1)

    def out_copy(r):
        return pltpu.make_async_copy(
            stage.at[lax.rem(r, 2)],
            g_enc.at[pl.ds(pl.multiple_of(256 * r, 256), 256)],
            out_sem.at[r],
        )

    def encoder_grad(r, carry):
        rows = pl.ds(pl.multiple_of(256 * r, 256), 256)
        slot = lax.rem(r, 2)
        for y in range(2):
            cols = slice(384 * y, 384 * y + 384)
            stage[slot, :, cols] = mt(k2[rows, :], sq[4, y].reshape(384, 768))
            stage[slot, :, cols] += mt(v2[rows, :], sq[5, y].reshape(384, 768))
        out_copy(r).start()
        return carry

    lax.fori_loop(0, 2, encoder_grad, 0)
    rs.two(0)
    m2.finish(1)
    m2.start(2)
    rs.three(1)
    finish(2)
    m2.finish(2)
    m2.start(3)
    rs.three(0)
    out_copy(0).wait()
    out_copy(1).wait()
    lax.fori_loop(2, 4, encoder_grad, 0)
    finish(1)
    m2.finish(3)
    reduced = m2.total()
    sums = jnp.concatenate(
        [
            jnp.concatenate([reduced[6 * i + j : 6 * i + j + 1, :] for j in range(6)], axis=1)
            for i in range(3)
        ],
        axis=0,
    )
    pick = (iota((768, 24), 0) == iota((768, 24), 1) + 24 * index).astype(F32)
    g_gain[...] = lax.dot_general(
        sums, pick, (((1,), (0,)), ((), ())), preferred_element_type=F32,
        precision=lax.Precision.HIGHEST,
    )
    distance = (iota((32, 128), 1) + 1) & 127
    level = jnp.minimum(distance, 16)
    for edge in thresholds:
        level = level + (distance >= edge).astype(jnp.int32)
    hot = (level == iota((32, 128), 0)).astype(F32)
    g_table[...] = lax.dot_general(
        hot, reduced[18:30, :], (((1,), (1,)), ((), ())), preferred_element_type=F32,
        precision=lax.Precision.HIGHEST,
    )
    finish(0)
    rs.drain()
    out_copy(2).wait()
    out_copy(3).wait()


VM = pl.BlockSpec(memory_space=pltpu.VMEM)
SM = pl.BlockSpec(memory_space=pltpu.SMEM)
ANY = pl.BlockSpec(memory_space=pl.ANY)


def layer_call(*args):
    shape = jax.ShapeDtypeStruct
    sems = [(7, 3)] * 2 + [(16, 4)] * 2 + [(6,)] * 2 + [(8, 3)] * 2 + [(16, 3)] * 2 + [(6,)] * 2
    half = lambda *dims: pltpu.VMEM(dims, BF)
    return pl.pallas_call(
        layer_kernel,
        out_shape=(
            shape((256, 768), BF),
            shape((256, 768), F32),
            shape((1024, 768), F32),
            shape((8, 24, 768), F32),
            shape((24, 3072), F32),
            shape((96, 768), F32),
            shape((3, 24), F32),
            shape((32, 12), F32),
        ),
        in_specs=[VM] * 12 + [SM] * 3 + [VM] * 3,
        out_specs=(VM, VM, ANY) + (VM,) * 5,
        scratch_shapes=[
            half(8, 2, 2, 2, 96, 768),
            half(4, 2, 2, 2, 96, 768),
            half(2, 2, 2, 4, 96, 768),
            half(4, 2, 2, 2, 96, 768),
            half(2, 2, 2, 4, 96, 768),
            half(8, 2, 2, 96, 768),
            half(16, 2, 96, 768),
            half(16, 96, 768),
            half(8, 4, 48, 768),
            half(8, 3, 48, 768),
            pltpu.VMEM((10, 8, 768), F32),
            pltpu.VMEM((10, 32, 128), F32),
            half(6, 128, 256),
            *[half(256, 768)] * 3,
            *[half(256, 768)] * 4,
            *[half(256, 768)] * 2,
            *[half(1024, 768)] * 2,
            *[half(256, 3072)] * 2,
            *[pltpu.VMEM((256, 768), F32)] * 2,
            pltpu.VMEM((2, 256, 768), F32),
            *[pltpu.SemaphoreType.DMA(dims) for dims in sems],
            pltpu.SemaphoreType.DMA((4,)),
            pltpu.SemaphoreType.REGULAR,
        ],
        compiler_params=pltpu.CompilerParams(
            collective_id=0, has_side_effects=True, vmem_limit_bytes=64 * 2**20 - 2**16
        ),
        name="layer",
    )(*args)


def by_kernel(
    decoder_in,
    encoder_out,
    self_query,
    self_key,
    self_value,
    self_output,
    cross_query,
    cross_key,
    cross_value,
    cross_output,
    hidden_in,
    hidden_out,
    norm_gains,
    bias_table,
    target_lengths,
    source_lengths,
    example_counts,
    cotangent,
):
    out, g_dec, g_enc, g_sq, g_up, g_down, g_gain, g_table = layer_call(
        self_query,
        self_key,
        self_value,
        self_output,
        cross_key,
        cross_value,
        cross_query,
        cross_output,
        hidden_in,
        hidden_out,
        norm_gains,
        bias_table,
        target_lengths,
        source_lengths,
        example_counts,
        decoder_in.reshape(256, 768),
        cotangent.reshape(256, 768),
        encoder_out.reshape(1024, 768),
    )
    return (
        out.reshape(decoder_in.shape),
        g_dec.reshape(decoder_in.shape),
        g_enc.reshape(encoder_out.shape),
        g_sq[0],
        g_sq[1],
        g_sq[2],
        g_sq[3],
        g_sq[6],
        g_sq[4],
        g_sq[5],
        g_sq[7],
        g_up,
        g_down,
        g_gain,
        g_table,
    )


def plain(
    decoder_in,
    encoder_out,
    self_query,
    self_key,
    self_value,
    self_output,
    cross_query,
    cross_key,
    cross_value,
    cross_output,
    hidden_in,
    hidden_out,
    norm_gains,
    bias_table,
    target_lengths,
    source_lengths,
    example_counts,
    cotangent,
):
    gathered = (
        lax.all_gather(self_query, AXES, axis=0, tiled=True),
        lax.all_gather(self_key, AXES, axis=0, tiled=True),
        lax.all_gather(self_value, AXES, axis=0, tiled=True),
        lax.all_gather(self_output, AXES, axis=0, tiled=True),
        lax.all_gather(cross_query, AXES, axis=0, tiled=True),
        lax.all_gather(cross_key, AXES, axis=0, tiled=True),
        lax.all_gather(cross_value, AXES, axis=0, tiled=True),
        lax.all_gather(cross_output, AXES, axis=0, tiled=True),
        lax.all_gather(hidden_in, AXES, axis=0, tiled=True),
        lax.all_gather(hidden_out, AXES, axis=0, tiled=True),
        lax.all_gather(norm_gains, AXES, axis=1, tiled=True),
    )
    w_query, w_key, w_value, w_out, x_query, x_key, x_value, x_out, w_up, w_down, gain_all = (
        gathered
    )
    slots = jnp.arange(decoder_in.shape[0], dtype=jnp.int32)
    length = decoder_in.shape[1]
    source = encoder_out.shape[1]
    width = decoder_in.shape[2]
    hidden_width = hidden_in.shape[1]
    place = jnp.arange(length, dtype=jnp.int32)
    source_place = jnp.arange(source, dtype=jnp.int32)
    live = (
        (slots < example_counts[0])[:, None] & (place[None, :] < target_lengths[:, None])
    ).astype(jnp.float32)[:, :, None]
    self_mask = (place[None, :] <= place[:, None])[None, None] & (
        place[None, None, None, :] < target_lengths[:, None, None, None]
    )
    cross_mask = source_place[None, None, None, :] < source_lengths[:, None, None, None]
    onehot = (
        buckets(length)[:, :, None] == jnp.arange(bias_table.shape[0], dtype=jnp.int32)
    ).astype(jnp.bfloat16)
    bias = jnp.einsum("lsn,nh->hls", onehot, bias_table, preferred_element_type=jnp.float32)
    gains = gain_all.astype(jnp.float32)
    inputs = decoder_in.astype(jnp.float32)
    first = normalize(inputs, gains[0]).astype(jnp.bfloat16)
    query = project(first, w_query).astype(jnp.bfloat16)
    key = project(first, w_key).astype(jnp.bfloat16)
    value = project(first, w_value).astype(jnp.bfloat16)
    mixed, logsum_self = attention_forward(
        split_heads(query), split_heads(key), split_heads(value), bias, self_mask
    )
    after_self = inputs + project(mixed, w_out)
    second = normalize(after_self, gains[1]).astype(jnp.bfloat16)
    cross_q = project(second, x_query).astype(jnp.bfloat16)
    cross_k = project(encoder_out, x_key).astype(jnp.bfloat16)
    cross_v = project(encoder_out, x_value).astype(jnp.bfloat16)
    crossed, logsum_cross = attention_forward(
        split_heads(cross_q), split_heads(cross_k), split_heads(cross_v), 0.0, cross_mask
    )
    after_cross = after_self + project(crossed, x_out)
    third = normalize(after_cross, gains[2]).astype(jnp.bfloat16)
    inner = project(third, w_up)
    active = jax.nn.gelu(inner).astype(jnp.bfloat16)
    result = after_cross + project(active, w_down)
    layer_out = (result * live).astype(jnp.bfloat16)
    regathered = (
        lax.all_gather(self_query, AXES, axis=0, tiled=True),
        lax.all_gather(self_key, AXES, axis=0, tiled=True),
        lax.all_gather(self_value, AXES, axis=0, tiled=True),
        lax.all_gather(self_output, AXES, axis=0, tiled=True),
        lax.all_gather(cross_query, AXES, axis=0, tiled=True),
        lax.all_gather(cross_key, AXES, axis=0, tiled=True),
        lax.all_gather(cross_value, AXES, axis=0, tiled=True),
        lax.all_gather(cross_output, AXES, axis=0, tiled=True),
        lax.all_gather(hidden_in, AXES, axis=0, tiled=True),
        lax.all_gather(hidden_out, AXES, axis=0, tiled=True),
        lax.all_gather(norm_gains, AXES, axis=1, tiled=True),
    )
    w_query, w_key, w_value, w_out, x_query, x_key, x_value, x_out, w_up, w_down, gain_all = (
        regathered
    )
    gains = gain_all.astype(jnp.float32)
    d_result = cotangent.astype(jnp.float32) * live
    d_branch = d_result.astype(jnp.bfloat16)
    grad_down = outer_sum(active, d_branch)
    d_inner = gelu_grad(inner, project_back(d_branch, w_down)).astype(jnp.bfloat16)
    grad_up = outer_sum(third, d_inner)
    d_cross, gain_three = norm_grad(after_cross, gains[2], project_back(d_inner, w_up))
    d_cross = d_cross + d_result
    d_branch = d_cross.astype(jnp.bfloat16)
    grad_x_out = outer_sum(crossed, d_branch)
    d_crossed = project_back(d_branch, x_out).astype(jnp.bfloat16)
    dq_cross, dk_cross, dv_cross, unused = attention_backward(
        split_heads(cross_q),
        split_heads(cross_k),
        split_heads(cross_v),
        0.0,
        cross_mask,
        logsum_cross,
        split_heads(d_crossed),
    )
    grad_x_query = outer_sum(second, dq_cross)
    grad_x_key = outer_sum(encoder_out, dk_cross)
    grad_x_value = outer_sum(encoder_out, dv_cross)
    grad_encoder = project_back(dk_cross, x_key) + project_back(dv_cross, x_value)
    d_self, gain_two = norm_grad(after_self, gains[1], project_back(dq_cross, x_query))
    d_self = d_self + d_cross
    d_branch = d_self.astype(jnp.bfloat16)
    grad_w_out = outer_sum(mixed, d_branch)
    d_mixed = project_back(d_branch, w_out).astype(jnp.bfloat16)
    dq_self, dk_self, dv_self, d_scores = attention_backward(
        split_heads(query),
        split_heads(key),
        split_heads(value),
        bias,
        self_mask,
        logsum_self,
        split_heads(d_mixed),
    )
    d_bias = jnp.sum(d_scores, axis=0, dtype=jnp.float32)
    table_term = jnp.einsum(
        "hls,lsn->nh", d_bias, onehot.astype(jnp.float32), precision=lax.Precision.HIGHEST
    )
    grad_w_query = outer_sum(first, dq_self)
    grad_w_key = outer_sum(first, dk_self)
    grad_w_value = outer_sum(first, dv_self)
    d_first = (
        project_back(dq_self, w_query)
        + project_back(dk_self, w_key)
        + project_back(dv_self, w_value)
    )
    d_inputs, gain_one = norm_grad(inputs, gains[0], d_first)
    grad_decoder = d_inputs + d_self
    gain_terms = jnp.stack([gain_one, gain_two, gain_three], axis=1)
    flats = flat_rows(
        (
            grad_w_query,
            grad_w_key,
            grad_w_value,
            grad_w_out,
            grad_x_query,
            grad_x_key,
            grad_x_value,
            grad_x_out,
            grad_up,
            grad_down,
            gain_terms,
        )
    )
    summed = (
        lax.psum_scatter(flats[0], AXES, scatter_dimension=0, tiled=True),
        lax.psum_scatter(flats[1], AXES, scatter_dimension=0, tiled=True),
        lax.psum_scatter(flats[2], AXES, scatter_dimension=0, tiled=True),
        lax.psum_scatter(flats[3], AXES, scatter_dimension=0, tiled=True),
        lax.psum_scatter(flats[4], AXES, scatter_dimension=0, tiled=True),
        lax.psum_scatter(flats[5], AXES, scatter_dimension=0, tiled=True),
        lax.psum_scatter(flats[6], AXES, scatter_dimension=0, tiled=True),
        lax.psum_scatter(flats[7], AXES, scatter_dimension=0, tiled=True),
        lax.psum_scatter(flats[8], AXES, scatter_dimension=0, tiled=True),
        lax.psum_scatter(flats[9], AXES, scatter_dimension=0, tiled=True),
        lax.psum_scatter(flats[10], AXES, scatter_dimension=0, tiled=True),
    )
    shaped = unflat_rows(
        summed, (width, width, width, width, width, width, width, width, hidden_width, width, 3)
    )
    sums = shaped[:10] + (jnp.transpose(shaped[10]),)
    grad_table = lax.psum(table_term, AXES)
    return (
        layer_out,
        grad_decoder,
        grad_encoder,
        sums[0],
        sums[1],
        sums[2],
        sums[3],
        sums[4],
        sums[5],
        sums[6],
        sums[7],
        sums[8],
        sums[9],
        sums[10],
        grad_table,
    )


def solution(mesh):
    rows = P(AXES, None)
    slots = P(AXES, None, None)
    flat = P(AXES)
    gains = P(None, AXES)
    small = mesh.shape["dp"] == 8 and mesh.shape["fsdp"] == 4
    return jax.shard_map(
        by_kernel if small else plain,
        mesh=mesh,
        in_specs=(slots, slots) + (rows,) * 10 + (gains, P(), flat, flat, flat, slots),
        out_specs=(slots, slots, slots) + (rows,) * 10 + (gains, P()),
        check_vma=False,
    )
```

```python
import functools

import jax
import jax.numpy as jnp
from jax import lax
from jax.experimental import pallas as pl
from jax.experimental.pallas import tpu as pltpu
from jax.sharding import PartitionSpec as P

H = 12
AXES = ("dp", "fsdp")
MESH = pl.DeviceIdType.MESH
BF = jnp.bfloat16
F32 = jnp.float32


eps = 1e-06
thresholds = [19, 21, 24, 27, 31, 35, 40, 46, 52, 59, 67, 77, 87, 99, 113]


def normalize(v, gain):
    return v * lax.rsqrt(jnp.mean(v * v, axis=-1, keepdims=True) + eps) * gain


def norm_grad(v, gain, grad):
    _, pullback = jax.vjp(normalize, v, gain)
    return pullback(grad)


def gelu_grad(v, grad):
    _, pullback = jax.vjp(jax.nn.gelu, v)
    return pullback(grad)[0]


def project(v, weight):
    return jnp.einsum("btd,df->btf", v, weight, preferred_element_type=jnp.float32)


def project_back(grad, weight):
    return jnp.einsum("btf,df->btd", grad, weight, preferred_element_type=jnp.float32)


def outer_sum(v, grad):
    return jnp.einsum("btd,btf->df", v, grad, preferred_element_type=jnp.float32)


def split_heads(v):
    return v.reshape(v.shape[0], v.shape[1], H, v.shape[2] // H)


def join_heads(v):
    return v.reshape(v.shape[0], v.shape[1], v.shape[2] * v.shape[3])


def flat_rows(items):
    return tuple((item.reshape(-1) for item in items))


def unflat_rows(items, widths):
    return tuple((item.reshape(-1, width) for item, width in zip(items, widths)))


def buckets(length):
    place = jnp.arange(length, dtype=jnp.int32)
    distance = jnp.maximum(place[:, None] - place[None, :], 0)
    level = jnp.minimum(distance, 16)
    for edge in thresholds:
        level = level + (distance >= edge).astype(jnp.int32)
    return level


def scores_of(query, key, bias, mask):
    scores = jnp.einsum("blhd,bshd->bhls", query, key, preferred_element_type=jnp.float32) + bias
    return jnp.where(mask, scores, -1e30)


def attention_forward(query, key, value, bias, mask):
    scores = scores_of(query, key, bias, mask)
    top = jnp.max(scores, axis=-1, keepdims=True)
    expo = jnp.exp(scores - top)
    total = jnp.sum(expo, axis=-1, keepdims=True)
    probs = (expo / total).astype(jnp.bfloat16)
    mixed = jnp.einsum("bhls,bshd->blhd", probs, value, preferred_element_type=jnp.float32)
    return (join_heads(mixed).astype(jnp.bfloat16), top + jnp.log(total))


def attention_backward(query, key, value, bias, mask, logsum, d_out):
    probs = jnp.exp(scores_of(query, key, bias, mask) - logsum)
    d_probs = jnp.einsum("blhd,bshd->bhls", d_out, value, preferred_element_type=jnp.float32)
    delta = jnp.sum(d_probs * probs, axis=-1, keepdims=True)
    d_scores = (probs * (d_probs - delta)).astype(jnp.bfloat16)
    d_query = jnp.einsum(
        "bhls,bshd->blhd", d_scores, key, preferred_element_type=jnp.float32
    ).astype(jnp.bfloat16)
    d_key = jnp.einsum(
        "bhls,blhd->bshd", d_scores, query, preferred_element_type=jnp.float32
    ).astype(jnp.bfloat16)
    d_value = jnp.einsum(
        "bhls,blhd->bshd", probs.astype(jnp.bfloat16), d_out, preferred_element_type=jnp.float32
    ).astype(jnp.bfloat16)
    return (join_heads(d_query), join_heads(d_key), join_heads(d_value), d_scores)


class Place:
    def __init__(self):
        d = lax.axis_index("dp")
        self.z = lax.axis_index("fsdp")
        self.c = lax.rem(d, 2)
        self.x = lax.rem(lax.div(d, 2), 2)
        self.y = lax.div(d, 4)

    def dev(self, y, x, c, z):
        return ((y * 2 + x) * 2 + c, z)

    @property
    def core(self):
        return self.dev(self.y, self.x, 1 - self.c, self.z)

    @property
    def xn(self):
        return self.dev(self.y, 1 - self.x, self.c, self.z)

    @property
    def yn(self):
        return self.dev(1 - self.y, self.x, self.c, self.z)

    def zn(self, step):
        return self.dev(self.y, self.x, self.c, lax.rem(self.z + step, 4))

    def enter(self):
        bar = pltpu.get_barrier_semaphore()
        others = [self.core, self.xn, self.yn] + [self.zn(s) for s in (1, 2, 3)]
        for other in others:
            pl.semaphore_signal(bar, inc=1, device_id=other, device_id_type=MESH)
        pl.semaphore_wait(bar, len(others))


def rcopy(src, dst, sems, index, device):
    send, recv = sems
    return pltpu.make_async_remote_copy(
        src_ref=src,
        dst_ref=dst,
        send_sem=send.at[index],
        recv_sem=recv.at[index],
        device_id=device,
        device_id_type=MESH,
    )


class Small:
    def __init__(self, here, buf, sems):
        self.here, self.buf, self.sems = here, buf, sems

    def pair(self, stage):
        h = self.here
        return rcopy(
            self.buf.at[2 * stage], self.buf.at[2 * stage + 1], self.sems, stage,
            (h.core, h.xn, h.yn)[stage],
        )

    def start(self, stage):
        if stage < 3:
            self.pair(stage).start()
        else:
            for s in (1, 2, 3):
                self.last(s).start()

    def last(self, s):
        return rcopy(self.buf.at[6], self.buf.at[6 + s], self.sems, 2 + s, self.here.zn(s))

    def finish(self, stage):
        b = self.buf
        if stage < 3:
            self.pair(stage).wait()
            b[2 * stage + 2] = b[2 * stage] + b[2 * stage + 1]
        else:
            for s in (1, 2, 3):
                self.last(s).wait()

    def total(self):
        b = self.buf
        return b[6] + b[7] + b[8] + b[9]


EVERY = slice(None)


class Gather:
    def __init__(self, here, sq, up, down, zland, zsems, sems, bsems, bzsems, bcsems):
        self.here, self.sq, self.up, self.down = here, sq, up, down
        self.zland, self.zsems, self.sems = zland, zsems, sems
        self.bsems, self.bzsems, self.bcsems = bsems, bzsems, bcsems

    def blk(self, u, y, x, c):
        if u < 8:
            return self.sq.at[u, y, x, c]
        if u < 12:
            return self.up.at[u - 8, y, x, c]
        return self.down.at[y, x, c, 2 * (u - 12) : 2 * (u - 12) + 2, 0]

    def zcopy(self, k, s):
        h = self.here
        if k < 6:
            ref = self.zland.at[k, h.z]
        else:
            ref = self.down.at[h.y, h.x, h.c, h.z, 0]
        return rcopy(ref, ref, self.zsems, (k, s - 1), h.zn(s))

    def z_start(self, k):
        for s in (1, 2, 3):
            self.zcopy(k, s).start()

    def z_finish(self, k):
        h = self.here
        for s in (1, 2, 3):
            self.zcopy(k, s).wait_recv()
        if k < 6:
            slabs = self.zland[k].astype(F32)
            for half in (0, 1):
                rows = jnp.concatenate(
                    [slabs[z, 24 * half : 24 * half + 24] for z in range(4)], axis=0
                ).astype(BF).reshape(2, 48, 768)
                u = 2 * k + half
                if u < 8:
                    self.sq[u, h.y, h.x, h.c] = rows
                else:
                    self.up[u - 8, h.y, h.x, h.c] = rows
        for u in (2 * k, 2 * k + 1):
            self.first(u).start()
            self.second(u).start()

    def nbrs(self, u):
        h = self.here
        return (h.yn, h.xn) if u % 2 == 0 else (h.xn, h.yn)

    def own(self, u):
        h = self.here
        return self.blk(u, h.y, h.x, h.c)

    def got(self, u):
        h = self.here
        return self.blk(u, 1 - h.y, h.x, h.c) if u % 2 == 0 else self.blk(u, h.y, 1 - h.x, h.c)

    def first(self, u):
        return rcopy(self.own(u), self.own(u), self.sems, (u, 0), self.nbrs(u)[0])

    def second(self, u):
        return rcopy(self.own(u), self.own(u), self.sems, (u, 1), self.nbrs(u)[1])

    def third(self, u):
        return rcopy(self.got(u), self.got(u), self.sems, (u, 2), self.nbrs(u)[1])

    def cross(self, u):
        ref = self.blk(u, EVERY, EVERY, self.here.c)
        return rcopy(ref, ref, self.sems, (u, 3), self.here.core)

    def mid(self, k):
        for u in (2 * k, 2 * k + 1):
            self.first(u).wait_recv()
            self.third(u).start()

    def core(self, k):
        for u in (2 * k, 2 * k + 1):
            self.second(u).wait_recv()
            self.third(u).wait_recv()
            self.cross(u).start()

    def done(self, k):
        for u in (2 * k, 2 * k + 1):
            self.cross(u).wait_recv()

    def bblk(self, w, y, x):
        h = self.here
        return self.down.at[y, x, h.c, h.z, 1, :, 384 * w : 384 * w + 384]

    def bfirst(self, w):
        h = self.here
        ref = self.bblk(w, h.y, h.x)
        return rcopy(ref, ref, self.bsems, (w, 0), self.nbrs(w)[0])

    def bsecond(self, w):
        h = self.here
        ref = self.bblk(w, h.y, h.x)
        return rcopy(ref, ref, self.bsems, (w, 1), self.nbrs(w)[1])

    def bthird(self, w):
        h = self.here
        ref = self.bblk(w, 1 - h.y, h.x) if w == 0 else self.bblk(w, h.y, 1 - h.x)
        return rcopy(ref, ref, self.bsems, (w, 2), self.nbrs(w)[1])

    def b_start(self):
        for w in (0, 1):
            self.bfirst(w).start()
            self.bsecond(w).start()

    def b_mid(self):
        for w in (0, 1):
            self.bfirst(w).wait_recv()
            self.bthird(w).start()

    def b_got(self):
        for w in (0, 1):
            self.bsecond(w).wait_recv()
            self.bthird(w).wait_recv()

    def bz(self, p, s):
        h = self.here
        ref = self.down.at[p // 2, p % 2, h.c, h.z, 1]
        return rcopy(ref, ref, self.bzsems, (p, s - 1), h.zn(s))

    def bz_start(self, p):
        for s in (1, 2, 3):
            self.bz(p, s).start()

    def bcross(self, y):
        ref = self.down.at[y, :, self.here.c, :, 1]
        return rcopy(ref, ref, self.bcsems, y, self.here.core)

    def b_core(self, y):
        for p in (2 * y, 2 * y + 1):
            for s in (1, 2, 3):
                self.bz(p, s).wait_recv()
        self.bcross(y).start()

    def b_done(self):
        for y in (0, 1):
            self.bcross(y).wait_recv()

    def drain(self):
        for k in range(7):
            for s in (1, 2, 3):
                self.zcopy(k, s).wait_send()
        for u in range(14):
            self.first(u).wait_send()
            self.second(u).wait_send()
            self.third(u).wait_send()
            self.cross(u).wait_send()
        for w in (0, 1):
            self.bfirst(w).wait_send()
            self.bsecond(w).wait_send()
            self.bthird(w).wait_send()
            self.bcross(w).wait_send()
        for p in range(4):
            for s in (1, 2, 3):
                self.bz(p, s).wait_send()


class Scatter:
    def __init__(
        self, here, up, down, gup, gdown, rc, r1, r2, zsend, zland, brest, bzland, br1, br2,
        sems, zsems, bzsems, bsems,
    ):
        self.here, self.up, self.down, self.gup, self.gdown = here, up, down, gup, gdown
        self.rc, self.r1, self.r2 = rc, r1, r2
        self.zsend, self.zland, self.sems, self.zsems = zsend, zland, sems, zsems
        self.brest, self.bzland, self.br1, self.br2 = brest, bzland, br1, br2
        self.bzsems, self.bsems = bzsems, bsems

    def blk(self, u, y, x, c):
        if u < 4:
            return self.up.at[u, y, x, c]
        if u < 8:
            return self.down.at[y, x, c, u - 4]
        if u < 12:
            return self.gup.at[u - 8, y, x, c]
        pair = (u - 12) % 2
        return self.gdown.at[y, x, c, 2 * pair : 2 * pair + 2, (u - 12) // 2]

    def put(self, u, y, cols, value):
        value = value.astype(BF).reshape(2, 2, 2, 48, 256)
        if u < 4:
            self.up[u, y, :, :, :, :, cols] = value
        else:
            self.down[y, :, :, u - 4, :, :, cols] = value

    def cross(self, u):
        h = self.here
        return rcopy(
            self.blk(u, EVERY, EVERY, 1 - h.c), self.rc.at[u % 8], self.sems, (u, 0), h.core
        )

    def first(self, u):
        h = self.here
        if u % 2 == 0:
            src, device = self.blk(u, EVERY, 1 - h.x, h.c), h.xn
        else:
            src, device = self.blk(u, 1 - h.y, EVERY, h.c), h.yn
        return rcopy(src, self.r1.at[u], self.sems, (u, 1), device)

    def second(self, u):
        h = self.here
        if u % 2 == 0:
            src, device = self.r1.at[u, 1 - h.y], h.yn
        else:
            src, device = self.r1.at[u, 1 - h.x], h.xn
        return rcopy(src, self.r2.at[u], self.sems, (u, 2), device)

    def start(self, k):
        for u in (2 * k, 2 * k + 1):
            self.cross(u).start()

    def add_core(self, u):
        self.cross(u).wait_recv()
        mine = self.blk(u, EVERY, EVERY, self.here.c)
        mine[...] = (mine[...].astype(F32) + self.rc[u % 8].astype(F32)).astype(BF)

    def one(self, k):
        for u in (2 * k, 2 * k + 1):
            self.add_core(u)
            self.first(u).start()

    def two(self, k):
        h = self.here
        for u in (2 * k, 2 * k + 1):
            self.first(u).wait_recv()
            if u % 2 == 0:
                mine = self.blk(u, EVERY, h.x, h.c)
            else:
                mine = self.blk(u, h.y, EVERY, h.c)
            self.r1[u] = (mine[...].astype(F32) + self.r1[u].astype(F32)).astype(BF)
            self.second(u).start()

    def three(self, k):
        h = self.here
        sums = []
        for u in (2 * k, 2 * k + 1):
            self.second(u).wait_recv()
            at = h.y if u % 2 == 0 else h.x
            sums.append(self.r1[u, at].astype(F32) + self.r2[u].astype(F32))
        if k < 6:
            sums = [item.reshape(96, 768) for item in sums]
            for z in range(4):
                self.zsend[k, z] = jnp.concatenate(
                    [item[24 * z : 24 * z + 24] for item in sums], axis=0
                ).astype(BF)
        else:
            for half in (0, 1):
                self.zsend[k, 2 * half : 2 * half + 2] = sums[half].astype(BF)
        for s in (1, 2, 3):
            self.zcopy(k, s).start()

    def zcopy(self, k, s):
        h = self.here
        return rcopy(
            self.zsend.at[k, lax.rem(h.z + s, 4)], self.zland.at[k, s - 1], self.zsems,
            (k, s - 1), h.zn(s),
        )

    def last(self, k):
        h = self.here
        for s in (1, 2, 3):
            self.zcopy(k, s).wait_recv()
        total = self.zsend[k, h.z].astype(F32)
        for s in (1, 2, 3):
            total = total + self.zland[k, s - 1].astype(F32)
        return total

    def bz(self, s):
        h = self.here
        src = self.gdown.at[:, :, h.c, lax.rem(h.z + s, 4), 1]
        return rcopy(src, self.bzland.at[s - 1], self.bzsems, s - 1, h.zn(s))

    def b_one(self):
        for u in (14, 15):
            self.add_core(u)
        for s in (1, 2, 3):
            self.bz(s).start()

    def bfirst(self, w):
        h = self.here
        if w == 0:
            src, device = self.brest.at[:, 1 - h.x, :, 0:384], h.xn
        else:
            src, device = self.brest.at[1 - h.y, :, :, 384:768], h.yn
        return rcopy(src, self.br1.at[w], self.bsems, (w, 0), device)

    def bsecond(self, w):
        h = self.here
        if w == 0:
            src, device = self.br1.at[w, 1 - h.y], h.yn
        else:
            src, device = self.br1.at[w, 1 - h.x], h.xn
        return rcopy(src, self.br2.at[w], self.bsems, (w, 1), device)

    def b_two(self):
        h = self.here
        for s in (1, 2, 3):
            self.bz(s).wait_recv()
        total = self.gdown[:, :, h.c, h.z, 1].astype(F32)
        for s in (1, 2, 3):
            total = total + self.bzland[s - 1].astype(F32)
        self.brest[...] = total.astype(BF)
        for w in (0, 1):
            self.bfirst(w).start()

    def b_three(self):
        h = self.here
        for w in (0, 1):
            self.bfirst(w).wait_recv()
            if w == 0:
                mine = self.brest[:, h.x, :, 0:384]
            else:
                mine = self.brest[h.y, :, :, 384:768]
            self.br1[w] = (mine.astype(F32) + self.br1[w].astype(F32)).astype(BF)
            self.bsecond(w).start()

    def b_last(self, w):
        h = self.here
        self.bsecond(w).wait_recv()
        at = h.y if w == 0 else h.x
        return self.br1[w, at].astype(F32) + self.br2[w].astype(F32)

    def drain(self):
        for u in range(16):
            self.cross(u).wait_send()
        for u in range(14):
            self.first(u).wait_send()
            self.second(u).wait_send()
        for k in range(7):
            for s in (1, 2, 3):
                self.zcopy(k, s).wait_send()
        for s in (1, 2, 3):
            self.bz(s).wait_send()
        for w in (0, 1):
            self.bfirst(w).wait_send()
            self.bsecond(w).wait_send()


Z_AFTER = ((1, 2), (3,), (7, 4), (5,), (8, 6), (9,), (10,))


def mm(a, b):
    return lax.dot_general(a, b, (((1,), (0,)), ((), ())), preferred_element_type=F32)


def mt(a, b):
    return lax.dot_general(a, b, (((1,), (1,)), ((), ())), preferred_element_type=F32)


def tm(a, b):
    return lax.dot_general(a, b, (((0,), (0,)), ((), ())), preferred_element_type=F32)


def iota(shape, axis):
    return lax.broadcasted_iota(jnp.int32, shape, axis)


def lanes(hp):
    return pl.ds(pl.multiple_of(hp * 128, 128), 128)


def both(q):
    low = iota(q.shape, 1) < 64
    zero = jnp.zeros_like(q)
    return jnp.concatenate([jnp.where(low, q, zero), jnp.where(low, zero, q)], axis=0)


def merge(pair):
    rows = pair.shape[0] // 2
    low = iota((rows, 128), 1) < 64
    return jnp.where(low, pair[:rows], pair[rows:]).astype(BF)


def probs(key, query, bias, mask):
    scores = mt(key, query)
    if bias is not None:
        scores = scores + bias.astype(F32)
    scores = jnp.where(mask, scores, -1e30)
    expo = jnp.exp(scores - jnp.max(scores, axis=0, keepdims=True))
    return expo * (1.0 / jnp.sum(expo, axis=0, keepdims=True))


def rms(v):
    return lax.rsqrt(jnp.mean(v * v, axis=-1, keepdims=True) + eps)


def norm_back(v, gain, grad):
    r = rms(v)
    scaled = grad * gain
    inner = jnp.mean(scaled * v, axis=-1, keepdims=True)
    return r * scaled - v * (r * r * r * inner), jnp.sum(grad * v * r, axis=0, keepdims=True)


def gelu_both(v):
    c = 0.7978845608028654
    square = v * v
    t = jnp.tanh(c * v * (1.0 + 0.044715 * square))
    half = 0.5 * (1.0 + t)
    slope = half + 0.5 * v * (1.0 - t * t) * (c * (1.0 + 3 * 0.044715 * square))
    return v * half, slope


def layer_kernel(*refs):
    squares, up_in, down_in, gain_in, table_in = refs[:8], refs[8], refs[9], refs[10], refs[11]
    tlen, slen, count, x_in, cot, enc = refs[12:18]
    layer_out, g_dec, g_enc = refs[18:21]
    g_sq, g_up, g_down, g_gain, g_table = refs[21:29], *refs[29:33]
    (
        sq, up, down, gup, gdown, rc, r1, r2, zland, zland2, brest, bzland, br1, br2, small, small2,
        bias, h1, h2, h3, q1, k1, v1, o1, q2, o2, k2, v2, g, gp, x1, x2, stage,
        zs, zr, ss, sr, bs, br, bzs, bzr, bcs, bcr, ms, mr,
        rzs, rzr, rss, rsr, rbzs, rbzr, rbs, rbr, m2s, m2r, out_sem, credit,
    ) = refs[33:]
    here = Place()
    index = (here.y * 4 + here.x * 2 + here.c) * 4 + here.z
    for k in range(4):
        zland[k, here.z] = jnp.concatenate(
            [squares[2 * k][...].astype(F32), squares[2 * k + 1][...].astype(F32)], axis=0
        ).astype(BF)
    for k in range(2):
        zland[4 + k, here.z] = jnp.concatenate(
            [up_in[:, 768 * n : 768 * n + 768].astype(F32) for n in (2 * k, 2 * k + 1)], axis=0
        ).astype(BF)
    down[here.y, here.x, here.c, here.z] = down_in[...].reshape(2, 48, 768)
    spot = (iota((24, 768), 1) == iota((24, 768), 0) + 24 * index).astype(BF)
    small[0] = jnp.zeros((8, 768), F32)
    small[0, 0:3] = mm(gain_in[...], spot)
    here.enter()
    ga = Gather(
        here, sq, up, down, zland, (zs, zr), (ss, sr), (bs, br), (bzs, bzr), (bcs, bcr)
    )
    m = Small(here, small, (ms, mr))
    rs = Scatter(
        here, up, down, gup, gdown, rc, r1, r2, zland, zland2, brest, bzland, br1, br2,
        (rss, rsr), (rzs, rzr), (rbzs, rbzr), (rbs, rbr),
    )
    m2 = Small(here, small2, (m2s, m2r))

    def tick(t):
        if t < 7:
            ga.z_finish(t)
            for item in Z_AFTER[t]:
                if item < 7:
                    ga.z_start(item)
                else:
                    ga.bz_start(item - 7)
        if t < 4:
            m.finish(t)
            if t < 3:
                m.start(t + 1)
        if 0 <= t - 1 < 7:
            ga.mid(t - 1)
        if 0 <= t - 2 < 7:
            ga.core(t - 2)
        if 0 <= t - 3 < 7:
            ga.done(t - 3)
        if t == 0:
            ga.b_mid()
        if t == 1:
            ga.b_got()
        if t == 6:
            ga.b_core(0)
        if t == 8:
            ga.b_core(1)
        if t == 9:
            ga.b_done()

    def weight(u):
        return sq[u].reshape(768, 768)

    def columns(u, n):
        return sq[u, :, :, :, :, :, 256 * n : 256 * n + 256].reshape(768, 256)

    ga.z_start(0)
    ga.b_start()
    m.start(0)

    def bucket_hot(rows_are_buckets):
        shape = (32, 128) if rows_are_buckets else (128, 32)
        distance = iota(shape, 1 if rows_are_buckets else 0)
        level = jnp.minimum(distance, 16)
        for edge in thresholds:
            level = level + (distance >= edge).astype(jnp.int32)
        return level == iota(shape, 0 if rows_are_buckets else 1)

    by_distance = mm(table_in[...], bucket_hot(True).astype(BF))
    for head in range(12):
        row = jnp.broadcast_to(by_distance[head : head + 1, :], (128, 128))
        bias[head // 2, :, 128 * (head % 2) : 128 * (head % 2) + 128] = pltpu.roll(
            row, 0, 1, stride=1, stride_axis=0
        ).astype(BF)

    key_place, target_place = iota((128, 256), 0), iota((128, 256), 1) & 127
    causal = key_place <= target_place
    source_place = iota((512, 256), 0)

    def self_mask(ex):
        return causal & (key_place < tlen[ex])

    def cross_mask(ex):
        return source_place < slen[ex]

    row_place = iota((256, 1), 0)
    live = (
        ((row_place < 128) & (row_place < tlen[0]) & (0 < count[0]))
        | ((row_place >= 128) & (row_place - 128 < tlen[1]) & (1 < count[0]))
    ).astype(F32)

    for t in range(4):
        tick(t)
    gains = m.total()
    gain = [gains[i : i + 1, :] for i in range(3)]

    first = x_in[...].astype(F32)
    h1[...] = (first * rms(first) * gain[0]).astype(BF)
    for n in range(3):
        cols = slice(256 * n, 256 * n + 256)
        q1[:, cols] = mm(h1[...], columns(0, n)).astype(BF)
        k1[:, cols] = mm(h1[...], columns(1, n)).astype(BF)
    tick(4)
    for n in range(3):
        cols = slice(256 * n, 256 * n + 256)
        v1[:, cols] = mm(h1[...], columns(2, n)).astype(BF)

    def self_forward(hp, carry):
        for ex in range(2):
            rows = slice(128 * ex, 128 * ex + 128)
            query = both(q1[rows, lanes(hp)])
            p = probs(k1[rows, lanes(hp)], query, bias[hp], self_mask(ex)).astype(BF)
            o1[rows, lanes(hp)] = merge(tm(p, v1[rows, lanes(hp)]))
        return carry

    lax.fori_loop(0, 6, self_forward, 0)
    tick(5)
    x1[...] = x_in[...].astype(F32) + mm(o1[...], weight(3))
    h2[...] = (x1[...] * rms(x1[...]) * gain[1]).astype(BF)

    def encode(r, carry):
        rows = pl.ds(pl.multiple_of(r * 256, 256), 256)
        for n in range(3):
            cols = slice(256 * n, 256 * n + 256)
            k2[rows, cols] = mm(enc[rows, :], columns(4, n)).astype(BF)
            v2[rows, cols] = mm(enc[rows, :], columns(5, n)).astype(BF)
        return carry

    lax.fori_loop(0, 4, encode, 0)
    tick(6)
    for n in range(3):
        cols = slice(256 * n, 256 * n + 256)
        q2[:, cols] = mm(h2[...], columns(6, n)).astype(BF)

    def cross_forward(hp, carry):
        for ex in range(2):
            rows = slice(128 * ex, 128 * ex + 128)
            keys = slice(512 * ex, 512 * ex + 512)
            query = both(q2[rows, lanes(hp)])
            p = probs(k2[keys, lanes(hp)], query, None, cross_mask(ex)).astype(BF)
            o2[rows, lanes(hp)] = merge(tm(p, v2[keys, lanes(hp)]))
        return carry

    lax.fori_loop(0, 3, cross_forward, 0)
    tick(7)
    lax.fori_loop(3, 6, cross_forward, 0)
    x2[...] = x1[...] + mm(o2[...], weight(7))
    h3[...] = (x2[...] * rms(x2[...]) * gain[2]).astype(BF)
    tick(8)
    def hidden(n, carry):
        for part in range(3):
            lo = 256 * part
            a = mm(h3[...], up[n, :, :, :, :, :, lo : lo + 256].reshape(768, 256))
            active, slope = gelu_both(a)
            cols = pl.ds(pl.multiple_of(768 * n + lo, 256), 256)
            g[:, cols] = active.astype(BF)
            gp[:, cols] = slope.astype(BF)
        return carry

    lax.fori_loop(0, 4, hidden, 0)

    def keep_gain(i, term):
        for j in range(6):
            small2[0, 6 * i + j : 6 * i + j + 1, :] = term[:, 128 * j : 128 * j + 128]

    def df(cols=slice(None)):
        return (cot[:, cols].astype(F32) * live).astype(BF)

    def wide(e):
        return pl.ds(pl.multiple_of(768 * e, 256), 768)

    def grad_down(e, carry):
        turned = g[:, wide(e)].T
        for n in range(3):
            cols = slice(256 * n, 256 * n + 256)
            grad = mm(turned, df(cols)).astype(BF)
            gdown[lax.div(e, 2), lax.rem(e, 2), :, :, :, :, cols] = grad.reshape(2, 4, 2, 48, 256)
        return carry

    lax.fori_loop(0, 4, grad_down, 0)
    rs.start(7)
    rs.start(6)
    tick(9)

    def down_block(e):
        return down[lax.div(e, 2), lax.rem(e, 2)].reshape(768, 768)

    def inner_grad(e, carry):
        dg = mt(df(), down_block(e))
        gp[:, wide(e)] = (dg * gp[:, wide(e)].astype(F32)).astype(BF)
        return carry

    lax.fori_loop(0, 2, inner_grad, 0)
    rs.b_one()
    rs.one(6)
    lax.fori_loop(2, 4, inner_grad, 0)

    def grad_up(n, carry):
        turned = h3[...].T
        for part in range(3):
            cols = slice(256 * part, 256 * part + 256)
            source = pl.ds(pl.multiple_of(768 * n + 256 * part, 256), 256)
            grad = mm(turned, gp[:, source]).astype(BF)
            gup[n, :, :, :, :, :, cols] = grad.reshape(2, 2, 2, 2, 48, 256)
        return carry

    lax.fori_loop(0, 2, grad_up, 0)
    rs.start(4)
    lax.fori_loop(2, 4, grad_up, 0)
    rs.start(5)
    stage[0] = x2[...]

    def result(e, carry):
        stage[0] += mm(g[:, wide(e)], down_block(e))
        return carry

    lax.fori_loop(0, 4, result, 0)
    layer_out[...] = (stage[0] * live).astype(BF)
    rs.one(4)
    stage[0] = jnp.zeros((256, 768), F32)

    def inner_back(n, carry):
        stage[0] += mt(gp[:, wide(n)], up[n].reshape(768, 768))
        return carry

    lax.fori_loop(0, 4, inner_back, 0)
    d_norm, gain_three = norm_back(x2[...], gain[2], stage[0])
    keep_gain(2, gain_three)
    x2[...] = cot[...].astype(F32) * live + d_norm
    rs.one(5)
    pl.semaphore_signal(credit, inc=1, device_id=here.core, device_id_type=MESH)
    rs.two(6)
    rs.b_two()
    ga.drain()

    def put_grads(value, rows, pairs):
        def half_rows(y, carry):
            turned = value[:, pl.ds(pl.multiple_of(384 * y, 128), 384)].T
            for u, ref in pairs:
                for n in range(3):
                    cols = slice(256 * n, 256 * n + 256)
                    rs.put(u, y, cols, mm(turned, ref[:, cols]))
            return carry

        lax.fori_loop(0, 2, half_rows, 0)

    h3[...] = x2[...].astype(BF)
    put_grads(o2, 256, ((7, h3),))
    rs.two(4)
    o2[...] = mt(h3[...], weight(7)).astype(BF)

    def cross_backward(hp, carry):
        for ex in range(2):
            rows = slice(128 * ex, 128 * ex + 128)
            keys = slice(512 * ex, 512 * ex + 512)
            query, d_out = both(q2[rows, lanes(hp)]), both(o2[rows, lanes(hp)])
            key, value = k2[keys, lanes(hp)], v2[keys, lanes(hp)]
            p = probs(key, query, None, cross_mask(ex))
            dp = mt(value, d_out)
            delta = jnp.sum(dp * p, axis=0, keepdims=True)
            ds = (p * (dp - delta)).astype(BF)
            q2[rows, lanes(hp)] = merge(tm(ds, key))
            k2[keys, lanes(hp)] = mm(ds, query).astype(BF)
            v2[keys, lanes(hp)] = mm(p.astype(BF), d_out).astype(BF)
        return carry

    lax.fori_loop(0, 2, cross_backward, 0)
    rs.three(6)
    rs.two(5)
    rs.b_three()
    lax.fori_loop(2, 4, cross_backward, 0)
    rs.three(4)
    lax.fori_loop(4, 6, cross_backward, 0)
    put_grads(h2, 256, ((6, q2),))
    pl.semaphore_wait(credit, 1)
    rs.start(3)
    rs.three(5)
    put_grads(enc, 1024, ((4, k2), (5, v2)))
    rs.start(2)

    def finish(k):
        total = rs.last(k)
        if k < 4:
            g_sq[2 * k][...] = total[:24]
            g_sq[2 * k + 1][...] = total[24:]
        elif k < 6:
            g_up[:, 1536 * (k - 4) : 1536 * (k - 4) + 768] = total[:24]
            g_up[:, 1536 * (k - 4) + 768 : 1536 * (k - 4) + 1536] = total[24:]
        else:
            g_down[0:48, :] = total

    rs.one(3)
    finish(6)
    for w in (0, 1):
        g_down[48:96, 384 * w : 384 * w + 384] = rs.b_last(w)
    d_norm, gain_two = norm_back(x1[...], gain[1], mt(q2[...], weight(6)))
    keep_gain(1, gain_two)
    x2[...] = x2[...] + d_norm
    rs.one(2)
    rs.two(3)
    finish(4)

    h3[...] = x2[...].astype(BF)
    put_grads(o1, 256, ((3, h3),))
    o1[...] = mt(h3[...], weight(3)).astype(BF)
    rs.two(2)
    turn = (iota((128, 256), 0) + (iota((128, 256), 1) & 127) == 127).astype(BF)

    def self_backward(hp, carry):
        scores = []
        for ex in range(2):
            rows = slice(128 * ex, 128 * ex + 128)
            query, d_out = both(q1[rows, lanes(hp)]), both(o1[rows, lanes(hp)])
            key, value = k1[rows, lanes(hp)], v1[rows, lanes(hp)]
            p = probs(key, query, bias[hp], self_mask(ex))
            dp = mt(value, d_out)
            delta = jnp.sum(dp * p, axis=0, keepdims=True)
            ds = (p * (dp - delta)).astype(BF)
            q1[rows, lanes(hp)] = merge(tm(ds, key))
            k1[rows, lanes(hp)] = mm(ds, query).astype(BF)
            v1[rows, lanes(hp)] = mm(p.astype(BF), d_out).astype(BF)
            scores.append(ds)
        pair = mm(turn, jnp.concatenate(scores, axis=0))
        for head in range(2):
            skew = pltpu.roll(pair[:, 128 * head : 128 * head + 128], 0, 1, stride=1, stride_axis=0)
            small2[0, pl.ds(18 + 2 * hp + head, 1), :] = jnp.sum(skew, axis=0, keepdims=True)
        return carry

    lax.fori_loop(0, 3, self_backward, 0)
    rs.three(3)
    lax.fori_loop(3, 6, self_backward, 0)
    finish(5)
    put_grads(h1, 256, ((2, v1), (0, q1), (1, k1)))
    rs.start(1)
    rs.start(0)
    rs.three(2)
    stage[0] = jnp.zeros((256, 768), F32)

    def first_back(y, carry):
        cols = pl.ds(pl.multiple_of(384 * y, 128), 384)
        for u, ref in ((0, q1), (1, k1), (2, v1)):
            stage[0, :, cols] += mt(ref[...], sq[u, y].reshape(384, 768))
        return carry

    lax.fori_loop(0, 2, first_back, 0)
    rs.one(1)
    d_norm, gain_one = norm_back(x_in[...].astype(F32), gain[0], stage[0])
    g_dec[...] = x2[...] + d_norm
    keep_gain(0, gain_one)
    small2[0, 30:32, :] = jnp.zeros((2, 128), F32)
    m2.start(0)
    rs.one(0)
    finish(3)
    rs.two(1)
    m2.finish(0)
    m2.start(1)

    def out_copy(r):
        return pltpu.make_async_copy(
            stage.at[lax.rem(r, 2)],
            g_enc.at[pl.ds(pl.multiple_of(256 * r, 256), 256)],
            out_sem.at[r],
        )

    def encoder_grad(r, carry):
        rows = pl.ds(pl.multiple_of(256 * r, 256), 256)
        slot = lax.rem(r, 2)
        for y in range(2):
            cols = slice(384 * y, 384 * y + 384)
            stage[slot, :, cols] = mt(k2[rows, :], sq[4, y].reshape(384, 768))
            stage[slot, :, cols] += mt(v2[rows, :], sq[5, y].reshape(384, 768))
        out_copy(r).start()
        return carry

    lax.fori_loop(0, 2, encoder_grad, 0)
    rs.two(0)
    m2.finish(1)
    m2.start(2)
    rs.three(1)
    finish(2)
    m2.finish(2)
    m2.start(3)
    rs.three(0)
    out_copy(0).wait()
    out_copy(1).wait()
    lax.fori_loop(2, 4, encoder_grad, 0)
    finish(1)
    m2.finish(3)
    reduced = m2.total()
    sums = jnp.concatenate(
        [
            jnp.concatenate([reduced[6 * i + j : 6 * i + j + 1, :] for j in range(6)], axis=1)
            for i in range(3)
        ],
        axis=0,
    )
    pick = (iota((768, 24), 0) == iota((768, 24), 1) + 24 * index).astype(F32)
    g_gain[...] = lax.dot_general(
        sums, pick, (((1,), (0,)), ((), ())), preferred_element_type=F32,
        precision=lax.Precision.HIGHEST,
    )
    distance = (iota((32, 128), 1) + 1) & 127
    level = jnp.minimum(distance, 16)
    for edge in thresholds:
        level = level + (distance >= edge).astype(jnp.int32)
    hot = (level == iota((32, 128), 0)).astype(F32)
    g_table[...] = lax.dot_general(
        reduced[18:30, :], hot, (((1,), (1,)), ((), ())), preferred_element_type=F32,
        precision=lax.Precision.HIGHEST,
    )
    finish(0)
    rs.drain()
    out_copy(2).wait()
    out_copy(3).wait()


VM = pl.BlockSpec(memory_space=pltpu.VMEM)
SM = pl.BlockSpec(memory_space=pltpu.SMEM)
ANY = pl.BlockSpec(memory_space=pl.ANY)


def layer_call(*args):
    shape = jax.ShapeDtypeStruct
    dims = ((7, 3), (14, 4), (2, 3), (4, 3), (2,), (6,), (7, 3), (16, 3), (3,), (2, 2), (6,))
    half = lambda *dims: pltpu.VMEM(dims, BF)
    return pl.pallas_call(
        layer_kernel,
        out_shape=(
            shape((256, 768), BF),
            shape((256, 768), F32),
            shape((1024, 768), F32),
            *[shape((24, 768), F32)] * 8,
            shape((24, 3072), F32),
            shape((96, 768), F32),
            shape((3, 24), F32),
            shape((12, 32), F32),
        ),
        in_specs=[VM] * 12 + [SM] * 3 + [VM] * 3,
        out_specs=(VM, VM, ANY) + (VM,) * 12,
        scratch_shapes=[
            half(8, 2, 2, 2, 2, 48, 768),
            half(4, 2, 2, 2, 2, 48, 768),
            half(2, 2, 2, 4, 2, 48, 768),
            half(4, 2, 2, 2, 2, 48, 768),
            half(2, 2, 2, 4, 2, 48, 768),
            half(8, 2, 2, 2, 48, 768),
            half(14, 2, 2, 48, 768),
            half(14, 2, 48, 768),
            half(7, 4, 48, 768),
            half(7, 3, 48, 768),
            half(2, 2, 48, 768),
            half(3, 2, 2, 48, 768),
            half(2, 2, 48, 384),
            half(2, 48, 384),
            pltpu.VMEM((10, 8, 768), F32),
            pltpu.VMEM((10, 32, 128), F32),
            half(6, 128, 256),
            *[half(256, 768)] * 3,
            *[half(256, 768)] * 4,
            *[half(256, 768)] * 2,
            *[half(1024, 768)] * 2,
            *[half(256, 3072)] * 2,
            *[pltpu.VMEM((256, 768), F32)] * 2,
            pltpu.VMEM((2, 256, 768), F32),
            *[pltpu.SemaphoreType.DMA(each) for each in dims for _ in range(2)],
            pltpu.SemaphoreType.DMA((4,)),
            pltpu.SemaphoreType.REGULAR,
        ],
        compiler_params=pltpu.CompilerParams(
            collective_id=0, has_side_effects=True, vmem_limit_bytes=64 * 2**20 - 2**16
        ),
        name="layer",
    )(*args)


def hand_out_kernel(*refs):
    count = (len(refs) - 2) // 3
    source, target, held = refs[:count], refs[count : 2 * count], refs[2 * count : 3 * count]
    got, put = refs[3 * count :]
    ins = [pltpu.make_async_copy(source[i], held[i], got.at[i]) for i in range(count)]
    outs = [pltpu.make_async_copy(held[i], target[i], put.at[i]) for i in range(count)]
    for copy in ins:
        copy.start()
    for i in range(count):
        ins[i].wait()
        outs[i].start()
    for copy in outs:
        copy.wait()


def hand_out(arrays):
    return pl.pallas_call(
        hand_out_kernel,
        out_shape=tuple(jax.ShapeDtypeStruct(item.shape, item.dtype) for item in arrays),
        in_specs=[ANY] * len(arrays),
        out_specs=(ANY,) * len(arrays),
        scratch_shapes=[pltpu.VMEM(item.shape, item.dtype) for item in arrays]
        + [pltpu.SemaphoreType.DMA((len(arrays),))] * 2,
        name="hand_out",
    )(*arrays)


def by_kernel(
    decoder_in,
    encoder_out,
    self_query,
    self_key,
    self_value,
    self_output,
    cross_query,
    cross_key,
    cross_value,
    cross_output,
    hidden_in,
    hidden_out,
    norm_gains,
    bias_table,
    target_lengths,
    source_lengths,
    example_counts,
    cotangent,
):
    results = layer_call(
        self_query,
        self_key,
        self_value,
        self_output,
        cross_key,
        cross_value,
        cross_query,
        cross_output,
        hidden_in,
        hidden_out,
        norm_gains,
        bias_table.T,
        target_lengths,
        source_lengths,
        example_counts,
        decoder_in.reshape(256, 768),
        cotangent.reshape(256, 768),
        encoder_out.reshape(1024, 768),
    )
    out, g_dec, g_enc, *g_sq, g_up, g_down, g_gain, g_table = hand_out(results)
    return (
        out.reshape(decoder_in.shape),
        g_dec.reshape(decoder_in.shape),
        g_enc.reshape(encoder_out.shape),
        *g_sq[:4],
        g_sq[6],
        g_sq[4],
        g_sq[5],
        g_sq[7],
        g_up,
        g_down,
        g_gain,
        g_table.T,
    )


def plain(
    decoder_in,
    encoder_out,
    self_query,
    self_key,
    self_value,
    self_output,
    cross_query,
    cross_key,
    cross_value,
    cross_output,
    hidden_in,
    hidden_out,
    norm_gains,
    bias_table,
    target_lengths,
    source_lengths,
    example_counts,
    cotangent,
):
    gathered = (
        lax.all_gather(self_query, AXES, axis=0, tiled=True),
        lax.all_gather(self_key, AXES, axis=0, tiled=True),
        lax.all_gather(self_value, AXES, axis=0, tiled=True),
        lax.all_gather(self_output, AXES, axis=0, tiled=True),
        lax.all_gather(cross_query, AXES, axis=0, tiled=True),
        lax.all_gather(cross_key, AXES, axis=0, tiled=True),
        lax.all_gather(cross_value, AXES, axis=0, tiled=True),
        lax.all_gather(cross_output, AXES, axis=0, tiled=True),
        lax.all_gather(hidden_in, AXES, axis=0, tiled=True),
        lax.all_gather(hidden_out, AXES, axis=0, tiled=True),
        lax.all_gather(norm_gains, AXES, axis=1, tiled=True),
    )
    w_query, w_key, w_value, w_out, x_query, x_key, x_value, x_out, w_up, w_down, gain_all = (
        gathered
    )
    slots = jnp.arange(decoder_in.shape[0], dtype=jnp.int32)
    length = decoder_in.shape[1]
    source = encoder_out.shape[1]
    width = decoder_in.shape[2]
    hidden_width = hidden_in.shape[1]
    place = jnp.arange(length, dtype=jnp.int32)
    source_place = jnp.arange(source, dtype=jnp.int32)
    live = (
        (slots < example_counts[0])[:, None] & (place[None, :] < target_lengths[:, None])
    ).astype(jnp.float32)[:, :, None]
    self_mask = (place[None, :] <= place[:, None])[None, None] & (
        place[None, None, None, :] < target_lengths[:, None, None, None]
    )
    cross_mask = source_place[None, None, None, :] < source_lengths[:, None, None, None]
    onehot = (
        buckets(length)[:, :, None] == jnp.arange(bias_table.shape[0], dtype=jnp.int32)
    ).astype(jnp.bfloat16)
    bias = jnp.einsum("lsn,nh->hls", onehot, bias_table, preferred_element_type=jnp.float32)
    gains = gain_all.astype(jnp.float32)
    inputs = decoder_in.astype(jnp.float32)
    first = normalize(inputs, gains[0]).astype(jnp.bfloat16)
    query = project(first, w_query).astype(jnp.bfloat16)
    key = project(first, w_key).astype(jnp.bfloat16)
    value = project(first, w_value).astype(jnp.bfloat16)
    mixed, logsum_self = attention_forward(
        split_heads(query), split_heads(key), split_heads(value), bias, self_mask
    )
    after_self = inputs + project(mixed, w_out)
    second = normalize(after_self, gains[1]).astype(jnp.bfloat16)
    cross_q = project(second, x_query).astype(jnp.bfloat16)
    cross_k = project(encoder_out, x_key).astype(jnp.bfloat16)
    cross_v = project(encoder_out, x_value).astype(jnp.bfloat16)
    crossed, logsum_cross = attention_forward(
        split_heads(cross_q), split_heads(cross_k), split_heads(cross_v), 0.0, cross_mask
    )
    after_cross = after_self + project(crossed, x_out)
    third = normalize(after_cross, gains[2]).astype(jnp.bfloat16)
    inner = project(third, w_up)
    active = jax.nn.gelu(inner).astype(jnp.bfloat16)
    result = after_cross + project(active, w_down)
    layer_out = (result * live).astype(jnp.bfloat16)
    regathered = (
        lax.all_gather(self_query, AXES, axis=0, tiled=True),
        lax.all_gather(self_key, AXES, axis=0, tiled=True),
        lax.all_gather(self_value, AXES, axis=0, tiled=True),
        lax.all_gather(self_output, AXES, axis=0, tiled=True),
        lax.all_gather(cross_query, AXES, axis=0, tiled=True),
        lax.all_gather(cross_key, AXES, axis=0, tiled=True),
        lax.all_gather(cross_value, AXES, axis=0, tiled=True),
        lax.all_gather(cross_output, AXES, axis=0, tiled=True),
        lax.all_gather(hidden_in, AXES, axis=0, tiled=True),
        lax.all_gather(hidden_out, AXES, axis=0, tiled=True),
        lax.all_gather(norm_gains, AXES, axis=1, tiled=True),
    )
    w_query, w_key, w_value, w_out, x_query, x_key, x_value, x_out, w_up, w_down, gain_all = (
        regathered
    )
    gains = gain_all.astype(jnp.float32)
    d_result = cotangent.astype(jnp.float32) * live
    d_branch = d_result.astype(jnp.bfloat16)
    grad_down = outer_sum(active, d_branch)
    d_inner = gelu_grad(inner, project_back(d_branch, w_down)).astype(jnp.bfloat16)
    grad_up = outer_sum(third, d_inner)
    d_cross, gain_three = norm_grad(after_cross, gains[2], project_back(d_inner, w_up))
    d_cross = d_cross + d_result
    d_branch = d_cross.astype(jnp.bfloat16)
    grad_x_out = outer_sum(crossed, d_branch)
    d_crossed = project_back(d_branch, x_out).astype(jnp.bfloat16)
    dq_cross, dk_cross, dv_cross, unused = attention_backward(
        split_heads(cross_q),
        split_heads(cross_k),
        split_heads(cross_v),
        0.0,
        cross_mask,
        logsum_cross,
        split_heads(d_crossed),
    )
    grad_x_query = outer_sum(second, dq_cross)
    grad_x_key = outer_sum(encoder_out, dk_cross)
    grad_x_value = outer_sum(encoder_out, dv_cross)
    grad_encoder = project_back(dk_cross, x_key) + project_back(dv_cross, x_value)
    d_self, gain_two = norm_grad(after_self, gains[1], project_back(dq_cross, x_query))
    d_self = d_self + d_cross
    d_branch = d_self.astype(jnp.bfloat16)
    grad_w_out = outer_sum(mixed, d_branch)
    d_mixed = project_back(d_branch, w_out).astype(jnp.bfloat16)
    dq_self, dk_self, dv_self, d_scores = attention_backward(
        split_heads(query),
        split_heads(key),
        split_heads(value),
        bias,
        self_mask,
        logsum_self,
        split_heads(d_mixed),
    )
    d_bias = jnp.sum(d_scores, axis=0, dtype=jnp.float32)
    table_term = jnp.einsum(
        "hls,lsn->nh", d_bias, onehot.astype(jnp.float32), precision=lax.Precision.HIGHEST
    )
    grad_w_query = outer_sum(first, dq_self)
    grad_w_key = outer_sum(first, dk_self)
    grad_w_value = outer_sum(first, dv_self)
    d_first = (
        project_back(dq_self, w_query)
        + project_back(dk_self, w_key)
        + project_back(dv_self, w_value)
    )
    d_inputs, gain_one = norm_grad(inputs, gains[0], d_first)
    grad_decoder = d_inputs + d_self
    gain_terms = jnp.stack([gain_one, gain_two, gain_three], axis=1)
    flats = flat_rows(
        (
            grad_w_query,
            grad_w_key,
            grad_w_value,
            grad_w_out,
            grad_x_query,
            grad_x_key,
            grad_x_value,
            grad_x_out,
            grad_up,
            grad_down,
            gain_terms,
        )
    )
    summed = (
        lax.psum_scatter(flats[0], AXES, scatter_dimension=0, tiled=True),
        lax.psum_scatter(flats[1], AXES, scatter_dimension=0, tiled=True),
        lax.psum_scatter(flats[2], AXES, scatter_dimension=0, tiled=True),
        lax.psum_scatter(flats[3], AXES, scatter_dimension=0, tiled=True),
        lax.psum_scatter(flats[4], AXES, scatter_dimension=0, tiled=True),
        lax.psum_scatter(flats[5], AXES, scatter_dimension=0, tiled=True),
        lax.psum_scatter(flats[6], AXES, scatter_dimension=0, tiled=True),
        lax.psum_scatter(flats[7], AXES, scatter_dimension=0, tiled=True),
        lax.psum_scatter(flats[8], AXES, scatter_dimension=0, tiled=True),
        lax.psum_scatter(flats[9], AXES, scatter_dimension=0, tiled=True),
        lax.psum_scatter(flats[10], AXES, scatter_dimension=0, tiled=True),
    )
    shaped = unflat_rows(
        summed, (width, width, width, width, width, width, width, width, hidden_width, width, 3)
    )
    sums = shaped[:10] + (jnp.transpose(shaped[10]),)
    grad_table = lax.psum(table_term, AXES)
    return (
        layer_out,
        grad_decoder,
        grad_encoder,
        sums[0],
        sums[1],
        sums[2],
        sums[3],
        sums[4],
        sums[5],
        sums[6],
        sums[7],
        sums[8],
        sums[9],
        sums[10],
        grad_table,
    )


def solution(mesh):
    rows = P(AXES, None)
    slots = P(AXES, None, None)
    flat = P(AXES)
    gains = P(None, AXES)
    small = mesh.shape["dp"] == 8 and mesh.shape["fsdp"] == 4
    return jax.shard_map(
        by_kernel if small else plain,
        mesh=mesh,
        in_specs=(slots, slots) + (rows,) * 10 + (gains, P(), flat, flat, flat, slots),
        out_specs=(slots, slots, slots) + (rows,) * 10 + (gains, P()),
        check_vma=False,
    )
```

```python
import functools

import jax
import jax.numpy as jnp
from jax import lax
from jax.experimental import pallas as pl
from jax.experimental.pallas import tpu as pltpu
from jax.sharding import PartitionSpec as P

H = 12
AXES = ("dp", "fsdp")
MESH = pl.DeviceIdType.MESH
BF = jnp.bfloat16
F32 = jnp.float32


eps = 1e-06
thresholds = [19, 21, 24, 27, 31, 35, 40, 46, 52, 59, 67, 77, 87, 99, 113]


def normalize(v, gain):
    return v * lax.rsqrt(jnp.mean(v * v, axis=-1, keepdims=True) + eps) * gain


def norm_grad(v, gain, grad):
    _, pullback = jax.vjp(normalize, v, gain)
    return pullback(grad)


def gelu_grad(v, grad):
    _, pullback = jax.vjp(jax.nn.gelu, v)
    return pullback(grad)[0]


def project(v, weight):
    return jnp.einsum("btd,df->btf", v, weight, preferred_element_type=jnp.float32)


def project_back(grad, weight):
    return jnp.einsum("btf,df->btd", grad, weight, preferred_element_type=jnp.float32)


def outer_sum(v, grad):
    return jnp.einsum("btd,btf->df", v, grad, preferred_element_type=jnp.float32)


def split_heads(v):
    return v.reshape(v.shape[0], v.shape[1], H, v.shape[2] // H)


def join_heads(v):
    return v.reshape(v.shape[0], v.shape[1], v.shape[2] * v.shape[3])


def flat_rows(items):
    return tuple((item.reshape(-1) for item in items))


def unflat_rows(items, widths):
    return tuple((item.reshape(-1, width) for item, width in zip(items, widths)))


def buckets(length):
    place = jnp.arange(length, dtype=jnp.int32)
    distance = jnp.maximum(place[:, None] - place[None, :], 0)
    level = jnp.minimum(distance, 16)
    for edge in thresholds:
        level = level + (distance >= edge).astype(jnp.int32)
    return level


def scores_of(query, key, bias, mask):
    scores = jnp.einsum("blhd,bshd->bhls", query, key, preferred_element_type=jnp.float32) + bias
    return jnp.where(mask, scores, -1e30)


def attention_forward(query, key, value, bias, mask):
    scores = scores_of(query, key, bias, mask)
    top = jnp.max(scores, axis=-1, keepdims=True)
    expo = jnp.exp(scores - top)
    total = jnp.sum(expo, axis=-1, keepdims=True)
    probs = (expo / total).astype(jnp.bfloat16)
    mixed = jnp.einsum("bhls,bshd->blhd", probs, value, preferred_element_type=jnp.float32)
    return (join_heads(mixed).astype(jnp.bfloat16), top + jnp.log(total))


def attention_backward(query, key, value, bias, mask, logsum, d_out):
    probs = jnp.exp(scores_of(query, key, bias, mask) - logsum)
    d_probs = jnp.einsum("blhd,bshd->bhls", d_out, value, preferred_element_type=jnp.float32)
    delta = jnp.sum(d_probs * probs, axis=-1, keepdims=True)
    d_scores = (probs * (d_probs - delta)).astype(jnp.bfloat16)
    d_query = jnp.einsum(
        "bhls,bshd->blhd", d_scores, key, preferred_element_type=jnp.float32
    ).astype(jnp.bfloat16)
    d_key = jnp.einsum(
        "bhls,blhd->bshd", d_scores, query, preferred_element_type=jnp.float32
    ).astype(jnp.bfloat16)
    d_value = jnp.einsum(
        "bhls,blhd->bshd", probs.astype(jnp.bfloat16), d_out, preferred_element_type=jnp.float32
    ).astype(jnp.bfloat16)
    return (join_heads(d_query), join_heads(d_key), join_heads(d_value), d_scores)


class Place:
    def __init__(self):
        d = lax.axis_index("dp")
        self.z = lax.axis_index("fsdp")
        self.c = lax.rem(d, 2)
        self.x = lax.rem(lax.div(d, 2), 2)
        self.y = lax.div(d, 4)

    def dev(self, y, x, c, z):
        return ((y * 2 + x) * 2 + c, z)

    @property
    def core(self):
        return self.dev(self.y, self.x, 1 - self.c, self.z)

    @property
    def xn(self):
        return self.dev(self.y, 1 - self.x, self.c, self.z)

    @property
    def yn(self):
        return self.dev(1 - self.y, self.x, self.c, self.z)

    def zn(self, step):
        return self.dev(self.y, self.x, self.c, lax.rem(self.z + step, 4))

    def enter(self):
        bar = pltpu.get_barrier_semaphore()
        others = [self.core, self.xn, self.yn] + [self.zn(s) for s in (1, 2, 3)]
        for other in others:
            pl.semaphore_signal(bar, inc=1, device_id=other, device_id_type=MESH)
        pl.semaphore_wait(bar, len(others))


def rcopy(src, dst, sems, index, device, landing=None):
    send, recv = sems
    return pltpu.make_async_remote_copy(
        src_ref=src,
        dst_ref=dst,
        send_sem=send.at[index],
        recv_sem=recv.at[index if landing is None else landing],
        device_id=device,
        device_id_type=MESH,
    )


class Small:
    def __init__(self, here, buf, sems):
        self.here, self.buf, self.sems = here, buf, sems

    def pair(self, stage):
        h = self.here
        return rcopy(
            self.buf.at[2 * stage], self.buf.at[2 * stage + 1], self.sems, stage,
            (h.core, h.xn, h.yn)[stage],
        )

    def start(self, stage):
        if stage < 3:
            self.pair(stage).start()
        else:
            for s in (1, 2, 3):
                self.last(s).start()

    def last(self, s):
        return rcopy(self.buf.at[6], self.buf.at[6 + s], self.sems, 2 + s, self.here.zn(s))

    def finish(self, stage):
        b = self.buf
        if stage < 3:
            self.pair(stage).wait()
            b[2 * stage + 2] = b[2 * stage] + b[2 * stage + 1]
        else:
            for s in (1, 2, 3):
                self.last(s).wait()

    def total(self):
        b = self.buf
        return b[6] + b[7] + b[8] + b[9]


EVERY = slice(None)


class Gather:
    def __init__(self, here, sq, up, down, zland, zsems, sems, bsems, bcsems):
        self.here, self.sq, self.up, self.down = here, sq, up, down
        self.zland, self.zsems, self.sems = zland, zsems, sems
        self.bsems, self.bcsems = bsems, bcsems

    def blk(self, u, y, x, c):
        if u < 8:
            return self.sq.at[u, y, x, c]
        if u < 12:
            return self.up.at[u - 8, y, x, c]
        return self.down.at[y, x, c, 2 * (u - 12) : 2 * (u - 12) + 2, 0]

    def zpath(self, j):
        z = self.here.z
        low = z < 2
        if j == 0:
            source, target = z, jnp.where(low, z + 1, z - 1)
        elif j == 1:
            far = jnp.where(z == 0, 2, 1)
            near = jnp.where(z == 1, 0, 3)
            source, target = z, jnp.where((z == 0) | (z == 3), far, near)
        else:
            source = jnp.where(z == 1, 2, jnp.where(z == 2, 1, z))
            target = jnp.where(low, 3, 0)
            target = jnp.where(z == 1, 0, jnp.where(z == 2, 3, target))
        return source, target, lax.rem(source - target + 4, 4) - 1

    def zwait(self):
        return jnp.where(self.here.z < 2, 0, 2)

    def zref(self, k, z):
        h = self.here
        if k < 6:
            return self.zland.at[k, z]
        if k == 6:
            return self.down.at[h.y, h.x, h.c, z, 0]
        p = k - 7
        return self.down.at[p // 2, p % 2, h.c, z, 1]

    def zcopy(self, k, j):
        h = self.here
        source, target, landing = self.zpath(j)
        ref = self.zref(k, source)
        return rcopy(ref, ref, self.zsems, (k, j), h.dev(h.y, h.x, h.c, target), (k, landing))

    def zgot(self, k, r):
        h = self.here
        ref = self.zref(k, lax.rem(h.z + 1 + r, 4))
        return rcopy(ref, ref, self.zsems, (k, 0), h.zn(1), (k, r))

    def z_start(self, k):
        self.zcopy(k, 0).start()
        self.zcopy(k, 1).start()

    def z_pass(self, k):
        self.zgot(k, self.zwait()).wait_recv()
        self.zcopy(k, 2).start()

    def z_wait(self, k):
        self.zgot(k, 1).wait_recv()
        self.zgot(k, 2 - self.zwait()).wait_recv()

    def z_finish(self, k):
        h = self.here
        self.z_wait(k)
        if k < 6:
            slabs = self.zland[k].astype(F32)
            for half in (0, 1):
                rows = jnp.concatenate(
                    [slabs[z, 24 * half : 24 * half + 24] for z in range(4)], axis=0
                ).astype(BF).reshape(2, 48, 768)
                u = 2 * k + half
                if u < 8:
                    self.sq[u, h.y, h.x, h.c] = rows
                else:
                    self.up[u - 8, h.y, h.x, h.c] = rows
        for u in (2 * k, 2 * k + 1):
            self.first(u).start()
            self.second(u).start()

    def nbrs(self, u):
        h = self.here
        return (h.yn, h.xn) if u % 2 == 0 else (h.xn, h.yn)

    def own(self, u):
        h = self.here
        return self.blk(u, h.y, h.x, h.c)

    def got(self, u):
        h = self.here
        return self.blk(u, 1 - h.y, h.x, h.c) if u % 2 == 0 else self.blk(u, h.y, 1 - h.x, h.c)

    def first(self, u):
        return rcopy(self.own(u), self.own(u), self.sems, (u, 0), self.nbrs(u)[0])

    def second(self, u):
        return rcopy(self.own(u), self.own(u), self.sems, (u, 1), self.nbrs(u)[1])

    def third(self, u):
        return rcopy(self.got(u), self.got(u), self.sems, (u, 2), self.nbrs(u)[1])

    def cross(self, u):
        ref = self.blk(u, EVERY, EVERY, self.here.c)
        return rcopy(ref, ref, self.sems, (u, 3), self.here.core)

    def mid(self, k):
        for u in (2 * k, 2 * k + 1):
            self.first(u).wait_recv()
            self.third(u).start()

    def core(self, k):
        for u in (2 * k, 2 * k + 1):
            self.second(u).wait_recv()
            self.third(u).wait_recv()
            self.cross(u).start()

    def done(self, k):
        for u in (2 * k, 2 * k + 1):
            self.cross(u).wait_recv()

    def bblk(self, w, y, x):
        h = self.here
        return self.down.at[y, x, h.c, h.z, 1, :, 384 * w : 384 * w + 384]

    def bfirst(self, w):
        h = self.here
        ref = self.bblk(w, h.y, h.x)
        return rcopy(ref, ref, self.bsems, (w, 0), self.nbrs(w)[0])

    def bsecond(self, w):
        h = self.here
        ref = self.bblk(w, h.y, h.x)
        return rcopy(ref, ref, self.bsems, (w, 1), self.nbrs(w)[1])

    def bthird(self, w):
        h = self.here
        ref = self.bblk(w, 1 - h.y, h.x) if w == 0 else self.bblk(w, h.y, 1 - h.x)
        return rcopy(ref, ref, self.bsems, (w, 2), self.nbrs(w)[1])

    def b_start(self):
        for w in (0, 1):
            self.bfirst(w).start()
            self.bsecond(w).start()

    def b_mid(self):
        for w in (0, 1):
            self.bfirst(w).wait_recv()
            self.bthird(w).start()

    def b_got(self):
        for w in (0, 1):
            self.bsecond(w).wait_recv()
            self.bthird(w).wait_recv()

    def bcross(self, y):
        ref = self.down.at[y, :, self.here.c, :, 1]
        return rcopy(ref, ref, self.bcsems, y, self.here.core)

    def b_core(self, y):
        for p in (2 * y, 2 * y + 1):
            self.z_wait(7 + p)
        self.bcross(y).start()

    def b_done(self):
        for y in (0, 1):
            self.bcross(y).wait_recv()

    def drain(self):
        for k in range(11):
            for j in range(3):
                self.zcopy(k, j).wait_send()
        for u in range(14):
            self.first(u).wait_send()
            self.second(u).wait_send()
            self.third(u).wait_send()
            self.cross(u).wait_send()
        for w in (0, 1):
            self.bfirst(w).wait_send()
            self.bsecond(w).wait_send()
            self.bthird(w).wait_send()
            self.bcross(w).wait_send()


class Scatter:
    def __init__(
        self, here, up, down, gup, gdown, rc, r1, r2, zsend, zland, brest, bzland, br1, br2,
        sems, zsems, bzsems, bsems,
    ):
        self.here, self.up, self.down, self.gup, self.gdown = here, up, down, gup, gdown
        self.rc, self.r1, self.r2 = rc, r1, r2
        self.zsend, self.zland, self.sems, self.zsems = zsend, zland, sems, zsems
        self.brest, self.bzland, self.br1, self.br2 = brest, bzland, br1, br2
        self.bzsems, self.bsems = bzsems, bsems

    def blk(self, u, y, x, c):
        if u < 4:
            return self.down.at[y, x, c, u]
        if u < 8:
            return self.up.at[u - 4, y, x, c]
        if u < 12:
            return self.gup.at[u - 8, y, x, c]
        pair = (u - 12) % 2
        return self.gdown.at[y, x, c, 2 * pair : 2 * pair + 2, (u - 12) // 2]

    def put(self, u, y, cols, value):
        value = value.astype(BF).reshape(2, 2, 2, 48, 256)
        if u < 4:
            self.down[y, :, :, u, :, :, cols] = value
        else:
            self.up[u - 4, y, :, :, :, :, cols] = value

    def cross(self, u):
        h = self.here
        return rcopy(
            self.blk(u, EVERY, EVERY, 1 - h.c), self.rc.at[u % 8], self.sems, (u, 0), h.core
        )

    def first(self, u):
        h = self.here
        if u % 2 == 0:
            src, device = self.blk(u, EVERY, 1 - h.x, h.c), h.xn
        else:
            src, device = self.blk(u, 1 - h.y, EVERY, h.c), h.yn
        return rcopy(src, self.r1.at[u], self.sems, (u, 1), device)

    def second(self, u):
        h = self.here
        if u % 2 == 0:
            src, device = self.r1.at[u, 1 - h.y], h.yn
        else:
            src, device = self.r1.at[u, 1 - h.x], h.xn
        return rcopy(src, self.r2.at[u], self.sems, (u, 2), device)

    def start(self, k):
        for u in (2 * k, 2 * k + 1):
            self.cross(u).start()

    def add_core(self, u):
        self.cross(u).wait_recv()
        mine = self.blk(u, EVERY, EVERY, self.here.c)
        mine[...] = (mine[...].astype(F32) + self.rc[u % 8].astype(F32)).astype(BF)

    def one(self, k):
        for u in (2 * k, 2 * k + 1):
            self.add_core(u)
            self.first(u).start()

    def two(self, k):
        h = self.here
        for u in (2 * k, 2 * k + 1):
            self.first(u).wait_recv()
            if u % 2 == 0:
                mine = self.blk(u, EVERY, h.x, h.c)
            else:
                mine = self.blk(u, h.y, EVERY, h.c)
            self.r1[u] = (mine[...].astype(F32) + self.r1[u].astype(F32)).astype(BF)
            self.second(u).start()

    def three(self, k):
        h = self.here
        sums = []
        for u in (2 * k, 2 * k + 1):
            self.second(u).wait_recv()
            at = h.y if u % 2 == 0 else h.x
            sums.append(self.r1[u, at].astype(F32) + self.r2[u].astype(F32))
        if k < 6:
            sums = [item.reshape(96, 768) for item in sums]
            for z in range(4):
                self.zsend[k, z] = jnp.concatenate(
                    [item[24 * z : 24 * z + 24] for item in sums], axis=0
                ).astype(BF)
        else:
            for half in (0, 1):
                self.zsend[k, 2 * half : 2 * half + 2] = sums[half].astype(BF)
        for s in (1, 2, 3):
            self.zcopy(k, s).start()

    def zcopy(self, k, s):
        h = self.here
        return rcopy(
            self.zsend.at[k, lax.rem(h.z + s, 4)], self.zland.at[k, s - 1], self.zsems,
            (k, s - 1), h.zn(s),
        )

    def last(self, k):
        h = self.here
        for s in (1, 2, 3):
            self.zcopy(k, s).wait_recv()
        total = self.zsend[k, h.z].astype(F32)
        for s in (1, 2, 3):
            total = total + self.zland[k, s - 1].astype(F32)
        return total

    def bz(self, s):
        h = self.here
        src = self.gdown.at[:, :, h.c, lax.rem(h.z + s, 4), 1]
        return rcopy(src, self.bzland.at[s - 1], self.bzsems, s - 1, h.zn(s))

    def b_one(self):
        for u in (14, 15):
            self.add_core(u)
        for s in (1, 2, 3):
            self.bz(s).start()

    def bfirst(self, w):
        h = self.here
        if w == 0:
            src, device = self.brest.at[:, 1 - h.x, :, 0:384], h.xn
        else:
            src, device = self.brest.at[1 - h.y, :, :, 384:768], h.yn
        return rcopy(src, self.br1.at[w], self.bsems, (w, 0), device)

    def bsecond(self, w):
        h = self.here
        if w == 0:
            src, device = self.br1.at[w, 1 - h.y], h.yn
        else:
            src, device = self.br1.at[w, 1 - h.x], h.xn
        return rcopy(src, self.br2.at[w], self.bsems, (w, 1), device)

    def b_two(self):
        h = self.here
        for s in (1, 2, 3):
            self.bz(s).wait_recv()
        total = self.gdown[:, :, h.c, h.z, 1].astype(F32)
        for s in (1, 2, 3):
            total = total + self.bzland[s - 1].astype(F32)
        self.brest[...] = total.astype(BF)
        for w in (0, 1):
            self.bfirst(w).start()

    def b_three(self):
        h = self.here
        for w in (0, 1):
            self.bfirst(w).wait_recv()
            if w == 0:
                mine = self.brest[:, h.x, :, 0:384]
            else:
                mine = self.brest[h.y, :, :, 384:768]
            self.br1[w] = (mine.astype(F32) + self.br1[w].astype(F32)).astype(BF)
            self.bsecond(w).start()

    def b_last(self, w):
        h = self.here
        self.bsecond(w).wait_recv()
        at = h.y if w == 0 else h.x
        return self.br1[w, at].astype(F32) + self.br2[w].astype(F32)

    def drain(self):
        for u in range(16):
            self.cross(u).wait_send()
        for u in range(14):
            self.first(u).wait_send()
            self.second(u).wait_send()
        for k in range(7):
            for s in (1, 2, 3):
                self.zcopy(k, s).wait_send()
        for s in (1, 2, 3):
            self.bz(s).wait_send()
        for w in (0, 1):
            self.bfirst(w).wait_send()
            self.bsecond(w).wait_send()


Z_START = ((1, 2), (3,), (7, 4), (5, 8), (6, 9), (10,), ())
Z_PASS = ((1,), (2,), (3, 7), (4,), (5, 8), (6, 9), (10,), (), (), (), ())


def mm(a, b):
    return lax.dot_general(a, b, (((1,), (0,)), ((), ())), preferred_element_type=F32)


def mt(a, b):
    return lax.dot_general(a, b, (((1,), (1,)), ((), ())), preferred_element_type=F32)


def tm(a, b):
    return lax.dot_general(a, b, (((0,), (0,)), ((), ())), preferred_element_type=F32)


def iota(shape, axis):
    return lax.broadcasted_iota(jnp.int32, shape, axis)


def lanes(hp):
    return pl.ds(pl.multiple_of(hp * 128, 128), 128)


def both(q):
    low = iota(q.shape, 1) < 64
    zero = jnp.zeros_like(q)
    return jnp.concatenate([jnp.where(low, q, zero), jnp.where(low, zero, q)], axis=0)


def merge(pair):
    rows = pair.shape[0] // 2
    low = iota((rows, 128), 1) < 64
    return jnp.where(low, pair[:rows], pair[rows:]).astype(BF)


def probs(key, query, bias, mask):
    scores = mt(key, query)
    if bias is not None:
        scores = scores + bias.astype(F32)
    scores = jnp.where(mask, scores, -1e30)
    expo = jnp.exp(scores - jnp.max(scores, axis=0, keepdims=True))
    return expo * (1.0 / jnp.sum(expo, axis=0, keepdims=True))


def rms(v):
    return lax.rsqrt(jnp.mean(v * v, axis=-1, keepdims=True) + eps)


def norm_back(v, gain, grad):
    r = rms(v)
    scaled = grad * gain
    inner = jnp.mean(scaled * v, axis=-1, keepdims=True)
    return r * scaled - v * (r * r * r * inner), jnp.sum(grad * v * r, axis=0, keepdims=True)


def gelu_both(v):
    c = 0.7978845608028654
    square = v * v
    t = jnp.tanh(c * v * (1.0 + 0.044715 * square))
    half = 0.5 * (1.0 + t)
    slope = half + 0.5 * v * (1.0 - t * t) * (c * (1.0 + 3 * 0.044715 * square))
    return v * half, slope


def layer_kernel(*refs):
    squares, up_in, down_in, gain_in, table_in = refs[:8], refs[8], refs[9], refs[10], refs[11]
    tlen, slen, count, x_in, cot, enc = refs[12:18]
    layer_out, g_dec, g_enc = refs[18:21]
    g_sq, g_up, g_down, g_gain, g_table = refs[21:29], *refs[29:33]
    (
        sq, up, down, gup, gdown, rc, r1, r2, zland, zland2, brest, bzland, br1, br2, small, small2,
        bias, h1, h2, h3, q1, k1, v1, o1, q2, o2, k2, v2, g, gp, x1, x2, stage,
        zs, zr, ss, sr, bs, br, bcs, bcr, ms, mr,
        rzs, rzr, rss, rsr, rbzs, rbzr, rbs, rbr, m2s, m2r, out_sem, credit,
    ) = refs[33:]
    here = Place()
    index = (here.y * 4 + here.x * 2 + here.c) * 4 + here.z
    for k in range(4):
        zland[k, here.z] = jnp.concatenate(
            [squares[2 * k][...].astype(F32), squares[2 * k + 1][...].astype(F32)], axis=0
        ).astype(BF)
    for k in range(2):
        zland[4 + k, here.z] = jnp.concatenate(
            [up_in[:, 768 * n : 768 * n + 768].astype(F32) for n in (2 * k, 2 * k + 1)], axis=0
        ).astype(BF)
    down[here.y, here.x, here.c, here.z] = down_in[...].reshape(2, 48, 768)
    spot = (iota((24, 768), 1) == iota((24, 768), 0) + 24 * index).astype(BF)
    small[0] = jnp.zeros((8, 768), F32)
    small[0, 0:3] = mm(gain_in[...], spot)
    here.enter()
    ga = Gather(
        here, sq, up, down, zland, (zs, zr), (ss, sr), (bs, br), (bcs, bcr)
    )
    m = Small(here, small, (ms, mr))
    rs = Scatter(
        here, up, down, gup, gdown, rc, r1, r2, zland, zland2, brest, bzland, br1, br2,
        (rss, rsr), (rzs, rzr), (rbzs, rbzr), (rbs, rbr),
    )
    m2 = Small(here, small2, (m2s, m2r))

    def tick(t):
        if t < 7:
            ga.z_finish(t)
            for item in Z_START[t]:
                ga.z_start(item)
        for item in Z_PASS[t]:
            ga.z_pass(item)
        if t < 4:
            m.finish(t)
            if t < 3:
                m.start(t + 1)
        if 0 <= t - 1 < 7:
            ga.mid(t - 1)
        if 0 <= t - 2 < 7:
            ga.core(t - 2)
        if 0 <= t - 3 < 7:
            ga.done(t - 3)
        if t == 0:
            ga.b_mid()
        if t == 1:
            ga.b_got()
        if t == 5:
            ga.b_core(0)
        if t == 7:
            ga.b_core(1)
        if t == 8:
            ga.b_done()

    def weight(u):
        return sq[u].reshape(768, 768)

    def columns(u, n):
        return sq[u, :, :, :, :, :, 256 * n : 256 * n + 256].reshape(768, 256)

    ga.z_start(0)
    ga.b_start()
    ga.z_pass(0)
    m.start(0)

    def bucket_hot(rows_are_buckets):
        shape = (32, 128) if rows_are_buckets else (128, 32)
        distance = iota(shape, 1 if rows_are_buckets else 0)
        level = jnp.minimum(distance, 16)
        for edge in thresholds:
            level = level + (distance >= edge).astype(jnp.int32)
        return level == iota(shape, 0 if rows_are_buckets else 1)

    by_distance = mm(table_in[...], bucket_hot(True).astype(BF))
    for head in range(12):
        row = jnp.broadcast_to(by_distance[head : head + 1, :], (128, 128))
        bias[head // 2, :, 128 * (head % 2) : 128 * (head % 2) + 128] = pltpu.roll(
            row, 0, 1, stride=1, stride_axis=0
        ).astype(BF)

    key_place, target_place = iota((128, 256), 0), iota((128, 256), 1) & 127
    causal = key_place <= target_place
    source_place = iota((512, 256), 0)

    def self_mask(ex):
        return causal & (key_place < tlen[ex])

    def cross_mask(ex):
        return source_place < slen[ex]

    row_place = iota((256, 1), 0)
    live = (
        ((row_place < 128) & (row_place < tlen[0]) & (0 < count[0]))
        | ((row_place >= 128) & (row_place - 128 < tlen[1]) & (1 < count[0]))
    ).astype(F32)

    for t in range(4):
        tick(t)
    gains = m.total()
    gain = [gains[i : i + 1, :] for i in range(3)]

    first = x_in[...].astype(F32)
    h1[...] = (first * rms(first) * gain[0]).astype(BF)
    for n in range(3):
        cols = slice(256 * n, 256 * n + 256)
        q1[:, cols] = mm(h1[...], columns(0, n)).astype(BF)
        k1[:, cols] = mm(h1[...], columns(1, n)).astype(BF)
    tick(4)
    for n in range(3):
        cols = slice(256 * n, 256 * n + 256)
        v1[:, cols] = mm(h1[...], columns(2, n)).astype(BF)

    def self_forward(hp, carry):
        for ex in range(2):
            rows = slice(128 * ex, 128 * ex + 128)
            query = both(q1[rows, lanes(hp)])
            p = probs(k1[rows, lanes(hp)], query, bias[hp], self_mask(ex)).astype(BF)
            o1[rows, lanes(hp)] = merge(tm(p, v1[rows, lanes(hp)]))
        return carry

    lax.fori_loop(0, 6, self_forward, 0)
    tick(5)
    x1[...] = x_in[...].astype(F32) + mm(o1[...], weight(3))
    h2[...] = (x1[...] * rms(x1[...]) * gain[1]).astype(BF)

    def encode(r, carry):
        rows = pl.ds(pl.multiple_of(r * 256, 256), 256)
        for n in range(3):
            cols = slice(256 * n, 256 * n + 256)
            k2[rows, cols] = mm(enc[rows, :], columns(4, n)).astype(BF)
            v2[rows, cols] = mm(enc[rows, :], columns(5, n)).astype(BF)
        return carry

    lax.fori_loop(0, 4, encode, 0)
    tick(6)
    for n in range(3):
        cols = slice(256 * n, 256 * n + 256)
        q2[:, cols] = mm(h2[...], columns(6, n)).astype(BF)

    def cross_forward(hp, carry):
        for ex in range(2):
            rows = slice(128 * ex, 128 * ex + 128)
            keys = slice(512 * ex, 512 * ex + 512)
            query = both(q2[rows, lanes(hp)])
            p = probs(k2[keys, lanes(hp)], query, None, cross_mask(ex)).astype(BF)
            o2[rows, lanes(hp)] = merge(tm(p, v2[keys, lanes(hp)]))
        return carry

    lax.fori_loop(0, 3, cross_forward, 0)
    tick(7)
    lax.fori_loop(3, 6, cross_forward, 0)
    x2[...] = x1[...] + mm(o2[...], weight(7))
    h3[...] = (x2[...] * rms(x2[...]) * gain[2]).astype(BF)
    tick(8)
    def hidden(n, carry):
        for part in range(3):
            lo = 256 * part
            a = mm(h3[...], up[n, :, :, :, :, :, lo : lo + 256].reshape(768, 256))
            active, slope = gelu_both(a)
            cols = pl.ds(pl.multiple_of(768 * n + lo, 256), 256)
            g[:, cols] = active.astype(BF)
            gp[:, cols] = slope.astype(BF)
        return carry

    lax.fori_loop(0, 4, hidden, 0)

    def keep_gain(i, term):
        for j in range(6):
            small2[0, 6 * i + j : 6 * i + j + 1, :] = term[:, 128 * j : 128 * j + 128]

    def df(cols=slice(None)):
        return (cot[:, cols].astype(F32) * live).astype(BF)

    def wide(e):
        return pl.ds(pl.multiple_of(768 * e, 256), 768)

    def grad_down(e, carry):
        turned = g[:, wide(e)].T
        for n in range(3):
            cols = slice(256 * n, 256 * n + 256)
            grad = mm(turned, df(cols)).astype(BF)
            gdown[lax.div(e, 2), lax.rem(e, 2), :, :, :, :, cols] = grad.reshape(2, 4, 2, 48, 256)
        return carry

    lax.fori_loop(0, 4, grad_down, 0)
    rs.start(6)
    rs.start(7)
    tick(9)

    def down_block(e):
        return down[lax.div(e, 2), lax.rem(e, 2)].reshape(768, 768)

    def inner_grad(e, carry):
        dg = mt(df(), down_block(e))
        gp[:, wide(e)] = (dg * gp[:, wide(e)].astype(F32)).astype(BF)
        return carry

    lax.fori_loop(0, 2, inner_grad, 0)
    rs.one(6)
    lax.fori_loop(2, 4, inner_grad, 0)
    rs.b_one()

    def grad_up(n, carry):
        turned = h3[...].T
        for part in range(3):
            cols = slice(256 * part, 256 * part + 256)
            source = pl.ds(pl.multiple_of(768 * n + 256 * part, 256), 256)
            grad = mm(turned, gp[:, source]).astype(BF)
            gup[n, :, :, :, :, :, cols] = grad.reshape(2, 2, 2, 2, 48, 256)
        return carry

    lax.fori_loop(0, 2, grad_up, 0)
    rs.start(4)
    lax.fori_loop(2, 4, grad_up, 0)
    rs.start(5)
    rs.one(4)
    stage[0] = jnp.zeros((256, 768), F32)
    stage[1] = x2[...]

    def inner_back(n, carry):
        stage[0] += mt(gp[:, wide(n)], up[n].reshape(768, 768))
        return carry

    lax.fori_loop(0, 4, inner_back, 0)
    rs.one(5)
    pl.semaphore_signal(credit, inc=1, device_id=here.core, device_id_type=MESH)
    rs.two(6)
    d_norm, gain_three = norm_back(x2[...], gain[2], stage[0])
    keep_gain(2, gain_three)
    x2[...] = cot[...].astype(F32) * live + d_norm
    ga.drain()

    def put_grads(value, rows, pairs):
        def half_rows(y, carry):
            turned = value[:, pl.ds(pl.multiple_of(384 * y, 128), 384)].T
            for u, ref in pairs:
                for n in range(3):
                    cols = slice(256 * n, 256 * n + 256)
                    rs.put(u, y, cols, mm(turned, ref[:, cols]))
            return carry

        lax.fori_loop(0, 2, half_rows, 0)

    h3[...] = x2[...].astype(BF)
    put_grads(o2, 256, ((7, h3),))
    o2[...] = mt(h3[...], weight(7)).astype(BF)

    def cross_backward(hp, carry):
        for ex in range(2):
            rows = slice(128 * ex, 128 * ex + 128)
            keys = slice(512 * ex, 512 * ex + 512)
            query, d_out = both(q2[rows, lanes(hp)]), both(o2[rows, lanes(hp)])
            key, value = k2[keys, lanes(hp)], v2[keys, lanes(hp)]
            p = probs(key, query, None, cross_mask(ex))
            dp = mt(value, d_out)
            delta = jnp.sum(dp * p, axis=0, keepdims=True)
            ds = (p * (dp - delta)).astype(BF)
            q2[rows, lanes(hp)] = merge(tm(ds, key))
            k2[keys, lanes(hp)] = mm(ds, query).astype(BF)
            v2[keys, lanes(hp)] = mm(p.astype(BF), d_out).astype(BF)
        return carry

    lax.fori_loop(0, 2, cross_backward, 0)
    rs.two(4)
    lax.fori_loop(2, 4, cross_backward, 0)
    rs.three(6)
    lax.fori_loop(4, 6, cross_backward, 0)
    rs.two(5)
    put_grads(h2, 256, ((6, q2),))
    pl.semaphore_wait(credit, 1)
    rs.start(3)
    put_grads(enc, 1024, ((4, k2), (5, v2)))
    rs.start(2)

    def finish(k):
        total = rs.last(k)
        if k < 4:
            g_sq[2 * k][...] = total[:24]
            g_sq[2 * k + 1][...] = total[24:]
        elif k < 6:
            g_up[:, 1536 * (k - 4) : 1536 * (k - 4) + 768] = total[:24]
            g_up[:, 1536 * (k - 4) + 768 : 1536 * (k - 4) + 1536] = total[24:]
        else:
            g_down[0:48, :] = total

    rs.one(3)
    d_norm, gain_two = norm_back(x1[...], gain[1], mt(q2[...], weight(6)))
    keep_gain(1, gain_two)
    x2[...] = x2[...] + d_norm
    rs.one(2)
    rs.three(4)
    rs.b_two()

    def result(e, carry):
        stage[1] += mm(g[:, wide(e)], down_block(e))
        return carry

    lax.fori_loop(0, 4, result, 0)
    layer_out[...] = (stage[1] * live).astype(BF)
    h3[...] = x2[...].astype(BF)
    put_grads(o1, 256, ((3, h3),))
    o1[...] = mt(h3[...], weight(3)).astype(BF)
    rs.three(5)
    turn = (iota((128, 256), 0) + (iota((128, 256), 1) & 127) == 127).astype(BF)

    def self_backward(hp, carry):
        scores = []
        for ex in range(2):
            rows = slice(128 * ex, 128 * ex + 128)
            query, d_out = both(q1[rows, lanes(hp)]), both(o1[rows, lanes(hp)])
            key, value = k1[rows, lanes(hp)], v1[rows, lanes(hp)]
            p = probs(key, query, bias[hp], self_mask(ex))
            dp = mt(value, d_out)
            delta = jnp.sum(dp * p, axis=0, keepdims=True)
            ds = (p * (dp - delta)).astype(BF)
            q1[rows, lanes(hp)] = merge(tm(ds, key))
            k1[rows, lanes(hp)] = mm(ds, query).astype(BF)
            v1[rows, lanes(hp)] = mm(p.astype(BF), d_out).astype(BF)
            scores.append(ds)
        pair = mm(turn, jnp.concatenate(scores, axis=0))
        for head in range(2):
            skew = pltpu.roll(pair[:, 128 * head : 128 * head + 128], 0, 1, stride=1, stride_axis=0)
            small2[0, pl.ds(18 + 2 * hp + head, 1), :] = jnp.sum(skew, axis=0, keepdims=True)
        return carry

    lax.fori_loop(0, 6, self_backward, 0)
    rs.two(3)
    rs.b_three()
    put_grads(h1, 256, ((2, v1), (0, q1), (1, k1)))
    rs.start(1)
    rs.start(0)
    rs.two(2)
    rs.one(1)
    rs.one(0)
    rs.three(3)
    stage[0] = jnp.zeros((256, 768), F32)

    def first_back(y, carry):
        cols = pl.ds(pl.multiple_of(384 * y, 128), 384)
        for u, ref in ((0, q1), (1, k1), (2, v1)):
            stage[0, :, cols] += mt(ref[...], sq[u, y].reshape(384, 768))
        return carry

    lax.fori_loop(0, 2, first_back, 0)
    d_norm, gain_one = norm_back(x_in[...].astype(F32), gain[0], stage[0])
    g_dec[...] = x2[...] + d_norm
    keep_gain(0, gain_one)
    small2[0, 30:32, :] = jnp.zeros((2, 128), F32)
    m2.start(0)
    rs.three(2)
    finish(6)
    finish(4)
    finish(5)
    m2.finish(0)
    m2.start(1)

    def out_copy(r):
        return pltpu.make_async_copy(
            stage.at[lax.rem(r, 2)],
            g_enc.at[pl.ds(pl.multiple_of(256 * r, 256), 256)],
            out_sem.at[r],
        )

    def encoder_grad(r, carry):
        rows = pl.ds(pl.multiple_of(256 * r, 256), 256)
        slot = lax.rem(r, 2)
        for y in range(2):
            cols = slice(384 * y, 384 * y + 384)
            stage[slot, :, cols] = mt(k2[rows, :], sq[4, y].reshape(384, 768))
            stage[slot, :, cols] += mt(v2[rows, :], sq[5, y].reshape(384, 768))
        out_copy(r).start()
        return carry

    lax.fori_loop(0, 2, encoder_grad, 0)
    rs.two(1)
    m2.finish(1)
    m2.start(2)
    for w in (0, 1):
        g_down[48:96, 384 * w : 384 * w + 384] = rs.b_last(w)
    finish(3)
    out_copy(0).wait()
    out_copy(1).wait()
    lax.fori_loop(2, 4, encoder_grad, 0)
    rs.two(0)
    m2.finish(2)
    m2.start(3)
    rs.three(1)
    finish(2)
    rs.three(0)
    m2.finish(3)
    reduced = m2.total()
    sums = jnp.concatenate(
        [
            jnp.concatenate([reduced[6 * i + j : 6 * i + j + 1, :] for j in range(6)], axis=1)
            for i in range(3)
        ],
        axis=0,
    )
    pick = (iota((768, 24), 0) == iota((768, 24), 1) + 24 * index).astype(F32)
    g_gain[...] = lax.dot_general(
        sums, pick, (((1,), (0,)), ((), ())), preferred_element_type=F32,
        precision=lax.Precision.HIGHEST,
    )
    distance = (iota((32, 128), 1) + 1) & 127
    level = jnp.minimum(distance, 16)
    for edge in thresholds:
        level = level + (distance >= edge).astype(jnp.int32)
    hot = (level == iota((32, 128), 0)).astype(F32)
    g_table[...] = lax.dot_general(
        reduced[18:30, :], hot, (((1,), (1,)), ((), ())), preferred_element_type=F32,
        precision=lax.Precision.HIGHEST,
    )
    finish(1)
    finish(0)
    rs.drain()
    out_copy(2).wait()
    out_copy(3).wait()


VM = pl.BlockSpec(memory_space=pltpu.VMEM)
SM = pl.BlockSpec(memory_space=pltpu.SMEM)
ANY = pl.BlockSpec(memory_space=pl.ANY)


def layer_call(*args):
    shape = jax.ShapeDtypeStruct
    dims = ((11, 3), (14, 4), (2, 3), (2,), (6,), (7, 3), (16, 3), (3,), (2, 2), (6,))
    half = lambda *dims: pltpu.VMEM(dims, BF)
    return pl.pallas_call(
        layer_kernel,
        out_shape=(
            shape((256, 768), BF),
            shape((256, 768), F32),
            shape((1024, 768), F32),
            *[shape((24, 768), F32)] * 8,
            shape((24, 3072), F32),
            shape((96, 768), F32),
            shape((3, 24), F32),
            shape((12, 32), F32),
        ),
        in_specs=[VM] * 12 + [SM] * 3 + [VM] * 3,
        out_specs=(VM, VM, ANY) + (VM,) * 12,
        scratch_shapes=[
            half(8, 2, 2, 2, 2, 48, 768),
            half(4, 2, 2, 2, 2, 48, 768),
            half(2, 2, 2, 4, 2, 48, 768),
            half(4, 2, 2, 2, 2, 48, 768),
            half(2, 2, 2, 4, 2, 48, 768),
            half(8, 2, 2, 2, 48, 768),
            half(14, 2, 2, 48, 768),
            half(14, 2, 48, 768),
            half(7, 4, 48, 768),
            half(7, 3, 48, 768),
            half(2, 2, 48, 768),
            half(3, 2, 2, 48, 768),
            half(2, 2, 48, 384),
            half(2, 48, 384),
            pltpu.VMEM((10, 8, 768), F32),
            pltpu.VMEM((10, 32, 128), F32),
            half(6, 128, 256),
            *[half(256, 768)] * 3,
            *[half(256, 768)] * 4,
            *[half(256, 768)] * 2,
            *[half(1024, 768)] * 2,
            *[half(256, 3072)] * 2,
            *[pltpu.VMEM((256, 768), F32)] * 2,
            pltpu.VMEM((2, 256, 768), F32),
            *[pltpu.SemaphoreType.DMA(each) for each in dims for _ in range(2)],
            pltpu.SemaphoreType.DMA((4,)),
            pltpu.SemaphoreType.REGULAR,
        ],
        compiler_params=pltpu.CompilerParams(
            collective_id=0, has_side_effects=True, vmem_limit_bytes=64 * 2**20 - 2**16
        ),
        name="layer",
    )(*args)


def hand_out_kernel(*refs):
    count = (len(refs) - 2) // 3
    source, target, held = refs[:count], refs[count : 2 * count], refs[2 * count : 3 * count]
    got, put = refs[3 * count :]
    ins = [pltpu.make_async_copy(source[i], held[i], got.at[i]) for i in range(count)]
    outs = [pltpu.make_async_copy(held[i], target[i], put.at[i]) for i in range(count)]
    for copy in ins:
        copy.start()
    for i in range(count):
        ins[i].wait()
        outs[i].start()
    for copy in outs:
        copy.wait()


def hand_out(arrays):
    return pl.pallas_call(
        hand_out_kernel,
        out_shape=tuple(jax.ShapeDtypeStruct(item.shape, item.dtype) for item in arrays),
        in_specs=[ANY] * len(arrays),
        out_specs=(ANY,) * len(arrays),
        scratch_shapes=[pltpu.VMEM(item.shape, item.dtype) for item in arrays]
        + [pltpu.SemaphoreType.DMA((len(arrays),))] * 2,
        name="hand_out",
    )(*arrays)


def by_kernel(
    decoder_in,
    encoder_out,
    self_query,
    self_key,
    self_value,
    self_output,
    cross_query,
    cross_key,
    cross_value,
    cross_output,
    hidden_in,
    hidden_out,
    norm_gains,
    bias_table,
    target_lengths,
    source_lengths,
    example_counts,
    cotangent,
):
    results = layer_call(
        self_query,
        self_key,
        self_value,
        self_output,
        cross_key,
        cross_value,
        cross_query,
        cross_output,
        hidden_in,
        hidden_out,
        norm_gains,
        bias_table.T,
        target_lengths,
        source_lengths,
        example_counts,
        decoder_in.reshape(256, 768),
        cotangent.reshape(256, 768),
        encoder_out.reshape(1024, 768),
    )
    out, g_dec, g_enc, *g_sq, g_up, g_down, g_gain, g_table = hand_out(results)
    return (
        out.reshape(decoder_in.shape),
        g_dec.reshape(decoder_in.shape),
        g_enc.reshape(encoder_out.shape),
        *g_sq[:4],
        g_sq[6],
        g_sq[4],
        g_sq[5],
        g_sq[7],
        g_up,
        g_down,
        g_gain,
        g_table.T,
    )


def plain(
    decoder_in,
    encoder_out,
    self_query,
    self_key,
    self_value,
    self_output,
    cross_query,
    cross_key,
    cross_value,
    cross_output,
    hidden_in,
    hidden_out,
    norm_gains,
    bias_table,
    target_lengths,
    source_lengths,
    example_counts,
    cotangent,
):
    gathered = (
        lax.all_gather(self_query, AXES, axis=0, tiled=True),
        lax.all_gather(self_key, AXES, axis=0, tiled=True),
        lax.all_gather(self_value, AXES, axis=0, tiled=True),
        lax.all_gather(self_output, AXES, axis=0, tiled=True),
        lax.all_gather(cross_query, AXES, axis=0, tiled=True),
        lax.all_gather(cross_key, AXES, axis=0, tiled=True),
        lax.all_gather(cross_value, AXES, axis=0, tiled=True),
        lax.all_gather(cross_output, AXES, axis=0, tiled=True),
        lax.all_gather(hidden_in, AXES, axis=0, tiled=True),
        lax.all_gather(hidden_out, AXES, axis=0, tiled=True),
        lax.all_gather(norm_gains, AXES, axis=1, tiled=True),
    )
    w_query, w_key, w_value, w_out, x_query, x_key, x_value, x_out, w_up, w_down, gain_all = (
        gathered
    )
    slots = jnp.arange(decoder_in.shape[0], dtype=jnp.int32)
    length = decoder_in.shape[1]
    source = encoder_out.shape[1]
    width = decoder_in.shape[2]
    hidden_width = hidden_in.shape[1]
    place = jnp.arange(length, dtype=jnp.int32)
    source_place = jnp.arange(source, dtype=jnp.int32)
    live = (
        (slots < example_counts[0])[:, None] & (place[None, :] < target_lengths[:, None])
    ).astype(jnp.float32)[:, :, None]
    self_mask = (place[None, :] <= place[:, None])[None, None] & (
        place[None, None, None, :] < target_lengths[:, None, None, None]
    )
    cross_mask = source_place[None, None, None, :] < source_lengths[:, None, None, None]
    onehot = (
        buckets(length)[:, :, None] == jnp.arange(bias_table.shape[0], dtype=jnp.int32)
    ).astype(jnp.bfloat16)
    bias = jnp.einsum("lsn,nh->hls", onehot, bias_table, preferred_element_type=jnp.float32)
    gains = gain_all.astype(jnp.float32)
    inputs = decoder_in.astype(jnp.float32)
    first = normalize(inputs, gains[0]).astype(jnp.bfloat16)
    query = project(first, w_query).astype(jnp.bfloat16)
    key = project(first, w_key).astype(jnp.bfloat16)
    value = project(first, w_value).astype(jnp.bfloat16)
    mixed, logsum_self = attention_forward(
        split_heads(query), split_heads(key), split_heads(value), bias, self_mask
    )
    after_self = inputs + project(mixed, w_out)
    second = normalize(after_self, gains[1]).astype(jnp.bfloat16)
    cross_q = project(second, x_query).astype(jnp.bfloat16)
    cross_k = project(encoder_out, x_key).astype(jnp.bfloat16)
    cross_v = project(encoder_out, x_value).astype(jnp.bfloat16)
    crossed, logsum_cross = attention_forward(
        split_heads(cross_q), split_heads(cross_k), split_heads(cross_v), 0.0, cross_mask
    )
    after_cross = after_self + project(crossed, x_out)
    third = normalize(after_cross, gains[2]).astype(jnp.bfloat16)
    inner = project(third, w_up)
    active = jax.nn.gelu(inner).astype(jnp.bfloat16)
    result = after_cross + project(active, w_down)
    layer_out = (result * live).astype(jnp.bfloat16)
    regathered = (
        lax.all_gather(self_query, AXES, axis=0, tiled=True),
        lax.all_gather(self_key, AXES, axis=0, tiled=True),
        lax.all_gather(self_value, AXES, axis=0, tiled=True),
        lax.all_gather(self_output, AXES, axis=0, tiled=True),
        lax.all_gather(cross_query, AXES, axis=0, tiled=True),
        lax.all_gather(cross_key, AXES, axis=0, tiled=True),
        lax.all_gather(cross_value, AXES, axis=0, tiled=True),
        lax.all_gather(cross_output, AXES, axis=0, tiled=True),
        lax.all_gather(hidden_in, AXES, axis=0, tiled=True),
        lax.all_gather(hidden_out, AXES, axis=0, tiled=True),
        lax.all_gather(norm_gains, AXES, axis=1, tiled=True),
    )
    w_query, w_key, w_value, w_out, x_query, x_key, x_value, x_out, w_up, w_down, gain_all = (
        regathered
    )
    gains = gain_all.astype(jnp.float32)
    d_result = cotangent.astype(jnp.float32) * live
    d_branch = d_result.astype(jnp.bfloat16)
    grad_down = outer_sum(active, d_branch)
    d_inner = gelu_grad(inner, project_back(d_branch, w_down)).astype(jnp.bfloat16)
    grad_up = outer_sum(third, d_inner)
    d_cross, gain_three = norm_grad(after_cross, gains[2], project_back(d_inner, w_up))
    d_cross = d_cross + d_result
    d_branch = d_cross.astype(jnp.bfloat16)
    grad_x_out = outer_sum(crossed, d_branch)
    d_crossed = project_back(d_branch, x_out).astype(jnp.bfloat16)
    dq_cross, dk_cross, dv_cross, unused = attention_backward(
        split_heads(cross_q),
        split_heads(cross_k),
        split_heads(cross_v),
        0.0,
        cross_mask,
        logsum_cross,
        split_heads(d_crossed),
    )
    grad_x_query = outer_sum(second, dq_cross)
    grad_x_key = outer_sum(encoder_out, dk_cross)
    grad_x_value = outer_sum(encoder_out, dv_cross)
    grad_encoder = project_back(dk_cross, x_key) + project_back(dv_cross, x_value)
    d_self, gain_two = norm_grad(after_self, gains[1], project_back(dq_cross, x_query))
    d_self = d_self + d_cross
    d_branch = d_self.astype(jnp.bfloat16)
    grad_w_out = outer_sum(mixed, d_branch)
    d_mixed = project_back(d_branch, w_out).astype(jnp.bfloat16)
    dq_self, dk_self, dv_self, d_scores = attention_backward(
        split_heads(query),
        split_heads(key),
        split_heads(value),
        bias,
        self_mask,
        logsum_self,
        split_heads(d_mixed),
    )
    d_bias = jnp.sum(d_scores, axis=0, dtype=jnp.float32)
    table_term = jnp.einsum(
        "hls,lsn->nh", d_bias, onehot.astype(jnp.float32), precision=lax.Precision.HIGHEST
    )
    grad_w_query = outer_sum(first, dq_self)
    grad_w_key = outer_sum(first, dk_self)
    grad_w_value = outer_sum(first, dv_self)
    d_first = (
        project_back(dq_self, w_query)
        + project_back(dk_self, w_key)
        + project_back(dv_self, w_value)
    )
    d_inputs, gain_one = norm_grad(inputs, gains[0], d_first)
    grad_decoder = d_inputs + d_self
    gain_terms = jnp.stack([gain_one, gain_two, gain_three], axis=1)
    flats = flat_rows(
        (
            grad_w_query,
            grad_w_key,
            grad_w_value,
            grad_w_out,
            grad_x_query,
            grad_x_key,
            grad_x_value,
            grad_x_out,
            grad_up,
            grad_down,
            gain_terms,
        )
    )
    summed = (
        lax.psum_scatter(flats[0], AXES, scatter_dimension=0, tiled=True),
        lax.psum_scatter(flats[1], AXES, scatter_dimension=0, tiled=True),
        lax.psum_scatter(flats[2], AXES, scatter_dimension=0, tiled=True),
        lax.psum_scatter(flats[3], AXES, scatter_dimension=0, tiled=True),
        lax.psum_scatter(flats[4], AXES, scatter_dimension=0, tiled=True),
        lax.psum_scatter(flats[5], AXES, scatter_dimension=0, tiled=True),
        lax.psum_scatter(flats[6], AXES, scatter_dimension=0, tiled=True),
        lax.psum_scatter(flats[7], AXES, scatter_dimension=0, tiled=True),
        lax.psum_scatter(flats[8], AXES, scatter_dimension=0, tiled=True),
        lax.psum_scatter(flats[9], AXES, scatter_dimension=0, tiled=True),
        lax.psum_scatter(flats[10], AXES, scatter_dimension=0, tiled=True),
    )
    shaped = unflat_rows(
        summed, (width, width, width, width, width, width, width, width, hidden_width, width, 3)
    )
    sums = shaped[:10] + (jnp.transpose(shaped[10]),)
    grad_table = lax.psum(table_term, AXES)
    return (
        layer_out,
        grad_decoder,
        grad_encoder,
        sums[0],
        sums[1],
        sums[2],
        sums[3],
        sums[4],
        sums[5],
        sums[6],
        sums[7],
        sums[8],
        sums[9],
        sums[10],
        grad_table,
    )


def solution(mesh):
    rows = P(AXES, None)
    slots = P(AXES, None, None)
    flat = P(AXES)
    gains = P(None, AXES)
    small = mesh.shape["dp"] == 8 and mesh.shape["fsdp"] == 4
    return jax.shard_map(
        by_kernel if small else plain,
        mesh=mesh,
        in_specs=(slots, slots) + (rows,) * 10 + (gains, P(), flat, flat, flat, slots),
        out_specs=(slots, slots, slots) + (rows,) * 10 + (gains, P()),
        check_vma=False,
    )
```

```python
import functools

import jax
import jax.numpy as jnp
from jax import lax
from jax.experimental import pallas as pl
from jax.experimental.pallas import tpu as pltpu
from jax.sharding import PartitionSpec as P

H = 12
AXES = ("dp", "fsdp")
MESH = pl.DeviceIdType.MESH
BF = jnp.bfloat16
F32 = jnp.float32


eps = 1e-06
thresholds = [19, 21, 24, 27, 31, 35, 40, 46, 52, 59, 67, 77, 87, 99, 113]


def normalize(v, gain):
    return v * lax.rsqrt(jnp.mean(v * v, axis=-1, keepdims=True) + eps) * gain


def norm_grad(v, gain, grad):
    _, pullback = jax.vjp(normalize, v, gain)
    return pullback(grad)


def gelu_grad(v, grad):
    _, pullback = jax.vjp(jax.nn.gelu, v)
    return pullback(grad)[0]


def project(v, weight):
    return jnp.einsum("btd,df->btf", v, weight, preferred_element_type=jnp.float32)


def project_back(grad, weight):
    return jnp.einsum("btf,df->btd", grad, weight, preferred_element_type=jnp.float32)


def outer_sum(v, grad):
    return jnp.einsum("btd,btf->df", v, grad, preferred_element_type=jnp.float32)


def split_heads(v):
    return v.reshape(v.shape[0], v.shape[1], H, v.shape[2] // H)


def join_heads(v):
    return v.reshape(v.shape[0], v.shape[1], v.shape[2] * v.shape[3])


def flat_rows(items):
    return tuple((item.reshape(-1) for item in items))


def unflat_rows(items, widths):
    return tuple((item.reshape(-1, width) for item, width in zip(items, widths)))


def buckets(length):
    place = jnp.arange(length, dtype=jnp.int32)
    distance = jnp.maximum(place[:, None] - place[None, :], 0)
    level = jnp.minimum(distance, 16)
    for edge in thresholds:
        level = level + (distance >= edge).astype(jnp.int32)
    return level


def scores_of(query, key, bias, mask):
    scores = jnp.einsum("blhd,bshd->bhls", query, key, preferred_element_type=jnp.float32) + bias
    return jnp.where(mask, scores, -1e30)


def attention_forward(query, key, value, bias, mask):
    scores = scores_of(query, key, bias, mask)
    top = jnp.max(scores, axis=-1, keepdims=True)
    expo = jnp.exp(scores - top)
    total = jnp.sum(expo, axis=-1, keepdims=True)
    probs = (expo / total).astype(jnp.bfloat16)
    mixed = jnp.einsum("bhls,bshd->blhd", probs, value, preferred_element_type=jnp.float32)
    return (join_heads(mixed).astype(jnp.bfloat16), top + jnp.log(total))


def attention_backward(query, key, value, bias, mask, logsum, d_out):
    probs = jnp.exp(scores_of(query, key, bias, mask) - logsum)
    d_probs = jnp.einsum("blhd,bshd->bhls", d_out, value, preferred_element_type=jnp.float32)
    delta = jnp.sum(d_probs * probs, axis=-1, keepdims=True)
    d_scores = (probs * (d_probs - delta)).astype(jnp.bfloat16)
    d_query = jnp.einsum(
        "bhls,bshd->blhd", d_scores, key, preferred_element_type=jnp.float32
    ).astype(jnp.bfloat16)
    d_key = jnp.einsum(
        "bhls,blhd->bshd", d_scores, query, preferred_element_type=jnp.float32
    ).astype(jnp.bfloat16)
    d_value = jnp.einsum(
        "bhls,blhd->bshd", probs.astype(jnp.bfloat16), d_out, preferred_element_type=jnp.float32
    ).astype(jnp.bfloat16)
    return (join_heads(d_query), join_heads(d_key), join_heads(d_value), d_scores)


class Place:
    def __init__(self):
        d = lax.axis_index("dp")
        self.z = lax.axis_index("fsdp")
        self.c = lax.rem(d, 2)
        self.x = lax.rem(lax.div(d, 2), 2)
        self.y = lax.div(d, 4)

    def dev(self, y, x, c, z):
        return ((y * 2 + x) * 2 + c, z)

    @property
    def core(self):
        return self.dev(self.y, self.x, 1 - self.c, self.z)

    @property
    def xn(self):
        return self.dev(self.y, 1 - self.x, self.c, self.z)

    @property
    def yn(self):
        return self.dev(1 - self.y, self.x, self.c, self.z)

    @property
    def across(self):
        return self.dev(1 - self.y, 1 - self.x, self.c, self.z)

    def zn(self, step):
        return self.dev(self.y, self.x, self.c, lax.rem(self.z + step, 4))

    def greet(self):
        bar = pltpu.get_barrier_semaphore()
        others = [self.core, self.xn, self.yn, self.across] + [self.zn(s) for s in (1, 2, 3)]
        for other in others:
            pl.semaphore_signal(bar, inc=1, device_id=other, device_id_type=MESH)

    def enter(self):
        pl.semaphore_wait(pltpu.get_barrier_semaphore(), 7)


def rcopy(src, dst, sems, landing, device, leaving=None):
    send, recv = sems
    return pltpu.make_async_remote_copy(
        src_ref=src,
        dst_ref=dst,
        send_sem=send.at[landing if leaving is None else leaving],
        recv_sem=recv.at[landing],
        device_id=device,
        device_id_type=MESH,
    )


class Small:
    def __init__(self, here, buf, sems):
        self.here, self.buf, self.sems = here, buf, sems

    def copies(self, stage):
        h = self.here
        base, devices = (
            (0, (h.core,)),
            (2, (h.xn, h.yn, h.across)),
            (6, (h.zn(1), h.zn(2), h.zn(3))),
        )[stage]
        at = (0, 1, 4)[stage]
        return [
            rcopy(self.buf.at[base], self.buf.at[base + 1 + i], self.sems, at + i, device)
            for i, device in enumerate(devices)
        ]

    def start(self, stage):
        for copy in self.copies(stage):
            copy.start()

    def finish(self, stage):
        for copy in self.copies(stage):
            copy.wait()
        b = self.buf
        if stage == 0:
            b[2] = b[0] + b[1]
        if stage == 1:
            b[6] = b[2] + b[3] + (b[4] + b[5])

    def total(self):
        b = self.buf
        return b[6] + b[7] + (b[8] + b[9])


EVERY = slice(None)


def sent(here, sems, leaving, ref):
    send, recv = sems
    pltpu.make_async_remote_copy(
        src_ref=ref, dst_ref=ref, send_sem=send.at[leaving], recv_sem=recv.at[0], device_id=here.core,
        device_id_type=MESH,
    ).wait_send()


class Gather:
    def __init__(self, here, sq, up, down, zland, early, zsems, sems, bsems, bcsems, like):
        self.here, self.sq, self.up, self.down = here, sq, up, down
        self.zland, self.early, self.zsems, self.sems = zland, early, zsems, sems
        self.bsems, self.bcsems, self.like = bsems, bcsems, like

    def blk(self, u, y, x, c):
        if u < 8:
            return self.sq.at[u, y, x, c]
        if u < 12:
            return self.up.at[u - 8, y, x, c]
        return self.down.at[y, x, c, 2 * (u - 12) : 2 * (u - 12) + 2, 0]

    def zpath(self, j):
        z = self.here.z
        low = z < 2
        if j == 0:
            source, target = z, jnp.where(low, z + 1, z - 1)
        elif j == 1:
            far = jnp.where(z == 0, 2, 1)
            near = jnp.where(z == 1, 0, 3)
            source, target = z, jnp.where((z == 0) | (z == 3), far, near)
        else:
            source = jnp.where(z == 1, 2, jnp.where(z == 2, 1, z))
            target = jnp.where(low, 3, 0)
            target = jnp.where(z == 1, 0, jnp.where(z == 2, 3, target))
        return source, target, lax.rem(source - target + 4, 4) - 1

    def zwait(self):
        return jnp.where(self.here.z < 2, 0, 2)

    def zref(self, k, z):
        h = self.here
        if k < 6:
            return self.zland.at[k, z]
        if k == 6:
            return self.down.at[h.y, h.x, h.c, z, 0]
        p = (k - 7) % 4
        if k < 11:
            return self.down.at[p // 2, p % 2, h.c, z, 1]
        return self.early.at[p // 2, p % 2, lax.div(z, 2), lax.rem(z, 2)]

    def zcopy(self, k, j):
        h = self.here
        source, target, landing = self.zpath(j)
        ref = self.zref(k, source)
        target = h.dev(h.y, h.x, h.c, target)
        return rcopy(ref, ref, self.zsems, 3 * k + landing, target, 0 if k < 8 else 1 if k < 11 else 2)

    def zgot(self, k, r):
        h = self.here
        ref = self.zref(k, lax.rem(h.z + 1 + r, 4))
        return rcopy(ref, ref, self.zsems, 3 * k + r, h.zn(1), 0)

    def z_start(self, k):
        z = self.here.z
        self.zcopy(k, 0).start()
        self.zcopy(k, 1).start()

        @pl.when((z == 0) | (z == 3))
        def _():
            self.zcopy(k, 2).start()

    def z_pass(self, k):
        z = self.here.z

        @pl.when((z == 1) | (z == 2))
        def _():
            self.zgot(k, self.zwait()).wait_recv()
            self.zcopy(k, 2).start()

    def z_wait(self, k):
        z = self.here.z
        self.zgot(k, 1).wait_recv()
        self.zgot(k, 2 - self.zwait()).wait_recv()

        @pl.when((z == 0) | (z == 3))
        def _():
            self.zgot(k, self.zwait()).wait_recv()

    def z_finish(self, k):
        h = self.here
        self.z_wait(k)
        if k < 6:
            slabs = self.zland[k].astype(F32)
            for half in (0, 1):
                rows = jnp.concatenate(
                    [slabs[z, 24 * half : 24 * half + 24] for z in range(4)], axis=0
                ).astype(BF).reshape(2, 48, 768)
                u = 2 * k + half
                if u < 8:
                    self.sq[u, h.y, h.x, h.c] = rows
                else:
                    self.up[u - 8, h.y, h.x, h.c] = rows
        for u in (2 * k, 2 * k + 1):
            self.first(u).start()
            self.second(u).start()

    def nbrs(self, u):
        h = self.here
        return (h.yn, h.xn) if u % 2 == 0 else (h.xn, h.yn)

    def group(self, u):
        return 0 if u < 4 else 2 if u > 9 else 1

    def own(self, u):
        h = self.here
        return self.blk(u, h.y, h.x, h.c)

    def got(self, u):
        h = self.here
        return self.blk(u, 1 - h.y, h.x, h.c) if u % 2 == 0 else self.blk(u, h.y, 1 - h.x, h.c)

    def first(self, u):
        return rcopy(self.own(u), self.own(u), self.sems, 4 * u, self.nbrs(u)[0], self.group(u))

    def second(self, u):
        return rcopy(self.own(u), self.own(u), self.sems, 4 * u + 1, self.nbrs(u)[1], self.group(u))

    def third(self, u):
        return rcopy(self.got(u), self.got(u), self.sems, 4 * u + 2, self.nbrs(u)[1], self.group(u))

    def cross(self, u):
        ref = self.blk(u, EVERY, EVERY, self.here.c)
        return rcopy(ref, ref, self.sems, 4 * u + 3, self.here.core, 3)

    def mid(self, k):
        for u in (2 * k, 2 * k + 1):
            self.first(u).wait_recv()
            self.third(u).start()

    def core(self, k):
        for u in (2 * k, 2 * k + 1):
            self.second(u).wait_recv()
            self.third(u).wait_recv()
            self.cross(u).start()

    def done(self, k):
        for u in (2 * k, 2 * k + 1):
            self.cross(u).wait_recv()

    def bblk(self, w, y, x):
        h = self.here
        cols = slice(384 * (w % 2), 384 * (w % 2) + 384)
        if w < 2:
            return self.down.at[y, x, h.c, h.z, 1, :, cols]
        return self.early.at[y, x, lax.div(h.z, 2), lax.rem(h.z, 2), :, cols]

    def bfirst(self, w):
        h = self.here
        ref = self.bblk(w, h.y, h.x)
        return rcopy(ref, ref, self.bsems, 3 * w + 0, self.nbrs(w)[0], w // 2)

    def bsecond(self, w):
        h = self.here
        ref = self.bblk(w, h.y, h.x)
        return rcopy(ref, ref, self.bsems, 3 * w + 1, self.nbrs(w)[1], w // 2)

    def bthird(self, w):
        h = self.here
        ref = self.bblk(w, 1 - h.y, h.x) if w % 2 == 0 else self.bblk(w, h.y, 1 - h.x)
        return rcopy(ref, ref, self.bsems, 3 * w + 2, self.nbrs(w)[1], w // 2)

    def b_start(self, *ws):
        for w in ws:
            self.bfirst(w).start()
            self.bsecond(w).start()

    def b_mid(self, *ws):
        for w in ws:
            self.bfirst(w).wait_recv()
            self.bthird(w).start()

    def b_got(self, *ws):
        for w in ws:
            self.bsecond(w).wait_recv()
            self.bthird(w).wait_recv()

    def early_finish(self):
        h = self.here
        for p in range(4):
            self.z_wait(11 + p)
        for p in range(4):
            slabs = self.early[p // 2, p % 2].astype(F32)
            for half in (0, 1):
                rows = [
                    slabs[z // 2, z % 2, 24 * half : 24 * half + 24] for z in range(4)
                ]
                self.sq[6 + half, p // 2, p % 2, h.c] = (
                    jnp.concatenate(rows, axis=0).astype(BF).reshape(2, 48, 768)
                )
        sent(h, self.zsems, 2, self.like[12])
        sent(h, self.bsems, 1, self.like[3])
        for u in (6, 7):
            self.cross(u).start()

    def bcross(self, y):
        ref = self.down.at[y, :, self.here.c, :, 1]
        return rcopy(ref, ref, self.bcsems, y, self.here.core, 0)

    def b_core(self, y):
        for p in (2 * y, 2 * y + 1):
            self.z_wait(7 + p)
        self.bcross(y).start()

    def b_done(self):
        for y in (0, 1):
            self.bcross(y).wait_recv()

    def drain(self):
        like = self.like
        sent(self.here, self.zsems, 0, like[21])
        sent(self.here, self.zsems, 1, like[9])
        for group in (0, 1, 2):
            sent(self.here, self.sems, group, like[24])
        sent(self.here, self.sems, 3, like[112])
        sent(self.here, self.bsems, 0, like[3])
        sent(self.here, self.bcsems, 0, like[16])


class Scatter:
    def __init__(
        self, here, up, down, gup, gdown, rc, r1, r2, zsend, zland, brest, bzland, br1, br2,
        sems, zsems, bzsems, bsems, tsems,
    ):
        self.here, self.up, self.down, self.gup, self.gdown = here, up, down, gup, gdown
        self.rc, self.r1, self.r2 = rc, r1, r2
        self.zsend, self.zland, self.sems, self.zsems = zsend, zland, sems, zsems
        self.brest, self.bzland, self.br1, self.br2 = brest, bzland, br1, br2
        self.bzsems, self.bsems, self.tsems = bzsems, bsems, tsems

    def blk(self, u, y, x, c):
        if u < 4:
            return self.down.at[y, x, c, u]
        if u < 8:
            return self.up.at[u - 4, y, x, c]
        if u < 12:
            return self.gup.at[u - 8, y, x, c]
        pair = (u - 12) % 2
        return self.gdown.at[y, x, c, 2 * pair : 2 * pair + 2, (u - 12) // 2]

    def put(self, u, y, cols, value):
        value = value.astype(BF).reshape(2, 2, 2, 48, 256)
        if u < 4:
            self.down[y, :, :, u, :, :, cols] = value
        else:
            self.up[u - 4, y, :, :, :, :, cols] = value

    def cross(self, u):
        h = self.here
        return rcopy(
            self.blk(u, EVERY, EVERY, 1 - h.c), self.rc.at[u % 8], self.sems, 3 * u, h.core, 0
        )

    def first(self, u):
        h = self.here
        if u % 2 == 0:
            src, device = self.blk(u, EVERY, 1 - h.x, h.c), h.xn
        else:
            src, device = self.blk(u, 1 - h.y, EVERY, h.c), h.yn
        return rcopy(src, self.r1.at[u], self.sems, 3 * u + 1, device, 1)

    def second(self, u):
        h = self.here
        if u % 2 == 0:
            src, device = self.r1.at[u, 1 - h.y], h.yn
        else:
            src, device = self.r1.at[u, 1 - h.x], h.xn
        return rcopy(src, self.r2.at[u], self.sems, 3 * u + 2, device, 2)

    def start(self, k):
        for u in (2 * k, 2 * k + 1):
            self.cross(u).start()

    def add_core(self, u):
        self.cross(u).wait_recv()
        mine = self.blk(u, EVERY, EVERY, self.here.c)
        mine[...] = (mine[...].astype(F32) + self.rc[u % 8].astype(F32)).astype(BF)

    def one(self, k):
        for u in (2 * k, 2 * k + 1):
            self.add_core(u)
            self.first(u).start()

    def two(self, k):
        h = self.here
        for u in (2 * k, 2 * k + 1):
            self.first(u).wait_recv()
            if u % 2 == 0:
                mine = self.blk(u, EVERY, h.x, h.c)
            else:
                mine = self.blk(u, h.y, EVERY, h.c)
            self.r1[u] = (mine[...].astype(F32) + self.r1[u].astype(F32)).astype(BF)
            self.second(u).start()

    def three(self, k):
        h = self.here
        sums = []
        for u in (2 * k, 2 * k + 1):
            self.second(u).wait_recv()
            at = h.y if u % 2 == 0 else h.x
            sums.append(self.r1[u, at].astype(F32) + self.r2[u].astype(F32))
        if k < 6:
            sums = [item.reshape(96, 768) for item in sums]
            for z in range(4):
                self.zsend[k, z] = jnp.concatenate(
                    [item[24 * z : 24 * z + 24] for item in sums], axis=0
                ).astype(BF)
        else:
            for half in (0, 1):
                self.zsend[k, 2 * half : 2 * half + 2] = sums[half].astype(BF)
        for s in (1, 2, 3):
            self.zcopy(k, s).start()

    def zcopy(self, k, s):
        h = self.here
        return rcopy(
            self.zsend.at[k, lax.rem(h.z + s, 4)], self.zland.at[k, s - 1], self.zsems,
            3 * k + s - 1, h.zn(s), 0,
        )

    def last(self, k):
        h = self.here
        for s in (1, 2, 3):
            self.zcopy(k, s).wait_recv()
        total = self.zsend[k, h.z].astype(F32)
        for s in (1, 2, 3):
            total = total + self.zland[k, s - 1].astype(F32)
        return total

    def tail_first(self, u, w):
        h = self.here
        cols = slice(384 * w, 384 * w + 384)
        if u % 2 == 0:
            src, device = self.blk(u, EVERY, 1 - h.x, h.c), h.xn
        else:
            src, device = self.blk(u, 1 - h.y, EVERY, h.c), h.yn
        return rcopy(
            src.at[:, :, :, cols], self.r1.at[u, :, :, :, cols], self.tsems, 2 * u + w, device, 0
        )

    def tail_second(self, u, w):
        h = self.here
        cols = slice(384 * w, 384 * w + 384)
        at, device = (1 - h.y, h.yn) if u % 2 == 0 else (1 - h.x, h.xn)
        return rcopy(
            self.r1.at[u, at, :, :, cols], self.r2.at[u, :, :, cols], self.tsems, 4 + 2 * u + w,
            device, 1,
        )

    def tail_zcopy(self, w, s):
        h = self.here
        cols = slice(384 * w, 384 * w + 384)
        return rcopy(
            self.zsend.at[0, lax.rem(h.z + s, 4), :, cols], self.zland.at[0, s - 1, :, cols],
            self.tsems, 8 + 3 * w + s - 1, h.zn(s), 2,
        )

    def tail_one(self):
        for u in (0, 1):
            self.add_core(u)
        for w in (0, 1):
            for u in (0, 1):
                self.tail_first(u, w).start()

    def tail_two(self, w):
        h = self.here
        cols = slice(384 * w, 384 * w + 384)
        for u in (0, 1):
            self.tail_first(u, w).wait_recv()
            if u % 2 == 0:
                mine = self.blk(u, EVERY, h.x, h.c)
            else:
                mine = self.blk(u, h.y, EVERY, h.c)
            mine = mine[:, :, :, cols].astype(F32)
            self.r1[u, :, :, :, cols] = (
                mine + self.r1[u, :, :, :, cols].astype(F32)
            ).astype(BF)
            self.tail_second(u, w).start()

    def tail_three(self, w):
        h = self.here
        cols = slice(384 * w, 384 * w + 384)
        sums = []
        for u in (0, 1):
            self.tail_second(u, w).wait_recv()
            at = h.y if u % 2 == 0 else h.x
            total = self.r1[u, at, :, :, cols].astype(F32) + self.r2[u, :, :, cols].astype(F32)
            sums.append(total.reshape(96, 384))
        for z in range(4):
            self.zsend[0, z, :, cols] = jnp.concatenate(
                [item[24 * z : 24 * z + 24] for item in sums], axis=0
            ).astype(BF)
        for s in (1, 2, 3):
            self.tail_zcopy(w, s).start()

    def tail_last(self, w):
        h = self.here
        cols = slice(384 * w, 384 * w + 384)
        for s in (1, 2, 3):
            self.tail_zcopy(w, s).wait_recv()
        total = self.zsend[0, h.z, :, cols].astype(F32)
        for s in (1, 2, 3):
            total = total + self.zland[0, s - 1, :, cols].astype(F32)
        return total

    def bz(self, s):
        h = self.here
        src = self.gdown.at[:, :, h.c, lax.rem(h.z + s, 4), 1]
        return rcopy(src, self.bzland.at[s - 1], self.bzsems, s - 1, h.zn(s), 0)

    def b_one(self):
        for u in (14, 15):
            self.add_core(u)
        for s in (1, 2, 3):
            self.bz(s).start()

    def bfirst(self, w):
        h = self.here
        if w == 0:
            src, device = self.brest.at[:, 1 - h.x, :, 0:384], h.xn
        else:
            src, device = self.brest.at[1 - h.y, :, :, 384:768], h.yn
        return rcopy(src, self.br1.at[w], self.bsems, 2 * w, device, 0)

    def bsecond(self, w):
        h = self.here
        if w == 0:
            src, device = self.br1.at[w, 1 - h.y], h.yn
        else:
            src, device = self.br1.at[w, 1 - h.x], h.xn
        return rcopy(src, self.br2.at[w], self.bsems, 2 * w + 1, device, 1)

    def b_two(self):
        h = self.here
        for s in (1, 2, 3):
            self.bz(s).wait_recv()
        total = self.gdown[:, :, h.c, h.z, 1].astype(F32)
        for s in (1, 2, 3):
            total = total + self.bzland[s - 1].astype(F32)
        self.brest[...] = total.astype(BF)
        for w in (0, 1):
            self.bfirst(w).start()

    def b_three(self):
        h = self.here
        for w in (0, 1):
            self.bfirst(w).wait_recv()
            if w == 0:
                mine = self.brest[:, h.x, :, 0:384]
            else:
                mine = self.brest[h.y, :, :, 384:768]
            self.br1[w] = (mine.astype(F32) + self.br1[w].astype(F32)).astype(BF)
            self.bsecond(w).start()

    def b_last(self, w):
        h = self.here
        self.bsecond(w).wait_recv()
        at = h.y if w == 0 else h.x
        return self.br1[w, at].astype(F32) + self.br2[w].astype(F32)

    def drain(self, slabs128):
        sent(self.here, self.sems, 0, slabs128)
        sent(self.here, self.sems, 1, self.r1.at[0:12])
        sent(self.here, self.sems, 2, self.r2.at[0:12])
        sent(self.here, self.zsems, 0, self.zland.at[0:6])
        sent(self.here, self.bzsems, 0, self.bzland)
        sent(self.here, self.bsems, 0, self.r2.at[0])
        sent(self.here, self.bsems, 1, self.r2.at[0, 0])
        sent(self.here, self.tsems, 0, self.r1.at[0:2])
        sent(self.here, self.tsems, 1, self.r2.at[0:2])
        sent(self.here, self.tsems, 2, self.zland.at[0])


def mm(a, b):
    return lax.dot_general(a, b, (((1,), (0,)), ((), ())), preferred_element_type=F32)


def mt(a, b):
    return lax.dot_general(a, b, (((1,), (1,)), ((), ())), preferred_element_type=F32)


def tm(a, b):
    return lax.dot_general(a, b, (((0,), (0,)), ((), ())), preferred_element_type=F32)


def iota(shape, axis):
    return lax.broadcasted_iota(jnp.int32, shape, axis)


def lanes(hp):
    return pl.ds(pl.multiple_of(hp * 128, 128), 128)


def both(q):
    low = iota(q.shape, 1) < 64
    zero = jnp.zeros_like(q)
    return jnp.concatenate([jnp.where(low, q, zero), jnp.where(low, zero, q)], axis=0)


def merge(pair):
    rows = pair.shape[0] // 2
    low = iota((rows, 128), 1) < 64
    return jnp.where(low, pair[:rows], pair[rows:]).astype(BF)


def probs(key, query, bias, mask):
    scores = mt(key, query)
    if bias is not None:
        scores = scores + bias.astype(F32)
    scores = jnp.where(mask, scores, -1e30)
    expo = jnp.exp(scores - jnp.max(scores, axis=0, keepdims=True))
    return expo * (1.0 / jnp.sum(expo, axis=0, keepdims=True))


def rms(v):
    return lax.rsqrt(jnp.mean(v * v, axis=-1, keepdims=True) + eps)


def norm_back(v, gain, grad):
    r = rms(v)
    scaled = grad * gain
    inner = jnp.mean(scaled * v, axis=-1, keepdims=True)
    return r * scaled - v * (r * r * r * inner), jnp.sum(grad * v * r, axis=0, keepdims=True)


def gelu_both(v):
    c = 0.7978845608028654
    square = v * v
    t = jnp.tanh(c * v * (1.0 + 0.044715 * square))
    half = 0.5 * (1.0 + t)
    slope = half + 0.5 * v * (1.0 - t * t) * (c * (1.0 + 3 * 0.044715 * square))
    return v * half, slope


def layer_kernel(*refs):
    given, (tlen, slen, count) = refs[:15], refs[15:18]
    g_enc, results = refs[18], refs[19:33]
    (
        sq, up, down, gup, gdown, rc, r1, r2, zland, zland2, brest, bzland, br1, br2, small, small2,
        bias, h1, h2, h3, q1, k1, v1, o1, q2, o2, k2, v2, g, gp, x1, x2, stage,
        zs, zr, ss, sr, bs, br, bcs, bcr, ms, mr,
        rzs, rzr, rss, rsr, rbzs, rbzr, rbs, rbr, rts, rtr, m2s, m2r, out_sem, done_sem, in_sem, credit,
        *held,
    ) = refs[33:]
    held, kept = held[:14], held[14:]
    layer_out, g_dec, *g_sq, g_up, g_down, g_gain, g_table = held
    *squares, up_in, down_in, gain_in, table_in, x_in, cot, enc = kept

    def hand(i):
        return pltpu.make_async_copy(held[i], results[i], done_sem.at[i])

    def fetch(i):
        return pltpu.make_async_copy(given[i], kept[i], in_sem.at[i])

    here = Place()
    here.greet()
    for i in range(15):
        fetch(i).start()
    for i in range(12):
        fetch(i).wait()
    index = (here.y * 4 + here.x * 2 + here.c) * 4 + here.z
    for k in range(4):
        slab = jnp.concatenate(
            [squares[2 * k][...].astype(F32), squares[2 * k + 1][...].astype(F32)], axis=0
        ).astype(BF)
        if k < 3:
            zland[k, here.z] = slab
        else:
            rc[here.y, here.x, lax.div(here.z, 2), lax.rem(here.z, 2)] = slab
    for k in range(2):
        zland[4 + k, here.z] = jnp.concatenate(
            [up_in[:, 768 * n : 768 * n + 768].astype(F32) for n in (2 * k, 2 * k + 1)], axis=0
        ).astype(BF)
    down[here.y, here.x, here.c, here.z] = down_in[...].reshape(2, 48, 768)
    spot = (iota((24, 768), 1) == iota((24, 768), 0) + 24 * index).astype(BF)
    small[0] = jnp.zeros((8, 768), F32)
    small[0, 0:3] = mm(gain_in[...], spot)
    here.enter()
    like = {
        3: zland2.at[0], 9: zland2.at[0:3], 12: bzland, 16: rc.at[0:2], 21: zland2,
        24: r2.at[0:12], 112: sq.at[0:7],
    }
    ga = Gather(
        here, sq, up, down, zland, rc, (zs, zr), (ss, sr), (bs, br), (bcs, bcr), like
    )
    m = Small(here, small, (ms, mr))
    rs = Scatter(
        here, up, down, gup, gdown, rc, r1, r2, zland, zland2, brest, bzland, br1, br2,
        (rss, rsr), (rzs, rzr), (rbzs, rbzr), (rbs, rbr), (rts, rtr),
    )
    m2 = Small(here, small2, (m2s, m2r))

    def weight(u):
        return sq[u].reshape(768, 768)

    def columns(u, n):
        return sq[u, :, :, :, :, :, 256 * n : 256 * n + 256].reshape(768, 256)

    def z_starts(*items):
        for item in items:
            ga.z_start(item)

    def z_passes(*items):
        for item in items:
            ga.z_pass(item)

    m.start(0)
    ga.z_start(0)
    ga.b_start(2, 3, 0, 1)
    m.finish(0)
    m.start(1)
    ga.z_pass(0)
    z_starts(1)
    ga.b_mid(2, 3, 0, 1)

    def bucket_hot(rows_are_buckets):
        shape = (32, 128) if rows_are_buckets else (128, 32)
        distance = iota(shape, 1 if rows_are_buckets else 0)
        level = jnp.minimum(distance, 16)
        for edge in thresholds:
            level = level + (distance >= edge).astype(jnp.int32)
        return level == iota(shape, 0 if rows_are_buckets else 1)

    by_distance = mm(table_in[...], bucket_hot(True).astype(BF))
    for head in range(12):
        row = jnp.broadcast_to(by_distance[head : head + 1, :], (128, 128))
        bias[head // 2, :, 128 * (head % 2) : 128 * (head % 2) + 128] = pltpu.roll(
            row, 0, 1, stride=1, stride_axis=0
        ).astype(BF)

    key_place, target_place = iota((128, 256), 0), iota((128, 256), 1) & 127
    causal = key_place <= target_place
    source_place = iota((512, 256), 0)

    def self_mask(ex):
        return causal & (key_place < tlen[ex])

    def cross_mask(ex):
        return source_place < slen[ex]

    row_place = iota((256, 1), 0)
    live = (
        ((row_place < 128) & (row_place < tlen[0]) & (0 < count[0]))
        | ((row_place >= 128) & (row_place - 128 < tlen[1]) & (1 < count[0]))
    ).astype(F32)

    ga.z_finish(0)
    ga.b_got(2, 3)
    m.finish(1)
    m.start(2)
    z_starts(2, 11)
    ga.z_pass(1)
    ga.mid(0)
    ga.z_finish(1)
    z_starts(12, 4)
    z_passes(2, 11)
    ga.core(0)
    ga.z_finish(2)
    z_starts(5, 13)
    ga.mid(1)
    m.finish(2)
    gains = m.total()
    gain = [gains[i : i + 1, :] for i in range(3)]

    fetch(12).wait()
    first = x_in[...].astype(F32)
    h1[...] = (first * rms(first) * gain[0]).astype(BF)
    z_passes(12, 4)
    ga.core(1)
    ga.mid(2)
    ga.done(0)
    for n in range(3):
        cols = slice(256 * n, 256 * n + 256)
        q1[:, cols] = mm(h1[...], columns(0, n)).astype(BF)
        k1[:, cols] = mm(h1[...], columns(1, n)).astype(BF)
    ga.z_finish(4)
    z_starts(14)
    z_passes(5, 13)
    ga.core(2)
    ga.done(1)
    for n in range(3):
        cols = slice(256 * n, 256 * n + 256)
        v1[:, cols] = mm(h1[...], columns(2, n)).astype(BF)

    def self_forward(hp, carry):
        for ex in range(2):
            rows = slice(128 * ex, 128 * ex + 128)
            query = both(q1[rows, lanes(hp)])
            p = probs(k1[rows, lanes(hp)], query, bias[hp], self_mask(ex)).astype(BF)
            o1[rows, lanes(hp)] = merge(tm(p, v1[rows, lanes(hp)]))
        return carry

    lax.fori_loop(0, 6, self_forward, 0)
    ga.z_finish(5)
    ga.b_got(0, 1)
    z_starts(6)
    z_passes(14)
    ga.mid(4)
    x1[...] = x_in[...].astype(F32) + mm(o1[...], weight(3))
    h2[...] = (x1[...] * rms(x1[...]) * gain[1]).astype(BF)
    ga.done(2)

    def encode(r, carry):
        rows = pl.ds(pl.multiple_of(r * 256, 256), 256)
        for n in range(3):
            cols = slice(256 * n, 256 * n + 256)
            k2[rows, cols] = mm(enc[rows, :], columns(4, n)).astype(BF)
            v2[rows, cols] = mm(enc[rows, :], columns(5, n)).astype(BF)
        return carry

    fetch(14).wait()
    lax.fori_loop(0, 4, encode, 0)
    z_starts(7)
    ga.early_finish()
    ga.mid(5)
    z_passes(6)
    z_starts(8)
    ga.done(3)
    for n in range(3):
        cols = slice(256 * n, 256 * n + 256)
        q2[:, cols] = mm(h2[...], columns(6, n)).astype(BF)

    def cross_forward(hp, carry):
        for ex in range(2):
            rows = slice(128 * ex, 128 * ex + 128)
            keys = slice(512 * ex, 512 * ex + 512)
            query = both(q2[rows, lanes(hp)])
            p = probs(k2[keys, lanes(hp)], query, None, cross_mask(ex)).astype(BF)
            o2[rows, lanes(hp)] = merge(tm(p, v2[keys, lanes(hp)]))
        return carry

    lax.fori_loop(0, 2, cross_forward, 0)
    ga.z_finish(6)
    z_starts(9)
    z_passes(7)
    lax.fori_loop(2, 4, cross_forward, 0)
    ga.core(4)
    z_passes(8)
    z_starts(10)
    lax.fori_loop(4, 6, cross_forward, 0)
    ga.core(5)
    ga.mid(6)
    x2[...] = x1[...] + mm(o2[...], weight(7))
    h3[...] = (x2[...] * rms(x2[...]) * gain[2]).astype(BF)
    ga.done(4)

    def hidden(n, carry):
        for part in range(3):
            lo = 256 * part
            a = mm(h3[...], up[n, :, :, :, :, :, lo : lo + 256].reshape(768, 256))
            active, slope = gelu_both(a)
            cols = pl.ds(pl.multiple_of(768 * n + lo, 256), 256)
            g[:, cols] = active.astype(BF)
            gp[:, cols] = slope.astype(BF)
        return carry

    def keep_gain(i, term):
        for j in range(6):
            small2[0, 6 * i + j : 6 * i + j + 1, :] = term[:, 128 * j : 128 * j + 128]

    fetch(13).wait()

    def df(cols=slice(None)):
        return (cot[:, cols].astype(F32) * live).astype(BF)

    def wide(e):
        return pl.ds(pl.multiple_of(768 * e, 256), 768)

    def grad_down(e, carry):
        turned = g[:, wide(e)].T
        for n in range(3):
            cols = slice(256 * n, 256 * n + 256)
            grad = mm(turned, df(cols)).astype(BF)
            gdown[lax.div(e, 2), lax.rem(e, 2), :, :, :, :, cols] = grad.reshape(2, 4, 2, 48, 256)
        return carry

    lax.fori_loop(0, 2, hidden, 0)
    lax.fori_loop(0, 2, grad_down, 0)
    z_passes(9, 10)
    ga.done(5)
    lax.fori_loop(2, 4, hidden, 0)
    lax.fori_loop(2, 4, grad_down, 0)
    rs.start(6)
    rs.start(7)
    ga.b_core(0)
    ga.core(6)
    rs.one(6)
    ga.b_core(1)
    rs.b_one()
    ga.done(6)
    ga.b_done()

    def down_block(e):
        return down[lax.div(e, 2), lax.rem(e, 2)].reshape(768, 768)

    def inner_grad(e, carry):
        dg = mt(df(), down_block(e))
        gp[:, wide(e)] = (dg * gp[:, wide(e)].astype(F32)).astype(BF)
        return carry

    def grad_up(n, carry):
        turned = h3[...].T
        for part in range(3):
            cols = slice(256 * part, 256 * part + 256)
            source = pl.ds(pl.multiple_of(768 * n + 256 * part, 256), 256)
            grad = mm(turned, gp[:, source]).astype(BF)
            gup[n, :, :, :, :, :, cols] = grad.reshape(2, 2, 2, 2, 48, 256)
        return carry

    lax.fori_loop(0, 2, inner_grad, 0)
    lax.fori_loop(0, 2, grad_up, 0)
    rs.start(4)
    lax.fori_loop(2, 4, inner_grad, 0)
    rs.one(4)
    lax.fori_loop(2, 4, grad_up, 0)
    rs.start(5)
    rs.two(6)
    stage[0] = jnp.zeros((256, 768), F32)
    stage[1] = x2[...]

    def inner_back(n, carry):
        stage[0] += mt(gp[:, wide(n)], up[n].reshape(768, 768))
        return carry

    lax.fori_loop(0, 4, inner_back, 0)
    rs.one(5)
    pl.semaphore_signal(credit, inc=1, device_id=here.core, device_id_type=MESH)
    d_norm, gain_three = norm_back(x2[...], gain[2], stage[0])
    keep_gain(2, gain_three)
    x2[...] = cot[...].astype(F32) * live + d_norm
    ga.drain()

    def put_grads(value, rows, pairs):
        def half_rows(y, carry):
            turned = value[:, pl.ds(pl.multiple_of(384 * y, 128), 384)].T
            for u, ref in pairs:
                for n in range(3):
                    cols = slice(256 * n, 256 * n + 256)
                    rs.put(u, y, cols, mm(turned, ref[:, cols]))
            return carry

        lax.fori_loop(0, 2, half_rows, 0)

    h3[...] = x2[...].astype(BF)
    put_grads(o2, 256, ((7, h3),))
    o2[...] = mt(h3[...], weight(7)).astype(BF)

    def cross_backward(hp, carry):
        for ex in range(2):
            rows = slice(128 * ex, 128 * ex + 128)
            keys = slice(512 * ex, 512 * ex + 512)
            query, d_out = both(q2[rows, lanes(hp)]), both(o2[rows, lanes(hp)])
            key, value = k2[keys, lanes(hp)], v2[keys, lanes(hp)]
            p = probs(key, query, None, cross_mask(ex))
            dp = mt(value, d_out)
            delta = jnp.sum(dp * p, axis=0, keepdims=True)
            ds = (p * (dp - delta)).astype(BF)
            q2[rows, lanes(hp)] = merge(tm(ds, key))
            k2[keys, lanes(hp)] = mm(ds, query).astype(BF)
            v2[keys, lanes(hp)] = mm(p.astype(BF), d_out).astype(BF)
        return carry

    lax.fori_loop(0, 2, cross_backward, 0)
    lax.fori_loop(2, 4, cross_backward, 0)
    rs.two(4)
    rs.three(6)
    lax.fori_loop(4, 6, cross_backward, 0)
    put_grads(h2, 256, ((6, q2),))
    pl.semaphore_wait(credit, 1)
    rs.start(3)
    rs.two(5)
    rs.one(3)
    put_grads(enc, 1024, ((4, k2), (5, v2)))
    rs.start(2)

    def finish(k):
        total = rs.last(k)
        if k < 4:
            g_sq[2 * k][...] = total[:24]
            g_sq[2 * k + 1][...] = total[24:]
            hand(2 + 2 * k).start()
            hand(3 + 2 * k).start()
        elif k < 6:
            g_up[:, 1536 * (k - 4) : 1536 * (k - 4) + 768] = total[:24]
            g_up[:, 1536 * (k - 4) + 768 : 1536 * (k - 4) + 1536] = total[24:]
        else:
            g_down[0:48, :] = total

    d_norm, gain_two = norm_back(x1[...], gain[1], mt(q2[...], weight(6)))
    keep_gain(1, gain_two)
    x2[...] = x2[...] + d_norm
    rs.one(2)
    rs.three(4)

    def result(e, carry):
        stage[1] += mm(g[:, wide(e)], down_block(e))
        return carry

    lax.fori_loop(0, 4, result, 0)
    layer_out[...] = (stage[1] * live).astype(BF)
    hand(0).start()
    h3[...] = x2[...].astype(BF)
    put_grads(o1, 256, ((3, h3),))
    o1[...] = mt(h3[...], weight(3)).astype(BF)
    rs.b_two()
    rs.three(5)
    turn = (iota((128, 256), 0) + (iota((128, 256), 1) & 127) == 127).astype(BF)

    def self_backward(hp, carry):
        scores = []
        for ex in range(2):
            rows = slice(128 * ex, 128 * ex + 128)
            query, d_out = both(q1[rows, lanes(hp)]), both(o1[rows, lanes(hp)])
            key, value = k1[rows, lanes(hp)], v1[rows, lanes(hp)]
            p = probs(key, query, bias[hp], self_mask(ex))
            dp = mt(value, d_out)
            delta = jnp.sum(dp * p, axis=0, keepdims=True)
            ds = (p * (dp - delta)).astype(BF)
            q1[rows, lanes(hp)] = merge(tm(ds, key))
            k1[rows, lanes(hp)] = mm(ds, query).astype(BF)
            v1[rows, lanes(hp)] = mm(p.astype(BF), d_out).astype(BF)
            scores.append(ds)
        pair = mm(turn, jnp.concatenate(scores, axis=0))
        for head in range(2):
            skew = pltpu.roll(pair[:, 128 * head : 128 * head + 128], 0, 1, stride=1, stride_axis=0)
            small2[0, pl.ds(18 + 2 * hp + head, 1), :] = jnp.sum(skew, axis=0, keepdims=True)
        return carry

    lax.fori_loop(0, 6, self_backward, 0)
    rs.two(3)
    stage[0] = jnp.zeros((256, 768), F32)

    def first_back(y, carry):
        cols = pl.ds(pl.multiple_of(384 * y, 128), 384)
        for u, ref in ((0, q1), (1, k1), (2, v1)):
            stage[0, :, cols] += mt(ref[...], sq[u, y].reshape(384, 768))
        return carry

    lax.fori_loop(0, 2, first_back, 0)
    d_norm, gain_one = norm_back(x_in[...].astype(F32), gain[0], stage[0])
    g_dec[...] = x2[...] + d_norm
    hand(1).start()
    keep_gain(0, gain_one)
    small2[0, 30:32, :] = jnp.zeros((2, 128), F32)
    m2.start(0)
    put_grads(h1, 256, ((2, v1), (0, q1), (1, k1)))
    rs.start(1)
    rs.start(0)
    m2.finish(0)
    m2.start(1)
    rs.b_three()
    rs.one(1)
    rs.two(2)
    rs.three(3)

    def out_copy(r):
        return pltpu.make_async_copy(
            stage.at[lax.rem(r, 2)],
            g_enc.at[pl.ds(pl.multiple_of(256 * r, 256), 256)],
            out_sem.at[r],
        )

    def encoder_grad(r, carry):
        rows = pl.ds(pl.multiple_of(256 * r, 256), 256)
        slot = lax.rem(r, 2)
        for y in range(2):
            cols = slice(384 * y, 384 * y + 384)
            stage[slot, :, cols] = mt(k2[rows, :], sq[4, y].reshape(384, 768))
            stage[slot, :, cols] += mt(v2[rows, :], sq[5, y].reshape(384, 768))
        out_copy(r).start()
        return carry

    lax.fori_loop(0, 2, encoder_grad, 0)
    m2.finish(1)
    m2.start(2)
    finish(6)
    finish(4)
    finish(5)
    out_copy(0).wait()
    out_copy(1).wait()
    lax.fori_loop(2, 4, encoder_grad, 0)
    rs.two(1)
    rs.tail_one()
    rs.three(2)
    for w in (0, 1):
        g_down[48:96, 384 * w : 384 * w + 384] = rs.b_last(w)
    hand(10).start()
    hand(11).start()
    m2.finish(2)
    reduced = m2.total()
    sums = jnp.concatenate(
        [
            jnp.concatenate([reduced[6 * i + j : 6 * i + j + 1, :] for j in range(6)], axis=1)
            for i in range(3)
        ],
        axis=0,
    )
    pick = (iota((768, 24), 0) == iota((768, 24), 1) + 24 * index).astype(F32)
    g_gain[...] = lax.dot_general(
        sums, pick, (((1,), (0,)), ((), ())), preferred_element_type=F32,
        precision=lax.Precision.HIGHEST,
    )
    distance = (iota((32, 128), 1) + 1) & 127
    level = jnp.minimum(distance, 16)
    for edge in thresholds:
        level = level + (distance >= edge).astype(jnp.int32)
    hot = (level == iota((32, 128), 0)).astype(F32)
    g_table[...] = lax.dot_general(
        reduced[18:30, :], hot, (((1,), (1,)), ((), ())), preferred_element_type=F32,
        precision=lax.Precision.HIGHEST,
    )
    hand(12).start()
    hand(13).start()
    rs.three(1)
    rs.tail_two(0)
    finish(3)
    rs.tail_two(1)
    rs.tail_three(0)
    rs.tail_three(1)
    finish(2)
    finish(1)
    for w in (0, 1):
        total = rs.tail_last(w)
        g_sq[0][:, 384 * w : 384 * w + 384] = total[:24]
        g_sq[1][:, 384 * w : 384 * w + 384] = total[24:]
    hand(2).start()
    hand(3).start()
    rs.drain(sq)
    out_copy(2).wait()
    out_copy(3).wait()
    for i in range(14):
        hand(i).wait()


SM = pl.BlockSpec(memory_space=pltpu.SMEM)
ANY = pl.BlockSpec(memory_space=pl.ANY)


def layer_call(*args):
    shape = jax.ShapeDtypeStruct
    dims = (3, 45, 4, 56, 2, 12, 1, 2, 7, 7, 1, 21, 3, 48, 1, 3, 2, 4, 3, 14, 7, 7)
    half = lambda *dims: pltpu.VMEM(dims, BF)
    results = (
        ((256, 768), BF),
        ((256, 768), F32),
        *[((24, 768), F32)] * 8,
        ((24, 3072), F32),
        ((96, 768), F32),
        ((3, 24), F32),
        ((12, 32), F32),
    )
    return pl.pallas_call(
        layer_kernel,
        out_shape=(
            shape((1024, 768), F32),
            *[shape(*each) for each in results],
        ),
        in_specs=[ANY] * 15 + [SM] * 3,
        out_specs=(ANY,) * 15,
        scratch_shapes=[
            half(8, 2, 2, 2, 2, 48, 768),
            half(4, 2, 2, 2, 2, 48, 768),
            half(2, 2, 2, 4, 2, 48, 768),
            half(4, 2, 2, 2, 2, 48, 768),
            half(2, 2, 2, 4, 2, 48, 768),
            half(8, 2, 2, 2, 48, 768),
            half(14, 2, 2, 48, 768),
            half(14, 2, 48, 768),
            half(7, 4, 48, 768),
            half(7, 3, 48, 768),
            half(2, 2, 48, 768),
            half(3, 2, 2, 48, 768),
            half(2, 2, 48, 384),
            half(2, 48, 384),
            pltpu.VMEM((10, 8, 768), F32),
            pltpu.VMEM((10, 32, 128), F32),
            half(6, 128, 256),
            *[half(256, 768)] * 3,
            *[half(256, 768)] * 4,
            *[half(256, 768)] * 2,
            *[half(1024, 768)] * 2,
            *[half(256, 3072)] * 2,
            *[pltpu.VMEM((256, 768), F32)] * 2,
            pltpu.VMEM((2, 256, 768), F32),
            *[pltpu.SemaphoreType.DMA((each,)) for each in dims],
            pltpu.SemaphoreType.DMA((4,)),
            pltpu.SemaphoreType.DMA((14,)),
            pltpu.SemaphoreType.DMA((15,)),
            pltpu.SemaphoreType.REGULAR,
            *[pltpu.VMEM(*each) for each in results],
            *[pltpu.VMEM(each.shape, each.dtype) for each in args[:15]],
        ],
        compiler_params=pltpu.CompilerParams(
            collective_id=0, has_side_effects=True, vmem_limit_bytes=64 * 2**20 - 2**16
        ),
        name="layer",
    )(*args)


def hand_out_kernel(*refs):
    count = (len(refs) - 2) // 3
    source, target, held = refs[:count], refs[count : 2 * count], refs[2 * count : 3 * count]
    got, put = refs[3 * count :]
    ins = [pltpu.make_async_copy(source[i], held[i], got.at[i]) for i in range(count)]
    outs = [pltpu.make_async_copy(held[i], target[i], put.at[i]) for i in range(count)]
    for copy in ins:
        copy.start()
    for i in range(count):
        ins[i].wait()
        outs[i].start()
    for copy in outs:
        copy.wait()


def hand_out(arrays):
    return pl.pallas_call(
        hand_out_kernel,
        out_shape=tuple(jax.ShapeDtypeStruct(item.shape, item.dtype) for item in arrays),
        in_specs=[ANY] * len(arrays),
        out_specs=(ANY,) * len(arrays),
        scratch_shapes=[pltpu.VMEM(item.shape, item.dtype) for item in arrays]
        + [pltpu.SemaphoreType.DMA((len(arrays),))] * 2,
        name="hand_out",
    )(*arrays)


def by_kernel(
    decoder_in,
    encoder_out,
    self_query,
    self_key,
    self_value,
    self_output,
    cross_query,
    cross_key,
    cross_value,
    cross_output,
    hidden_in,
    hidden_out,
    norm_gains,
    bias_table,
    target_lengths,
    source_lengths,
    example_counts,
    cotangent,
):
    results = layer_call(
        self_query,
        self_key,
        self_value,
        self_output,
        cross_key,
        cross_value,
        cross_query,
        cross_output,
        hidden_in,
        hidden_out,
        norm_gains,
        bias_table.T,
        decoder_in.reshape(256, 768),
        cotangent.reshape(256, 768),
        encoder_out.reshape(1024, 768),
        target_lengths,
        source_lengths,
        example_counts,
    )
    g_enc, out, g_dec, *g_sq, g_up, g_down, g_gain, g_table = hand_out(results)
    return (
        out.reshape(decoder_in.shape),
        g_dec.reshape(decoder_in.shape),
        g_enc.reshape(encoder_out.shape),
        *g_sq[:4],
        g_sq[6],
        g_sq[4],
        g_sq[5],
        g_sq[7],
        g_up,
        g_down,
        g_gain,
        g_table.T,
    )


def plain(
    decoder_in,
    encoder_out,
    self_query,
    self_key,
    self_value,
    self_output,
    cross_query,
    cross_key,
    cross_value,
    cross_output,
    hidden_in,
    hidden_out,
    norm_gains,
    bias_table,
    target_lengths,
    source_lengths,
    example_counts,
    cotangent,
):
    gathered = (
        lax.all_gather(self_query, AXES, axis=0, tiled=True),
        lax.all_gather(self_key, AXES, axis=0, tiled=True),
        lax.all_gather(self_value, AXES, axis=0, tiled=True),
        lax.all_gather(self_output, AXES, axis=0, tiled=True),
        lax.all_gather(cross_query, AXES, axis=0, tiled=True),
        lax.all_gather(cross_key, AXES, axis=0, tiled=True),
        lax.all_gather(cross_value, AXES, axis=0, tiled=True),
        lax.all_gather(cross_output, AXES, axis=0, tiled=True),
        lax.all_gather(hidden_in, AXES, axis=0, tiled=True),
        lax.all_gather(hidden_out, AXES, axis=0, tiled=True),
        lax.all_gather(norm_gains, AXES, axis=1, tiled=True),
    )
    w_query, w_key, w_value, w_out, x_query, x_key, x_value, x_out, w_up, w_down, gain_all = (
        gathered
    )
    slots = jnp.arange(decoder_in.shape[0], dtype=jnp.int32)
    length = decoder_in.shape[1]
    source = encoder_out.shape[1]
    width = decoder_in.shape[2]
    hidden_width = hidden_in.shape[1]
    place = jnp.arange(length, dtype=jnp.int32)
    source_place = jnp.arange(source, dtype=jnp.int32)
    live = (
        (slots < example_counts[0])[:, None] & (place[None, :] < target_lengths[:, None])
    ).astype(jnp.float32)[:, :, None]
    self_mask = (place[None, :] <= place[:, None])[None, None] & (
        place[None, None, None, :] < target_lengths[:, None, None, None]
    )
    cross_mask = source_place[None, None, None, :] < source_lengths[:, None, None, None]
    onehot = (
        buckets(length)[:, :, None] == jnp.arange(bias_table.shape[0], dtype=jnp.int32)
    ).astype(jnp.bfloat16)
    bias = jnp.einsum("lsn,nh->hls", onehot, bias_table, preferred_element_type=jnp.float32)
    gains = gain_all.astype(jnp.float32)
    inputs = decoder_in.astype(jnp.float32)
    first = normalize(inputs, gains[0]).astype(jnp.bfloat16)
    query = project(first, w_query).astype(jnp.bfloat16)
    key = project(first, w_key).astype(jnp.bfloat16)
    value = project(first, w_value).astype(jnp.bfloat16)
    mixed, logsum_self = attention_forward(
        split_heads(query), split_heads(key), split_heads(value), bias, self_mask
    )
    after_self = inputs + project(mixed, w_out)
    second = normalize(after_self, gains[1]).astype(jnp.bfloat16)
    cross_q = project(second, x_query).astype(jnp.bfloat16)
    cross_k = project(encoder_out, x_key).astype(jnp.bfloat16)
    cross_v = project(encoder_out, x_value).astype(jnp.bfloat16)
    crossed, logsum_cross = attention_forward(
        split_heads(cross_q), split_heads(cross_k), split_heads(cross_v), 0.0, cross_mask
    )
    after_cross = after_self + project(crossed, x_out)
    third = normalize(after_cross, gains[2]).astype(jnp.bfloat16)
    inner = project(third, w_up)
    active = jax.nn.gelu(inner).astype(jnp.bfloat16)
    result = after_cross + project(active, w_down)
    layer_out = (result * live).astype(jnp.bfloat16)
    regathered = (
        lax.all_gather(self_query, AXES, axis=0, tiled=True),
        lax.all_gather(self_key, AXES, axis=0, tiled=True),
        lax.all_gather(self_value, AXES, axis=0, tiled=True),
        lax.all_gather(self_output, AXES, axis=0, tiled=True),
        lax.all_gather(cross_query, AXES, axis=0, tiled=True),
        lax.all_gather(cross_key, AXES, axis=0, tiled=True),
        lax.all_gather(cross_value, AXES, axis=0, tiled=True),
        lax.all_gather(cross_output, AXES, axis=0, tiled=True),
        lax.all_gather(hidden_in, AXES, axis=0, tiled=True),
        lax.all_gather(hidden_out, AXES, axis=0, tiled=True),
        lax.all_gather(norm_gains, AXES, axis=1, tiled=True),
    )
    w_query, w_key, w_value, w_out, x_query, x_key, x_value, x_out, w_up, w_down, gain_all = (
        regathered
    )
    gains = gain_all.astype(jnp.float32)
    d_result = cotangent.astype(jnp.float32) * live
    d_branch = d_result.astype(jnp.bfloat16)
    grad_down = outer_sum(active, d_branch)
    d_inner = gelu_grad(inner, project_back(d_branch, w_down)).astype(jnp.bfloat16)
    grad_up = outer_sum(third, d_inner)
    d_cross, gain_three = norm_grad(after_cross, gains[2], project_back(d_inner, w_up))
    d_cross = d_cross + d_result
    d_branch = d_cross.astype(jnp.bfloat16)
    grad_x_out = outer_sum(crossed, d_branch)
    d_crossed = project_back(d_branch, x_out).astype(jnp.bfloat16)
    dq_cross, dk_cross, dv_cross, unused = attention_backward(
        split_heads(cross_q),
        split_heads(cross_k),
        split_heads(cross_v),
        0.0,
        cross_mask,
        logsum_cross,
        split_heads(d_crossed),
    )
    grad_x_query = outer_sum(second, dq_cross)
    grad_x_key = outer_sum(encoder_out, dk_cross)
    grad_x_value = outer_sum(encoder_out, dv_cross)
    grad_encoder = project_back(dk_cross, x_key) + project_back(dv_cross, x_value)
    d_self, gain_two = norm_grad(after_self, gains[1], project_back(dq_cross, x_query))
    d_self = d_self + d_cross
    d_branch = d_self.astype(jnp.bfloat16)
    grad_w_out = outer_sum(mixed, d_branch)
    d_mixed = project_back(d_branch, w_out).astype(jnp.bfloat16)
    dq_self, dk_self, dv_self, d_scores = attention_backward(
        split_heads(query),
        split_heads(key),
        split_heads(value),
        bias,
        self_mask,
        logsum_self,
        split_heads(d_mixed),
    )
    d_bias = jnp.sum(d_scores, axis=0, dtype=jnp.float32)
    table_term = jnp.einsum(
        "hls,lsn->nh", d_bias, onehot.astype(jnp.float32), precision=lax.Precision.HIGHEST
    )
    grad_w_query = outer_sum(first, dq_self)
    grad_w_key = outer_sum(first, dk_self)
    grad_w_value = outer_sum(first, dv_self)
    d_first = (
        project_back(dq_self, w_query)
        + project_back(dk_self, w_key)
        + project_back(dv_self, w_value)
    )
    d_inputs, gain_one = norm_grad(inputs, gains[0], d_first)
    grad_decoder = d_inputs + d_self
    gain_terms = jnp.stack([gain_one, gain_two, gain_three], axis=1)
    flats = flat_rows(
        (
            grad_w_query,
            grad_w_key,
            grad_w_value,
            grad_w_out,
            grad_x_query,
            grad_x_key,
            grad_x_value,
            grad_x_out,
            grad_up,
            grad_down,
            gain_terms,
        )
    )
    summed = (
        lax.psum_scatter(flats[0], AXES, scatter_dimension=0, tiled=True),
        lax.psum_scatter(flats[1], AXES, scatter_dimension=0, tiled=True),
        lax.psum_scatter(flats[2], AXES, scatter_dimension=0, tiled=True),
        lax.psum_scatter(flats[3], AXES, scatter_dimension=0, tiled=True),
        lax.psum_scatter(flats[4], AXES, scatter_dimension=0, tiled=True),
        lax.psum_scatter(flats[5], AXES, scatter_dimension=0, tiled=True),
        lax.psum_scatter(flats[6], AXES, scatter_dimension=0, tiled=True),
        lax.psum_scatter(flats[7], AXES, scatter_dimension=0, tiled=True),
        lax.psum_scatter(flats[8], AXES, scatter_dimension=0, tiled=True),
        lax.psum_scatter(flats[9], AXES, scatter_dimension=0, tiled=True),
        lax.psum_scatter(flats[10], AXES, scatter_dimension=0, tiled=True),
    )
    shaped = unflat_rows(
        summed, (width, width, width, width, width, width, width, width, hidden_width, width, 3)
    )
    sums = shaped[:10] + (jnp.transpose(shaped[10]),)
    grad_table = lax.psum(table_term, AXES)
    return (
        layer_out,
        grad_decoder,
        grad_encoder,
        sums[0],
        sums[1],
        sums[2],
        sums[3],
        sums[4],
        sums[5],
        sums[6],
        sums[7],
        sums[8],
        sums[9],
        sums[10],
        grad_table,
    )


def solution(mesh):
    rows = P(AXES, None)
    slots = P(AXES, None, None)
    flat = P(AXES)
    gains = P(None, AXES)
    small = mesh.shape["dp"] == 8 and mesh.shape["fsdp"] == 4
    return jax.shard_map(
        by_kernel if small else plain,
        mesh=mesh,
        in_specs=(slots, slots) + (rows,) * 10 + (gains, P(), flat, flat, flat, slots),
        out_specs=(slots, slots, slots) + (rows,) * 10 + (gains, P()),
        check_vma=False,
    )
```

```python
import functools

import jax
import jax.numpy as jnp
from jax import lax
from jax.experimental import pallas as pl
from jax.experimental.pallas import tpu as pltpu
from jax.sharding import PartitionSpec as P

H = 12
AXES = ("dp", "fsdp")
MESH = pl.DeviceIdType.MESH
BF = jnp.bfloat16
F32 = jnp.float32


eps = 1e-06
thresholds = [19, 21, 24, 27, 31, 35, 40, 46, 52, 59, 67, 77, 87, 99, 113]


def normalize(v, gain):
    return v * lax.rsqrt(jnp.mean(v * v, axis=-1, keepdims=True) + eps) * gain


def norm_grad(v, gain, grad):
    _, pullback = jax.vjp(normalize, v, gain)
    return pullback(grad)


def gelu_grad(v, grad):
    _, pullback = jax.vjp(jax.nn.gelu, v)
    return pullback(grad)[0]


def project(v, weight):
    return jnp.einsum("btd,df->btf", v, weight, preferred_element_type=jnp.float32)


def project_back(grad, weight):
    return jnp.einsum("btf,df->btd", grad, weight, preferred_element_type=jnp.float32)


def outer_sum(v, grad):
    return jnp.einsum("btd,btf->df", v, grad, preferred_element_type=jnp.float32)


def split_heads(v):
    return v.reshape(v.shape[0], v.shape[1], H, v.shape[2] // H)


def join_heads(v):
    return v.reshape(v.shape[0], v.shape[1], v.shape[2] * v.shape[3])


def flat_rows(items):
    return tuple((item.reshape(-1) for item in items))


def unflat_rows(items, widths):
    return tuple((item.reshape(-1, width) for item, width in zip(items, widths)))


def buckets(length):
    place = jnp.arange(length, dtype=jnp.int32)
    distance = jnp.maximum(place[:, None] - place[None, :], 0)
    level = jnp.minimum(distance, 16)
    for edge in thresholds:
        level = level + (distance >= edge).astype(jnp.int32)
    return level


def scores_of(query, key, bias, mask):
    scores = jnp.einsum("blhd,bshd->bhls", query, key, preferred_element_type=jnp.float32) + bias
    return jnp.where(mask, scores, -1e30)


def attention_forward(query, key, value, bias, mask):
    scores = scores_of(query, key, bias, mask)
    top = jnp.max(scores, axis=-1, keepdims=True)
    expo = jnp.exp(scores - top)
    total = jnp.sum(expo, axis=-1, keepdims=True)
    probs = (expo / total).astype(jnp.bfloat16)
    mixed = jnp.einsum("bhls,bshd->blhd", probs, value, preferred_element_type=jnp.float32)
    return (join_heads(mixed).astype(jnp.bfloat16), top + jnp.log(total))


def attention_backward(query, key, value, bias, mask, logsum, d_out):
    probs = jnp.exp(scores_of(query, key, bias, mask) - logsum)
    d_probs = jnp.einsum("blhd,bshd->bhls", d_out, value, preferred_element_type=jnp.float32)
    delta = jnp.sum(d_probs * probs, axis=-1, keepdims=True)
    d_scores = (probs * (d_probs - delta)).astype(jnp.bfloat16)
    d_query = jnp.einsum(
        "bhls,bshd->blhd", d_scores, key, preferred_element_type=jnp.float32
    ).astype(jnp.bfloat16)
    d_key = jnp.einsum(
        "bhls,blhd->bshd", d_scores, query, preferred_element_type=jnp.float32
    ).astype(jnp.bfloat16)
    d_value = jnp.einsum(
        "bhls,blhd->bshd", probs.astype(jnp.bfloat16), d_out, preferred_element_type=jnp.float32
    ).astype(jnp.bfloat16)
    return (join_heads(d_query), join_heads(d_key), join_heads(d_value), d_scores)


class Place:
    def __init__(self):
        d = lax.axis_index("dp")
        self.z = lax.axis_index("fsdp")
        self.c = lax.rem(d, 2)
        self.x = lax.rem(lax.div(d, 2), 2)
        self.y = lax.div(d, 4)

    def dev(self, y, x, c, z):
        return ((y * 2 + x) * 2 + c, z)

    @property
    def core(self):
        return self.dev(self.y, self.x, 1 - self.c, self.z)

    @property
    def xn(self):
        return self.dev(self.y, 1 - self.x, self.c, self.z)

    @property
    def yn(self):
        return self.dev(1 - self.y, self.x, self.c, self.z)

    @property
    def across(self):
        return self.dev(1 - self.y, 1 - self.x, self.c, self.z)

    def zn(self, step):
        return self.dev(self.y, self.x, self.c, lax.rem(self.z + step, 4))

    def greet(self):
        bar = pltpu.get_barrier_semaphore()
        others = [self.core, self.xn, self.yn, self.across] + [self.zn(s) for s in (1, 2, 3)]
        for other in others:
            pl.semaphore_signal(bar, inc=1, device_id=other, device_id_type=MESH)

    def enter(self):
        pl.semaphore_wait(pltpu.get_barrier_semaphore(), 7)


def rcopy(src, dst, sems, landing, device, leaving=None):
    send, recv = sems
    return pltpu.make_async_remote_copy(
        src_ref=src,
        dst_ref=dst,
        send_sem=send.at[landing if leaving is None else leaving],
        recv_sem=recv.at[landing],
        device_id=device,
        device_id_type=MESH,
    )


class Small:
    def __init__(self, here, buf, sems):
        self.here, self.buf, self.sems = here, buf, sems

    def copies(self, stage):
        h = self.here
        base, devices = (
            (0, (h.core,)),
            (2, (h.xn, h.yn, h.across)),
            (6, (h.zn(1), h.zn(2), h.zn(3))),
        )[stage]
        at = (0, 1, 4)[stage]
        return [
            rcopy(self.buf.at[base], self.buf.at[base + 1 + i], self.sems, at + i, device)
            for i, device in enumerate(devices)
        ]

    def start(self, stage):
        for copy in self.copies(stage):
            copy.start()

    def finish(self, stage):
        for copy in self.copies(stage):
            copy.wait()
        b = self.buf
        if stage == 0:
            b[2] = b[0] + b[1]
        if stage == 1:
            b[6] = b[2] + b[3] + (b[4] + b[5])

    def total(self):
        b = self.buf
        return b[6] + b[7] + (b[8] + b[9])


EVERY = slice(None)


def sent(here, sems, leaving, ref):
    send, recv = sems
    pltpu.make_async_remote_copy(
        src_ref=ref, dst_ref=ref, send_sem=send.at[leaving], recv_sem=recv.at[0], device_id=here.core,
        device_id_type=MESH,
    ).wait_send()


class Gather:
    def __init__(self, here, sq, up, down, zland, early, zsems, sems, bsems, bcsems, like):
        self.here, self.sq, self.up, self.down = here, sq, up, down
        self.zland, self.early, self.zsems, self.sems = zland, early, zsems, sems
        self.bsems, self.bcsems, self.like = bsems, bcsems, like

    def blk(self, u, y, x, c):
        if u < 8:
            return self.sq.at[u, y, x, c]
        if u < 12:
            return self.up.at[u - 8, y, x, c]
        return self.down.at[y, x, c, 2 * (u - 12) : 2 * (u - 12) + 2, 0]

    def zpath(self, j):
        z = self.here.z
        low = z < 2
        if j == 0:
            source, target = z, jnp.where(low, z + 1, z - 1)
        elif j == 1:
            far = jnp.where(z == 0, 2, 1)
            near = jnp.where(z == 1, 0, 3)
            source, target = z, jnp.where((z == 0) | (z == 3), far, near)
        else:
            source = jnp.where(z == 1, 2, jnp.where(z == 2, 1, z))
            target = jnp.where(low, 3, 0)
            target = jnp.where(z == 1, 0, jnp.where(z == 2, 3, target))
        return source, target, lax.rem(source - target + 4, 4) - 1

    def zwait(self):
        return jnp.where(self.here.z < 2, 0, 2)

    def zref(self, k, z):
        h = self.here
        if k < 6:
            return self.zland.at[k, z]
        if k == 6:
            return self.down.at[h.y, h.x, h.c, z, 0]
        p = (k - 7) % 4
        if k < 11:
            return self.down.at[p // 2, p % 2, h.c, z, 1]
        return self.early.at[p // 2, p % 2, lax.div(z, 2), lax.rem(z, 2)]

    def zcopy(self, k, j):
        h = self.here
        source, target, landing = self.zpath(j)
        ref = self.zref(k, source)
        target = h.dev(h.y, h.x, h.c, target)
        return rcopy(ref, ref, self.zsems, 3 * k + landing, target, 0 if k < 8 else 1 if k < 11 else 2)

    def zgot(self, k, r):
        h = self.here
        ref = self.zref(k, lax.rem(h.z + 1 + r, 4))
        return rcopy(ref, ref, self.zsems, 3 * k + r, h.zn(1), 0)

    def z_start(self, k):
        z = self.here.z
        self.zcopy(k, 0).start()
        self.zcopy(k, 1).start()

        @pl.when((z == 0) | (z == 3))
        def _():
            self.zcopy(k, 2).start()

    def z_pass(self, k):
        z = self.here.z

        @pl.when((z == 1) | (z == 2))
        def _():
            self.zgot(k, self.zwait()).wait_recv()
            self.zcopy(k, 2).start()

    def z_wait(self, k):
        z = self.here.z
        self.zgot(k, 1).wait_recv()
        self.zgot(k, 2 - self.zwait()).wait_recv()

        @pl.when((z == 0) | (z == 3))
        def _():
            self.zgot(k, self.zwait()).wait_recv()

    def z_finish(self, k):
        h = self.here
        self.z_wait(k)
        if k < 6:
            slabs = self.zland[k].astype(F32)
            for half in (0, 1):
                rows = jnp.concatenate(
                    [slabs[z, 24 * half : 24 * half + 24] for z in range(4)], axis=0
                ).astype(BF).reshape(2, 48, 768)
                u = 2 * k + half
                if u < 8:
                    self.sq[u, h.y, h.x, h.c] = rows
                else:
                    self.up[u - 8, h.y, h.x, h.c] = rows
        for u in (2 * k, 2 * k + 1):
            self.first(u).start()
            self.second(u).start()

    def nbrs(self, u):
        h = self.here
        return (h.yn, h.xn) if u % 2 == 0 else (h.xn, h.yn)

    def group(self, u):
        return 0 if u < 4 else 2 if u > 9 else 1

    def own(self, u):
        h = self.here
        return self.blk(u, h.y, h.x, h.c)

    def got(self, u):
        h = self.here
        return self.blk(u, 1 - h.y, h.x, h.c) if u % 2 == 0 else self.blk(u, h.y, 1 - h.x, h.c)

    def first(self, u):
        return rcopy(self.own(u), self.own(u), self.sems, 4 * u, self.nbrs(u)[0], self.group(u))

    def second(self, u):
        return rcopy(self.own(u), self.own(u), self.sems, 4 * u + 1, self.nbrs(u)[1], self.group(u))

    def third(self, u):
        return rcopy(self.got(u), self.got(u), self.sems, 4 * u + 2, self.nbrs(u)[1], self.group(u))

    def cross(self, u):
        ref = self.blk(u, EVERY, EVERY, self.here.c)
        return rcopy(ref, ref, self.sems, 4 * u + 3, self.here.core, 3)

    def mid(self, k):
        for u in (2 * k, 2 * k + 1):
            self.first(u).wait_recv()
            self.third(u).start()

    def core(self, k):
        for u in (2 * k, 2 * k + 1):
            self.second(u).wait_recv()
            self.third(u).wait_recv()
            self.cross(u).start()

    def done(self, k):
        for u in (2 * k, 2 * k + 1):
            self.cross(u).wait_recv()

    def bblk(self, w, y, x):
        h = self.here
        cols = slice(384 * (w % 2), 384 * (w % 2) + 384)
        if w < 2:
            return self.down.at[y, x, h.c, h.z, 1, :, cols]
        return self.early.at[y, x, lax.div(h.z, 2), lax.rem(h.z, 2), :, cols]

    def bfirst(self, w):
        h = self.here
        ref = self.bblk(w, h.y, h.x)
        return rcopy(ref, ref, self.bsems, 3 * w + 0, self.nbrs(w)[0], w // 2)

    def bsecond(self, w):
        h = self.here
        ref = self.bblk(w, h.y, h.x)
        return rcopy(ref, ref, self.bsems, 3 * w + 1, self.nbrs(w)[1], w // 2)

    def bthird(self, w):
        h = self.here
        ref = self.bblk(w, 1 - h.y, h.x) if w % 2 == 0 else self.bblk(w, h.y, 1 - h.x)
        return rcopy(ref, ref, self.bsems, 3 * w + 2, self.nbrs(w)[1], w // 2)

    def b_start(self, *ws):
        for w in ws:
            self.bfirst(w).start()
            self.bsecond(w).start()

    def b_mid(self, *ws):
        for w in ws:
            self.bfirst(w).wait_recv()
            self.bthird(w).start()

    def b_got(self, *ws):
        for w in ws:
            self.bsecond(w).wait_recv()
            self.bthird(w).wait_recv()

    def early_finish(self):
        h = self.here
        for p in range(4):
            self.z_wait(11 + p)
        for p in range(4):
            slabs = self.early[p // 2, p % 2].astype(F32)
            for half in (0, 1):
                rows = [
                    slabs[z // 2, z % 2, 24 * half : 24 * half + 24] for z in range(4)
                ]
                self.sq[6 + half, p // 2, p % 2, h.c] = (
                    jnp.concatenate(rows, axis=0).astype(BF).reshape(2, 48, 768)
                )
        sent(h, self.zsems, 2, self.like[12])
        sent(h, self.bsems, 1, self.like[3])
        for u in (6, 7):
            self.cross(u).start()

    def bcross(self, y):
        ref = self.down.at[y, :, self.here.c, :, 1]
        return rcopy(ref, ref, self.bcsems, y, self.here.core, 0)

    def b_core(self, y):
        for p in (2 * y, 2 * y + 1):
            self.z_wait(7 + p)
        self.bcross(y).start()

    def b_done(self):
        for y in (0, 1):
            self.bcross(y).wait_recv()

    def drain(self):
        like = self.like
        sent(self.here, self.zsems, 0, like[21])
        sent(self.here, self.zsems, 1, like[9])
        for group in (0, 1, 2):
            sent(self.here, self.sems, group, like[24])
        sent(self.here, self.sems, 3, like[112])
        sent(self.here, self.bsems, 0, like[3])
        sent(self.here, self.bcsems, 0, like[16])


class Scatter:
    def __init__(
        self, here, up, down, gup, gdown, rc, r1, r2, zsend, zland, brest, bzland, br1, br2,
        sems, zsems, bzsems, bsems, tsems,
    ):
        self.here, self.up, self.down, self.gup, self.gdown = here, up, down, gup, gdown
        self.rc, self.r1, self.r2 = rc, r1, r2
        self.zsend, self.zland, self.sems, self.zsems = zsend, zland, sems, zsems
        self.brest, self.bzland, self.br1, self.br2 = brest, bzland, br1, br2
        self.bzsems, self.bsems, self.tsems = bzsems, bsems, tsems

    def blk(self, u, y, x, c):
        if u < 4:
            return self.down.at[y, x, c, u]
        if u < 8:
            return self.up.at[u - 4, y, x, c]
        if u < 12:
            return self.gup.at[u - 8, y, x, c]
        pair = (u - 12) % 2
        return self.gdown.at[y, x, c, 2 * pair : 2 * pair + 2, (u - 12) // 2]

    def put(self, u, y, cols, value):
        value = value.astype(BF).reshape(2, 2, 2, 48, 256)
        if u < 4:
            self.down[y, :, :, u, :, :, cols] = value
        else:
            self.up[u - 4, y, :, :, :, :, cols] = value

    def cross(self, u):
        h = self.here
        return rcopy(
            self.blk(u, EVERY, EVERY, 1 - h.c), self.rc.at[u % 8], self.sems, 3 * u, h.core, 0
        )

    def first(self, u):
        h = self.here
        if u % 2 == 0:
            src, device = self.blk(u, EVERY, 1 - h.x, h.c), h.xn
        else:
            src, device = self.blk(u, 1 - h.y, EVERY, h.c), h.yn
        return rcopy(src, self.r1.at[u], self.sems, 3 * u + 1, device, 1)

    def second(self, u):
        h = self.here
        if u % 2 == 0:
            src, device = self.r1.at[u, 1 - h.y], h.yn
        else:
            src, device = self.r1.at[u, 1 - h.x], h.xn
        return rcopy(src, self.r2.at[u], self.sems, 3 * u + 2, device, 2)

    def start(self, k):
        for u in (2 * k, 2 * k + 1):
            self.cross(u).start()

    def add_core(self, u):
        self.cross(u).wait_recv()
        mine = self.blk(u, EVERY, EVERY, self.here.c)
        mine[...] = (mine[...].astype(F32) + self.rc[u % 8].astype(F32)).astype(BF)

    def one(self, k):
        for u in (2 * k, 2 * k + 1):
            self.add_core(u)
            self.first(u).start()

    def two(self, k):
        h = self.here
        for u in (2 * k, 2 * k + 1):
            self.first(u).wait_recv()
            if u % 2 == 0:
                mine = self.blk(u, EVERY, h.x, h.c)
            else:
                mine = self.blk(u, h.y, EVERY, h.c)
            self.r1[u] = (mine[...].astype(F32) + self.r1[u].astype(F32)).astype(BF)
            self.second(u).start()

    def three(self, k):
        h = self.here
        sums = []
        for u in (2 * k, 2 * k + 1):
            self.second(u).wait_recv()
            at = h.y if u % 2 == 0 else h.x
            sums.append(self.r1[u, at].astype(F32) + self.r2[u].astype(F32))
        if k < 6:
            sums = [item.reshape(96, 768) for item in sums]
            for z in range(4):
                self.zsend[k, z] = jnp.concatenate(
                    [item[24 * z : 24 * z + 24] for item in sums], axis=0
                ).astype(BF)
        else:
            for half in (0, 1):
                self.zsend[k, 2 * half : 2 * half + 2] = sums[half].astype(BF)
        for s in (1, 2, 3):
            self.zcopy(k, s).start()

    def zcopy(self, k, s):
        h = self.here
        return rcopy(
            self.zsend.at[k, lax.rem(h.z + s, 4)], self.zland.at[k, s - 1], self.zsems,
            3 * k + s - 1, h.zn(s), 0,
        )

    def last(self, k):
        h = self.here
        for s in (1, 2, 3):
            self.zcopy(k, s).wait_recv()
        total = self.zsend[k, h.z].astype(F32)
        for s in (1, 2, 3):
            total = total + self.zland[k, s - 1].astype(F32)
        return total

    def tail_first(self, u, w):
        h = self.here
        cols = slice(384 * w, 384 * w + 384)
        if u % 2 == 0:
            src, device = self.blk(u, EVERY, 1 - h.x, h.c), h.xn
        else:
            src, device = self.blk(u, 1 - h.y, EVERY, h.c), h.yn
        return rcopy(
            src.at[:, :, :, cols], self.r1.at[u, :, :, :, cols], self.tsems, 2 * u + w, device, 0
        )

    def tail_second(self, u, w):
        h = self.here
        cols = slice(384 * w, 384 * w + 384)
        at, device = (1 - h.y, h.yn) if u % 2 == 0 else (1 - h.x, h.xn)
        return rcopy(
            self.r1.at[u, at, :, :, cols], self.r2.at[u, :, :, cols], self.tsems, 4 + 2 * u + w,
            device, 1,
        )

    def tail_zcopy(self, w, s):
        h = self.here
        cols = slice(384 * w, 384 * w + 384)
        return rcopy(
            self.zsend.at[0, lax.rem(h.z + s, 4), :, cols], self.zland.at[0, s - 1, :, cols],
            self.tsems, 8 + 3 * w + s - 1, h.zn(s), 2,
        )

    def tail_one(self):
        for u in (0, 1):
            self.add_core(u)
        for w in (0, 1):
            for u in (0, 1):
                self.tail_first(u, w).start()

    def tail_two(self, w):
        h = self.here
        cols = slice(384 * w, 384 * w + 384)
        for u in (0, 1):
            self.tail_first(u, w).wait_recv()
            if u % 2 == 0:
                mine = self.blk(u, EVERY, h.x, h.c)
            else:
                mine = self.blk(u, h.y, EVERY, h.c)
            mine = mine[:, :, :, cols].astype(F32)
            self.r1[u, :, :, :, cols] = (
                mine + self.r1[u, :, :, :, cols].astype(F32)
            ).astype(BF)
            self.tail_second(u, w).start()

    def tail_three(self, w):
        h = self.here
        cols = slice(384 * w, 384 * w + 384)
        sums = []
        for u in (0, 1):
            self.tail_second(u, w).wait_recv()
            at = h.y if u % 2 == 0 else h.x
            total = self.r1[u, at, :, :, cols].astype(F32) + self.r2[u, :, :, cols].astype(F32)
            sums.append(total.reshape(96, 384))
        for z in range(4):
            self.zsend[0, z, :, cols] = jnp.concatenate(
                [item[24 * z : 24 * z + 24] for item in sums], axis=0
            ).astype(BF)
        for s in (1, 2, 3):
            self.tail_zcopy(w, s).start()

    def tail_last(self, w):
        h = self.here
        cols = slice(384 * w, 384 * w + 384)
        for s in (1, 2, 3):
            self.tail_zcopy(w, s).wait_recv()
        total = self.zsend[0, h.z, :, cols].astype(F32)
        for s in (1, 2, 3):
            total = total + self.zland[0, s - 1, :, cols].astype(F32)
        return total

    def bz(self, s):
        h = self.here
        src = self.gdown.at[:, :, h.c, lax.rem(h.z + s, 4), 1]
        return rcopy(src, self.bzland.at[s - 1], self.bzsems, s - 1, h.zn(s), 0)

    def b_one(self):
        for u in (14, 15):
            self.add_core(u)
        for s in (1, 2, 3):
            self.bz(s).start()

    def bfirst(self, w):
        h = self.here
        if w == 0:
            src, device = self.brest.at[:, 1 - h.x, :, 0:384], h.xn
        else:
            src, device = self.brest.at[1 - h.y, :, :, 384:768], h.yn
        return rcopy(src, self.br1.at[w], self.bsems, 2 * w, device, 0)

    def bsecond(self, w):
        h = self.here
        if w == 0:
            src, device = self.br1.at[w, 1 - h.y], h.yn
        else:
            src, device = self.br1.at[w, 1 - h.x], h.xn
        return rcopy(src, self.br2.at[w], self.bsems, 2 * w + 1, device, 1)

    def b_two(self):
        h = self.here
        for s in (1, 2, 3):
            self.bz(s).wait_recv()
        total = self.gdown[:, :, h.c, h.z, 1].astype(F32)
        for s in (1, 2, 3):
            total = total + self.bzland[s - 1].astype(F32)
        self.brest[...] = total.astype(BF)
        for w in (0, 1):
            self.bfirst(w).start()

    def b_three(self):
        h = self.here
        for w in (0, 1):
            self.bfirst(w).wait_recv()
            if w == 0:
                mine = self.brest[:, h.x, :, 0:384]
            else:
                mine = self.brest[h.y, :, :, 384:768]
            self.br1[w] = (mine.astype(F32) + self.br1[w].astype(F32)).astype(BF)
            self.bsecond(w).start()

    def b_last(self, w):
        h = self.here
        self.bsecond(w).wait_recv()
        at = h.y if w == 0 else h.x
        return self.br1[w, at].astype(F32) + self.br2[w].astype(F32)

    def drain(self, slabs128):
        sent(self.here, self.sems, 0, slabs128)
        sent(self.here, self.sems, 1, self.r1.at[0:12])
        sent(self.here, self.sems, 2, self.r2.at[0:12])
        sent(self.here, self.zsems, 0, self.zland.at[0:6])
        sent(self.here, self.bzsems, 0, self.bzland)
        sent(self.here, self.bsems, 0, self.r2.at[0])
        sent(self.here, self.bsems, 1, self.r2.at[0, 0])
        sent(self.here, self.tsems, 0, self.r1.at[0:2])
        sent(self.here, self.tsems, 1, self.r2.at[0:2])
        sent(self.here, self.tsems, 2, self.zland.at[0])


def mm(a, b):
    return lax.dot_general(a, b, (((1,), (0,)), ((), ())), preferred_element_type=F32)


def mt(a, b):
    return lax.dot_general(a, b, (((1,), (1,)), ((), ())), preferred_element_type=F32)


def tm(a, b):
    return lax.dot_general(a, b, (((0,), (0,)), ((), ())), preferred_element_type=F32)


def iota(shape, axis):
    return lax.broadcasted_iota(jnp.int32, shape, axis)


def lanes(hp):
    return pl.ds(pl.multiple_of(hp * 128, 128), 128)


def both(q):
    low = iota(q.shape, 1) < 64
    zero = jnp.zeros_like(q)
    return jnp.concatenate([jnp.where(low, q, zero), jnp.where(low, zero, q)], axis=0)


def merge(pair):
    rows = pair.shape[0] // 2
    low = iota((rows, 128), 1) < 64
    return jnp.where(low, pair[:rows], pair[rows:]).astype(BF)


def probs(key, query, bias, mask):
    scores = mt(key, query)
    if bias is not None:
        scores = scores + bias.astype(F32)
    scores = jnp.where(mask, scores, -1e30)
    expo = jnp.exp(scores - jnp.max(scores, axis=0, keepdims=True))
    return expo * (1.0 / jnp.sum(expo, axis=0, keepdims=True))


def rms(v):
    return lax.rsqrt(jnp.mean(v * v, axis=-1, keepdims=True) + eps)


def norm_back(v, gain, grad):
    r = rms(v)
    scaled = grad * gain
    inner = jnp.mean(scaled * v, axis=-1, keepdims=True)
    return r * scaled - v * (r * r * r * inner), jnp.sum(grad * v * r, axis=0, keepdims=True)


def gelu(v):
    c = 0.7978845608028654
    return v * (0.5 + 0.5 * jnp.tanh(v * (c + c * 0.044715 * (v * v))))


def gelu_slope(v):
    c = 0.7978845608028654
    square = v * v
    t = jnp.tanh(v * (c + c * 0.044715 * square))
    return (0.5 + 0.5 * t) + v * (1.0 - t * t) * (0.5 * c + 1.5 * c * 0.044715 * square)


def layer_kernel(*refs):
    given, (tlen, slen, count) = refs[:15], refs[15:18]
    g_enc, results = refs[18], refs[19:33]
    (
        sq, up, down, gup, gdown, rc, r1, r2, zland, zland2, brest, bzland, br1, br2, small, small2,
        bias, h2, h3, q1, k1, v1, o1, q2, o2, k2, v2, g, gp, x1, x2, stage,
        zs, zr, ss, sr, bs, br, bcs, bcr, ms, mr,
        rzs, rzr, rss, rsr, rbzs, rbzr, rbs, rbr, rts, rtr, m2s, m2r, out_sem, done_sem, in_sem, credit,
        *held,
    ) = refs[33:]
    held, kept = [h2, x1, *held[:12]], held[12:]
    layer_out, g_dec, *g_sq, g_up, g_down, g_gain, g_table = held
    *squares, up_in, down_in, gain_in, table_in, x_in, cot, enc = kept

    def hand(i):
        return pltpu.make_async_copy(held[i], results[i], done_sem.at[i])

    def fetch(i):
        return pltpu.make_async_copy(given[i], kept[i], in_sem.at[i])

    here = Place()
    here.greet()
    for i in range(15):
        fetch(i).start()
    for i in range(12):
        fetch(i).wait()
    index = (here.y * 4 + here.x * 2 + here.c) * 4 + here.z
    for k in range(4):
        slab = jnp.concatenate(
            [squares[2 * k][...].astype(F32), squares[2 * k + 1][...].astype(F32)], axis=0
        ).astype(BF)
        if k < 3:
            zland[k, here.z] = slab
        else:
            rc[here.y, here.x, lax.div(here.z, 2), lax.rem(here.z, 2)] = slab
    for k in range(2):
        zland[4 + k, here.z] = jnp.concatenate(
            [up_in[:, 768 * n : 768 * n + 768].astype(F32) for n in (2 * k, 2 * k + 1)], axis=0
        ).astype(BF)
    down[here.y, here.x, here.c, here.z] = down_in[...].reshape(2, 48, 768)
    spot = (iota((24, 768), 1) == iota((24, 768), 0) + 24 * index).astype(BF)
    small[0] = jnp.zeros((8, 768), F32)
    small[0, 0:3] = mm(gain_in[...], spot)
    here.enter()
    like = {
        3: zland2.at[0], 9: zland2.at[0:3], 12: bzland, 16: rc.at[0:2], 21: zland2,
        24: r2.at[0:12], 112: sq.at[0:7],
    }
    ga = Gather(
        here, sq, up, down, zland, rc, (zs, zr), (ss, sr), (bs, br), (bcs, bcr), like
    )
    m = Small(here, small, (ms, mr))
    rs = Scatter(
        here, up, down, gup, gdown, rc, r1, r2, zland, zland2, brest, bzland, br1, br2,
        (rss, rsr), (rzs, rzr), (rbzs, rbzr), (rbs, rbr), (rts, rtr),
    )
    m2 = Small(here, small2, (m2s, m2r))

    def weight(u):
        return sq[u].reshape(768, 768)

    def columns(u, n):
        return sq[u, :, :, :, :, :, 256 * n : 256 * n + 256].reshape(768, 256)

    def z_starts(*items):
        for item in items:
            ga.z_start(item)

    def z_passes(*items):
        for item in items:
            ga.z_pass(item)

    m.start(0)
    ga.z_start(0)
    ga.b_start(2, 3, 0, 1)
    m.finish(0)
    m.start(1)
    ga.z_pass(0)
    z_starts(1)
    ga.b_mid(2, 3, 0, 1)

    def bucket_hot(rows_are_buckets):
        shape = (32, 128) if rows_are_buckets else (128, 32)
        distance = iota(shape, 1 if rows_are_buckets else 0)
        level = jnp.minimum(distance, 16)
        for edge in thresholds:
            level = level + (distance >= edge).astype(jnp.int32)
        return level == iota(shape, 0 if rows_are_buckets else 1)

    by_distance = mm(table_in[...], bucket_hot(True).astype(BF))
    for head in range(12):
        row = jnp.broadcast_to(by_distance[head : head + 1, :], (128, 128))
        bias[head // 2, :, 128 * (head % 2) : 128 * (head % 2) + 128] = pltpu.roll(
            row, 0, 1, stride=1, stride_axis=0
        ).astype(BF)

    key_place, target_place = iota((128, 256), 0), iota((128, 256), 1) & 127
    causal = key_place <= target_place
    source_place = iota((512, 256), 0)

    def self_mask(ex):
        return causal & (key_place < tlen[ex])

    def cross_mask(ex):
        return source_place < slen[ex]

    row_place = iota((256, 1), 0)
    live = (
        ((row_place < 128) & (row_place < tlen[0]) & (0 < count[0]))
        | ((row_place >= 128) & (row_place - 128 < tlen[1]) & (1 < count[0]))
    ).astype(F32)

    ga.z_finish(0)
    ga.b_got(2, 3)
    m.finish(1)
    m.start(2)
    z_starts(2, 11)
    ga.z_pass(1)
    ga.mid(0)
    ga.z_finish(1)
    z_starts(12, 4)
    z_passes(2, 11)
    ga.core(0)
    ga.z_finish(2)
    z_starts(5, 13)
    ga.mid(1)
    m.finish(2)
    gains = m.total()
    gain = [gains[i : i + 1, :] for i in range(3)]

    fetch(12).wait()

    def normed_input():
        first = x_in[...].astype(F32)
        return (first * rms(first) * gain[0]).astype(BF)

    h3[...] = normed_input()
    z_passes(12, 4)
    ga.core(1)
    ga.mid(2)
    ga.done(0)
    for n in range(3):
        cols = slice(256 * n, 256 * n + 256)
        q1[:, cols] = mm(h3[...], columns(0, n)).astype(BF)
        k1[:, cols] = mm(h3[...], columns(1, n)).astype(BF)
    ga.z_finish(4)
    z_starts(14)
    z_passes(5, 13)
    ga.core(2)
    ga.done(1)
    for n in range(3):
        cols = slice(256 * n, 256 * n + 256)
        v1[:, cols] = mm(h3[...], columns(2, n)).astype(BF)

    def self_forward(hp, carry):
        for ex in range(2):
            rows = slice(128 * ex, 128 * ex + 128)
            query = both(q1[rows, lanes(hp)])
            p = probs(k1[rows, lanes(hp)], query, bias[hp], self_mask(ex)).astype(BF)
            o1[rows, lanes(hp)] = merge(tm(p, v1[rows, lanes(hp)]))
        return carry

    lax.fori_loop(0, 6, self_forward, 0, unroll=2)
    ga.z_finish(5)
    ga.b_got(0, 1)
    z_starts(6)
    z_passes(14)
    ga.mid(4)
    x1[...] = x_in[...].astype(F32) + mm(o1[...], weight(3))
    h2[...] = (x1[...] * rms(x1[...]) * gain[1]).astype(BF)
    ga.done(2)

    def encode(r, carry):
        rows = pl.ds(pl.multiple_of(r * 256, 256), 256)
        for n in range(3):
            cols = slice(256 * n, 256 * n + 256)
            k2[rows, cols] = mm(enc[rows, :], columns(4, n)).astype(BF)
            v2[rows, cols] = mm(enc[rows, :], columns(5, n)).astype(BF)
        return carry

    fetch(14).wait()
    lax.fori_loop(0, 4, encode, 0)
    z_starts(7)
    ga.early_finish()
    ga.mid(5)
    z_passes(6)
    z_starts(8)
    ga.done(3)
    for n in range(3):
        cols = slice(256 * n, 256 * n + 256)
        q2[:, cols] = mm(h2[...], columns(6, n)).astype(BF)

    beyond = [jnp.where(iota((1, 512), 1) < slen[ex], 0.0, -1e30) for ex in range(2)]

    def cross_forward(hp, carry):
        for ex in range(2):
            rows = slice(128 * ex, 128 * ex + 128)
            keys = slice(512 * ex, 512 * ex + 512)
            query = both(q2[rows, lanes(hp)])
            scores = mt(query, k2[keys, lanes(hp)]) + beyond[ex]
            expo = jnp.exp(scores - jnp.max(scores, axis=1, keepdims=True))
            scale = 1.0 / jnp.sum(expo, axis=1, keepdims=True)
            o2[rows, lanes(hp)] = merge(mm(expo.astype(BF), v2[keys, lanes(hp)]) * scale)
        return carry

    def cross_step(i, carry):
        cross_forward(2 * i, carry)
        cross_forward(2 * i + 1, carry)

        @pl.when(i == 0)
        def _():
            ga.z_finish(6)
            ga.z_start(9)
            ga.z_pass(7)

        @pl.when(i == 1)
        def _():
            ga.core(4)
            ga.z_pass(8)
            ga.z_start(10)

        return carry

    lax.fori_loop(0, 3, cross_step, 0)
    ga.core(5)
    ga.mid(6)
    x2[...] = x1[...] + mm(o2[...], weight(7))
    h3[...] = (x2[...] * rms(x2[...]) * gain[2]).astype(BF)
    ga.done(4)

    def hidden(n, carry):
        for part in range(3):
            lo = 256 * part
            a = mm(h3[...], up[n, :, :, :, :, :, lo : lo + 256].reshape(768, 256))
            cols = pl.ds(pl.multiple_of(768 * n + lo, 256), 256)
            g[:, cols] = gelu(a).astype(BF)
            gp[:, cols] = a.astype(BF)
        return carry

    def keep_gain(i, term):
        for j in range(6):
            small2[0, 6 * i + j : 6 * i + j + 1, :] = term[:, 128 * j : 128 * j + 128]

    fetch(13).wait()

    def df(cols=slice(None)):
        return (cot[:, cols].astype(F32) * live).astype(BF)

    def wide(e):
        return pl.ds(pl.multiple_of(768 * e, 256), 768)

    def grad_down(e, carry):
        turned = g[:, wide(e)].T
        for n in range(3):
            cols = slice(256 * n, 256 * n + 256)
            grad = mm(turned, df(cols)).astype(BF)
            gdown[lax.div(e, 2), lax.rem(e, 2), :, :, :, :, cols] = grad.reshape(2, 4, 2, 48, 256)
        return carry

    def hidden_step(i, carry):
        for e in (2 * i, 2 * i + 1):
            hidden(e, carry)
        for e in (2 * i, 2 * i + 1):
            grad_down(e, carry)

        @pl.when(i == 0)
        def _():
            ga.z_pass(9)
            ga.z_pass(10)
            ga.done(5)

        return carry

    lax.fori_loop(0, 2, hidden_step, 0)
    rs.start(6)
    rs.start(7)
    ga.b_core(0)
    ga.core(6)
    rs.one(6)
    ga.b_core(1)
    rs.b_one()

    def slopes(n, carry):
        for part in range(3):
            cols = pl.ds(pl.multiple_of(768 * n + 256 * part, 256), 256)
            gp[:, cols] = gelu_slope(gp[:, cols].astype(F32)).astype(BF)
        return carry

    lax.fori_loop(0, 4, slopes, 0)
    ga.done(6)
    ga.b_done()

    def down_block(e):
        return down[lax.div(e, 2), lax.rem(e, 2)].reshape(768, 768)

    def inner_grad(e, carry):
        dg = mt(df(), down_block(e))
        gp[:, wide(e)] = (dg * gp[:, wide(e)].astype(F32)).astype(BF)
        return carry

    def grad_up(n, carry):
        turned = h3[...].T
        for part in range(3):
            cols = slice(256 * part, 256 * part + 256)
            source = pl.ds(pl.multiple_of(768 * n + 256 * part, 256), 256)
            grad = mm(turned, gp[:, source]).astype(BF)
            gup[n, :, :, :, :, :, cols] = grad.reshape(2, 2, 2, 2, 48, 256)
        return carry

    def inner_step(i, carry):
        for e in (2 * i, 2 * i + 1):
            inner_grad(e, carry)
        for e in (2 * i, 2 * i + 1):
            grad_up(e, carry)

        @pl.when(i == 0)
        def _():
            rs.start(4)

        return carry

    lax.fori_loop(0, 2, inner_step, 0)
    rs.start(5)
    rs.one(4)
    rs.two(6)
    stage[0] = jnp.zeros((256, 768), F32)
    stage[1] = x2[...]

    def inner_back(n, carry):
        stage[0] += mt(gp[:, wide(n)], up[n].reshape(768, 768))
        return carry

    lax.fori_loop(0, 4, inner_back, 0, unroll=2)
    rs.one(5)
    pl.semaphore_signal(credit, inc=1, device_id=here.core, device_id_type=MESH)
    d_norm, gain_three = norm_back(x2[...], gain[2], stage[0])
    keep_gain(2, gain_three)
    x2[...] = cot[...].astype(F32) * live + d_norm
    ga.drain()

    def put_grads(value, rows, pairs):
        def half_rows(y, carry):
            turned = value[:, pl.ds(pl.multiple_of(384 * y, 128), 384)].T
            for u, ref in pairs:
                for n in range(3):
                    cols = slice(256 * n, 256 * n + 256)
                    rs.put(u, y, cols, mm(turned, ref[:, cols]))
            return carry

        lax.fori_loop(0, 2, half_rows, 0)

    h3[...] = x2[...].astype(BF)
    put_grads(o2, 256, ((7, h3),))
    o2[...] = mt(h3[...], weight(7)).astype(BF)

    beyond_rows = [jnp.where(iota((512, 1), 0) < slen[ex], 0.0, -1e30) for ex in range(2)]

    def cross_backward(hp, carry):
        for ex in range(2):
            rows = slice(128 * ex, 128 * ex + 128)
            keys = slice(512 * ex, 512 * ex + 512)
            query, d_out = both(q2[rows, lanes(hp)]), both(o2[rows, lanes(hp)])
            key, value = k2[keys, lanes(hp)], v2[keys, lanes(hp)]
            scores = mt(key, query) + beyond_rows[ex]
            expo = jnp.exp(scores - jnp.max(scores, axis=0, keepdims=True))
            scale = 1.0 / jnp.sum(expo, axis=0, keepdims=True)
            dp = mt(value, d_out)
            delta = jnp.sum(dp * expo, axis=0, keepdims=True) * scale
            p = expo * scale
            ds = (p * (dp - delta)).astype(BF)
            turned = mm(key.T, ds).T
            q2[rows, lanes(hp)] = merge(turned)
            k2[keys, lanes(hp)] = mm(ds, query).astype(BF)
            v2[keys, lanes(hp)] = mm(p.astype(BF), d_out).astype(BF)
        return carry

    def cross_back_step(i, carry):
        cross_backward(2 * i, carry)
        cross_backward(2 * i + 1, carry)

        @pl.when(i == 1)
        def _():
            rs.two(4)

        return carry

    lax.fori_loop(0, 3, cross_back_step, 0)
    rs.three(6)
    put_grads(h2, 256, ((6, q2),))
    pl.semaphore_wait(credit, 1)
    rs.start(3)

    def result(e, carry):
        stage[1] += mm(g[:, wide(e)], down_block(e))
        return carry

    lax.fori_loop(0, 4, result, 0, unroll=2)
    layer_out[...] = (stage[1] * live).astype(BF)
    hand(0).start()
    rs.two(5)
    rs.one(3)
    put_grads(enc, 1024, ((4, k2), (5, v2)))
    rs.start(2)

    def finish(k):
        total = rs.last(k)
        if k < 4:
            g_sq[2 * k][...] = total[:24]
            g_sq[2 * k + 1][...] = total[24:]
            hand(2 + 2 * k).start()
            hand(3 + 2 * k).start()
        elif k < 6:
            g_up[:, 1536 * (k - 4) : 1536 * (k - 4) + 768] = total[:24]
            g_up[:, 1536 * (k - 4) + 768 : 1536 * (k - 4) + 1536] = total[24:]
        else:
            g_down[0:48, :] = total

    d_norm, gain_two = norm_back(x1[...], gain[1], mt(q2[...], weight(6)))
    keep_gain(1, gain_two)
    x2[...] = x2[...] + d_norm
    rs.one(2)
    rs.three(4)

    h3[...] = x2[...].astype(BF)
    put_grads(o1, 256, ((3, h3),))
    o1[...] = mt(h3[...], weight(3)).astype(BF)
    rs.b_two()
    rs.three(5)
    turn = (iota((128, 256), 0) + (iota((128, 256), 1) & 127) == 127).astype(BF)

    def self_backward(hp, carry):
        scores = []
        for ex in range(2):
            rows = slice(128 * ex, 128 * ex + 128)
            query, d_out = both(q1[rows, lanes(hp)]), both(o1[rows, lanes(hp)])
            key, value = k1[rows, lanes(hp)], v1[rows, lanes(hp)]
            p = probs(key, query, bias[hp], self_mask(ex))
            dp = mt(value, d_out)
            delta = jnp.sum(dp * p, axis=0, keepdims=True)
            ds = (p * (dp - delta)).astype(BF)
            q1[rows, lanes(hp)] = merge(tm(ds, key))
            k1[rows, lanes(hp)] = mm(ds, query).astype(BF)
            v1[rows, lanes(hp)] = mm(p.astype(BF), d_out).astype(BF)
            scores.append(ds)
        pair = mm(turn, jnp.concatenate(scores, axis=0))
        for head in range(2):
            skew = pltpu.roll(pair[:, 128 * head : 128 * head + 128], 0, 1, stride=1, stride_axis=0)
            small2[0, pl.ds(18 + 2 * hp + head, 1), :] = jnp.sum(skew, axis=0, keepdims=True)
        return carry

    lax.fori_loop(0, 6, self_backward, 0, unroll=2)
    h3[...] = normed_input()
    put_grads(h3, 256, ((2, v1), (0, q1), (1, k1)))
    rs.start(1)
    rs.two(3)
    rs.start(0)
    stage[0] = jnp.zeros((256, 768), F32)

    def first_back(y, carry):
        cols = pl.ds(pl.multiple_of(384 * y, 128), 384)
        for u, ref in ((0, q1), (1, k1), (2, v1)):
            stage[0, :, cols] += mt(ref[...], sq[u, y].reshape(384, 768))
        return carry

    lax.fori_loop(0, 2, first_back, 0, unroll=2)
    d_norm, gain_one = norm_back(x_in[...].astype(F32), gain[0], stage[0])
    g_dec[...] = x2[...] + d_norm
    hand(1).start()
    keep_gain(0, gain_one)
    small2[0, 30:32, :] = jnp.zeros((2, 128), F32)
    m2.start(0)
    rs.one(1)
    m2.finish(0)
    m2.start(1)
    rs.two(2)
    rs.b_three()
    rs.three(3)

    def out_copy(r):
        return pltpu.make_async_copy(
            stage.at[lax.rem(r, 2)],
            g_enc.at[pl.ds(pl.multiple_of(256 * r, 256), 256)],
            out_sem.at[r],
        )

    def encoder_grad(r, carry):
        @pl.when(r >= 2)
        def _():
            out_copy(r - 2).wait()

        rows = pl.ds(pl.multiple_of(256 * r, 256), 256)
        slot = lax.rem(r, 2)
        for y in range(2):
            cols = slice(384 * y, 384 * y + 384)
            stage[slot, :, cols] = mt(k2[rows, :], sq[4, y].reshape(384, 768))
            stage[slot, :, cols] += mt(v2[rows, :], sq[5, y].reshape(384, 768))
        out_copy(r).start()
        return carry

    lax.fori_loop(0, 4, encoder_grad, 0)
    finish(6)
    finish(4)
    finish(5)
    rs.two(1)
    m2.finish(1)
    m2.start(2)
    rs.tail_one()
    rs.three(2)
    for w in (0, 1):
        g_down[48:96, 384 * w : 384 * w + 384] = rs.b_last(w)
    hand(10).start()
    hand(11).start()
    rs.three(1)
    rs.tail_two(0)
    finish(3)
    rs.tail_two(1)
    rs.tail_three(0)
    rs.tail_three(1)
    m2.finish(2)
    reduced = m2.total()
    sums = jnp.concatenate(
        [
            jnp.concatenate([reduced[6 * i + j : 6 * i + j + 1, :] for j in range(6)], axis=1)
            for i in range(3)
        ],
        axis=0,
    )
    pick = (iota((768, 24), 0) == iota((768, 24), 1) + 24 * index).astype(F32)
    g_gain[...] = lax.dot_general(
        sums, pick, (((1,), (0,)), ((), ())), preferred_element_type=F32,
        precision=lax.Precision.HIGHEST,
    )
    distance = (iota((32, 128), 1) + 1) & 127
    level = jnp.minimum(distance, 16)
    for edge in thresholds:
        level = level + (distance >= edge).astype(jnp.int32)
    hot = (level == iota((32, 128), 0)).astype(F32)
    g_table[...] = lax.dot_general(
        reduced[18:30, :], hot, (((1,), (1,)), ((), ())), preferred_element_type=F32,
        precision=lax.Precision.HIGHEST,
    )
    hand(12).start()
    hand(13).start()
    finish(2)
    finish(1)
    for w in (0, 1):
        total = rs.tail_last(w)
        g_sq[0][:, 384 * w : 384 * w + 384] = total[:24]
        g_sq[1][:, 384 * w : 384 * w + 384] = total[24:]
    hand(2).start()
    hand(3).start()
    rs.drain(sq)
    out_copy(2).wait()
    out_copy(3).wait()
    for i in range(14):
        hand(i).wait()


SM = pl.BlockSpec(memory_space=pltpu.SMEM)
ANY = pl.BlockSpec(memory_space=pl.ANY)


def layer_call(*args):
    shape = jax.ShapeDtypeStruct
    dims = (3, 45, 4, 56, 2, 12, 1, 2, 7, 7, 1, 21, 3, 48, 1, 3, 2, 4, 3, 14, 7, 7)
    half = lambda *dims: pltpu.VMEM(dims, BF)
    results = (
        ((256, 768), BF),
        ((256, 768), F32),
        *[((24, 768), F32)] * 8,
        ((24, 3072), F32),
        ((96, 768), F32),
        ((3, 24), F32),
        ((12, 32), F32),
    )
    return pl.pallas_call(
        layer_kernel,
        out_shape=(
            shape((1024, 768), F32),
            *[shape(*each) for each in results],
        ),
        in_specs=[ANY] * 15 + [SM] * 3,
        out_specs=(ANY,) * 15,
        scratch_shapes=[
            half(8, 2, 2, 2, 2, 48, 768),
            half(4, 2, 2, 2, 2, 48, 768),
            half(2, 2, 2, 4, 2, 48, 768),
            half(4, 2, 2, 2, 2, 48, 768),
            half(2, 2, 2, 4, 2, 48, 768),
            half(8, 2, 2, 2, 48, 768),
            half(14, 2, 2, 48, 768),
            half(14, 2, 48, 768),
            half(7, 4, 48, 768),
            half(7, 3, 48, 768),
            half(2, 2, 48, 768),
            half(3, 2, 2, 48, 768),
            half(2, 2, 48, 384),
            half(2, 48, 384),
            pltpu.VMEM((10, 8, 768), F32),
            pltpu.VMEM((10, 32, 128), F32),
            half(6, 128, 256),
            *[half(256, 768)] * 2,
            *[half(256, 768)] * 4,
            *[half(256, 768)] * 2,
            *[half(1024, 768)] * 2,
            *[half(256, 3072)] * 2,
            *[pltpu.VMEM((256, 768), F32)] * 2,
            pltpu.VMEM((2, 256, 768), F32),
            *[pltpu.SemaphoreType.DMA((each,)) for each in dims],
            pltpu.SemaphoreType.DMA((4,)),
            pltpu.SemaphoreType.DMA((14,)),
            pltpu.SemaphoreType.DMA((15,)),
            pltpu.SemaphoreType.REGULAR,
            *[pltpu.VMEM(*each) for each in results[2:]],
            *[pltpu.VMEM(each.shape, each.dtype) for each in args[:15]],
        ],
        compiler_params=pltpu.CompilerParams(
            collective_id=0, has_side_effects=True, vmem_limit_bytes=64 * 2**20 - 2**16
        ),
        name="layer",
    )(*args)


def hand_out_kernel(*refs):
    count = (len(refs) - 2) // 3
    source, target, held = refs[:count], refs[count : 2 * count], refs[2 * count : 3 * count]
    got, put = refs[3 * count :]
    pieces = []
    for i in range(count):
        rows = source[i].shape[0]
        parts = 4 if rows % 256 == 0 else 1
        for part in range(parts):
            at = pl.ds(part * (rows // parts), rows // parts)
            pieces.append((source[i].at[at], held[i].at[at], target[i].at[at]))
    ins = [pltpu.make_async_copy(p[0], p[1], got.at[i]) for i, p in enumerate(pieces)]
    outs = [pltpu.make_async_copy(p[1], p[2], put.at[i]) for i, p in enumerate(pieces)]
    for copy in ins:
        copy.start()
    for copy, out in zip(ins, outs):
        copy.wait()
        out.start()
    for copy in outs:
        copy.wait()


def hand_out(arrays):
    return pl.pallas_call(
        hand_out_kernel,
        out_shape=tuple(jax.ShapeDtypeStruct(item.shape, item.dtype) for item in arrays),
        in_specs=[ANY] * len(arrays),
        out_specs=(ANY,) * len(arrays),
        scratch_shapes=[pltpu.VMEM(item.shape, item.dtype) for item in arrays]
        + [pltpu.SemaphoreType.DMA((len(arrays) + 9,))] * 2,
        name="hand_out",
    )(*arrays)


def by_kernel(
    decoder_in,
    encoder_out,
    self_query,
    self_key,
    self_value,
    self_output,
    cross_query,
    cross_key,
    cross_value,
    cross_output,
    hidden_in,
    hidden_out,
    norm_gains,
    bias_table,
    target_lengths,
    source_lengths,
    example_counts,
    cotangent,
):
    results = layer_call(
        self_query,
        self_key,
        self_value,
        self_output,
        cross_key,
        cross_value,
        cross_query,
        cross_output,
        hidden_in,
        hidden_out,
        norm_gains,
        bias_table.T,
        decoder_in.reshape(256, 768),
        cotangent.reshape(256, 768),
        encoder_out.reshape(1024, 768),
        target_lengths,
        source_lengths,
        example_counts,
    )
    g_enc, out, g_dec, *g_sq, g_up, g_down, g_gain, g_table = hand_out(results)
    return (
        out.reshape(decoder_in.shape),
        g_dec.reshape(decoder_in.shape),
        g_enc.reshape(encoder_out.shape),
        *g_sq[:4],
        g_sq[6],
        g_sq[4],
        g_sq[5],
        g_sq[7],
        g_up,
        g_down,
        g_gain,
        g_table.T,
    )


def plain(
    decoder_in,
    encoder_out,
    self_query,
    self_key,
    self_value,
    self_output,
    cross_query,
    cross_key,
    cross_value,
    cross_output,
    hidden_in,
    hidden_out,
    norm_gains,
    bias_table,
    target_lengths,
    source_lengths,
    example_counts,
    cotangent,
):
    gathered = (
        lax.all_gather(self_query, AXES, axis=0, tiled=True),
        lax.all_gather(self_key, AXES, axis=0, tiled=True),
        lax.all_gather(self_value, AXES, axis=0, tiled=True),
        lax.all_gather(self_output, AXES, axis=0, tiled=True),
        lax.all_gather(cross_query, AXES, axis=0, tiled=True),
        lax.all_gather(cross_key, AXES, axis=0, tiled=True),
        lax.all_gather(cross_value, AXES, axis=0, tiled=True),
        lax.all_gather(cross_output, AXES, axis=0, tiled=True),
        lax.all_gather(hidden_in, AXES, axis=0, tiled=True),
        lax.all_gather(hidden_out, AXES, axis=0, tiled=True),
        lax.all_gather(norm_gains, AXES, axis=1, tiled=True),
    )
    w_query, w_key, w_value, w_out, x_query, x_key, x_value, x_out, w_up, w_down, gain_all = (
        gathered
    )
    slots = jnp.arange(decoder_in.shape[0], dtype=jnp.int32)
    length = decoder_in.shape[1]
    source = encoder_out.shape[1]
    width = decoder_in.shape[2]
    hidden_width = hidden_in.shape[1]
    place = jnp.arange(length, dtype=jnp.int32)
    source_place = jnp.arange(source, dtype=jnp.int32)
    live = (
        (slots < example_counts[0])[:, None] & (place[None, :] < target_lengths[:, None])
    ).astype(jnp.float32)[:, :, None]
    self_mask = (place[None, :] <= place[:, None])[None, None] & (
        place[None, None, None, :] < target_lengths[:, None, None, None]
    )
    cross_mask = source_place[None, None, None, :] < source_lengths[:, None, None, None]
    onehot = (
        buckets(length)[:, :, None] == jnp.arange(bias_table.shape[0], dtype=jnp.int32)
    ).astype(jnp.bfloat16)
    bias = jnp.einsum("lsn,nh->hls", onehot, bias_table, preferred_element_type=jnp.float32)
    gains = gain_all.astype(jnp.float32)
    inputs = decoder_in.astype(jnp.float32)
    first = normalize(inputs, gains[0]).astype(jnp.bfloat16)
    query = project(first, w_query).astype(jnp.bfloat16)
    key = project(first, w_key).astype(jnp.bfloat16)
    value = project(first, w_value).astype(jnp.bfloat16)
    mixed, logsum_self = attention_forward(
        split_heads(query), split_heads(key), split_heads(value), bias, self_mask
    )
    after_self = inputs + project(mixed, w_out)
    second = normalize(after_self, gains[1]).astype(jnp.bfloat16)
    cross_q = project(second, x_query).astype(jnp.bfloat16)
    cross_k = project(encoder_out, x_key).astype(jnp.bfloat16)
    cross_v = project(encoder_out, x_value).astype(jnp.bfloat16)
    crossed, logsum_cross = attention_forward(
        split_heads(cross_q), split_heads(cross_k), split_heads(cross_v), 0.0, cross_mask
    )
    after_cross = after_self + project(crossed, x_out)
    third = normalize(after_cross, gains[2]).astype(jnp.bfloat16)
    inner = project(third, w_up)
    active = jax.nn.gelu(inner).astype(jnp.bfloat16)
    result = after_cross + project(active, w_down)
    layer_out = (result * live).astype(jnp.bfloat16)
    regathered = (
        lax.all_gather(self_query, AXES, axis=0, tiled=True),
        lax.all_gather(self_key, AXES, axis=0, tiled=True),
        lax.all_gather(self_value, AXES, axis=0, tiled=True),
        lax.all_gather(self_output, AXES, axis=0, tiled=True),
        lax.all_gather(cross_query, AXES, axis=0, tiled=True),
        lax.all_gather(cross_key, AXES, axis=0, tiled=True),
        lax.all_gather(cross_value, AXES, axis=0, tiled=True),
        lax.all_gather(cross_output, AXES, axis=0, tiled=True),
        lax.all_gather(hidden_in, AXES, axis=0, tiled=True),
        lax.all_gather(hidden_out, AXES, axis=0, tiled=True),
        lax.all_gather(norm_gains, AXES, axis=1, tiled=True),
    )
    w_query, w_key, w_value, w_out, x_query, x_key, x_value, x_out, w_up, w_down, gain_all = (
        regathered
    )
    gains = gain_all.astype(jnp.float32)
    d_result = cotangent.astype(jnp.float32) * live
    d_branch = d_result.astype(jnp.bfloat16)
    grad_down = outer_sum(active, d_branch)
    d_inner = gelu_grad(inner, project_back(d_branch, w_down)).astype(jnp.bfloat16)
    grad_up = outer_sum(third, d_inner)
    d_cross, gain_three = norm_grad(after_cross, gains[2], project_back(d_inner, w_up))
    d_cross = d_cross + d_result
    d_branch = d_cross.astype(jnp.bfloat16)
    grad_x_out = outer_sum(crossed, d_branch)
    d_crossed = project_back(d_branch, x_out).astype(jnp.bfloat16)
    dq_cross, dk_cross, dv_cross, unused = attention_backward(
        split_heads(cross_q),
        split_heads(cross_k),
        split_heads(cross_v),
        0.0,
        cross_mask,
        logsum_cross,
        split_heads(d_crossed),
    )
    grad_x_query = outer_sum(second, dq_cross)
    grad_x_key = outer_sum(encoder_out, dk_cross)
    grad_x_value = outer_sum(encoder_out, dv_cross)
    grad_encoder = project_back(dk_cross, x_key) + project_back(dv_cross, x_value)
    d_self, gain_two = norm_grad(after_self, gains[1], project_back(dq_cross, x_query))
    d_self = d_self + d_cross
    d_branch = d_self.astype(jnp.bfloat16)
    grad_w_out = outer_sum(mixed, d_branch)
    d_mixed = project_back(d_branch, w_out).astype(jnp.bfloat16)
    dq_self, dk_self, dv_self, d_scores = attention_backward(
        split_heads(query),
        split_heads(key),
        split_heads(value),
        bias,
        self_mask,
        logsum_self,
        split_heads(d_mixed),
    )
    d_bias = jnp.sum(d_scores, axis=0, dtype=jnp.float32)
    table_term = jnp.einsum(
        "hls,lsn->nh", d_bias, onehot.astype(jnp.float32), precision=lax.Precision.HIGHEST
    )
    grad_w_query = outer_sum(first, dq_self)
    grad_w_key = outer_sum(first, dk_self)
    grad_w_value = outer_sum(first, dv_self)
    d_first = (
        project_back(dq_self, w_query)
        + project_back(dk_self, w_key)
        + project_back(dv_self, w_value)
    )
    d_inputs, gain_one = norm_grad(inputs, gains[0], d_first)
    grad_decoder = d_inputs + d_self
    gain_terms = jnp.stack([gain_one, gain_two, gain_three], axis=1)
    flats = flat_rows(
        (
            grad_w_query,
            grad_w_key,
            grad_w_value,
            grad_w_out,
            grad_x_query,
            grad_x_key,
            grad_x_value,
            grad_x_out,
            grad_up,
            grad_down,
            gain_terms,
        )
    )
    summed = (
        lax.psum_scatter(flats[0], AXES, scatter_dimension=0, tiled=True),
        lax.psum_scatter(flats[1], AXES, scatter_dimension=0, tiled=True),
        lax.psum_scatter(flats[2], AXES, scatter_dimension=0, tiled=True),
        lax.psum_scatter(flats[3], AXES, scatter_dimension=0, tiled=True),
        lax.psum_scatter(flats[4], AXES, scatter_dimension=0, tiled=True),
        lax.psum_scatter(flats[5], AXES, scatter_dimension=0, tiled=True),
        lax.psum_scatter(flats[6], AXES, scatter_dimension=0, tiled=True),
        lax.psum_scatter(flats[7], AXES, scatter_dimension=0, tiled=True),
        lax.psum_scatter(flats[8], AXES, scatter_dimension=0, tiled=True),
        lax.psum_scatter(flats[9], AXES, scatter_dimension=0, tiled=True),
        lax.psum_scatter(flats[10], AXES, scatter_dimension=0, tiled=True),
    )
    shaped = unflat_rows(
        summed, (width, width, width, width, width, width, width, width, hidden_width, width, 3)
    )
    sums = shaped[:10] + (jnp.transpose(shaped[10]),)
    grad_table = lax.psum(table_term, AXES)
    return (
        layer_out,
        grad_decoder,
        grad_encoder,
        sums[0],
        sums[1],
        sums[2],
        sums[3],
        sums[4],
        sums[5],
        sums[6],
        sums[7],
        sums[8],
        sums[9],
        sums[10],
        grad_table,
    )


def solution(mesh):
    rows = P(AXES, None)
    slots = P(AXES, None, None)
    flat = P(AXES)
    gains = P(None, AXES)
    small = mesh.shape["dp"] == 8 and mesh.shape["fsdp"] == 4
    return jax.shard_map(
        by_kernel if small else plain,
        mesh=mesh,
        in_specs=(slots, slots) + (rows,) * 10 + (gains, P(), flat, flat, flat, slots),
        out_specs=(slots, slots, slots) + (rows,) * 10 + (gains, P()),
        check_vma=False,
    )
```

```python
import functools

import jax
import jax.numpy as jnp
from jax import lax
from jax.experimental import pallas as pl
from jax.experimental.pallas import tpu as pltpu
from jax.sharding import PartitionSpec as P

H = 12
AXES = ("dp", "fsdp")
MESH = pl.DeviceIdType.MESH
BF = jnp.bfloat16
F32 = jnp.float32


eps = 1e-06
thresholds = [19, 21, 24, 27, 31, 35, 40, 46, 52, 59, 67, 77, 87, 99, 113]


def normalize(v, gain):
    return v * lax.rsqrt(jnp.mean(v * v, axis=-1, keepdims=True) + eps) * gain


def norm_grad(v, gain, grad):
    _, pullback = jax.vjp(normalize, v, gain)
    return pullback(grad)


def gelu_grad(v, grad):
    _, pullback = jax.vjp(jax.nn.gelu, v)
    return pullback(grad)[0]


def project(v, weight):
    return jnp.einsum("btd,df->btf", v, weight, preferred_element_type=jnp.float32)


def project_back(grad, weight):
    return jnp.einsum("btf,df->btd", grad, weight, preferred_element_type=jnp.float32)


def outer_sum(v, grad):
    return jnp.einsum("btd,btf->df", v, grad, preferred_element_type=jnp.float32)


def split_heads(v):
    return v.reshape(v.shape[0], v.shape[1], H, v.shape[2] // H)


def join_heads(v):
    return v.reshape(v.shape[0], v.shape[1], v.shape[2] * v.shape[3])


def flat_rows(items):
    return tuple((item.reshape(-1) for item in items))


def unflat_rows(items, widths):
    return tuple((item.reshape(-1, width) for item, width in zip(items, widths)))


def buckets(length):
    place = jnp.arange(length, dtype=jnp.int32)
    distance = jnp.maximum(place[:, None] - place[None, :], 0)
    level = jnp.minimum(distance, 16)
    for edge in thresholds:
        level = level + (distance >= edge).astype(jnp.int32)
    return level


def scores_of(query, key, bias, mask):
    scores = jnp.einsum("blhd,bshd->bhls", query, key, preferred_element_type=jnp.float32) + bias
    return jnp.where(mask, scores, -1e30)


def attention_forward(query, key, value, bias, mask):
    scores = scores_of(query, key, bias, mask)
    top = jnp.max(scores, axis=-1, keepdims=True)
    expo = jnp.exp(scores - top)
    total = jnp.sum(expo, axis=-1, keepdims=True)
    probs = (expo / total).astype(jnp.bfloat16)
    mixed = jnp.einsum("bhls,bshd->blhd", probs, value, preferred_element_type=jnp.float32)
    return (join_heads(mixed).astype(jnp.bfloat16), top + jnp.log(total))


def attention_backward(query, key, value, bias, mask, logsum, d_out):
    probs = jnp.exp(scores_of(query, key, bias, mask) - logsum)
    d_probs = jnp.einsum("blhd,bshd->bhls", d_out, value, preferred_element_type=jnp.float32)
    delta = jnp.sum(d_probs * probs, axis=-1, keepdims=True)
    d_scores = (probs * (d_probs - delta)).astype(jnp.bfloat16)
    d_query = jnp.einsum(
        "bhls,bshd->blhd", d_scores, key, preferred_element_type=jnp.float32
    ).astype(jnp.bfloat16)
    d_key = jnp.einsum(
        "bhls,blhd->bshd", d_scores, query, preferred_element_type=jnp.float32
    ).astype(jnp.bfloat16)
    d_value = jnp.einsum(
        "bhls,blhd->bshd", probs.astype(jnp.bfloat16), d_out, preferred_element_type=jnp.float32
    ).astype(jnp.bfloat16)
    return (join_heads(d_query), join_heads(d_key), join_heads(d_value), d_scores)


class Place:
    def __init__(self):
        d = lax.axis_index("dp")
        self.z = lax.axis_index("fsdp")
        self.c = lax.rem(d, 2)
        self.x = lax.rem(lax.div(d, 2), 2)
        self.y = lax.div(d, 4)

    def dev(self, y, x, c, z):
        return ((y * 2 + x) * 2 + c, z)

    @property
    def core(self):
        return self.dev(self.y, self.x, 1 - self.c, self.z)

    @property
    def xn(self):
        return self.dev(self.y, 1 - self.x, self.c, self.z)

    @property
    def yn(self):
        return self.dev(1 - self.y, self.x, self.c, self.z)

    @property
    def across(self):
        return self.dev(1 - self.y, 1 - self.x, self.c, self.z)

    def zn(self, step):
        return self.dev(self.y, self.x, self.c, lax.rem(self.z + step, 4))

    def greet(self):
        bar = pltpu.get_barrier_semaphore()
        others = [self.core, self.xn, self.yn, self.across] + [self.zn(s) for s in (1, 2, 3)]
        for other in others:
            pl.semaphore_signal(bar, inc=1, device_id=other, device_id_type=MESH)

    def enter(self):
        pl.semaphore_wait(pltpu.get_barrier_semaphore(), 7)


def rcopy(src, dst, sems, landing, device, leaving=None):
    send, recv = sems
    return pltpu.make_async_remote_copy(
        src_ref=src,
        dst_ref=dst,
        send_sem=send.at[landing if leaving is None else leaving],
        recv_sem=recv.at[landing],
        device_id=device,
        device_id_type=MESH,
    )


class Small:
    def __init__(self, here, buf, sems):
        self.here, self.buf, self.sems = here, buf, sems

    def copies(self, stage):
        h = self.here
        base, devices = (
            (0, (h.core,)),
            (2, (h.xn, h.yn, h.across)),
            (6, (h.zn(1), h.zn(2), h.zn(3))),
        )[stage]
        at = (0, 1, 4)[stage]
        return [
            rcopy(self.buf.at[base], self.buf.at[base + 1 + i], self.sems, at + i, device)
            for i, device in enumerate(devices)
        ]

    def start(self, stage):
        for copy in self.copies(stage):
            copy.start()

    def finish(self, stage):
        for copy in self.copies(stage):
            copy.wait()
        b = self.buf
        if stage == 0:
            b[2] = b[0] + b[1]
        if stage == 1:
            b[6] = b[2] + b[3] + (b[4] + b[5])

    def total(self):
        b = self.buf
        return b[6] + b[7] + (b[8] + b[9])


EVERY = slice(None)


def sent(here, sems, leaving, ref):
    send, recv = sems
    pltpu.make_async_remote_copy(
        src_ref=ref, dst_ref=ref, send_sem=send.at[leaving], recv_sem=recv.at[0], device_id=here.core,
        device_id_type=MESH,
    ).wait_send()


class Gather:
    def __init__(self, here, sq, up, down, zland, early, zsems, sems, bsems, bcsems, like):
        self.here, self.sq, self.up, self.down = here, sq, up, down
        self.zland, self.early, self.zsems, self.sems = zland, early, zsems, sems
        self.bsems, self.bcsems, self.like = bsems, bcsems, like

    def blk(self, u, y, x, c):
        if u < 8:
            return self.sq.at[u, y, x, c]
        if u < 12:
            return self.up.at[u - 8, y, x, c]
        return self.down.at[y, x, c, 2 * (u - 12) : 2 * (u - 12) + 2, 0]

    def zpath(self, j):
        z = self.here.z
        low = z < 2
        if j == 0:
            source, target = z, jnp.where(low, z + 1, z - 1)
        elif j == 1:
            far = jnp.where(z == 0, 2, 1)
            near = jnp.where(z == 1, 0, 3)
            source, target = z, jnp.where((z == 0) | (z == 3), far, near)
        else:
            source = jnp.where(z == 1, 2, jnp.where(z == 2, 1, z))
            target = jnp.where(low, 3, 0)
            target = jnp.where(z == 1, 0, jnp.where(z == 2, 3, target))
        return source, target, lax.rem(source - target + 4, 4) - 1

    def zwait(self):
        return jnp.where(self.here.z < 2, 0, 2)

    def zref(self, k, z):
        h = self.here
        if k < 6:
            return self.zland.at[k, z]
        if k == 6:
            return self.down.at[h.y, h.x, h.c, z, 0]
        p = (k - 7) % 4
        if k < 11:
            return self.down.at[p // 2, p % 2, h.c, z, 1]
        return self.early.at[p // 2, p % 2, lax.div(z, 2), lax.rem(z, 2)]

    def zcopy(self, k, j):
        h = self.here
        source, target, landing = self.zpath(j)
        ref = self.zref(k, source)
        target = h.dev(h.y, h.x, h.c, target)
        return rcopy(ref, ref, self.zsems, 3 * k + landing, target, 0 if k < 8 else 1 if k < 11 else 2)

    def zgot(self, k, r):
        h = self.here
        ref = self.zref(k, lax.rem(h.z + 1 + r, 4))
        return rcopy(ref, ref, self.zsems, 3 * k + r, h.zn(1), 0)

    def z_start(self, k):
        z = self.here.z
        self.zcopy(k, 0).start()
        self.zcopy(k, 1).start()

        @pl.when((z == 0) | (z == 3))
        def _():
            self.zcopy(k, 2).start()

    def z_pass(self, k):
        z = self.here.z

        @pl.when((z == 1) | (z == 2))
        def _():
            self.zgot(k, self.zwait()).wait_recv()
            self.zcopy(k, 2).start()

    def z_wait(self, k):
        z = self.here.z
        self.zgot(k, 1).wait_recv()
        self.zgot(k, 2 - self.zwait()).wait_recv()

        @pl.when((z == 0) | (z == 3))
        def _():
            self.zgot(k, self.zwait()).wait_recv()

    def z_finish(self, k):
        h = self.here
        self.z_wait(k)
        if k < 6:
            slabs = self.zland[k].astype(F32)
            for half in (0, 1):
                rows = jnp.concatenate(
                    [slabs[z, 24 * half : 24 * half + 24] for z in range(4)], axis=0
                ).astype(BF).reshape(2, 48, 768)
                u = 2 * k + half
                if u < 8:
                    self.sq[u, h.y, h.x, h.c] = rows
                else:
                    self.up[u - 8, h.y, h.x, h.c] = rows
        for u in (2 * k, 2 * k + 1):
            self.first(u).start()
            self.second(u).start()

    def nbrs(self, u):
        h = self.here
        return (h.yn, h.xn) if u % 2 == 0 else (h.xn, h.yn)

    def group(self, u):
        return 0 if u < 4 else 2 if u > 9 else 1

    def own(self, u):
        h = self.here
        return self.blk(u, h.y, h.x, h.c)

    def got(self, u):
        h = self.here
        return self.blk(u, 1 - h.y, h.x, h.c) if u % 2 == 0 else self.blk(u, h.y, 1 - h.x, h.c)

    def first(self, u):
        return rcopy(self.own(u), self.own(u), self.sems, 4 * u, self.nbrs(u)[0], self.group(u))

    def second(self, u):
        return rcopy(self.own(u), self.own(u), self.sems, 4 * u + 1, self.nbrs(u)[1], self.group(u))

    def third(self, u):
        return rcopy(self.got(u), self.got(u), self.sems, 4 * u + 2, self.nbrs(u)[1], self.group(u))

    def cross(self, u):
        ref = self.blk(u, EVERY, EVERY, self.here.c)
        return rcopy(ref, ref, self.sems, 4 * u + 3, self.here.core, 3)

    def mid(self, k):
        for u in (2 * k, 2 * k + 1):
            self.first(u).wait_recv()
            self.third(u).start()

    def core(self, k):
        for u in (2 * k, 2 * k + 1):
            self.second(u).wait_recv()
            self.third(u).wait_recv()
            self.cross(u).start()

    def done(self, k):
        for u in (2 * k, 2 * k + 1):
            self.cross(u).wait_recv()

    def bblk(self, w, y, x):
        h = self.here
        cols = slice(384 * (w % 2), 384 * (w % 2) + 384)
        if w < 2:
            return self.down.at[y, x, h.c, h.z, 1, :, cols]
        return self.early.at[y, x, lax.div(h.z, 2), lax.rem(h.z, 2), :, cols]

    def bfirst(self, w):
        h = self.here
        ref = self.bblk(w, h.y, h.x)
        return rcopy(ref, ref, self.bsems, 3 * w + 0, self.nbrs(w)[0], w // 2)

    def bsecond(self, w):
        h = self.here
        ref = self.bblk(w, h.y, h.x)
        return rcopy(ref, ref, self.bsems, 3 * w + 1, self.nbrs(w)[1], w // 2)

    def bthird(self, w):
        h = self.here
        ref = self.bblk(w, 1 - h.y, h.x) if w % 2 == 0 else self.bblk(w, h.y, 1 - h.x)
        return rcopy(ref, ref, self.bsems, 3 * w + 2, self.nbrs(w)[1], w // 2)

    def b_start(self, *ws):
        for w in ws:
            self.bfirst(w).start()
            self.bsecond(w).start()

    def b_mid(self, *ws):
        for w in ws:
            self.bfirst(w).wait_recv()
            self.bthird(w).start()

    def b_got(self, *ws):
        for w in ws:
            self.bsecond(w).wait_recv()
            self.bthird(w).wait_recv()

    def early_finish(self):
        h = self.here
        for p in range(4):
            self.z_wait(11 + p)
        for p in range(4):
            slabs = self.early[p // 2, p % 2].astype(F32)
            for half in (0, 1):
                rows = [
                    slabs[z // 2, z % 2, 24 * half : 24 * half + 24] for z in range(4)
                ]
                self.sq[6 + half, p // 2, p % 2, h.c] = (
                    jnp.concatenate(rows, axis=0).astype(BF).reshape(2, 48, 768)
                )
        sent(h, self.zsems, 2, self.like[12])
        sent(h, self.bsems, 1, self.like[3])
        for u in (6, 7):
            self.cross(u).start()

    def bcross(self, y):
        ref = self.down.at[y, :, self.here.c, :, 1]
        return rcopy(ref, ref, self.bcsems, y, self.here.core, 0)

    def b_core(self, y):
        for p in (2 * y, 2 * y + 1):
            self.z_wait(7 + p)
        self.bcross(y).start()

    def b_done(self):
        for y in (0, 1):
            self.bcross(y).wait_recv()

    def drain(self):
        like = self.like
        sent(self.here, self.zsems, 0, like[21])
        sent(self.here, self.zsems, 1, like[9])
        for group in (0, 1, 2):
            sent(self.here, self.sems, group, like[24])
        sent(self.here, self.sems, 3, like[112])
        sent(self.here, self.bsems, 0, like[3])
        sent(self.here, self.bcsems, 0, like[16])


class Scatter:
    def __init__(
        self, here, up, down, gup, gdown, rc, r1, r2, zsend, zland, brest, bzland, br1, br2,
        sems, zsems, bzsems, bsems, tsems,
    ):
        self.here, self.up, self.down, self.gup, self.gdown = here, up, down, gup, gdown
        self.rc, self.r1, self.r2 = rc, r1, r2
        self.zsend, self.zland, self.sems, self.zsems = zsend, zland, sems, zsems
        self.brest, self.bzland, self.br1, self.br2 = brest, bzland, br1, br2
        self.bzsems, self.bsems, self.tsems = bzsems, bsems, tsems

    def blk(self, u, y, x, c):
        if u < 4:
            return self.down.at[y, x, c, u]
        if u < 8:
            return self.up.at[u - 4, y, x, c]
        if u < 12:
            return self.gup.at[u - 8, y, x, c]
        pair = (u - 12) % 2
        return self.gdown.at[y, x, c, 2 * pair : 2 * pair + 2, (u - 12) // 2]

    def put(self, u, y, cols, value):
        value = value.astype(BF).reshape(2, 2, 2, 48, 256)
        if u < 4:
            self.down[y, :, :, u, :, :, cols] = value
        else:
            self.up[u - 4, y, :, :, :, :, cols] = value

    def cross(self, u):
        h = self.here
        return rcopy(
            self.blk(u, EVERY, EVERY, 1 - h.c), self.rc.at[u % 8], self.sems, 3 * u, h.core, 0
        )

    def first(self, u):
        h = self.here
        if u % 2 == 0:
            src, device = self.blk(u, EVERY, 1 - h.x, h.c), h.xn
        else:
            src, device = self.blk(u, 1 - h.y, EVERY, h.c), h.yn
        return rcopy(src, self.r1.at[u], self.sems, 3 * u + 1, device, 1)

    def second(self, u):
        h = self.here
        if u % 2 == 0:
            src, device = self.r1.at[u, 1 - h.y], h.yn
        else:
            src, device = self.r1.at[u, 1 - h.x], h.xn
        return rcopy(src, self.r2.at[u], self.sems, 3 * u + 2, device, 2)

    def start(self, k):
        for u in (2 * k, 2 * k + 1):
            self.cross(u).start()

    def add_core(self, u):
        self.cross(u).wait_recv()
        mine = self.blk(u, EVERY, EVERY, self.here.c)
        mine[...] = (mine[...].astype(F32) + self.rc[u % 8].astype(F32)).astype(BF)

    def one(self, k):
        for u in (2 * k, 2 * k + 1):
            self.add_core(u)
            self.first(u).start()

    def two(self, k):
        h = self.here
        for u in (2 * k, 2 * k + 1):
            self.first(u).wait_recv()
            if u % 2 == 0:
                mine = self.blk(u, EVERY, h.x, h.c)
            else:
                mine = self.blk(u, h.y, EVERY, h.c)
            self.r1[u] = (mine[...].astype(F32) + self.r1[u].astype(F32)).astype(BF)
            self.second(u).start()

    def three(self, k):
        h = self.here
        sums = []
        for u in (2 * k, 2 * k + 1):
            self.second(u).wait_recv()
            at = h.y if u % 2 == 0 else h.x
            sums.append(self.r1[u, at].astype(F32) + self.r2[u].astype(F32))
        if k < 6:
            sums = [item.reshape(96, 768) for item in sums]
            for z in range(4):
                self.zsend[k, z] = jnp.concatenate(
                    [item[24 * z : 24 * z + 24] for item in sums], axis=0
                ).astype(BF)
        else:
            for half in (0, 1):
                self.zsend[k, 2 * half : 2 * half + 2] = sums[half].astype(BF)
        for s in (1, 2, 3):
            self.zcopy(k, s).start()

    def zcopy(self, k, s):
        h = self.here
        return rcopy(
            self.zsend.at[k, lax.rem(h.z + s, 4)], self.zland.at[k, s - 1], self.zsems,
            3 * k + s - 1, h.zn(s), 0,
        )

    def last(self, k):
        h = self.here
        for s in (1, 2, 3):
            self.zcopy(k, s).wait_recv()
        total = self.zsend[k, h.z].astype(F32)
        for s in (1, 2, 3):
            total = total + self.zland[k, s - 1].astype(F32)
        return total

    def tail_first(self, u, w):
        h = self.here
        cols = slice(384 * w, 384 * w + 384)
        if u % 2 == 0:
            src, device = self.blk(u, EVERY, 1 - h.x, h.c), h.xn
        else:
            src, device = self.blk(u, 1 - h.y, EVERY, h.c), h.yn
        return rcopy(
            src.at[:, :, :, cols], self.r1.at[u, :, :, :, cols], self.tsems, 2 * u + w, device, 0
        )

    def tail_second(self, u, w):
        h = self.here
        cols = slice(384 * w, 384 * w + 384)
        at, device = (1 - h.y, h.yn) if u % 2 == 0 else (1 - h.x, h.xn)
        return rcopy(
            self.r1.at[u, at, :, :, cols], self.r2.at[u, :, :, cols], self.tsems, 4 + 2 * u + w,
            device, 1,
        )

    def tail_zcopy(self, w, s):
        h = self.here
        cols = slice(384 * w, 384 * w + 384)
        return rcopy(
            self.zsend.at[0, lax.rem(h.z + s, 4), :, cols], self.zland.at[0, s - 1, :, cols],
            self.tsems, 8 + 3 * w + s - 1, h.zn(s), 2,
        )

    def tail_one(self):
        for u in (0, 1):
            self.add_core(u)
            self.tail_first(u, 0).start()

    def tail_rest(self):
        for u in (0, 1):
            self.tail_first(u, 1).start()

    def tail_two(self, w):
        h = self.here
        cols = slice(384 * w, 384 * w + 384)
        for u in (0, 1):
            self.tail_first(u, w).wait_recv()
            if u % 2 == 0:
                mine = self.blk(u, EVERY, h.x, h.c)
            else:
                mine = self.blk(u, h.y, EVERY, h.c)
            mine = mine[:, :, :, cols].astype(F32)
            self.r1[u, :, :, :, cols] = (
                mine + self.r1[u, :, :, :, cols].astype(F32)
            ).astype(BF)
            self.tail_second(u, w).start()

    def tail_three(self, w):
        h = self.here
        cols = slice(384 * w, 384 * w + 384)
        sums = []
        for u in (0, 1):
            self.tail_second(u, w).wait_recv()
            at = h.y if u % 2 == 0 else h.x
            total = self.r1[u, at, :, :, cols].astype(F32) + self.r2[u, :, :, cols].astype(F32)
            sums.append(total.reshape(96, 384))
        for z in range(4):
            self.zsend[0, z, :, cols] = jnp.concatenate(
                [item[24 * z : 24 * z + 24] for item in sums], axis=0
            ).astype(BF)
        for s in (1, 2, 3):
            self.tail_zcopy(w, s).start()

    def tail_last(self, w):
        h = self.here
        cols = slice(384 * w, 384 * w + 384)
        for s in (1, 2, 3):
            self.tail_zcopy(w, s).wait_recv()
        total = self.zsend[0, h.z, :, cols].astype(F32)
        for s in (1, 2, 3):
            total = total + self.zland[0, s - 1, :, cols].astype(F32)
        return total

    def bz(self, s):
        h = self.here
        src = self.gdown.at[:, :, h.c, lax.rem(h.z + s, 4), 1]
        return rcopy(src, self.bzland.at[s - 1], self.bzsems, s - 1, h.zn(s), 0)

    def b_one(self):
        for u in (14, 15):
            self.add_core(u)
        for s in (1, 2, 3):
            self.bz(s).start()

    def bfirst(self, w):
        h = self.here
        if w == 0:
            src, device = self.brest.at[:, 1 - h.x, :, 0:384], h.xn
        else:
            src, device = self.brest.at[1 - h.y, :, :, 384:768], h.yn
        return rcopy(src, self.br1.at[w], self.bsems, 2 * w, device, 0)

    def bsecond(self, w):
        h = self.here
        if w == 0:
            src, device = self.br1.at[w, 1 - h.y], h.yn
        else:
            src, device = self.br1.at[w, 1 - h.x], h.xn
        return rcopy(src, self.br2.at[w], self.bsems, 2 * w + 1, device, 1)

    def b_two(self):
        h = self.here
        for s in (1, 2, 3):
            self.bz(s).wait_recv()
        total = self.gdown[:, :, h.c, h.z, 1].astype(F32)
        for s in (1, 2, 3):
            total = total + self.bzland[s - 1].astype(F32)
        self.brest[...] = total.astype(BF)
        for w in (0, 1):
            self.bfirst(w).start()

    def b_three(self):
        h = self.here
        for w in (0, 1):
            self.bfirst(w).wait_recv()
            if w == 0:
                mine = self.brest[:, h.x, :, 0:384]
            else:
                mine = self.brest[h.y, :, :, 384:768]
            self.br1[w] = (mine.astype(F32) + self.br1[w].astype(F32)).astype(BF)
            self.bsecond(w).start()

    def b_last(self, w):
        h = self.here
        self.bsecond(w).wait_recv()
        at = h.y if w == 0 else h.x
        return self.br1[w, at].astype(F32) + self.br2[w].astype(F32)

    def drain(self, slabs128):
        sent(self.here, self.sems, 0, slabs128)
        sent(self.here, self.sems, 1, self.r1.at[0:12])
        sent(self.here, self.sems, 2, self.r2.at[0:12])
        sent(self.here, self.zsems, 0, self.zland.at[0:6])
        sent(self.here, self.bzsems, 0, self.bzland)
        sent(self.here, self.bsems, 0, self.r2.at[0])
        sent(self.here, self.bsems, 1, self.r2.at[0, 0])
        sent(self.here, self.tsems, 0, self.r1.at[0:2])
        sent(self.here, self.tsems, 1, self.r2.at[0:2])
        sent(self.here, self.tsems, 2, self.zland.at[0])


def mm(a, b):
    return lax.dot_general(a, b, (((1,), (0,)), ((), ())), preferred_element_type=F32)


def mt(a, b):
    return lax.dot_general(a, b, (((1,), (1,)), ((), ())), preferred_element_type=F32)


def tm(a, b):
    return lax.dot_general(a, b, (((0,), (0,)), ((), ())), preferred_element_type=F32)


def iota(shape, axis):
    return lax.broadcasted_iota(jnp.int32, shape, axis)


def lanes(hp):
    return pl.ds(pl.multiple_of(hp * 128, 128), 128)


def both(q):
    low = iota(q.shape, 1) < 64
    zero = jnp.zeros_like(q)
    return jnp.concatenate([jnp.where(low, q, zero), jnp.where(low, zero, q)], axis=0)


def merge(pair):
    rows = pair.shape[0] // 2
    low = iota((rows, 128), 1) < 64
    return jnp.where(low, pair[:rows], pair[rows:]).astype(BF)


def probs(key, query, bias, mask):
    scores = mt(key, query)
    if bias is not None:
        scores = scores + bias.astype(F32)
    scores = jnp.where(mask, scores, -1e30)
    expo = jnp.exp(scores - jnp.max(scores, axis=0, keepdims=True))
    return expo * (1.0 / jnp.sum(expo, axis=0, keepdims=True))


def rms(v):
    return lax.rsqrt(jnp.mean(v * v, axis=-1, keepdims=True) + eps)


def norm_back(v, gain, grad):
    r = rms(v)
    scaled = grad * gain
    inner = jnp.mean(scaled * v, axis=-1, keepdims=True)
    return r * scaled - v * (r * r * r * inner), jnp.sum(grad * v * r, axis=0, keepdims=True)


def gelu(v):
    c = 0.7978845608028654
    return v * (0.5 + 0.5 * jnp.tanh(v * (c + c * 0.044715 * (v * v))))


def gelu_slope(v):
    c = 0.7978845608028654
    square = v * v
    t = jnp.tanh(v * (c + c * 0.044715 * square))
    return (0.5 + 0.5 * t) + v * (1.0 - t * t) * (0.5 * c + 1.5 * c * 0.044715 * square)


def layer_kernel(*refs):
    given, (tlen, slen, count) = refs[:15], refs[15:18]
    g_enc, results = refs[18], refs[19:33]
    (
        sq, up, down, gup, gdown, rc, r1, r2, zland, zland2, brest, bzland, br1, br2, small, small2,
        bias, h2, h3, q1, k1, v1, o1, q2, o2, k2, v2, g, gp, x1, x2, stage,
        zs, zr, ss, sr, bs, br, bcs, bcr, ms, mr,
        rzs, rzr, rss, rsr, rbzs, rbzr, rbs, rbr, rts, rtr, m2s, m2r, out_sem, done_sem, in_sem, credit,
        *held,
    ) = refs[33:]
    held, kept = [h2, x1, *held[:10], *refs[31:33]], held[10:]
    layer_out, g_dec, *g_sq, g_up, g_down, g_gain, g_table = held
    *squares, up_in, down_in, gain_in, table_in = given[:12]
    x_in, cot, enc = kept

    def hand(i):
        return pltpu.make_async_copy(held[i], results[i], done_sem.at[i])

    def fetch(i):
        return pltpu.make_async_copy(given[12 + i], kept[i], in_sem.at[i])

    here = Place()
    here.greet()
    for i in range(3):
        fetch(i).start()
    index = (here.y * 4 + here.x * 2 + here.c) * 4 + here.z
    for k in range(4):
        slab = jnp.concatenate(
            [squares[2 * k][...].astype(F32), squares[2 * k + 1][...].astype(F32)], axis=0
        ).astype(BF)
        if k < 3:
            zland[k, here.z] = slab
        else:
            rc[here.y, here.x, lax.div(here.z, 2), lax.rem(here.z, 2)] = slab
    for k in range(2):
        zland[4 + k, here.z] = jnp.concatenate(
            [up_in[:, 768 * n : 768 * n + 768].astype(F32) for n in (2 * k, 2 * k + 1)], axis=0
        ).astype(BF)
    down[here.y, here.x, here.c, here.z] = down_in[...].reshape(2, 48, 768)
    spot = (iota((24, 768), 1) == iota((24, 768), 0) + 24 * index).astype(BF)
    small[0] = jnp.zeros((8, 768), F32)
    small[0, 0:3] = mm(gain_in[...], spot)
    here.enter()
    like = {
        3: zland2.at[0], 9: zland2.at[0:3], 12: bzland, 16: rc.at[0:2], 21: zland2,
        24: r2.at[0:12], 112: sq.at[0:7],
    }
    ga = Gather(
        here, sq, up, down, zland, rc, (zs, zr), (ss, sr), (bs, br), (bcs, bcr), like
    )
    m = Small(here, small, (ms, mr))
    rs = Scatter(
        here, up, down, gup, gdown, rc, r1, r2, zland, zland2, brest, bzland, br1, br2,
        (rss, rsr), (rzs, rzr), (rbzs, rbzr), (rbs, rbr), (rts, rtr),
    )
    m2 = Small(here, small2, (m2s, m2r))

    def weight(u):
        return sq[u].reshape(768, 768)

    def columns(u, n):
        return sq[u, :, :, :, :, :, 256 * n : 256 * n + 256].reshape(768, 256)

    def z_starts(*items):
        for item in items:
            ga.z_start(item)

    def z_passes(*items):
        for item in items:
            ga.z_pass(item)

    m.start(0)
    ga.z_start(0)
    ga.b_start(2, 3, 0, 1)
    m.finish(0)
    m.start(1)
    ga.z_pass(0)
    z_starts(1)
    ga.b_mid(2, 3, 0, 1)

    def bucket_hot(rows_are_buckets):
        shape = (32, 128) if rows_are_buckets else (128, 32)
        distance = iota(shape, 1 if rows_are_buckets else 0)
        level = jnp.minimum(distance, 16)
        for edge in thresholds:
            level = level + (distance >= edge).astype(jnp.int32)
        return level == iota(shape, 0 if rows_are_buckets else 1)

    by_distance = mm(table_in[...], bucket_hot(True).astype(BF))
    for head in range(12):
        row = jnp.broadcast_to(by_distance[head : head + 1, :], (128, 128))
        bias[head // 2, :, 128 * (head % 2) : 128 * (head % 2) + 128] = pltpu.roll(
            row, 0, 1, stride=1, stride_axis=0
        ).astype(BF)

    key_place, target_place = iota((128, 256), 0), iota((128, 256), 1) & 127
    causal = key_place <= target_place
    source_place = iota((512, 256), 0)

    def self_mask(ex):
        return causal & (key_place < tlen[ex])

    def cross_mask(ex):
        return source_place < slen[ex]

    row_place = iota((256, 1), 0)
    live = (
        ((row_place < 128) & (row_place < tlen[0]) & (0 < count[0]))
        | ((row_place >= 128) & (row_place - 128 < tlen[1]) & (1 < count[0]))
    ).astype(F32)

    ga.z_finish(0)
    ga.b_got(2, 3)
    m.finish(1)
    m.start(2)
    z_starts(2, 11)
    ga.z_pass(1)
    ga.mid(0)
    ga.z_finish(1)
    z_starts(12, 4)
    z_passes(2, 11)
    ga.core(0)
    ga.z_finish(2)
    z_starts(5, 13)
    ga.mid(1)
    m.finish(2)
    gains = m.total()
    gain = [gains[i : i + 1, :] for i in range(3)]

    fetch(0).wait()

    def normed_input():
        first = x_in[...].astype(F32)
        return (first * rms(first) * gain[0]).astype(BF)

    h3[...] = normed_input()
    z_passes(12, 4)
    ga.core(1)
    ga.mid(2)
    ga.done(0)
    for n in range(3):
        cols = slice(256 * n, 256 * n + 256)
        q1[:, cols] = mm(h3[...], columns(0, n)).astype(BF)
        k1[:, cols] = mm(h3[...], columns(1, n)).astype(BF)
    ga.z_finish(4)
    z_starts(14)
    z_passes(5, 13)
    ga.core(2)
    ga.done(1)
    for n in range(3):
        cols = slice(256 * n, 256 * n + 256)
        v1[:, cols] = mm(h3[...], columns(2, n)).astype(BF)

    def self_forward(hp, carry):
        for ex in range(2):
            rows = slice(128 * ex, 128 * ex + 128)
            query = both(q1[rows, lanes(hp)])
            p = probs(k1[rows, lanes(hp)], query, bias[hp], self_mask(ex)).astype(BF)
            o1[rows, lanes(hp)] = merge(tm(p, v1[rows, lanes(hp)]))
        return carry

    lax.fori_loop(0, 6, self_forward, 0, unroll=2)
    ga.z_finish(5)
    ga.b_got(0, 1)
    z_starts(6)
    z_passes(14)
    ga.mid(4)
    x1[...] = x_in[...].astype(F32) + mm(o1[...], weight(3))
    h2[...] = (x1[...] * rms(x1[...]) * gain[1]).astype(BF)
    ga.done(2)

    def encode(r, carry):
        rows = pl.ds(pl.multiple_of(r * 256, 256), 256)
        for n in range(3):
            cols = slice(256 * n, 256 * n + 256)
            k2[rows, cols] = mm(enc[rows, :], columns(4, n)).astype(BF)
            v2[rows, cols] = mm(enc[rows, :], columns(5, n)).astype(BF)
        return carry

    fetch(2).wait()
    lax.fori_loop(0, 4, encode, 0)
    z_starts(7)
    ga.early_finish()
    ga.mid(5)
    z_passes(6)
    z_starts(8)
    ga.done(3)
    for n in range(3):
        cols = slice(256 * n, 256 * n + 256)
        q2[:, cols] = mm(h2[...], columns(6, n)).astype(BF)

    beyond = [jnp.where(iota((1, 512), 1) < slen[ex], 0.0, -1e30) for ex in range(2)]

    def cross_forward(hp, carry):
        for ex in range(2):
            rows = slice(128 * ex, 128 * ex + 128)
            keys = slice(512 * ex, 512 * ex + 512)
            query = both(q2[rows, lanes(hp)])
            scores = mt(query, k2[keys, lanes(hp)]) + beyond[ex]
            expo = jnp.exp(scores - jnp.max(scores, axis=1, keepdims=True))
            scale = 1.0 / jnp.sum(expo, axis=1, keepdims=True)
            o2[rows, lanes(hp)] = merge(mm(expo.astype(BF), v2[keys, lanes(hp)]) * scale)
        return carry

    def cross_step(i, carry):
        cross_forward(2 * i, carry)
        cross_forward(2 * i + 1, carry)

        @pl.when(i == 0)
        def _():
            ga.z_finish(6)
            ga.z_start(9)
            ga.z_pass(7)

        @pl.when(i == 1)
        def _():
            ga.core(4)
            ga.z_pass(8)
            ga.z_start(10)

        return carry

    lax.fori_loop(0, 3, cross_step, 0)
    ga.core(5)
    ga.mid(6)
    x2[...] = x1[...] + mm(o2[...], weight(7))
    h3[...] = (x2[...] * rms(x2[...]) * gain[2]).astype(BF)
    ga.done(4)

    def hidden(n, carry):
        for part in range(3):
            lo = 256 * part
            a = mm(h3[...], up[n, :, :, :, :, :, lo : lo + 256].reshape(768, 256))
            cols = pl.ds(pl.multiple_of(768 * n + lo, 256), 256)
            g[:, cols] = gelu(a).astype(BF)
            gp[:, cols] = a.astype(BF)
        return carry

    def keep_gain(i, term):
        for j in range(6):
            small2[0, 6 * i + j : 6 * i + j + 1, :] = term[:, 128 * j : 128 * j + 128]

    fetch(1).wait()

    def df(cols=slice(None)):
        return (cot[:, cols].astype(F32) * live).astype(BF)

    def wide(e):
        return pl.ds(pl.multiple_of(768 * e, 256), 768)

    def grad_down(e, carry):
        turned = g[:, wide(e)].T
        for n in range(3):
            cols = slice(256 * n, 256 * n + 256)
            grad = mm(turned, df(cols)).astype(BF)
            gdown[lax.div(e, 2), lax.rem(e, 2), :, :, :, :, cols] = grad.reshape(2, 4, 2, 48, 256)
        return carry

    def hidden_step(i, carry):
        for e in (2 * i, 2 * i + 1):
            hidden(e, carry)
        for e in (2 * i, 2 * i + 1):
            grad_down(e, carry)

        @pl.when(i == 0)
        def _():
            ga.z_pass(9)
            ga.z_pass(10)
            ga.done(5)

        return carry

    lax.fori_loop(0, 2, hidden_step, 0)
    rs.start(6)
    rs.start(7)
    ga.b_core(0)
    ga.core(6)
    rs.one(6)
    ga.b_core(1)
    rs.b_one()

    def slopes(n, carry):
        for part in range(3):
            cols = pl.ds(pl.multiple_of(768 * n + 256 * part, 256), 256)
            gp[:, cols] = gelu_slope(gp[:, cols].astype(F32)).astype(BF)
        return carry

    lax.fori_loop(0, 4, slopes, 0)
    ga.done(6)
    ga.b_done()

    def down_block(e):
        return down[lax.div(e, 2), lax.rem(e, 2)].reshape(768, 768)

    def inner_grad(e, carry):
        dg = mt(df(), down_block(e))
        gp[:, wide(e)] = (dg * gp[:, wide(e)].astype(F32)).astype(BF)
        return carry

    def grad_up(n, carry):
        turned = h3[...].T
        for part in range(3):
            cols = slice(256 * part, 256 * part + 256)
            source = pl.ds(pl.multiple_of(768 * n + 256 * part, 256), 256)
            grad = mm(turned, gp[:, source]).astype(BF)
            gup[n, :, :, :, :, :, cols] = grad.reshape(2, 2, 2, 2, 48, 256)
        return carry

    def inner_step(i, carry):
        for e in (2 * i, 2 * i + 1):
            inner_grad(e, carry)
        for e in (2 * i, 2 * i + 1):
            grad_up(e, carry)

        @pl.when(i == 0)
        def _():
            rs.start(4)

        return carry

    lax.fori_loop(0, 2, inner_step, 0)
    rs.start(5)
    rs.one(4)
    rs.two(6)
    stage[0] = jnp.zeros((256, 768), F32)
    stage[1] = x2[...]

    def inner_back(n, carry):
        stage[0] += mt(gp[:, wide(n)], up[n].reshape(768, 768))
        return carry

    lax.fori_loop(0, 4, inner_back, 0, unroll=2)
    rs.one(5)
    pl.semaphore_signal(credit, inc=1, device_id=here.core, device_id_type=MESH)
    d_norm, gain_three = norm_back(x2[...], gain[2], stage[0])
    keep_gain(2, gain_three)
    x2[...] = cot[...].astype(F32) * live + d_norm
    ga.drain()

    def put_grads(value, rows, pairs):
        def half_rows(y, carry):
            turned = value[:, pl.ds(pl.multiple_of(384 * y, 128), 384)].T
            for u, ref in pairs:
                for n in range(3):
                    cols = slice(256 * n, 256 * n + 256)
                    rs.put(u, y, cols, mm(turned, ref[:, cols]))
            return carry

        lax.fori_loop(0, 2, half_rows, 0)

    h3[...] = x2[...].astype(BF)
    put_grads(o2, 256, ((7, h3),))
    o2[...] = mt(h3[...], weight(7)).astype(BF)

    beyond_rows = [jnp.where(iota((512, 1), 0) < slen[ex], 0.0, -1e30) for ex in range(2)]

    def cross_backward(hp, carry):
        for ex in range(2):
            rows = slice(128 * ex, 128 * ex + 128)
            keys = slice(512 * ex, 512 * ex + 512)
            query, d_out = both(q2[rows, lanes(hp)]), both(o2[rows, lanes(hp)])
            key, value = k2[keys, lanes(hp)], v2[keys, lanes(hp)]
            scores = mt(key, query) + beyond_rows[ex]
            expo = jnp.exp(scores - jnp.max(scores, axis=0, keepdims=True))
            scale = 1.0 / jnp.sum(expo, axis=0, keepdims=True)
            dp = mt(value, d_out)
            delta = jnp.sum(dp * expo, axis=0, keepdims=True) * scale
            p = expo * scale
            ds = (p * (dp - delta)).astype(BF)
            turned = mm(key.T, ds).T
            q2[rows, lanes(hp)] = merge(turned)
            k2[keys, lanes(hp)] = mm(ds, query).astype(BF)
            v2[keys, lanes(hp)] = mm(p.astype(BF), d_out).astype(BF)
        return carry

    def cross_back_step(i, carry):
        cross_backward(2 * i, carry)
        cross_backward(2 * i + 1, carry)

        @pl.when(i == 1)
        def _():
            rs.two(4)

        return carry

    lax.fori_loop(0, 3, cross_back_step, 0)
    rs.three(6)
    put_grads(h2, 256, ((6, q2),))
    pl.semaphore_wait(credit, 1)
    rs.start(3)

    def result(e, carry):
        stage[1] += mm(g[:, wide(e)], down_block(e))
        return carry

    lax.fori_loop(0, 4, result, 0, unroll=2)
    layer_out[...] = (stage[1] * live).astype(BF)
    hand(0).start()
    rs.two(5)
    rs.one(3)
    put_grads(enc, 1024, ((4, k2), (5, v2)))
    rs.start(2)

    def finish(k):
        total = rs.last(k)
        if k < 4:
            g_sq[2 * k][...] = total[:24]
            g_sq[2 * k + 1][...] = total[24:]
            hand(2 + 2 * k).start()
            hand(3 + 2 * k).start()
        elif k < 6:
            g_up[:, 1536 * (k - 4) : 1536 * (k - 4) + 768] = total[:24]
            g_up[:, 1536 * (k - 4) + 768 : 1536 * (k - 4) + 1536] = total[24:]
        else:
            g_down[0:48, :] = total

    d_norm, gain_two = norm_back(x1[...], gain[1], mt(q2[...], weight(6)))
    keep_gain(1, gain_two)
    x2[...] = x2[...] + d_norm
    rs.one(2)
    rs.three(4)

    h3[...] = x2[...].astype(BF)
    put_grads(o1, 256, ((3, h3),))
    o1[...] = mt(h3[...], weight(3)).astype(BF)
    rs.b_two()
    rs.three(5)
    turn = (iota((128, 256), 0) + (iota((128, 256), 1) & 127) == 127).astype(BF)

    def self_backward(hp, carry):
        scores = []
        for ex in range(2):
            rows = slice(128 * ex, 128 * ex + 128)
            query, d_out = both(q1[rows, lanes(hp)]), both(o1[rows, lanes(hp)])
            key, value = k1[rows, lanes(hp)], v1[rows, lanes(hp)]
            p = probs(key, query, bias[hp], self_mask(ex))
            dp = mt(value, d_out)
            delta = jnp.sum(dp * p, axis=0, keepdims=True)
            ds = (p * (dp - delta)).astype(BF)
            q1[rows, lanes(hp)] = merge(tm(ds, key))
            k1[rows, lanes(hp)] = mm(ds, query).astype(BF)
            v1[rows, lanes(hp)] = mm(p.astype(BF), d_out).astype(BF)
            scores.append(ds)
        pair = mm(turn, jnp.concatenate(scores, axis=0))
        for head in range(2):
            skew = pltpu.roll(pair[:, 128 * head : 128 * head + 128], 0, 1, stride=1, stride_axis=0)
            small2[0, pl.ds(18 + 2 * hp + head, 1), :] = jnp.sum(skew, axis=0, keepdims=True)
        return carry

    lax.fori_loop(0, 6, self_backward, 0, unroll=2)
    h3[...] = normed_input()
    put_grads(h3, 256, ((2, v1), (0, q1), (1, k1)))
    rs.start(1)
    rs.two(3)
    rs.start(0)
    stage[0] = jnp.zeros((256, 768), F32)

    def first_back(y, carry):
        cols = pl.ds(pl.multiple_of(384 * y, 128), 384)
        for u, ref in ((0, q1), (1, k1), (2, v1)):
            stage[0, :, cols] += mt(ref[...], sq[u, y].reshape(384, 768))
        return carry

    lax.fori_loop(0, 2, first_back, 0, unroll=2)
    d_norm, gain_one = norm_back(x_in[...].astype(F32), gain[0], stage[0])
    g_dec[...] = x2[...] + d_norm
    hand(1).start()
    keep_gain(0, gain_one)
    small2[0, 30:32, :] = jnp.zeros((2, 128), F32)
    m2.start(0)
    rs.one(1)
    m2.finish(0)
    m2.start(1)
    rs.two(2)
    rs.b_three()
    rs.three(3)

    def out_copy(r):
        return pltpu.make_async_copy(
            stage.at[lax.rem(r, 2)],
            g_enc.at[pl.ds(pl.multiple_of(256 * r, 256), 256)],
            out_sem.at[r],
        )

    def encoder_grad(r, carry):
        @pl.when(r >= 2)
        def _():
            out_copy(r - 2).wait()

        rows = pl.ds(pl.multiple_of(256 * r, 256), 256)
        slot = lax.rem(r, 2)
        for y in range(2):
            cols = slice(384 * y, 384 * y + 384)
            stage[slot, :, cols] = mt(k2[rows, :], sq[4, y].reshape(384, 768))
            stage[slot, :, cols] += mt(v2[rows, :], sq[5, y].reshape(384, 768))
        out_copy(r).start()
        return carry

    lax.fori_loop(0, 4, encoder_grad, 0)
    finish(6)
    finish(4)
    finish(5)
    rs.two(1)
    m2.finish(1)
    m2.start(2)
    rs.tail_one()
    rs.three(2)
    rs.tail_rest()
    for w in (0, 1):
        g_down[48:96, 384 * w : 384 * w + 384] = rs.b_last(w)
    hand(10).start()
    hand(11).start()
    rs.three(1)
    rs.tail_two(0)
    finish(3)
    rs.tail_two(1)
    rs.tail_three(0)
    rs.tail_three(1)
    m2.finish(2)
    reduced = m2.total()
    sums = jnp.concatenate(
        [
            jnp.concatenate([reduced[6 * i + j : 6 * i + j + 1, :] for j in range(6)], axis=1)
            for i in range(3)
        ],
        axis=0,
    )
    pick = (iota((768, 24), 0) == iota((768, 24), 1) + 24 * index).astype(F32)
    g_gain[...] = lax.dot_general(
        sums, pick, (((1,), (0,)), ((), ())), preferred_element_type=F32,
        precision=lax.Precision.HIGHEST,
    )
    distance = (iota((32, 128), 1) + 1) & 127
    level = jnp.minimum(distance, 16)
    for edge in thresholds:
        level = level + (distance >= edge).astype(jnp.int32)
    hot = (level == iota((32, 128), 0)).astype(F32)
    g_table[...] = lax.dot_general(
        reduced[18:30, :], hot, (((1,), (1,)), ((), ())), preferred_element_type=F32,
        precision=lax.Precision.HIGHEST,
    )
    finish(2)
    finish(1)
    for w in (0, 1):
        total = rs.tail_last(w)
        g_sq[0][:, 384 * w : 384 * w + 384] = total[:24]
        g_sq[1][:, 384 * w : 384 * w + 384] = total[24:]
    hand(2).start()
    hand(3).start()
    rs.drain(sq)
    out_copy(2).wait()
    out_copy(3).wait()
    for i in range(12):
        hand(i).wait()


VM = pl.BlockSpec(memory_space=pltpu.VMEM)
SM = pl.BlockSpec(memory_space=pltpu.SMEM)
ANY = pl.BlockSpec(memory_space=pl.ANY)


def layer_call(*args):
    shape = jax.ShapeDtypeStruct
    dims = (3, 45, 4, 56, 2, 12, 1, 2, 7, 7, 1, 21, 3, 48, 1, 3, 2, 4, 3, 14, 7, 7)
    half = lambda *dims: pltpu.VMEM(dims, BF)
    results = (
        ((256, 768), BF),
        ((256, 768), F32),
        *[((24, 768), F32)] * 8,
        ((24, 3072), F32),
        ((96, 768), F32),
        ((3, 24), F32),
        ((12, 32), F32),
    )
    return pl.pallas_call(
        layer_kernel,
        out_shape=(
            shape((1024, 768), F32),
            *[shape(*each) for each in results],
        ),
        in_specs=[VM] * 12 + [ANY] * 3 + [SM] * 3,
        out_specs=(ANY,) * 13 + (VM,) * 2,
        scratch_shapes=[
            half(8, 2, 2, 2, 2, 48, 768),
            half(4, 2, 2, 2, 2, 48, 768),
            half(2, 2, 2, 4, 2, 48, 768),
            half(4, 2, 2, 2, 2, 48, 768),
            half(2, 2, 2, 4, 2, 48, 768),
            half(8, 2, 2, 2, 48, 768),
            half(14, 2, 2, 48, 768),
            half(14, 2, 48, 768),
            half(7, 4, 48, 768),
            half(7, 3, 48, 768),
            half(2, 2, 48, 768),
            half(3, 2, 2, 48, 768),
            half(2, 2, 48, 384),
            half(2, 48, 384),
            pltpu.VMEM((10, 8, 768), F32),
            pltpu.VMEM((10, 32, 128), F32),
            half(6, 128, 256),
            *[half(256, 768)] * 2,
            *[half(256, 768)] * 4,
            *[half(256, 768)] * 2,
            *[half(1024, 768)] * 2,
            *[half(256, 3072)] * 2,
            *[pltpu.VMEM((256, 768), F32)] * 2,
            pltpu.VMEM((2, 256, 768), F32),
            *[pltpu.SemaphoreType.DMA((each,)) for each in dims],
            pltpu.SemaphoreType.DMA((4,)),
            pltpu.SemaphoreType.DMA((12,)),
            pltpu.SemaphoreType.DMA((3,)),
            pltpu.SemaphoreType.REGULAR,
            *[pltpu.VMEM(*each) for each in results[2:12]],
            *[pltpu.VMEM(each.shape, each.dtype) for each in args[12:15]],
        ],
        compiler_params=pltpu.CompilerParams(
            collective_id=0, has_side_effects=True, vmem_limit_bytes=64 * 2**20 - 2**16
        ),
        name="layer",
    )(*args)


def hand_out_kernel(*refs):
    count = (len(refs) - 2) // 3
    source, target, held = refs[:count], refs[count : 2 * count], refs[2 * count : 3 * count]
    got, put = refs[3 * count :]
    pieces = []
    for i in range(count):
        rows = source[i].shape[0]
        parts = 4 if rows % 256 == 0 else 1
        for part in range(parts):
            at = pl.ds(part * (rows // parts), rows // parts)
            pieces.append((source[i].at[at], held[i].at[at], target[i].at[at]))
    ins = [pltpu.make_async_copy(p[0], p[1], got.at[i]) for i, p in enumerate(pieces)]
    outs = [pltpu.make_async_copy(p[1], p[2], put.at[i]) for i, p in enumerate(pieces)]
    for copy in ins:
        copy.start()
    for copy, out in zip(ins, outs):
        copy.wait()
        out.start()
    for copy in outs:
        copy.wait()


def hand_out(arrays):
    return pl.pallas_call(
        hand_out_kernel,
        out_shape=tuple(jax.ShapeDtypeStruct(item.shape, item.dtype) for item in arrays),
        in_specs=[ANY] * len(arrays),
        out_specs=(ANY,) * len(arrays),
        scratch_shapes=[pltpu.VMEM(item.shape, item.dtype) for item in arrays]
        + [pltpu.SemaphoreType.DMA((len(arrays) + 9,))] * 2,
        name="hand_out",
    )(*arrays)


def by_kernel(
    decoder_in,
    encoder_out,
    self_query,
    self_key,
    self_value,
    self_output,
    cross_query,
    cross_key,
    cross_value,
    cross_output,
    hidden_in,
    hidden_out,
    norm_gains,
    bias_table,
    target_lengths,
    source_lengths,
    example_counts,
    cotangent,
):
    results = layer_call(
        self_query,
        self_key,
        self_value,
        self_output,
        cross_key,
        cross_value,
        cross_query,
        cross_output,
        hidden_in,
        hidden_out,
        norm_gains,
        bias_table.T,
        decoder_in.reshape(256, 768),
        cotangent.reshape(256, 768),
        encoder_out.reshape(1024, 768),
        target_lengths,
        source_lengths,
        example_counts,
    )
    g_enc, out, g_dec, *g_sq, g_up, g_down, g_gain, g_table = hand_out(results)
    return (
        out.reshape(decoder_in.shape),
        g_dec.reshape(decoder_in.shape),
        g_enc.reshape(encoder_out.shape),
        *g_sq[:4],
        g_sq[6],
        g_sq[4],
        g_sq[5],
        g_sq[7],
        g_up,
        g_down,
        g_gain,
        g_table.T,
    )


def plain(
    decoder_in,
    encoder_out,
    self_query,
    self_key,
    self_value,
    self_output,
    cross_query,
    cross_key,
    cross_value,
    cross_output,
    hidden_in,
    hidden_out,
    norm_gains,
    bias_table,
    target_lengths,
    source_lengths,
    example_counts,
    cotangent,
):
    gathered = (
        lax.all_gather(self_query, AXES, axis=0, tiled=True),
        lax.all_gather(self_key, AXES, axis=0, tiled=True),
        lax.all_gather(self_value, AXES, axis=0, tiled=True),
        lax.all_gather(self_output, AXES, axis=0, tiled=True),
        lax.all_gather(cross_query, AXES, axis=0, tiled=True),
        lax.all_gather(cross_key, AXES, axis=0, tiled=True),
        lax.all_gather(cross_value, AXES, axis=0, tiled=True),
        lax.all_gather(cross_output, AXES, axis=0, tiled=True),
        lax.all_gather(hidden_in, AXES, axis=0, tiled=True),
        lax.all_gather(hidden_out, AXES, axis=0, tiled=True),
        lax.all_gather(norm_gains, AXES, axis=1, tiled=True),
    )
    w_query, w_key, w_value, w_out, x_query, x_key, x_value, x_out, w_up, w_down, gain_all = (
        gathered
    )
    slots = jnp.arange(decoder_in.shape[0], dtype=jnp.int32)
    length = decoder_in.shape[1]
    source = encoder_out.shape[1]
    width = decoder_in.shape[2]
    hidden_width = hidden_in.shape[1]
    place = jnp.arange(length, dtype=jnp.int32)
    source_place = jnp.arange(source, dtype=jnp.int32)
    live = (
        (slots < example_counts[0])[:, None] & (place[None, :] < target_lengths[:, None])
    ).astype(jnp.float32)[:, :, None]
    self_mask = (place[None, :] <= place[:, None])[None, None] & (
        place[None, None, None, :] < target_lengths[:, None, None, None]
    )
    cross_mask = source_place[None, None, None, :] < source_lengths[:, None, None, None]
    onehot = (
        buckets(length)[:, :, None] == jnp.arange(bias_table.shape[0], dtype=jnp.int32)
    ).astype(jnp.bfloat16)
    bias = jnp.einsum("lsn,nh->hls", onehot, bias_table, preferred_element_type=jnp.float32)
    gains = gain_all.astype(jnp.float32)
    inputs = decoder_in.astype(jnp.float32)
    first = normalize(inputs, gains[0]).astype(jnp.bfloat16)
    query = project(first, w_query).astype(jnp.bfloat16)
    key = project(first, w_key).astype(jnp.bfloat16)
    value = project(first, w_value).astype(jnp.bfloat16)
    mixed, logsum_self = attention_forward(
        split_heads(query), split_heads(key), split_heads(value), bias, self_mask
    )
    after_self = inputs + project(mixed, w_out)
    second = normalize(after_self, gains[1]).astype(jnp.bfloat16)
    cross_q = project(second, x_query).astype(jnp.bfloat16)
    cross_k = project(encoder_out, x_key).astype(jnp.bfloat16)
    cross_v = project(encoder_out, x_value).astype(jnp.bfloat16)
    crossed, logsum_cross = attention_forward(
        split_heads(cross_q), split_heads(cross_k), split_heads(cross_v), 0.0, cross_mask
    )
    after_cross = after_self + project(crossed, x_out)
    third = normalize(after_cross, gains[2]).astype(jnp.bfloat16)
    inner = project(third, w_up)
    active = jax.nn.gelu(inner).astype(jnp.bfloat16)
    result = after_cross + project(active, w_down)
    layer_out = (result * live).astype(jnp.bfloat16)
    regathered = (
        lax.all_gather(self_query, AXES, axis=0, tiled=True),
        lax.all_gather(self_key, AXES, axis=0, tiled=True),
        lax.all_gather(self_value, AXES, axis=0, tiled=True),
        lax.all_gather(self_output, AXES, axis=0, tiled=True),
        lax.all_gather(cross_query, AXES, axis=0, tiled=True),
        lax.all_gather(cross_key, AXES, axis=0, tiled=True),
        lax.all_gather(cross_value, AXES, axis=0, tiled=True),
        lax.all_gather(cross_output, AXES, axis=0, tiled=True),
        lax.all_gather(hidden_in, AXES, axis=0, tiled=True),
        lax.all_gather(hidden_out, AXES, axis=0, tiled=True),
        lax.all_gather(norm_gains, AXES, axis=1, tiled=True),
    )
    w_query, w_key, w_value, w_out, x_query, x_key, x_value, x_out, w_up, w_down, gain_all = (
        regathered
    )
    gains = gain_all.astype(jnp.float32)
    d_result = cotangent.astype(jnp.float32) * live
    d_branch = d_result.astype(jnp.bfloat16)
    grad_down = outer_sum(active, d_branch)
    d_inner = gelu_grad(inner, project_back(d_branch, w_down)).astype(jnp.bfloat16)
    grad_up = outer_sum(third, d_inner)
    d_cross, gain_three = norm_grad(after_cross, gains[2], project_back(d_inner, w_up))
    d_cross = d_cross + d_result
    d_branch = d_cross.astype(jnp.bfloat16)
    grad_x_out = outer_sum(crossed, d_branch)
    d_crossed = project_back(d_branch, x_out).astype(jnp.bfloat16)
    dq_cross, dk_cross, dv_cross, unused = attention_backward(
        split_heads(cross_q),
        split_heads(cross_k),
        split_heads(cross_v),
        0.0,
        cross_mask,
        logsum_cross,
        split_heads(d_crossed),
    )
    grad_x_query = outer_sum(second, dq_cross)
    grad_x_key = outer_sum(encoder_out, dk_cross)
    grad_x_value = outer_sum(encoder_out, dv_cross)
    grad_encoder = project_back(dk_cross, x_key) + project_back(dv_cross, x_value)
    d_self, gain_two = norm_grad(after_self, gains[1], project_back(dq_cross, x_query))
    d_self = d_self + d_cross
    d_branch = d_self.astype(jnp.bfloat16)
    grad_w_out = outer_sum(mixed, d_branch)
    d_mixed = project_back(d_branch, w_out).astype(jnp.bfloat16)
    dq_self, dk_self, dv_self, d_scores = attention_backward(
        split_heads(query),
        split_heads(key),
        split_heads(value),
        bias,
        self_mask,
        logsum_self,
        split_heads(d_mixed),
    )
    d_bias = jnp.sum(d_scores, axis=0, dtype=jnp.float32)
    table_term = jnp.einsum(
        "hls,lsn->nh", d_bias, onehot.astype(jnp.float32), precision=lax.Precision.HIGHEST
    )
    grad_w_query = outer_sum(first, dq_self)
    grad_w_key = outer_sum(first, dk_self)
    grad_w_value = outer_sum(first, dv_self)
    d_first = (
        project_back(dq_self, w_query)
        + project_back(dk_self, w_key)
        + project_back(dv_self, w_value)
    )
    d_inputs, gain_one = norm_grad(inputs, gains[0], d_first)
    grad_decoder = d_inputs + d_self
    gain_terms = jnp.stack([gain_one, gain_two, gain_three], axis=1)
    flats = flat_rows(
        (
            grad_w_query,
            grad_w_key,
            grad_w_value,
            grad_w_out,
            grad_x_query,
            grad_x_key,
            grad_x_value,
            grad_x_out,
            grad_up,
            grad_down,
            gain_terms,
        )
    )
    summed = (
        lax.psum_scatter(flats[0], AXES, scatter_dimension=0, tiled=True),
        lax.psum_scatter(flats[1], AXES, scatter_dimension=0, tiled=True),
        lax.psum_scatter(flats[2], AXES, scatter_dimension=0, tiled=True),
        lax.psum_scatter(flats[3], AXES, scatter_dimension=0, tiled=True),
        lax.psum_scatter(flats[4], AXES, scatter_dimension=0, tiled=True),
        lax.psum_scatter(flats[5], AXES, scatter_dimension=0, tiled=True),
        lax.psum_scatter(flats[6], AXES, scatter_dimension=0, tiled=True),
        lax.psum_scatter(flats[7], AXES, scatter_dimension=0, tiled=True),
        lax.psum_scatter(flats[8], AXES, scatter_dimension=0, tiled=True),
        lax.psum_scatter(flats[9], AXES, scatter_dimension=0, tiled=True),
        lax.psum_scatter(flats[10], AXES, scatter_dimension=0, tiled=True),
    )
    shaped = unflat_rows(
        summed, (width, width, width, width, width, width, width, width, hidden_width, width, 3)
    )
    sums = shaped[:10] + (jnp.transpose(shaped[10]),)
    grad_table = lax.psum(table_term, AXES)
    return (
        layer_out,
        grad_decoder,
        grad_encoder,
        sums[0],
        sums[1],
        sums[2],
        sums[3],
        sums[4],
        sums[5],
        sums[6],
        sums[7],
        sums[8],
        sums[9],
        sums[10],
        grad_table,
    )


def solution(mesh):
    rows = P(AXES, None)
    slots = P(AXES, None, None)
    flat = P(AXES)
    gains = P(None, AXES)
    small = mesh.shape["dp"] == 8 and mesh.shape["fsdp"] == 4
    return jax.shard_map(
        by_kernel if small else plain,
        mesh=mesh,
        in_specs=(slots, slots) + (rows,) * 10 + (gains, P(), flat, flat, flat, slots),
        out_specs=(slots, slots, slots) + (rows,) * 10 + (gains, P()),
        check_vma=False,
    )
```

```python
import functools

import jax
import jax.numpy as jnp
from jax import lax
from jax.experimental import pallas as pl
from jax.experimental.pallas import tpu as pltpu
from jax.sharding import PartitionSpec as P

H = 12
AXES = ("dp", "fsdp")
MESH = pl.DeviceIdType.MESH
BF = jnp.bfloat16
F32 = jnp.float32


eps = 1e-06
thresholds = [19, 21, 24, 27, 31, 35, 40, 46, 52, 59, 67, 77, 87, 99, 113]


def normalize(v, gain):
    return v * lax.rsqrt(jnp.mean(v * v, axis=-1, keepdims=True) + eps) * gain


def norm_grad(v, gain, grad):
    _, pullback = jax.vjp(normalize, v, gain)
    return pullback(grad)


def gelu_grad(v, grad):
    _, pullback = jax.vjp(jax.nn.gelu, v)
    return pullback(grad)[0]


def project(v, weight):
    return jnp.einsum("btd,df->btf", v, weight, preferred_element_type=jnp.float32)


def project_back(grad, weight):
    return jnp.einsum("btf,df->btd", grad, weight, preferred_element_type=jnp.float32)


def outer_sum(v, grad):
    return jnp.einsum("btd,btf->df", v, grad, preferred_element_type=jnp.float32)


def split_heads(v):
    return v.reshape(v.shape[0], v.shape[1], H, v.shape[2] // H)


def join_heads(v):
    return v.reshape(v.shape[0], v.shape[1], v.shape[2] * v.shape[3])


def flat_rows(items):
    return tuple((item.reshape(-1) for item in items))


def unflat_rows(items, widths):
    return tuple((item.reshape(-1, width) for item, width in zip(items, widths)))


def buckets(length):
    place = jnp.arange(length, dtype=jnp.int32)
    distance = jnp.maximum(place[:, None] - place[None, :], 0)
    level = jnp.minimum(distance, 16)
    for edge in thresholds:
        level = level + (distance >= edge).astype(jnp.int32)
    return level


def scores_of(query, key, bias, mask):
    scores = jnp.einsum("blhd,bshd->bhls", query, key, preferred_element_type=jnp.float32) + bias
    return jnp.where(mask, scores, -1e30)


def attention_forward(query, key, value, bias, mask):
    scores = scores_of(query, key, bias, mask)
    top = jnp.max(scores, axis=-1, keepdims=True)
    expo = jnp.exp(scores - top)
    total = jnp.sum(expo, axis=-1, keepdims=True)
    probs = (expo / total).astype(jnp.bfloat16)
    mixed = jnp.einsum("bhls,bshd->blhd", probs, value, preferred_element_type=jnp.float32)
    return (join_heads(mixed).astype(jnp.bfloat16), top + jnp.log(total))


def attention_backward(query, key, value, bias, mask, logsum, d_out):
    probs = jnp.exp(scores_of(query, key, bias, mask) - logsum)
    d_probs = jnp.einsum("blhd,bshd->bhls", d_out, value, preferred_element_type=jnp.float32)
    delta = jnp.sum(d_probs * probs, axis=-1, keepdims=True)
    d_scores = (probs * (d_probs - delta)).astype(jnp.bfloat16)
    d_query = jnp.einsum(
        "bhls,bshd->blhd", d_scores, key, preferred_element_type=jnp.float32
    ).astype(jnp.bfloat16)
    d_key = jnp.einsum(
        "bhls,blhd->bshd", d_scores, query, preferred_element_type=jnp.float32
    ).astype(jnp.bfloat16)
    d_value = jnp.einsum(
        "bhls,blhd->bshd", probs.astype(jnp.bfloat16), d_out, preferred_element_type=jnp.float32
    ).astype(jnp.bfloat16)
    return (join_heads(d_query), join_heads(d_key), join_heads(d_value), d_scores)


class Place:
    def __init__(self):
        d = lax.axis_index("dp")
        self.z = lax.axis_index("fsdp")
        self.c = lax.rem(d, 2)
        self.x = lax.rem(lax.div(d, 2), 2)
        self.y = lax.div(d, 4)

    def dev(self, y, x, c, z):
        return ((y * 2 + x) * 2 + c, z)

    @property
    def core(self):
        return self.dev(self.y, self.x, 1 - self.c, self.z)

    @property
    def xn(self):
        return self.dev(self.y, 1 - self.x, self.c, self.z)

    @property
    def yn(self):
        return self.dev(1 - self.y, self.x, self.c, self.z)

    @property
    def across(self):
        return self.dev(1 - self.y, 1 - self.x, self.c, self.z)

    def zn(self, step):
        return self.dev(self.y, self.x, self.c, lax.rem(self.z + step, 4))

    def greet(self):
        bar = pltpu.get_barrier_semaphore()
        others = [self.core, self.xn, self.yn, self.across] + [self.zn(s) for s in (1, 2, 3)]
        for other in others:
            pl.semaphore_signal(bar, inc=1, device_id=other, device_id_type=MESH)

    def enter(self):
        pl.semaphore_wait(pltpu.get_barrier_semaphore(), 7)


def rcopy(src, dst, sems, landing, device, leaving=None):
    send, recv = sems
    return pltpu.make_async_remote_copy(
        src_ref=src,
        dst_ref=dst,
        send_sem=send.at[landing if leaving is None else leaving],
        recv_sem=recv.at[landing],
        device_id=device,
        device_id_type=MESH,
    )


class Small:
    def __init__(self, here, buf, sems):
        self.here, self.buf, self.sems = here, buf, sems

    def copies(self, stage):
        h = self.here
        base, devices = (
            (0, (h.core,)),
            (2, (h.xn, h.yn, h.across)),
            (6, (h.zn(1), h.zn(2), h.zn(3))),
        )[stage]
        at = (0, 1, 4)[stage]
        return [
            rcopy(self.buf.at[base], self.buf.at[base + 1 + i], self.sems, at + i, device)
            for i, device in enumerate(devices)
        ]

    def start(self, stage):
        for copy in self.copies(stage):
            copy.start()

    def finish(self, stage):
        for copy in self.copies(stage):
            copy.wait()
        b = self.buf
        if stage == 0:
            b[2] = b[0] + b[1]
        if stage == 1:
            b[6] = b[2] + b[3] + (b[4] + b[5])

    def total(self):
        b = self.buf
        return b[6] + b[7] + (b[8] + b[9])


EVERY = slice(None)


def sent(here, sems, leaving, ref):
    send, recv = sems
    pltpu.make_async_remote_copy(
        src_ref=ref, dst_ref=ref, send_sem=send.at[leaving], recv_sem=recv.at[0], device_id=here.core,
        device_id_type=MESH,
    ).wait_send()


class Gather:
    def __init__(self, here, sq, up, down, zland, early, zsems, sems, bsems, bcsems, like):
        self.here, self.sq, self.up, self.down = here, sq, up, down
        self.zland, self.early, self.zsems, self.sems = zland, early, zsems, sems
        self.bsems, self.bcsems, self.like = bsems, bcsems, like

    def blk(self, u, y, x, c):
        if u < 8:
            return self.sq.at[u, y, x, c]
        if u < 12:
            return self.up.at[u - 8, y, x, c]
        return self.down.at[y, x, c, 2 * (u - 12) : 2 * (u - 12) + 2, 0]

    def zpath(self, j):
        z = self.here.z
        low = z < 2
        if j == 0:
            source, target = z, jnp.where(low, z + 1, z - 1)
        elif j == 1:
            far = jnp.where(z == 0, 2, 1)
            near = jnp.where(z == 1, 0, 3)
            source, target = z, jnp.where((z == 0) | (z == 3), far, near)
        else:
            source = jnp.where(z == 1, 2, jnp.where(z == 2, 1, z))
            target = jnp.where(low, 3, 0)
            target = jnp.where(z == 1, 0, jnp.where(z == 2, 3, target))
        return source, target, lax.rem(source - target + 4, 4) - 1

    def zwait(self):
        return jnp.where(self.here.z < 2, 0, 2)

    def zref(self, k, z):
        h = self.here
        if k < 6:
            return self.zland.at[k, z]
        if k == 6:
            return self.down.at[h.y, h.x, h.c, z, 0]
        p = (k - 7) % 4
        if k < 11:
            return self.down.at[p // 2, p % 2, h.c, z, 1]
        return self.early.at[p // 2, p % 2, lax.div(z, 2), lax.rem(z, 2)]

    def zcopy(self, k, j):
        h = self.here
        source, target, landing = self.zpath(j)
        ref = self.zref(k, source)
        target = h.dev(h.y, h.x, h.c, target)
        return rcopy(ref, ref, self.zsems, 3 * k + landing, target, 0 if k < 8 else 1 if k < 11 else 2)

    def zgot(self, k, r):
        h = self.here
        ref = self.zref(k, lax.rem(h.z + 1 + r, 4))
        return rcopy(ref, ref, self.zsems, 3 * k + r, h.zn(1), 0)

    def z_start(self, k):
        z = self.here.z
        self.zcopy(k, 0).start()
        self.zcopy(k, 1).start()

        @pl.when((z == 0) | (z == 3))
        def _():
            self.zcopy(k, 2).start()

    def z_pass(self, k):
        z = self.here.z

        @pl.when((z == 1) | (z == 2))
        def _():
            self.zgot(k, self.zwait()).wait_recv()
            self.zcopy(k, 2).start()

    def z_wait(self, k):
        z = self.here.z
        self.zgot(k, 1).wait_recv()
        self.zgot(k, 2 - self.zwait()).wait_recv()

        @pl.when((z == 0) | (z == 3))
        def _():
            self.zgot(k, self.zwait()).wait_recv()

    def z_finish(self, k):
        h = self.here
        self.z_wait(k)
        if k < 6:
            slabs = self.zland[k].astype(F32)
            for half in (0, 1):
                rows = jnp.concatenate(
                    [slabs[z, 24 * half : 24 * half + 24] for z in range(4)], axis=0
                ).astype(BF).reshape(2, 48, 768)
                u = 2 * k + half
                if u < 8:
                    self.sq[u, h.y, h.x, h.c] = rows
                else:
                    self.up[u - 8, h.y, h.x, h.c] = rows
        for u in (2 * k, 2 * k + 1):
            self.first(u).start()
            self.second(u).start()

    def nbrs(self, u):
        h = self.here
        return (h.yn, h.xn) if u % 2 == 0 else (h.xn, h.yn)

    def group(self, u):
        return 0 if u < 4 else 2 if u > 9 else 1

    def own(self, u):
        h = self.here
        return self.blk(u, h.y, h.x, h.c)

    def got(self, u):
        h = self.here
        return self.blk(u, 1 - h.y, h.x, h.c) if u % 2 == 0 else self.blk(u, h.y, 1 - h.x, h.c)

    def first(self, u):
        return rcopy(self.own(u), self.own(u), self.sems, 4 * u, self.nbrs(u)[0], self.group(u))

    def second(self, u):
        return rcopy(self.own(u), self.own(u), self.sems, 4 * u + 1, self.nbrs(u)[1], self.group(u))

    def third(self, u):
        return rcopy(self.got(u), self.got(u), self.sems, 4 * u + 2, self.nbrs(u)[1], self.group(u))

    def cross(self, u):
        ref = self.blk(u, EVERY, EVERY, self.here.c)
        return rcopy(ref, ref, self.sems, 4 * u + 3, self.here.core, 3)

    def mid(self, k):
        for u in (2 * k, 2 * k + 1):
            self.first(u).wait_recv()
            self.third(u).start()

    def core(self, k):
        for u in (2 * k, 2 * k + 1):
            self.second(u).wait_recv()
            self.third(u).wait_recv()
            self.cross(u).start()

    def done(self, k):
        for u in (2 * k, 2 * k + 1):
            self.cross(u).wait_recv()

    def bblk(self, w, y, x):
        h = self.here
        cols = slice(384 * (w % 2), 384 * (w % 2) + 384)
        if w < 2:
            return self.down.at[y, x, h.c, h.z, 1, :, cols]
        return self.early.at[y, x, lax.div(h.z, 2), lax.rem(h.z, 2), :, cols]

    def bfirst(self, w):
        h = self.here
        ref = self.bblk(w, h.y, h.x)
        return rcopy(ref, ref, self.bsems, 3 * w + 0, self.nbrs(w)[0], w // 2)

    def bsecond(self, w):
        h = self.here
        ref = self.bblk(w, h.y, h.x)
        return rcopy(ref, ref, self.bsems, 3 * w + 1, self.nbrs(w)[1], w // 2)

    def bthird(self, w):
        h = self.here
        ref = self.bblk(w, 1 - h.y, h.x) if w % 2 == 0 else self.bblk(w, h.y, 1 - h.x)
        return rcopy(ref, ref, self.bsems, 3 * w + 2, self.nbrs(w)[1], w // 2)

    def b_start(self, *ws):
        for w in ws:
            self.bfirst(w).start()
            self.bsecond(w).start()

    def b_mid(self, *ws):
        for w in ws:
            self.bfirst(w).wait_recv()
            self.bthird(w).start()

    def b_got(self, *ws):
        for w in ws:
            self.bsecond(w).wait_recv()
            self.bthird(w).wait_recv()

    def early_finish(self):
        h = self.here
        for p in range(4):
            self.z_wait(11 + p)
        for p in range(4):
            slabs = self.early[p // 2, p % 2].astype(F32)
            for half in (0, 1):
                rows = [
                    slabs[z // 2, z % 2, 24 * half : 24 * half + 24] for z in range(4)
                ]
                self.sq[6 + half, p // 2, p % 2, h.c] = (
                    jnp.concatenate(rows, axis=0).astype(BF).reshape(2, 48, 768)
                )
        sent(h, self.zsems, 2, self.like[12])
        sent(h, self.bsems, 1, self.like[3])
        for u in (6, 7):
            self.cross(u).start()

    def bcross(self, y):
        ref = self.down.at[y, :, self.here.c, :, 1]
        return rcopy(ref, ref, self.bcsems, y, self.here.core, 0)

    def b_core(self, y):
        for p in (2 * y, 2 * y + 1):
            self.z_wait(7 + p)
        self.bcross(y).start()

    def b_done(self):
        for y in (0, 1):
            self.bcross(y).wait_recv()

    def drain(self):
        like = self.like
        sent(self.here, self.zsems, 0, like[21])
        sent(self.here, self.zsems, 1, like[9])
        for group in (0, 1, 2):
            sent(self.here, self.sems, group, like[24])
        sent(self.here, self.sems, 3, like[112])
        sent(self.here, self.bsems, 0, like[3])
        sent(self.here, self.bcsems, 0, like[16])


class Scatter:
    def __init__(
        self, here, up, down, gup, gdown, rc, r1, r2, zsend, zland, brest, bzland, br1, br2,
        sems, zsems, bzsems, bsems, tsems,
    ):
        self.here, self.up, self.down, self.gup, self.gdown = here, up, down, gup, gdown
        self.rc, self.r1, self.r2 = rc, r1, r2
        self.zsend, self.zland, self.sems, self.zsems = zsend, zland, sems, zsems
        self.brest, self.bzland, self.br1, self.br2 = brest, bzland, br1, br2
        self.bzsems, self.bsems, self.tsems = bzsems, bsems, tsems

    def blk(self, u, y, x, c):
        if u < 4:
            return self.down.at[y, x, c, u]
        if u < 8:
            return self.up.at[u - 4, y, x, c]
        if u < 12:
            return self.gup.at[u - 8, y, x, c]
        return self.gdown.at[y, x, c, 2 * (u - 12) : 2 * (u - 12) + 2, 0:32]

    def core_blk(self, u, c):
        if u < 12:
            return self.blk(u, EVERY, EVERY, c)
        pair, low = (u - 12) % 2, 48 * ((u - 12) // 2)
        return self.gdown.at[:, :, c, 2 * pair : 2 * pair + 2, low : low + 48]

    def rows(self, u):
        return slice(0, 48 if u < 12 else 32)

    def put(self, u, y, cols, value):
        value = value.astype(BF).reshape(2, 2, 2, 48, 256)
        if u < 4:
            self.down[y, :, :, u, :, :, cols] = value
        else:
            self.up[u - 4, y, :, :, :, :, cols] = value

    def cross(self, u):
        h = self.here
        return rcopy(
            self.core_blk(u, 1 - h.c), self.rc.at[u % 8], self.sems, 3 * u, h.core, 0
        )

    def first(self, u):
        h = self.here
        if u % 2 == 0:
            src, device = self.blk(u, EVERY, 1 - h.x, h.c), h.xn
        else:
            src, device = self.blk(u, 1 - h.y, EVERY, h.c), h.yn
        dst = self.r1.at[u, :, :, self.rows(u)]
        return rcopy(src, dst, self.sems, 3 * u + 1, device, 1 if u < 12 else 3)

    def second(self, u):
        h = self.here
        if u % 2 == 0:
            src, device = self.r1.at[u, 1 - h.y, :, self.rows(u)], h.yn
        else:
            src, device = self.r1.at[u, 1 - h.x, :, self.rows(u)], h.xn
        dst = self.r2.at[u, :, self.rows(u)]
        return rcopy(src, dst, self.sems, 3 * u + 2, device, 2 if u < 12 else 4)

    def start(self, k):
        for u in (2 * k, 2 * k + 1):
            self.cross(u).start()

    def add_core(self, u):
        self.cross(u).wait_recv()
        mine = self.core_blk(u, self.here.c)
        mine[...] = (mine[...].astype(F32) + self.rc[u % 8].astype(F32)).astype(BF)

    def one(self, k):
        for u in (2 * k, 2 * k + 1):
            self.add_core(u)
            self.first(u).start()

    def two(self, k):
        h = self.here
        for u in (2 * k, 2 * k + 1):
            self.first(u).wait_recv()
            if u % 2 == 0:
                mine = self.blk(u, EVERY, h.x, h.c)
            else:
                mine = self.blk(u, h.y, EVERY, h.c)
            rows = self.rows(u)
            total = mine[...].astype(F32) + self.r1[u, :, :, rows].astype(F32)
            self.r1[u, :, :, rows] = total.astype(BF)
            self.second(u).start()

    def three(self, k):
        h = self.here
        sums = []
        for u in (2 * k, 2 * k + 1):
            self.second(u).wait_recv()
            at = h.y if u % 2 == 0 else h.x
            rows = self.rows(u)
            sums.append(self.r1[u, at, :, rows].astype(F32) + self.r2[u, :, rows].astype(F32))
        if k < 6:
            sums = [item.reshape(96, 768) for item in sums]
            for z in range(4):
                self.zsend[k, z] = jnp.concatenate(
                    [item[24 * z : 24 * z + 24] for item in sums], axis=0
                ).astype(BF)
        else:
            for half in (0, 1):
                self.zsend[k, 2 * half : 2 * half + 2, 0:32] = sums[half].astype(BF)
        for s in (1, 2, 3):
            self.zcopy(k, s).start()

    def zcopy(self, k, s):
        h = self.here
        return rcopy(
            self.zsend.at[k, lax.rem(h.z + s, 4), self.rows(2 * k)],
            self.zland.at[k, s - 1, self.rows(2 * k)], self.zsems,
            3 * k + s - 1, h.zn(s), 0 if k < 6 else 1,
        )

    def last(self, k):
        h = self.here
        for s in (1, 2, 3):
            self.zcopy(k, s).wait_recv()
        rows = self.rows(2 * k)
        total = self.zsend[k, h.z, rows].astype(F32)
        for s in (1, 2, 3):
            total = total + self.zland[k, s - 1, rows].astype(F32)
        return total

    def tail_first(self, u, w):
        h = self.here
        cols = slice(384 * w, 384 * w + 384)
        if u % 2 == 0:
            src, device = self.blk(u, EVERY, 1 - h.x, h.c), h.xn
        else:
            src, device = self.blk(u, 1 - h.y, EVERY, h.c), h.yn
        return rcopy(
            src.at[:, :, :, cols], self.r1.at[u, :, :, :, cols], self.tsems, 2 * u + w, device, 0
        )

    def tail_second(self, u, w):
        h = self.here
        cols = slice(384 * w, 384 * w + 384)
        at, device = (1 - h.y, h.yn) if u % 2 == 0 else (1 - h.x, h.xn)
        return rcopy(
            self.r1.at[u, at, :, :, cols], self.r2.at[u, :, :, cols], self.tsems, 4 + 2 * u + w,
            device, 1,
        )

    def tail_zcopy(self, w, s):
        h = self.here
        cols = slice(384 * w, 384 * w + 384)
        return rcopy(
            self.zsend.at[0, lax.rem(h.z + s, 4), :, cols], self.zland.at[0, s - 1, :, cols],
            self.tsems, 8 + 3 * w + s - 1, h.zn(s), 2,
        )

    def tail_one(self):
        for u in (0, 1):
            self.add_core(u)
            self.tail_first(u, 0).start()

    def tail_rest(self):
        for u in (0, 1):
            self.tail_first(u, 1).start()

    def tail_two(self, w):
        h = self.here
        cols = slice(384 * w, 384 * w + 384)
        for u in (0, 1):
            self.tail_first(u, w).wait_recv()
            if u % 2 == 0:
                mine = self.blk(u, EVERY, h.x, h.c)
            else:
                mine = self.blk(u, h.y, EVERY, h.c)
            mine = mine[:, :, :, cols].astype(F32)
            self.r1[u, :, :, :, cols] = (
                mine + self.r1[u, :, :, :, cols].astype(F32)
            ).astype(BF)
            self.tail_second(u, w).start()

    def tail_three(self, w):
        h = self.here
        cols = slice(384 * w, 384 * w + 384)
        sums = []
        for u in (0, 1):
            self.tail_second(u, w).wait_recv()
            at = h.y if u % 2 == 0 else h.x
            total = self.r1[u, at, :, :, cols].astype(F32) + self.r2[u, :, :, cols].astype(F32)
            sums.append(total.reshape(96, 384))
        for z in range(4):
            self.zsend[0, z, :, cols] = jnp.concatenate(
                [item[24 * z : 24 * z + 24] for item in sums], axis=0
            ).astype(BF)
        for s in (1, 2, 3):
            self.tail_zcopy(w, s).start()

    def tail_last(self, w):
        h = self.here
        cols = slice(384 * w, 384 * w + 384)
        for s in (1, 2, 3):
            self.tail_zcopy(w, s).wait_recv()
        total = self.zsend[0, h.z, :, cols].astype(F32)
        for s in (1, 2, 3):
            total = total + self.zland[0, s - 1, :, cols].astype(F32)
        return total

    def bz(self, s):
        h = self.here
        src = self.gdown.at[:, :, h.c, lax.rem(h.z + s, 4), 32:96]
        return rcopy(src, self.bzland.at[s - 1], self.bzsems, s - 1, h.zn(s), 0)

    def b_one(self):
        for u in (14, 15):
            self.add_core(u)
        for s in (1, 2, 3):
            self.bz(s).start()

    def bfirst(self, w):
        h = self.here
        if w == 0:
            src, device = self.brest.at[:, 1 - h.x, :, 0:384], h.xn
        else:
            src, device = self.brest.at[1 - h.y, :, :, 384:768], h.yn
        return rcopy(src, self.br1.at[w], self.bsems, 2 * w, device, 0)

    def bsecond(self, w):
        h = self.here
        if w == 0:
            src, device = self.br1.at[w, 1 - h.y], h.yn
        else:
            src, device = self.br1.at[w, 1 - h.x], h.xn
        return rcopy(src, self.br2.at[w], self.bsems, 2 * w + 1, device, 1)

    def b_two(self):
        h = self.here
        for s in (1, 2, 3):
            self.bz(s).wait_recv()
        total = self.gdown[:, :, h.c, h.z, 32:96].astype(F32)
        for s in (1, 2, 3):
            total = total + self.bzland[s - 1].astype(F32)
        self.brest[...] = total.astype(BF)
        for w in (0, 1):
            self.bfirst(w).start()

    def b_three(self):
        h = self.here
        for w in (0, 1):
            self.bfirst(w).wait_recv()
            if w == 0:
                mine = self.brest[:, h.x, :, 0:384]
            else:
                mine = self.brest[h.y, :, :, 384:768]
            self.br1[w] = (mine.astype(F32) + self.br1[w].astype(F32)).astype(BF)
            self.bsecond(w).start()

    def b_last(self, w):
        h = self.here
        self.bsecond(w).wait_recv()
        at = h.y if w == 0 else h.x
        return self.br1[w, at].astype(F32) + self.br2[w].astype(F32)

    def drain(self, slabs128):
        sent(self.here, self.sems, 0, slabs128)
        sent(self.here, self.sems, 1, self.r1.at[0:10])
        sent(self.here, self.sems, 2, self.r2.at[0:10])
        sent(self.here, self.sems, 3, self.r1.at[0:2, :, :, 0:32])
        sent(self.here, self.sems, 4, self.r2.at[0:2, :, 0:32])
        sent(self.here, self.zsems, 0, self.zland.at[0:5])
        sent(self.here, self.zsems, 1, self.zland.at[0, :, 0:32])
        sent(self.here, self.bzsems, 0, self.bzland)
        sent(self.here, self.bsems, 0, self.brest.at[0])
        sent(self.here, self.bsems, 1, self.brest.at[0, 0])
        sent(self.here, self.tsems, 0, self.r1.at[0:2])
        sent(self.here, self.tsems, 1, self.r2.at[0:2])
        sent(self.here, self.tsems, 2, self.zland.at[0])


def mm(a, b):
    return lax.dot_general(a, b, (((1,), (0,)), ((), ())), preferred_element_type=F32)


def mt(a, b):
    return lax.dot_general(a, b, (((1,), (1,)), ((), ())), preferred_element_type=F32)


def tm(a, b):
    return lax.dot_general(a, b, (((0,), (0,)), ((), ())), preferred_element_type=F32)


def iota(shape, axis):
    return lax.broadcasted_iota(jnp.int32, shape, axis)


def lanes(hp):
    return pl.ds(pl.multiple_of(hp * 128, 128), 128)


def both(q):
    low = iota(q.shape, 1) < 64
    zero = jnp.zeros_like(q)
    return jnp.concatenate([jnp.where(low, q, zero), jnp.where(low, zero, q)], axis=0)


def merge(pair):
    rows = pair.shape[0] // 2
    low = iota((rows, 128), 1) < 64
    return jnp.where(low, pair[:rows], pair[rows:]).astype(BF)


def probs(key, query, bias, mask):
    scores = mt(key, query)
    if bias is not None:
        scores = scores + bias.astype(F32)
    scores = jnp.where(mask, scores, -1e30)
    expo = jnp.exp(scores - jnp.max(scores, axis=0, keepdims=True))
    return expo * (1.0 / jnp.sum(expo, axis=0, keepdims=True))


def rms(v):
    return lax.rsqrt(jnp.mean(v * v, axis=-1, keepdims=True) + eps)


def norm_back(v, gain, grad):
    r = rms(v)
    scaled = grad * gain
    inner = jnp.mean(scaled * v, axis=-1, keepdims=True)
    return r * scaled - v * (r * r * r * inner), jnp.sum(grad * v * r, axis=0, keepdims=True)


def gelu(v):
    c = 0.7978845608028654
    return v * (0.5 + 0.5 * jnp.tanh(v * (c + c * 0.044715 * (v * v))))


def gelu_slope(v):
    c = 0.7978845608028654
    square = v * v
    t = jnp.tanh(v * (c + c * 0.044715 * square))
    return (0.5 + 0.5 * t) + v * (1.0 - t * t) * (0.5 * c + 1.5 * c * 0.044715 * square)


def layer_kernel(*refs):
    given, (tlen, slen, count) = refs[:15], refs[15:18]
    g_enc, results = refs[18], refs[19:33]
    (
        sq, up, down, gup, gdown, rc, r1, r2, zland, zland2, brest, bzland, br1, br2, small, small2,
        bias, h2, h3, q1, k1, v1, o1, q2, o2, k2, v2, g, gp, x1, x2, stage,
        zs, zr, ss, sr, bs, br, bcs, bcr, ms, mr,
        rzs, rzr, rss, rsr, rbzs, rbzr, rbs, rbr, rts, rtr, m2s, m2r, out_sem, done_sem, in_sem, credit,
        *held,
    ) = refs[33:]
    held, kept = [h2, x1, *held[:10], *refs[31:33]], held[10:]
    layer_out, g_dec, *g_sq, g_up, g_down, g_gain, g_table = held
    *squares, up_in, down_in, gain_in, table_in = given[:12]
    x_in, cot, enc = kept

    def hand(i):
        return pltpu.make_async_copy(held[i], results[i], done_sem.at[i])

    def fetch(i):
        return pltpu.make_async_copy(given[12 + i], kept[i], in_sem.at[i])

    here = Place()
    here.greet()
    for i in range(3):
        fetch(i).start()
    index = (here.y * 4 + here.x * 2 + here.c) * 4 + here.z
    for k in range(4):
        slab = jnp.concatenate(
            [squares[2 * k][...].astype(F32), squares[2 * k + 1][...].astype(F32)], axis=0
        ).astype(BF)
        if k < 3:
            zland[k, here.z] = slab
        else:
            rc[here.y, here.x, lax.div(here.z, 2), lax.rem(here.z, 2)] = slab
    for k in range(2):
        zland[4 + k, here.z] = jnp.concatenate(
            [up_in[:, 768 * n : 768 * n + 768].astype(F32) for n in (2 * k, 2 * k + 1)], axis=0
        ).astype(BF)
    down[here.y, here.x, here.c, here.z] = down_in[...].reshape(2, 48, 768)
    spot = (iota((24, 768), 1) == iota((24, 768), 0) + 24 * index).astype(BF)
    small[0] = jnp.zeros((8, 768), F32)
    small[0, 0:3] = mm(gain_in[...], spot)
    here.enter()
    like = {
        3: zland2.at[0], 9: zland2.at[0:3], 12: zland2.at[0:4], 16: rc.at[0:2], 21: zland2,
        24: r2.at[0:12], 112: sq.at[0:7],
    }
    ga = Gather(
        here, sq, up, down, zland, rc, (zs, zr), (ss, sr), (bs, br), (bcs, bcr), like
    )
    m = Small(here, small, (ms, mr))
    rs = Scatter(
        here, up, down, gup, gdown, rc, r1, r2, zland, zland2, brest, bzland, br1, br2,
        (rss, rsr), (rzs, rzr), (rbzs, rbzr), (rbs, rbr), (rts, rtr),
    )
    m2 = Small(here, small2, (m2s, m2r))

    def weight(u):
        return sq[u].reshape(768, 768)

    def columns(u, n):
        return sq[u, :, :, :, :, :, 256 * n : 256 * n + 256].reshape(768, 256)

    def z_starts(*items):
        for item in items:
            ga.z_start(item)

    def z_passes(*items):
        for item in items:
            ga.z_pass(item)

    m.start(0)
    ga.z_start(0)
    ga.b_start(2, 3, 0, 1)
    m.finish(0)
    m.start(1)
    ga.z_pass(0)
    z_starts(1)
    ga.b_mid(2, 3, 0, 1)

    def bucket_hot(rows_are_buckets):
        shape = (32, 128) if rows_are_buckets else (128, 32)
        distance = iota(shape, 1 if rows_are_buckets else 0)
        level = jnp.minimum(distance, 16)
        for edge in thresholds:
            level = level + (distance >= edge).astype(jnp.int32)
        return level == iota(shape, 0 if rows_are_buckets else 1)

    by_distance = mm(table_in[...], bucket_hot(True).astype(BF))
    for head in range(12):
        row = jnp.broadcast_to(by_distance[head : head + 1, :], (128, 128))
        bias[head // 2, :, 128 * (head % 2) : 128 * (head % 2) + 128] = pltpu.roll(
            row, 0, 1, stride=1, stride_axis=0
        ).astype(BF)

    key_place, target_place = iota((128, 256), 0), iota((128, 256), 1) & 127
    causal = key_place <= target_place
    source_place = iota((512, 256), 0)

    def self_mask(ex):
        return causal & (key_place < tlen[ex])

    def cross_mask(ex):
        return source_place < slen[ex]

    row_place = iota((256, 1), 0)
    live = (
        ((row_place < 128) & (row_place < tlen[0]) & (0 < count[0]))
        | ((row_place >= 128) & (row_place - 128 < tlen[1]) & (1 < count[0]))
    ).astype(F32)

    ga.z_finish(0)
    ga.b_got(2, 3)
    m.finish(1)
    m.start(2)
    z_starts(2, 11)
    ga.z_pass(1)
    ga.mid(0)
    ga.z_finish(1)
    z_starts(12, 4)
    z_passes(2, 11)
    ga.core(0)
    ga.z_finish(2)
    z_starts(5, 13)
    ga.mid(1)
    m.finish(2)
    gains = m.total()
    gain = [gains[i : i + 1, :] for i in range(3)]

    fetch(0).wait()

    def normed_input():
        first = x_in[...].astype(F32)
        return (first * rms(first) * gain[0]).astype(BF)

    h3[...] = normed_input()
    z_passes(12, 4)
    ga.core(1)
    ga.mid(2)
    ga.done(0)
    for n in range(3):
        cols = slice(256 * n, 256 * n + 256)
        q1[:, cols] = mm(h3[...], columns(0, n)).astype(BF)
        k1[:, cols] = mm(h3[...], columns(1, n)).astype(BF)
    ga.z_finish(4)
    z_starts(14)
    z_passes(5, 13)
    ga.core(2)
    ga.done(1)
    for n in range(3):
        cols = slice(256 * n, 256 * n + 256)
        v1[:, cols] = mm(h3[...], columns(2, n)).astype(BF)

    def self_forward(hp, carry):
        for ex in range(2):
            rows = slice(128 * ex, 128 * ex + 128)
            query = both(q1[rows, lanes(hp)])
            p = probs(k1[rows, lanes(hp)], query, bias[hp], self_mask(ex)).astype(BF)
            o1[rows, lanes(hp)] = merge(tm(p, v1[rows, lanes(hp)]))
        return carry

    lax.fori_loop(0, 6, self_forward, 0, unroll=2)
    ga.z_finish(5)
    ga.b_got(0, 1)
    z_starts(6)
    z_passes(14)
    ga.mid(4)
    x1[...] = x_in[...].astype(F32) + mm(o1[...], weight(3))
    h2[...] = (x1[...] * rms(x1[...]) * gain[1]).astype(BF)
    ga.done(2)

    def encode(r, carry):
        rows = pl.ds(pl.multiple_of(r * 256, 256), 256)
        for n in range(3):
            cols = slice(256 * n, 256 * n + 256)
            k2[rows, cols] = mm(enc[rows, :], columns(4, n)).astype(BF)
            v2[rows, cols] = mm(enc[rows, :], columns(5, n)).astype(BF)
        return carry

    fetch(2).wait()
    lax.fori_loop(0, 4, encode, 0)
    z_starts(7)
    ga.early_finish()
    ga.mid(5)
    z_passes(6)
    z_starts(8)
    ga.done(3)
    for n in range(3):
        cols = slice(256 * n, 256 * n + 256)
        q2[:, cols] = mm(h2[...], columns(6, n)).astype(BF)

    beyond = [jnp.where(iota((1, 512), 1) < slen[ex], 0.0, -1e30) for ex in range(2)]

    def cross_forward(hp, carry):
        for ex in range(2):
            rows = slice(128 * ex, 128 * ex + 128)
            keys = slice(512 * ex, 512 * ex + 512)
            query = both(q2[rows, lanes(hp)])
            scores = mt(query, k2[keys, lanes(hp)]) + beyond[ex]
            expo = jnp.exp(scores - jnp.max(scores, axis=1, keepdims=True))
            scale = 1.0 / jnp.sum(expo, axis=1, keepdims=True)
            o2[rows, lanes(hp)] = merge(mm(expo.astype(BF), v2[keys, lanes(hp)]) * scale)
        return carry

    def cross_step(i, carry):
        cross_forward(2 * i, carry)
        cross_forward(2 * i + 1, carry)

        @pl.when(i == 0)
        def _():
            ga.z_finish(6)
            ga.z_start(9)
            ga.z_pass(7)

        @pl.when(i == 1)
        def _():
            ga.core(4)
            ga.z_pass(8)
            ga.z_start(10)

        return carry

    lax.fori_loop(0, 3, cross_step, 0)
    ga.core(5)
    ga.mid(6)
    x2[...] = x1[...] + mm(o2[...], weight(7))
    h3[...] = (x2[...] * rms(x2[...]) * gain[2]).astype(BF)
    ga.done(4)

    def hidden(n, carry):
        for part in range(3):
            lo = 256 * part
            a = mm(h3[...], up[n, :, :, :, :, :, lo : lo + 256].reshape(768, 256))
            cols = pl.ds(pl.multiple_of(768 * n + lo, 256), 256)
            g[:, cols] = gelu(a).astype(BF)
            gp[:, cols] = a.astype(BF)
        return carry

    def keep_gain(i, term):
        for j in range(6):
            small2[0, 6 * i + j : 6 * i + j + 1, :] = term[:, 128 * j : 128 * j + 128]

    fetch(1).wait()

    def df(cols=slice(None)):
        return (cot[:, cols].astype(F32) * live).astype(BF)

    def wide(e):
        return pl.ds(pl.multiple_of(768 * e, 256), 768)

    def grad_down(e, carry):
        turned = g[:, wide(e)].T
        for n in range(3):
            cols = slice(256 * n, 256 * n + 256)
            grad = mm(turned, df(cols)).astype(BF)
            gdown[lax.div(e, 2), lax.rem(e, 2), :, :, :, cols] = grad.reshape(2, 4, 96, 256)
        return carry

    def hidden_step(i, carry):
        for e in (2 * i, 2 * i + 1):
            hidden(e, carry)
        for e in (2 * i, 2 * i + 1):
            grad_down(e, carry)

        @pl.when(i == 0)
        def _():
            ga.z_pass(9)
            ga.z_pass(10)
            ga.done(5)

        return carry

    lax.fori_loop(0, 2, hidden_step, 0)
    rs.start(6)
    rs.start(7)
    ga.b_core(0)
    ga.core(6)
    rs.one(6)
    ga.b_core(1)
    rs.b_one()

    def slopes(n, carry):
        for part in range(3):
            cols = pl.ds(pl.multiple_of(768 * n + 256 * part, 256), 256)
            gp[:, cols] = gelu_slope(gp[:, cols].astype(F32)).astype(BF)
        return carry

    lax.fori_loop(0, 4, slopes, 0)
    ga.done(6)
    ga.b_done()

    def down_block(e):
        return down[lax.div(e, 2), lax.rem(e, 2)].reshape(768, 768)

    def inner_grad(e, carry):
        dg = mt(df(), down_block(e))
        gp[:, wide(e)] = (dg * gp[:, wide(e)].astype(F32)).astype(BF)
        return carry

    def grad_up(n, carry):
        turned = h3[...].T
        for part in range(3):
            cols = slice(256 * part, 256 * part + 256)
            source = pl.ds(pl.multiple_of(768 * n + 256 * part, 256), 256)
            grad = mm(turned, gp[:, source]).astype(BF)
            gup[n, :, :, :, :, :, cols] = grad.reshape(2, 2, 2, 2, 48, 256)
        return carry

    def inner_step(i, carry):
        for e in (2 * i, 2 * i + 1):
            inner_grad(e, carry)
        for e in (2 * i, 2 * i + 1):
            grad_up(e, carry)

        @pl.when(i == 0)
        def _():
            rs.start(4)

        return carry

    lax.fori_loop(0, 2, inner_step, 0)
    rs.start(5)
    rs.one(4)
    rs.two(6)
    stage[0] = jnp.zeros((256, 768), F32)
    stage[1] = x2[...]

    def inner_back(n, carry):
        stage[0] += mt(gp[:, wide(n)], up[n].reshape(768, 768))
        return carry

    lax.fori_loop(0, 4, inner_back, 0, unroll=2)
    rs.one(5)
    pl.semaphore_signal(credit, inc=1, device_id=here.core, device_id_type=MESH)
    d_norm, gain_three = norm_back(x2[...], gain[2], stage[0])
    keep_gain(2, gain_three)
    x2[...] = cot[...].astype(F32) * live + d_norm
    ga.drain()

    def put_grads(value, rows, pairs):
        def half_rows(y, carry):
            turned = value[:, pl.ds(pl.multiple_of(384 * y, 128), 384)].T
            for u, ref in pairs:
                for n in range(3):
                    cols = slice(256 * n, 256 * n + 256)
                    rs.put(u, y, cols, mm(turned, ref[:, cols]))
            return carry

        lax.fori_loop(0, 2, half_rows, 0)

    h3[...] = x2[...].astype(BF)
    put_grads(o2, 256, ((7, h3),))
    o2[...] = mt(h3[...], weight(7)).astype(BF)

    beyond_rows = [jnp.where(iota((512, 1), 0) < slen[ex], 0.0, -1e30) for ex in range(2)]

    def cross_backward(hp, carry):
        for ex in range(2):
            rows = slice(128 * ex, 128 * ex + 128)
            keys = slice(512 * ex, 512 * ex + 512)
            query, d_out = both(q2[rows, lanes(hp)]), both(o2[rows, lanes(hp)])
            key, value = k2[keys, lanes(hp)], v2[keys, lanes(hp)]
            scores = mt(key, query) + beyond_rows[ex]
            expo = jnp.exp(scores - jnp.max(scores, axis=0, keepdims=True))
            scale = 1.0 / jnp.sum(expo, axis=0, keepdims=True)
            dp = mt(value, d_out)
            delta = jnp.sum(dp * expo, axis=0, keepdims=True) * scale
            p = expo * scale
            ds = (p * (dp - delta)).astype(BF)
            turned = mm(key.T, ds).T
            q2[rows, lanes(hp)] = merge(turned)
            k2[keys, lanes(hp)] = mm(ds, query).astype(BF)
            v2[keys, lanes(hp)] = mm(p.astype(BF), d_out).astype(BF)
        return carry

    def cross_back_step(i, carry):
        cross_backward(2 * i, carry)
        cross_backward(2 * i + 1, carry)

        @pl.when(i == 1)
        def _():
            rs.two(4)

        return carry

    lax.fori_loop(0, 3, cross_back_step, 0)
    rs.three(6)
    put_grads(h2, 256, ((6, q2),))
    pl.semaphore_wait(credit, 1)
    rs.start(3)

    def result(e, carry):
        stage[1] += mm(g[:, wide(e)], down_block(e))
        return carry

    lax.fori_loop(0, 4, result, 0, unroll=2)
    layer_out[...] = (stage[1] * live).astype(BF)
    hand(0).start()
    rs.two(5)
    rs.one(3)
    put_grads(enc, 1024, ((4, k2), (5, v2)))
    rs.start(2)

    def finish(k):
        total = rs.last(k)
        if k < 4:
            g_sq[2 * k][...] = total[:24]
            g_sq[2 * k + 1][...] = total[24:]
            hand(2 + 2 * k).start()
            hand(3 + 2 * k).start()
        elif k < 6:
            g_up[:, 1536 * (k - 4) : 1536 * (k - 4) + 768] = total[:24]
            g_up[:, 1536 * (k - 4) + 768 : 1536 * (k - 4) + 1536] = total[24:]
        else:
            g_down[0:32, :] = total

    d_norm, gain_two = norm_back(x1[...], gain[1], mt(q2[...], weight(6)))
    keep_gain(1, gain_two)
    x2[...] = x2[...] + d_norm
    rs.one(2)
    rs.three(4)

    h3[...] = x2[...].astype(BF)
    put_grads(o1, 256, ((3, h3),))
    o1[...] = mt(h3[...], weight(3)).astype(BF)
    rs.three(5)
    turn = (iota((128, 256), 0) + (iota((128, 256), 1) & 127) == 127).astype(BF)

    def self_backward(hp, carry):
        scores = []
        for ex in range(2):
            rows = slice(128 * ex, 128 * ex + 128)
            query, d_out = both(q1[rows, lanes(hp)]), both(o1[rows, lanes(hp)])
            key, value = k1[rows, lanes(hp)], v1[rows, lanes(hp)]
            p = probs(key, query, bias[hp], self_mask(ex))
            dp = mt(value, d_out)
            delta = jnp.sum(dp * p, axis=0, keepdims=True)
            ds = (p * (dp - delta)).astype(BF)
            q1[rows, lanes(hp)] = merge(tm(ds, key))
            k1[rows, lanes(hp)] = mm(ds, query).astype(BF)
            v1[rows, lanes(hp)] = mm(p.astype(BF), d_out).astype(BF)
            scores.append(ds)
        pair = mm(turn, jnp.concatenate(scores, axis=0))
        for head in range(2):
            skew = pltpu.roll(pair[:, 128 * head : 128 * head + 128], 0, 1, stride=1, stride_axis=0)
            small2[0, pl.ds(18 + 2 * hp + head, 1), :] = jnp.sum(skew, axis=0, keepdims=True)
        return carry

    lax.fori_loop(0, 6, self_backward, 0, unroll=2)
    h3[...] = normed_input()
    put_grads(h3, 256, ((2, v1), (0, q1), (1, k1)))
    rs.start(1)
    rs.two(3)
    rs.start(0)
    stage[0] = jnp.zeros((256, 768), F32)

    def first_back(y, carry):
        cols = pl.ds(pl.multiple_of(384 * y, 128), 384)
        for u, ref in ((0, q1), (1, k1), (2, v1)):
            stage[0, :, cols] += mt(ref[...], sq[u, y].reshape(384, 768))
        return carry

    lax.fori_loop(0, 2, first_back, 0, unroll=2)
    d_norm, gain_one = norm_back(x_in[...].astype(F32), gain[0], stage[0])
    g_dec[...] = x2[...] + d_norm
    hand(1).start()
    keep_gain(0, gain_one)
    small2[0, 30:32, :] = jnp.zeros((2, 128), F32)
    m2.start(0)
    rs.one(1)
    m2.finish(0)
    m2.start(1)
    rs.two(2)
    rs.three(3)
    rs.b_two()

    def out_copy(r):
        return pltpu.make_async_copy(
            stage.at[lax.rem(r, 2)],
            g_enc.at[pl.ds(pl.multiple_of(256 * r, 256), 256)],
            out_sem.at[r],
        )

    def encoder_grad(r, carry):
        @pl.when(r >= 2)
        def _():
            out_copy(r - 2).wait()

        rows = pl.ds(pl.multiple_of(256 * r, 256), 256)
        slot = lax.rem(r, 2)
        for y in range(2):
            cols = slice(384 * y, 384 * y + 384)
            stage[slot, :, cols] = mt(k2[rows, :], sq[4, y].reshape(384, 768))
            stage[slot, :, cols] += mt(v2[rows, :], sq[5, y].reshape(384, 768))
        out_copy(r).start()
        return carry

    lax.fori_loop(0, 4, encoder_grad, 0)
    rs.two(1)
    m2.finish(1)
    m2.start(2)
    rs.tail_one()
    rs.three(2)
    rs.tail_rest()
    finish(6)
    finish(4)
    finish(5)
    hand(10).start()
    rs.three(1)
    rs.b_three()
    rs.tail_two(0)
    finish(3)
    rs.tail_two(1)
    rs.tail_three(0)
    rs.tail_three(1)
    for w in (0, 1):
        g_down[32:96, 384 * w : 384 * w + 384] = rs.b_last(w)
    hand(11).start()
    m2.finish(2)
    reduced = m2.total()
    sums = jnp.concatenate(
        [
            jnp.concatenate([reduced[6 * i + j : 6 * i + j + 1, :] for j in range(6)], axis=1)
            for i in range(3)
        ],
        axis=0,
    )
    pick = (iota((768, 24), 0) == iota((768, 24), 1) + 24 * index).astype(F32)
    g_gain[...] = lax.dot_general(
        sums, pick, (((1,), (0,)), ((), ())), preferred_element_type=F32,
        precision=lax.Precision.HIGHEST,
    )
    distance = (iota((32, 128), 1) + 1) & 127
    level = jnp.minimum(distance, 16)
    for edge in thresholds:
        level = level + (distance >= edge).astype(jnp.int32)
    hot = (level == iota((32, 128), 0)).astype(F32)
    g_table[...] = lax.dot_general(
        reduced[18:30, :], hot, (((1,), (1,)), ((), ())), preferred_element_type=F32,
        precision=lax.Precision.HIGHEST,
    )
    finish(2)
    finish(1)
    for w in (0, 1):
        total = rs.tail_last(w)
        g_sq[0][:, 384 * w : 384 * w + 384] = total[:24]
        g_sq[1][:, 384 * w : 384 * w + 384] = total[24:]
    hand(2).start()
    hand(3).start()
    rs.drain(sq)
    out_copy(2).wait()
    out_copy(3).wait()
    for i in range(12):
        hand(i).wait()


VM = pl.BlockSpec(memory_space=pltpu.VMEM)
SM = pl.BlockSpec(memory_space=pltpu.SMEM)
ANY = pl.BlockSpec(memory_space=pl.ANY)


def layer_call(*args):
    shape = jax.ShapeDtypeStruct
    dims = (3, 45, 4, 56, 2, 12, 1, 2, 7, 7, 2, 21, 5, 48, 1, 3, 2, 4, 3, 14, 7, 7)
    half = lambda *dims: pltpu.VMEM(dims, BF)
    results = (
        ((256, 768), BF),
        ((256, 768), F32),
        *[((24, 768), F32)] * 8,
        ((24, 3072), F32),
        ((96, 768), F32),
        ((3, 24), F32),
        ((12, 32), F32),
    )
    return pl.pallas_call(
        layer_kernel,
        out_shape=(
            shape((1024, 768), F32),
            *[shape(*each) for each in results],
        ),
        in_specs=[VM] * 12 + [ANY] * 3 + [SM] * 3,
        out_specs=(ANY,) * 13 + (VM,) * 2,
        scratch_shapes=[
            half(8, 2, 2, 2, 2, 48, 768),
            half(4, 2, 2, 2, 2, 48, 768),
            half(2, 2, 2, 4, 2, 48, 768),
            half(4, 2, 2, 2, 2, 48, 768),
            half(2, 2, 2, 4, 96, 768),
            half(8, 2, 2, 2, 48, 768),
            half(14, 2, 2, 48, 768),
            half(14, 2, 48, 768),
            half(7, 4, 48, 768),
            half(7, 3, 48, 768),
            half(2, 2, 64, 768),
            half(3, 2, 2, 64, 768),
            half(2, 2, 64, 384),
            half(2, 64, 384),
            pltpu.VMEM((10, 8, 768), F32),
            pltpu.VMEM((10, 32, 128), F32),
            half(6, 128, 256),
            *[half(256, 768)] * 2,
            *[half(256, 768)] * 4,
            *[half(256, 768)] * 2,
            *[half(1024, 768)] * 2,
            *[half(256, 3072)] * 2,
            *[pltpu.VMEM((256, 768), F32)] * 2,
            pltpu.VMEM((2, 256, 768), F32),
            *[pltpu.SemaphoreType.DMA((each,)) for each in dims],
            pltpu.SemaphoreType.DMA((4,)),
            pltpu.SemaphoreType.DMA((12,)),
            pltpu.SemaphoreType.DMA((3,)),
            pltpu.SemaphoreType.REGULAR,
            *[pltpu.VMEM(*each) for each in results[2:12]],
            *[pltpu.VMEM(each.shape, each.dtype) for each in args[12:15]],
        ],
        compiler_params=pltpu.CompilerParams(
            collective_id=0, has_side_effects=True, vmem_limit_bytes=64 * 2**20 - 2**16
        ),
        name="layer",
    )(*args)


def hand_out_kernel(*refs):
    count = (len(refs) - 2) // 3
    source, target, held = refs[:count], refs[count : 2 * count], refs[2 * count : 3 * count]
    got, put = refs[3 * count :]
    pieces = []
    for i in range(count):
        rows = source[i].shape[0]
        parts = 4 if rows % 256 == 0 else 1
        for part in range(parts):
            at = pl.ds(part * (rows // parts), rows // parts)
            pieces.append((source[i].at[at], held[i].at[at], target[i].at[at]))
    ins = [pltpu.make_async_copy(p[0], p[1], got.at[i]) for i, p in enumerate(pieces)]
    outs = [pltpu.make_async_copy(p[1], p[2], put.at[i]) for i, p in enumerate(pieces)]
    for copy in ins:
        copy.start()
    for copy, out in zip(ins, outs):
        copy.wait()
        out.start()
    for copy in outs:
        copy.wait()


def hand_out(arrays):
    return pl.pallas_call(
        hand_out_kernel,
        out_shape=tuple(jax.ShapeDtypeStruct(item.shape, item.dtype) for item in arrays),
        in_specs=[ANY] * len(arrays),
        out_specs=(ANY,) * len(arrays),
        scratch_shapes=[pltpu.VMEM(item.shape, item.dtype) for item in arrays]
        + [pltpu.SemaphoreType.DMA((len(arrays) + 9,))] * 2,
        name="hand_out",
    )(*arrays)


def by_kernel(
    decoder_in,
    encoder_out,
    self_query,
    self_key,
    self_value,
    self_output,
    cross_query,
    cross_key,
    cross_value,
    cross_output,
    hidden_in,
    hidden_out,
    norm_gains,
    bias_table,
    target_lengths,
    source_lengths,
    example_counts,
    cotangent,
):
    results = layer_call(
        self_query,
        self_key,
        self_value,
        self_output,
        cross_key,
        cross_value,
        cross_query,
        cross_output,
        hidden_in,
        hidden_out,
        norm_gains,
        bias_table.T,
        decoder_in.reshape(256, 768),
        cotangent.reshape(256, 768),
        encoder_out.reshape(1024, 768),
        target_lengths,
        source_lengths,
        example_counts,
    )
    g_enc, out, g_dec, *g_sq, g_up, g_down, g_gain, g_table = hand_out(results)
    return (
        out.reshape(decoder_in.shape),
        g_dec.reshape(decoder_in.shape),
        g_enc.reshape(encoder_out.shape),
        *g_sq[:4],
        g_sq[6],
        g_sq[4],
        g_sq[5],
        g_sq[7],
        g_up,
        g_down,
        g_gain,
        g_table.T,
    )


def plain(
    decoder_in,
    encoder_out,
    self_query,
    self_key,
    self_value,
    self_output,
    cross_query,
    cross_key,
    cross_value,
    cross_output,
    hidden_in,
    hidden_out,
    norm_gains,
    bias_table,
    target_lengths,
    source_lengths,
    example_counts,
    cotangent,
):
    gathered = (
        lax.all_gather(self_query, AXES, axis=0, tiled=True),
        lax.all_gather(self_key, AXES, axis=0, tiled=True),
        lax.all_gather(self_value, AXES, axis=0, tiled=True),
        lax.all_gather(self_output, AXES, axis=0, tiled=True),
        lax.all_gather(cross_query, AXES, axis=0, tiled=True),
        lax.all_gather(cross_key, AXES, axis=0, tiled=True),
        lax.all_gather(cross_value, AXES, axis=0, tiled=True),
        lax.all_gather(cross_output, AXES, axis=0, tiled=True),
        lax.all_gather(hidden_in, AXES, axis=0, tiled=True),
        lax.all_gather(hidden_out, AXES, axis=0, tiled=True),
        lax.all_gather(norm_gains, AXES, axis=1, tiled=True),
    )
    w_query, w_key, w_value, w_out, x_query, x_key, x_value, x_out, w_up, w_down, gain_all = (
        gathered
    )
    slots = jnp.arange(decoder_in.shape[0], dtype=jnp.int32)
    length = decoder_in.shape[1]
    source = encoder_out.shape[1]
    width = decoder_in.shape[2]
    hidden_width = hidden_in.shape[1]
    place = jnp.arange(length, dtype=jnp.int32)
    source_place = jnp.arange(source, dtype=jnp.int32)
    live = (
        (slots < example_counts[0])[:, None] & (place[None, :] < target_lengths[:, None])
    ).astype(jnp.float32)[:, :, None]
    self_mask = (place[None, :] <= place[:, None])[None, None] & (
        place[None, None, None, :] < target_lengths[:, None, None, None]
    )
    cross_mask = source_place[None, None, None, :] < source_lengths[:, None, None, None]
    onehot = (
        buckets(length)[:, :, None] == jnp.arange(bias_table.shape[0], dtype=jnp.int32)
    ).astype(jnp.bfloat16)
    bias = jnp.einsum("lsn,nh->hls", onehot, bias_table, preferred_element_type=jnp.float32)
    gains = gain_all.astype(jnp.float32)
    inputs = decoder_in.astype(jnp.float32)
    first = normalize(inputs, gains[0]).astype(jnp.bfloat16)
    query = project(first, w_query).astype(jnp.bfloat16)
    key = project(first, w_key).astype(jnp.bfloat16)
    value = project(first, w_value).astype(jnp.bfloat16)
    mixed, logsum_self = attention_forward(
        split_heads(query), split_heads(key), split_heads(value), bias, self_mask
    )
    after_self = inputs + project(mixed, w_out)
    second = normalize(after_self, gains[1]).astype(jnp.bfloat16)
    cross_q = project(second, x_query).astype(jnp.bfloat16)
    cross_k = project(encoder_out, x_key).astype(jnp.bfloat16)
    cross_v = project(encoder_out, x_value).astype(jnp.bfloat16)
    crossed, logsum_cross = attention_forward(
        split_heads(cross_q), split_heads(cross_k), split_heads(cross_v), 0.0, cross_mask
    )
    after_cross = after_self + project(crossed, x_out)
    third = normalize(after_cross, gains[2]).astype(jnp.bfloat16)
    inner = project(third, w_up)
    active = jax.nn.gelu(inner).astype(jnp.bfloat16)
    result = after_cross + project(active, w_down)
    layer_out = (result * live).astype(jnp.bfloat16)
    regathered = (
        lax.all_gather(self_query, AXES, axis=0, tiled=True),
        lax.all_gather(self_key, AXES, axis=0, tiled=True),
        lax.all_gather(self_value, AXES, axis=0, tiled=True),
        lax.all_gather(self_output, AXES, axis=0, tiled=True),
        lax.all_gather(cross_query, AXES, axis=0, tiled=True),
        lax.all_gather(cross_key, AXES, axis=0, tiled=True),
        lax.all_gather(cross_value, AXES, axis=0, tiled=True),
        lax.all_gather(cross_output, AXES, axis=0, tiled=True),
        lax.all_gather(hidden_in, AXES, axis=0, tiled=True),
        lax.all_gather(hidden_out, AXES, axis=0, tiled=True),
        lax.all_gather(norm_gains, AXES, axis=1, tiled=True),
    )
    w_query, w_key, w_value, w_out, x_query, x_key, x_value, x_out, w_up, w_down, gain_all = (
        regathered
    )
    gains = gain_all.astype(jnp.float32)
    d_result = cotangent.astype(jnp.float32) * live
    d_branch = d_result.astype(jnp.bfloat16)
    grad_down = outer_sum(active, d_branch)
    d_inner = gelu_grad(inner, project_back(d_branch, w_down)).astype(jnp.bfloat16)
    grad_up = outer_sum(third, d_inner)
    d_cross, gain_three = norm_grad(after_cross, gains[2], project_back(d_inner, w_up))
    d_cross = d_cross + d_result
    d_branch = d_cross.astype(jnp.bfloat16)
    grad_x_out = outer_sum(crossed, d_branch)
    d_crossed = project_back(d_branch, x_out).astype(jnp.bfloat16)
    dq_cross, dk_cross, dv_cross, unused = attention_backward(
        split_heads(cross_q),
        split_heads(cross_k),
        split_heads(cross_v),
        0.0,
        cross_mask,
        logsum_cross,
        split_heads(d_crossed),
    )
    grad_x_query = outer_sum(second, dq_cross)
    grad_x_key = outer_sum(encoder_out, dk_cross)
    grad_x_value = outer_sum(encoder_out, dv_cross)
    grad_encoder = project_back(dk_cross, x_key) + project_back(dv_cross, x_value)
    d_self, gain_two = norm_grad(after_self, gains[1], project_back(dq_cross, x_query))
    d_self = d_self + d_cross
    d_branch = d_self.astype(jnp.bfloat16)
    grad_w_out = outer_sum(mixed, d_branch)
    d_mixed = project_back(d_branch, w_out).astype(jnp.bfloat16)
    dq_self, dk_self, dv_self, d_scores = attention_backward(
        split_heads(query),
        split_heads(key),
        split_heads(value),
        bias,
        self_mask,
        logsum_self,
        split_heads(d_mixed),
    )
    d_bias = jnp.sum(d_scores, axis=0, dtype=jnp.float32)
    table_term = jnp.einsum(
        "hls,lsn->nh", d_bias, onehot.astype(jnp.float32), precision=lax.Precision.HIGHEST
    )
    grad_w_query = outer_sum(first, dq_self)
    grad_w_key = outer_sum(first, dk_self)
    grad_w_value = outer_sum(first, dv_self)
    d_first = (
        project_back(dq_self, w_query)
        + project_back(dk_self, w_key)
        + project_back(dv_self, w_value)
    )
    d_inputs, gain_one = norm_grad(inputs, gains[0], d_first)
    grad_decoder = d_inputs + d_self
    gain_terms = jnp.stack([gain_one, gain_two, gain_three], axis=1)
    flats = flat_rows(
        (
            grad_w_query,
            grad_w_key,
            grad_w_value,
            grad_w_out,
            grad_x_query,
            grad_x_key,
            grad_x_value,
            grad_x_out,
            grad_up,
            grad_down,
            gain_terms,
        )
    )
    summed = (
        lax.psum_scatter(flats[0], AXES, scatter_dimension=0, tiled=True),
        lax.psum_scatter(flats[1], AXES, scatter_dimension=0, tiled=True),
        lax.psum_scatter(flats[2], AXES, scatter_dimension=0, tiled=True),
        lax.psum_scatter(flats[3], AXES, scatter_dimension=0, tiled=True),
        lax.psum_scatter(flats[4], AXES, scatter_dimension=0, tiled=True),
        lax.psum_scatter(flats[5], AXES, scatter_dimension=0, tiled=True),
        lax.psum_scatter(flats[6], AXES, scatter_dimension=0, tiled=True),
        lax.psum_scatter(flats[7], AXES, scatter_dimension=0, tiled=True),
        lax.psum_scatter(flats[8], AXES, scatter_dimension=0, tiled=True),
        lax.psum_scatter(flats[9], AXES, scatter_dimension=0, tiled=True),
        lax.psum_scatter(flats[10], AXES, scatter_dimension=0, tiled=True),
    )
    shaped = unflat_rows(
        summed, (width, width, width, width, width, width, width, width, hidden_width, width, 3)
    )
    sums = shaped[:10] + (jnp.transpose(shaped[10]),)
    grad_table = lax.psum(table_term, AXES)
    return (
        layer_out,
        grad_decoder,
        grad_encoder,
        sums[0],
        sums[1],
        sums[2],
        sums[3],
        sums[4],
        sums[5],
        sums[6],
        sums[7],
        sums[8],
        sums[9],
        sums[10],
        grad_table,
    )


def solution(mesh):
    rows = P(AXES, None)
    slots = P(AXES, None, None)
    flat = P(AXES)
    gains = P(None, AXES)
    small = mesh.shape["dp"] == 8 and mesh.shape["fsdp"] == 4
    return jax.shard_map(
        by_kernel if small else plain,
        mesh=mesh,
        in_specs=(slots, slots) + (rows,) * 10 + (gains, P(), flat, flat, flat, slots),
        out_specs=(slots, slots, slots) + (rows,) * 10 + (gains, P()),
        check_vma=False,
    )
```

```python
import functools

import jax
import jax.numpy as jnp
from jax import lax
from jax.experimental import pallas as pl
from jax.experimental.pallas import tpu as pltpu
from jax.sharding import PartitionSpec as P

H = 12
AXES = ("dp", "fsdp")
MESH = pl.DeviceIdType.MESH
BF = jnp.bfloat16
F32 = jnp.float32


eps = 1e-06
thresholds = [19, 21, 24, 27, 31, 35, 40, 46, 52, 59, 67, 77, 87, 99, 113]


def normalize(v, gain):
    return v * lax.rsqrt(jnp.mean(v * v, axis=-1, keepdims=True) + eps) * gain


def norm_grad(v, gain, grad):
    _, pullback = jax.vjp(normalize, v, gain)
    return pullback(grad)


def gelu_grad(v, grad):
    _, pullback = jax.vjp(jax.nn.gelu, v)
    return pullback(grad)[0]


def project(v, weight):
    return jnp.einsum("btd,df->btf", v, weight, preferred_element_type=jnp.float32)


def project_back(grad, weight):
    return jnp.einsum("btf,df->btd", grad, weight, preferred_element_type=jnp.float32)


def outer_sum(v, grad):
    return jnp.einsum("btd,btf->df", v, grad, preferred_element_type=jnp.float32)


def split_heads(v):
    return v.reshape(v.shape[0], v.shape[1], H, v.shape[2] // H)


def join_heads(v):
    return v.reshape(v.shape[0], v.shape[1], v.shape[2] * v.shape[3])


def flat_rows(items):
    return tuple((item.reshape(-1) for item in items))


def unflat_rows(items, widths):
    return tuple((item.reshape(-1, width) for item, width in zip(items, widths)))


def buckets(length):
    place = jnp.arange(length, dtype=jnp.int32)
    distance = jnp.maximum(place[:, None] - place[None, :], 0)
    level = jnp.minimum(distance, 16)
    for edge in thresholds:
        level = level + (distance >= edge).astype(jnp.int32)
    return level


def scores_of(query, key, bias, mask):
    scores = jnp.einsum("blhd,bshd->bhls", query, key, preferred_element_type=jnp.float32) + bias
    return jnp.where(mask, scores, -1e30)


def attention_forward(query, key, value, bias, mask):
    scores = scores_of(query, key, bias, mask)
    top = jnp.max(scores, axis=-1, keepdims=True)
    expo = jnp.exp(scores - top)
    total = jnp.sum(expo, axis=-1, keepdims=True)
    probs = (expo / total).astype(jnp.bfloat16)
    mixed = jnp.einsum("bhls,bshd->blhd", probs, value, preferred_element_type=jnp.float32)
    return (join_heads(mixed).astype(jnp.bfloat16), top + jnp.log(total))


def attention_backward(query, key, value, bias, mask, logsum, d_out):
    probs = jnp.exp(scores_of(query, key, bias, mask) - logsum)
    d_probs = jnp.einsum("blhd,bshd->bhls", d_out, value, preferred_element_type=jnp.float32)
    delta = jnp.sum(d_probs * probs, axis=-1, keepdims=True)
    d_scores = (probs * (d_probs - delta)).astype(jnp.bfloat16)
    d_query = jnp.einsum(
        "bhls,bshd->blhd", d_scores, key, preferred_element_type=jnp.float32
    ).astype(jnp.bfloat16)
    d_key = jnp.einsum(
        "bhls,blhd->bshd", d_scores, query, preferred_element_type=jnp.float32
    ).astype(jnp.bfloat16)
    d_value = jnp.einsum(
        "bhls,blhd->bshd", probs.astype(jnp.bfloat16), d_out, preferred_element_type=jnp.float32
    ).astype(jnp.bfloat16)
    return (join_heads(d_query), join_heads(d_key), join_heads(d_value), d_scores)


class Place:
    def __init__(self):
        d = lax.axis_index("dp")
        self.z = lax.axis_index("fsdp")
        self.c = lax.rem(d, 2)
        self.x = lax.rem(lax.div(d, 2), 2)
        self.y = lax.div(d, 4)

    def dev(self, y, x, c, z):
        return ((y * 2 + x) * 2 + c, z)

    @property
    def core(self):
        return self.dev(self.y, self.x, 1 - self.c, self.z)

    @property
    def xn(self):
        return self.dev(self.y, 1 - self.x, self.c, self.z)

    @property
    def yn(self):
        return self.dev(1 - self.y, self.x, self.c, self.z)

    @property
    def across(self):
        return self.dev(1 - self.y, 1 - self.x, self.c, self.z)

    def zn(self, step):
        return self.dev(self.y, self.x, self.c, lax.rem(self.z + step, 4))

    def greet(self):
        bar = pltpu.get_barrier_semaphore()
        others = [self.core, self.xn, self.yn, self.across] + [self.zn(s) for s in (1, 2, 3)]
        for other in others:
            pl.semaphore_signal(bar, inc=1, device_id=other, device_id_type=MESH)

    def enter(self):
        pl.semaphore_wait(pltpu.get_barrier_semaphore(), 7)


def rcopy(src, dst, sems, landing, device, leaving=None):
    send, recv = sems
    return pltpu.make_async_remote_copy(
        src_ref=src,
        dst_ref=dst,
        send_sem=send.at[landing if leaving is None else leaving],
        recv_sem=recv.at[landing],
        device_id=device,
        device_id_type=MESH,
    )


class Small:
    def __init__(self, here, buf, sems):
        self.here, self.buf, self.sems = here, buf, sems

    def copies(self, stage):
        h = self.here
        base, devices = (
            (0, (h.core,)),
            (2, (h.xn, h.yn, h.across)),
            (6, (h.zn(1), h.zn(2), h.zn(3))),
        )[stage]
        at = (0, 1, 4)[stage]
        return [
            rcopy(self.buf.at[base], self.buf.at[base + 1 + i], self.sems, at + i, device)
            for i, device in enumerate(devices)
        ]

    def start(self, stage):
        for copy in self.copies(stage):
            copy.start()

    def finish(self, stage):
        for copy in self.copies(stage):
            copy.wait()
        b = self.buf
        if stage == 0:
            b[2] = b[0] + b[1]
        if stage == 1:
            b[6] = b[2] + b[3] + (b[4] + b[5])

    def total(self):
        b = self.buf
        return b[6] + b[7] + (b[8] + b[9])


EVERY = slice(None)


def sent(here, sems, leaving, ref):
    send, recv = sems
    pltpu.make_async_remote_copy(
        src_ref=ref, dst_ref=ref, send_sem=send.at[leaving], recv_sem=recv.at[0], device_id=here.core,
        device_id_type=MESH,
    ).wait_send()


class Gather:
    def __init__(self, here, sq, up, down, zland, early, zsems, sems, bsems, bcsems, like):
        self.here, self.sq, self.up, self.down = here, sq, up, down
        self.zland, self.early, self.zsems, self.sems = zland, early, zsems, sems
        self.bsems, self.bcsems, self.like = bsems, bcsems, like

    def blk(self, u, y, x, c):
        if u < 8:
            return self.sq.at[u, y, x, c]
        if u < 12:
            return self.up.at[u - 8, y, x, c]
        return self.down.at[y, x, c, 2 * (u - 12) : 2 * (u - 12) + 2, 0]

    def zpath(self, j):
        z = self.here.z
        low = z < 2
        if j == 0:
            source, target = z, jnp.where(low, z + 1, z - 1)
        elif j == 1:
            far = jnp.where(z == 0, 2, 1)
            near = jnp.where(z == 1, 0, 3)
            source, target = z, jnp.where((z == 0) | (z == 3), far, near)
        else:
            source = jnp.where(z == 1, 2, jnp.where(z == 2, 1, z))
            target = jnp.where(low, 3, 0)
            target = jnp.where(z == 1, 0, jnp.where(z == 2, 3, target))
        return source, target, lax.rem(source - target + 4, 4) - 1

    def zwait(self):
        return jnp.where(self.here.z < 2, 0, 2)

    def zref(self, k, z):
        h = self.here
        if k < 6:
            return self.zland.at[k, z]
        if k == 6:
            return self.down.at[h.y, h.x, h.c, z, 0]
        p = (k - 7) % 4
        if k < 11:
            return self.down.at[p // 2, p % 2, h.c, z, 1]
        return self.early.at[p // 2, p % 2, lax.div(z, 2), lax.rem(z, 2)]

    def zcopy(self, k, j):
        h = self.here
        source, target, landing = self.zpath(j)
        ref = self.zref(k, source)
        target = h.dev(h.y, h.x, h.c, target)
        return rcopy(ref, ref, self.zsems, 3 * k + landing, target, 0 if k < 8 else 1 if k < 11 else 2)

    def zgot(self, k, r):
        h = self.here
        ref = self.zref(k, lax.rem(h.z + 1 + r, 4))
        return rcopy(ref, ref, self.zsems, 3 * k + r, h.zn(1), 0)

    def z_start(self, k):
        z = self.here.z
        self.zcopy(k, 0).start()
        self.zcopy(k, 1).start()

        @pl.when((z == 0) | (z == 3))
        def _():
            self.zcopy(k, 2).start()

    def z_pass(self, k):
        z = self.here.z

        @pl.when((z == 1) | (z == 2))
        def _():
            self.zgot(k, self.zwait()).wait_recv()
            self.zcopy(k, 2).start()

    def z_wait(self, k):
        z = self.here.z
        self.zgot(k, 1).wait_recv()
        self.zgot(k, 2 - self.zwait()).wait_recv()

        @pl.when((z == 0) | (z == 3))
        def _():
            self.zgot(k, self.zwait()).wait_recv()

    def z_finish(self, k):
        h = self.here
        self.z_wait(k)
        if k < 6:
            slabs = self.zland[k].astype(F32)
            for half in (0, 1):
                rows = jnp.concatenate(
                    [slabs[z, 24 * half : 24 * half + 24] for z in range(4)], axis=0
                ).astype(BF).reshape(2, 48, 768)
                u = 2 * k + half
                if u < 8:
                    self.sq[u, h.y, h.x, h.c] = rows
                else:
                    self.up[u - 8, h.y, h.x, h.c] = rows
        for u in (2 * k, 2 * k + 1):
            self.first(u).start()
            self.second(u).start()

    def nbrs(self, u):
        h = self.here
        return (h.yn, h.xn) if u % 2 == 0 else (h.xn, h.yn)

    def group(self, u):
        return 0 if u < 4 else 2 if u > 9 else 1

    def own(self, u):
        h = self.here
        return self.blk(u, h.y, h.x, h.c)

    def got(self, u):
        h = self.here
        return self.blk(u, 1 - h.y, h.x, h.c) if u % 2 == 0 else self.blk(u, h.y, 1 - h.x, h.c)

    def first(self, u):
        return rcopy(self.own(u), self.own(u), self.sems, 4 * u, self.nbrs(u)[0], self.group(u))

    def second(self, u):
        return rcopy(self.own(u), self.own(u), self.sems, 4 * u + 1, self.nbrs(u)[1], self.group(u))

    def third(self, u):
        return rcopy(self.got(u), self.got(u), self.sems, 4 * u + 2, self.nbrs(u)[1], self.group(u))

    def cross(self, u):
        ref = self.blk(u, EVERY, EVERY, self.here.c)
        return rcopy(ref, ref, self.sems, 4 * u + 3, self.here.core, 3)

    def mid(self, k):
        for u in (2 * k, 2 * k + 1):
            self.first(u).wait_recv()
            self.third(u).start()

    def core(self, k):
        for u in (2 * k, 2 * k + 1):
            self.second(u).wait_recv()
            self.third(u).wait_recv()
            self.cross(u).start()

    def done(self, k):
        for u in (2 * k, 2 * k + 1):
            self.cross(u).wait_recv()

    def bblk(self, w, y, x):
        h = self.here
        cols = slice(384 * (w % 2), 384 * (w % 2) + 384)
        if w < 2:
            return self.down.at[y, x, h.c, h.z, 1, :, cols]
        return self.early.at[y, x, lax.div(h.z, 2), lax.rem(h.z, 2), :, cols]

    def bfirst(self, w):
        h = self.here
        ref = self.bblk(w, h.y, h.x)
        return rcopy(ref, ref, self.bsems, 3 * w + 0, self.nbrs(w)[0], w // 2)

    def bsecond(self, w):
        h = self.here
        ref = self.bblk(w, h.y, h.x)
        return rcopy(ref, ref, self.bsems, 3 * w + 1, self.nbrs(w)[1], w // 2)

    def bthird(self, w):
        h = self.here
        ref = self.bblk(w, 1 - h.y, h.x) if w % 2 == 0 else self.bblk(w, h.y, 1 - h.x)
        return rcopy(ref, ref, self.bsems, 3 * w + 2, self.nbrs(w)[1], w // 2)

    def b_start(self, *ws):
        for w in ws:
            self.bfirst(w).start()
            self.bsecond(w).start()

    def b_mid(self, *ws):
        for w in ws:
            self.bfirst(w).wait_recv()
            self.bthird(w).start()

    def b_got(self, *ws):
        for w in ws:
            self.bsecond(w).wait_recv()
            self.bthird(w).wait_recv()

    def early_finish(self):
        h = self.here
        for p in range(4):
            self.z_wait(11 + p)
        for p in range(4):
            slabs = self.early[p // 2, p % 2].astype(F32)
            for half in (0, 1):
                rows = [
                    slabs[z // 2, z % 2, 24 * half : 24 * half + 24] for z in range(4)
                ]
                self.sq[6 + half, p // 2, p % 2, h.c] = (
                    jnp.concatenate(rows, axis=0).astype(BF).reshape(2, 48, 768)
                )
        sent(h, self.zsems, 2, self.like[12])
        sent(h, self.bsems, 1, self.like[3])
        for u in (6, 7):
            self.cross(u).start()

    def bcross(self, y):
        ref = self.down.at[y, :, self.here.c, :, 1]
        return rcopy(ref, ref, self.bcsems, y, self.here.core, 0)

    def b_core(self, y):
        for p in (2 * y, 2 * y + 1):
            self.z_wait(7 + p)
        self.bcross(y).start()

    def b_done(self):
        for y in (0, 1):
            self.bcross(y).wait_recv()

    def drain(self):
        like = self.like
        sent(self.here, self.zsems, 0, like[21])
        sent(self.here, self.zsems, 1, like[9])
        for group in (0, 1, 2):
            sent(self.here, self.sems, group, like[24])
        sent(self.here, self.sems, 3, like[112])
        sent(self.here, self.bsems, 0, like[3])
        sent(self.here, self.bcsems, 0, like[16])


class Scatter:
    def __init__(
        self, here, up, down, gup, gdown, rc, r1, r2, zsend, zland, brest, bzland, br1, br2,
        sems, zsems, bzsems, bsems, tsems,
    ):
        self.here, self.up, self.down, self.gup, self.gdown = here, up, down, gup, gdown
        self.rc, self.r1, self.r2 = rc, r1, r2
        self.zsend, self.zland, self.sems, self.zsems = zsend, zland, sems, zsems
        self.brest, self.bzland, self.br1, self.br2 = brest, bzland, br1, br2
        self.bzsems, self.bsems, self.tsems = bzsems, bsems, tsems

    def blk(self, u, y, x, c):
        if u < 4:
            return self.down.at[y, x, c, u]
        if u < 8:
            return self.up.at[u - 4, y, x, c]
        if u < 12:
            return self.gup.at[u - 8, y, x, c]
        return self.gdown.at[y, x, c, 2 * (u - 12) : 2 * (u - 12) + 2, 0:32]

    def core_blk(self, u, c):
        if u < 12:
            return self.blk(u, EVERY, EVERY, c)
        pair, low = (u - 12) % 2, 48 * ((u - 12) // 2)
        return self.gdown.at[:, :, c, 2 * pair : 2 * pair + 2, low : low + 48]

    def rows(self, u):
        return slice(0, 48 if u < 12 else 32)

    def put(self, u, y, cols, value):
        value = value.astype(BF).reshape(2, 2, 2, 48, 256)
        if u < 4:
            self.down[y, :, :, u, :, :, cols] = value
        else:
            self.up[u - 4, y, :, :, :, :, cols] = value

    def cross(self, u):
        h = self.here
        return rcopy(
            self.core_blk(u, 1 - h.c), self.rc.at[u % 8], self.sems, 3 * u, h.core, 0
        )

    def first(self, u):
        h = self.here
        if u % 2 == 0:
            src, device = self.blk(u, EVERY, 1 - h.x, h.c), h.xn
        else:
            src, device = self.blk(u, 1 - h.y, EVERY, h.c), h.yn
        dst = self.r1.at[u, :, :, self.rows(u)]
        return rcopy(src, dst, self.sems, 3 * u + 1, device, 1 if u < 12 else 3)

    def second(self, u):
        h = self.here
        if u % 2 == 0:
            src, device = self.r1.at[u, 1 - h.y, :, self.rows(u)], h.yn
        else:
            src, device = self.r1.at[u, 1 - h.x, :, self.rows(u)], h.xn
        dst = self.r2.at[u, :, self.rows(u)]
        return rcopy(src, dst, self.sems, 3 * u + 2, device, 2 if u < 12 else 4)

    def start(self, k):
        for u in (2 * k, 2 * k + 1):
            self.cross(u).start()

    def add_core(self, u):
        self.cross(u).wait_recv()
        mine = self.core_blk(u, self.here.c)
        mine[...] = (mine[...].astype(F32) + self.rc[u % 8].astype(F32)).astype(BF)

    def one(self, k):
        for u in (2 * k, 2 * k + 1):
            self.add_core(u)
            self.first(u).start()

    def two(self, k):
        h = self.here
        for u in (2 * k, 2 * k + 1):
            self.first(u).wait_recv()
            if u % 2 == 0:
                mine = self.blk(u, EVERY, h.x, h.c)
            else:
                mine = self.blk(u, h.y, EVERY, h.c)
            rows = self.rows(u)
            total = mine[...].astype(F32) + self.r1[u, :, :, rows].astype(F32)
            self.r1[u, :, :, rows] = total.astype(BF)
            self.second(u).start()

    def three(self, k):
        h = self.here
        sums = []
        for u in (2 * k, 2 * k + 1):
            self.second(u).wait_recv()
            at = h.y if u % 2 == 0 else h.x
            rows = self.rows(u)
            sums.append(self.r1[u, at, :, rows].astype(F32) + self.r2[u, :, rows].astype(F32))
        if k < 6:
            sums = [item.reshape(96, 768) for item in sums]
            for z in range(4):
                self.zsend[k, z] = jnp.concatenate(
                    [item[24 * z : 24 * z + 24] for item in sums], axis=0
                ).astype(BF)
        else:
            for half in (0, 1):
                self.zsend[k, 2 * half : 2 * half + 2, 0:32] = sums[half].astype(BF)
        for s in (1, 2, 3):
            self.zcopy(k, s).start()

    def zcopy(self, k, s):
        h = self.here
        return rcopy(
            self.zsend.at[k, lax.rem(h.z + s, 4), self.rows(2 * k)],
            self.zland.at[k, s - 1, self.rows(2 * k)], self.zsems,
            3 * k + s - 1, h.zn(s), 0 if k < 6 else 1,
        )

    def last(self, k):
        h = self.here
        for s in (1, 2, 3):
            self.zcopy(k, s).wait_recv()
        rows = self.rows(2 * k)
        total = self.zsend[k, h.z, rows].astype(F32)
        for s in (1, 2, 3):
            total = total + self.zland[k, s - 1, rows].astype(F32)
        return total

    def tail_first(self, u, w):
        h = self.here
        cols = slice(384 * w, 384 * w + 384)
        if u % 2 == 0:
            src, device = self.blk(u, EVERY, 1 - h.x, h.c), h.xn
        else:
            src, device = self.blk(u, 1 - h.y, EVERY, h.c), h.yn
        return rcopy(
            src.at[:, :, :, cols], self.r1.at[u, :, :, :, cols], self.tsems, 2 * u + w, device, 0
        )

    def tail_second(self, u, w):
        h = self.here
        cols = slice(384 * w, 384 * w + 384)
        at, device = (1 - h.y, h.yn) if u % 2 == 0 else (1 - h.x, h.xn)
        return rcopy(
            self.r1.at[u, at, :, :, cols], self.r2.at[u, :, :, cols], self.tsems, 4 + 2 * u + w,
            device, 1,
        )

    def tail_zcopy(self, w, s):
        h = self.here
        cols = slice(384 * w, 384 * w + 384)
        return rcopy(
            self.zsend.at[0, lax.rem(h.z + s, 4), :, cols], self.zland.at[0, s - 1, :, cols],
            self.tsems, 8 + 3 * w + s - 1, h.zn(s), 2,
        )

    def tail_one(self):
        for u in (0, 1):
            self.add_core(u)
            self.tail_first(u, 0).start()

    def tail_rest(self):
        for u in (0, 1):
            self.tail_first(u, 1).start()

    def tail_two(self, w):
        h = self.here
        cols = slice(384 * w, 384 * w + 384)
        for u in (0, 1):
            self.tail_first(u, w).wait_recv()
            if u % 2 == 0:
                mine = self.blk(u, EVERY, h.x, h.c)
            else:
                mine = self.blk(u, h.y, EVERY, h.c)
            mine = mine[:, :, :, cols].astype(F32)
            self.r1[u, :, :, :, cols] = (
                mine + self.r1[u, :, :, :, cols].astype(F32)
            ).astype(BF)
            self.tail_second(u, w).start()

    def tail_three(self, w):
        h = self.here
        cols = slice(384 * w, 384 * w + 384)
        sums = []
        for u in (0, 1):
            self.tail_second(u, w).wait_recv()
            at = h.y if u % 2 == 0 else h.x
            total = self.r1[u, at, :, :, cols].astype(F32) + self.r2[u, :, :, cols].astype(F32)
            sums.append(total.reshape(96, 384))
        for z in range(4):
            self.zsend[0, z, :, cols] = jnp.concatenate(
                [item[24 * z : 24 * z + 24] for item in sums], axis=0
            ).astype(BF)
        for s in (1, 2, 3):
            self.tail_zcopy(w, s).start()

    def tail_last(self, w):
        h = self.here
        cols = slice(384 * w, 384 * w + 384)
        for s in (1, 2, 3):
            self.tail_zcopy(w, s).wait_recv()
        total = self.zsend[0, h.z, :, cols].astype(F32)
        for s in (1, 2, 3):
            total = total + self.zland[0, s - 1, :, cols].astype(F32)
        return total

    def bz(self, s):
        h = self.here
        src = self.gdown.at[:, :, h.c, lax.rem(h.z + s, 4), 32:96]
        return rcopy(src, self.bzland.at[s - 1], self.bzsems, s - 1, h.zn(s), 0)

    def b_one(self):
        for u in (14, 15):
            self.add_core(u)
        for s in (1, 2, 3):
            self.bz(s).start()

    def bfirst(self, w):
        h = self.here
        if w == 0:
            src, device = self.brest.at[:, 1 - h.x, :, 0:384], h.xn
        else:
            src, device = self.brest.at[1 - h.y, :, :, 384:768], h.yn
        return rcopy(src, self.br1.at[w], self.bsems, 2 * w, device, 0)

    def bsecond(self, w):
        h = self.here
        if w == 0:
            src, device = self.br1.at[w, 1 - h.y], h.yn
        else:
            src, device = self.br1.at[w, 1 - h.x], h.xn
        return rcopy(src, self.br2.at[w], self.bsems, 2 * w + 1, device, 1)

    def b_two(self):
        h = self.here
        for s in (1, 2, 3):
            self.bz(s).wait_recv()
        total = self.gdown[:, :, h.c, h.z, 32:96].astype(F32)
        for s in (1, 2, 3):
            total = total + self.bzland[s - 1].astype(F32)
        self.brest[...] = total.astype(BF)
        for w in (0, 1):
            self.bfirst(w).start()

    def b_three(self):
        h = self.here
        for w in (0, 1):
            self.bfirst(w).wait_recv()
            if w == 0:
                mine = self.brest[:, h.x, :, 0:384]
            else:
                mine = self.brest[h.y, :, :, 384:768]
            self.br1[w] = (mine.astype(F32) + self.br1[w].astype(F32)).astype(BF)
            self.bsecond(w).start()

    def b_last(self, w):
        h = self.here
        self.bsecond(w).wait_recv()
        at = h.y if w == 0 else h.x
        return self.br1[w, at].astype(F32) + self.br2[w].astype(F32)

    def drain(self, slabs128):
        sent(self.here, self.sems, 0, slabs128)
        sent(self.here, self.sems, 1, self.r1.at[0:10])
        sent(self.here, self.sems, 2, self.r2.at[0:10])
        sent(self.here, self.sems, 3, self.r1.at[0:2, :, :, 0:32])
        sent(self.here, self.sems, 4, self.r2.at[0:2, :, 0:32])
        sent(self.here, self.zsems, 0, self.zland.at[0:5])
        sent(self.here, self.zsems, 1, self.zland.at[0, :, 0:32])
        sent(self.here, self.bzsems, 0, self.bzland)
        sent(self.here, self.bsems, 0, self.brest.at[0])
        sent(self.here, self.bsems, 1, self.brest.at[0, 0])
        sent(self.here, self.tsems, 0, self.r1.at[0:2])
        sent(self.here, self.tsems, 1, self.r2.at[0:2])
        sent(self.here, self.tsems, 2, self.zland.at[0])


def mm(a, b):
    return lax.dot_general(a, b, (((1,), (0,)), ((), ())), preferred_element_type=F32)


def mt(a, b):
    return lax.dot_general(a, b, (((1,), (1,)), ((), ())), preferred_element_type=F32)


def tm(a, b):
    return lax.dot_general(a, b, (((0,), (0,)), ((), ())), preferred_element_type=F32)


def iota(shape, axis):
    return lax.broadcasted_iota(jnp.int32, shape, axis)


def lanes(hp):
    return pl.ds(pl.multiple_of(hp * 128, 128), 128)


def both(q):
    low = iota(q.shape, 1) < 64
    zero = jnp.zeros_like(q)
    return jnp.concatenate([jnp.where(low, q, zero), jnp.where(low, zero, q)], axis=0)


def merge(pair):
    rows = pair.shape[0] // 2
    low = iota((rows, 128), 1) < 64
    return jnp.where(low, pair[:rows], pair[rows:]).astype(BF)


def probs(key, query, bias, mask):
    scores = mt(key, query)
    if bias is not None:
        scores = scores + bias.astype(F32)
    scores = jnp.where(mask, scores, -1e30)
    expo = jnp.exp(scores - jnp.max(scores, axis=0, keepdims=True))
    return expo * (1.0 / jnp.sum(expo, axis=0, keepdims=True))


def rms(v):
    return lax.rsqrt(jnp.mean(v * v, axis=-1, keepdims=True) + eps)


def norm_back(v, gain, grad):
    r = rms(v)
    scaled = grad * gain
    inner = jnp.mean(scaled * v, axis=-1, keepdims=True)
    return r * scaled - v * (r * r * r * inner), jnp.sum(grad * v * r, axis=0, keepdims=True)


def gelu(v):
    c = 0.7978845608028654
    return v * (0.5 + 0.5 * jnp.tanh(v * (c + c * 0.044715 * (v * v))))


def gelu_slope(v):
    c = 0.7978845608028654
    square = v * v
    t = jnp.tanh(v * (c + c * 0.044715 * square))
    return (0.5 + 0.5 * t) + v * (1.0 - t * t) * (0.5 * c + 1.5 * c * 0.044715 * square)


def layer_kernel(*refs):
    given, (tlen, slen, count) = refs[:15], refs[15:18]
    g_enc, results = refs[18], refs[19:33]
    (
        sq, up, down, gup, gdown, rc, r1, r2, zland, zland2, brest, bzland, br1, br2, small, small2,
        bias, h2, h3, q1, k1, v1, o1, q2, o2, k2, v2, g, gp, x1, x2, stage,
        zs, zr, ss, sr, bs, br, bcs, bcr, ms, mr,
        rzs, rzr, rss, rsr, rbzs, rbzr, rbs, rbr, rts, rtr, m2s, m2r, out_sem, done_sem, in_sem, credit,
        *held,
    ) = refs[33:]
    held, kept = [h2, x1, *held[:10], *refs[31:33]], held[10:]
    layer_out, g_dec, *g_sq, g_up, g_down, g_gain, g_table = held
    *squares, up_in, down_in, gain_in, table_in = given[:12]
    x_in, cot, enc = kept

    def hand(i):
        return pltpu.make_async_copy(held[i], results[i], done_sem.at[i])

    def fetch(i):
        return pltpu.make_async_copy(given[12 + i], kept[i], in_sem.at[i])

    here = Place()
    here.greet()
    for i in range(3):
        fetch(i).start()
    index = (here.y * 4 + here.x * 2 + here.c) * 4 + here.z
    for k in range(4):
        slab = jnp.concatenate(
            [squares[2 * k][...].astype(F32), squares[2 * k + 1][...].astype(F32)], axis=0
        ).astype(BF)
        if k < 3:
            zland[k, here.z] = slab
        else:
            rc[here.y, here.x, lax.div(here.z, 2), lax.rem(here.z, 2)] = slab
    for k in range(2):
        zland[4 + k, here.z] = jnp.concatenate(
            [up_in[:, 768 * n : 768 * n + 768].astype(F32) for n in (2 * k, 2 * k + 1)], axis=0
        ).astype(BF)
    down[here.y, here.x, here.c, here.z] = down_in[...].reshape(2, 48, 768)
    spot = (iota((24, 768), 1) == iota((24, 768), 0) + 24 * index).astype(BF)
    small[0] = jnp.zeros((8, 768), F32)
    small[0, 0:3] = mm(gain_in[...], spot)
    here.enter()
    like = {
        3: zland2.at[0], 9: zland2.at[0:3], 12: zland2.at[0:4], 16: rc.at[0:2], 21: zland2,
        24: r2.at[0:12], 112: sq.at[0:7],
    }
    ga = Gather(
        here, sq, up, down, zland, rc, (zs, zr), (ss, sr), (bs, br), (bcs, bcr), like
    )
    m = Small(here, small, (ms, mr))
    rs = Scatter(
        here, up, down, gup, gdown, rc, r1, r2, zland, zland2, brest, bzland, br1, br2,
        (rss, rsr), (rzs, rzr), (rbzs, rbzr), (rbs, rbr), (rts, rtr),
    )
    m2 = Small(here, small2, (m2s, m2r))

    def weight(u):
        return sq[u].reshape(768, 768)

    def columns(u, n):
        return sq[u, :, :, :, :, :, 256 * n : 256 * n + 256].reshape(768, 256)

    def z_starts(*items):
        for item in items:
            ga.z_start(item)

    def z_passes(*items):
        for item in items:
            ga.z_pass(item)

    m.start(0)
    ga.z_start(0)
    ga.b_start(2, 3, 0, 1)
    m.finish(0)
    m.start(1)
    ga.z_pass(0)
    z_starts(1)
    ga.b_mid(2, 3, 0, 1)

    def bucket_hot(rows_are_buckets):
        shape = (32, 128) if rows_are_buckets else (128, 32)
        distance = iota(shape, 1 if rows_are_buckets else 0)
        level = jnp.minimum(distance, 16)
        for edge in thresholds:
            level = level + (distance >= edge).astype(jnp.int32)
        return level == iota(shape, 0 if rows_are_buckets else 1)

    by_distance = mm(table_in[...], bucket_hot(True).astype(BF))
    for head in range(12):
        row = jnp.broadcast_to(by_distance[head : head + 1, :], (128, 128))
        bias[head // 2, :, 128 * (head % 2) : 128 * (head % 2) + 128] = pltpu.roll(
            row, 0, 1, stride=1, stride_axis=0
        ).astype(BF)

    key_place, target_place = iota((128, 256), 0), iota((128, 256), 1) & 127
    causal = key_place <= target_place
    source_place = iota((512, 256), 0)

    def self_mask(ex):
        return causal & (key_place < tlen[ex])

    def cross_mask(ex):
        return source_place < slen[ex]

    row_place = iota((256, 1), 0)
    live = (
        ((row_place < 128) & (row_place < tlen[0]) & (0 < count[0]))
        | ((row_place >= 128) & (row_place - 128 < tlen[1]) & (1 < count[0]))
    ).astype(F32)

    ga.z_finish(0)
    ga.b_got(2, 3)
    m.finish(1)
    m.start(2)
    z_starts(2, 11)
    ga.z_pass(1)
    ga.mid(0)
    ga.z_finish(1)
    z_starts(12, 4)
    z_passes(2, 11)
    ga.core(0)
    ga.z_finish(2)
    z_starts(5, 13)
    ga.mid(1)
    m.finish(2)
    gains = m.total()
    gain = [gains[i : i + 1, :] for i in range(3)]

    fetch(0).wait()

    def normed_input():
        first = x_in[...].astype(F32)
        return (first * rms(first) * gain[0]).astype(BF)

    h3[...] = normed_input()
    z_passes(12, 4)
    ga.core(1)
    ga.mid(2)
    ga.done(0)
    for n in range(3):
        cols = slice(256 * n, 256 * n + 256)
        q1[:, cols] = mm(h3[...], columns(0, n)).astype(BF)
        k1[:, cols] = mm(h3[...], columns(1, n)).astype(BF)
    ga.z_finish(4)
    z_starts(14)
    z_passes(5, 13)
    ga.core(2)
    ga.done(1)
    for n in range(3):
        cols = slice(256 * n, 256 * n + 256)
        v1[:, cols] = mm(h3[...], columns(2, n)).astype(BF)

    def self_forward(hp, carry):
        for ex in range(2):
            rows = slice(128 * ex, 128 * ex + 128)
            query = both(q1[rows, lanes(hp)])
            p = probs(k1[rows, lanes(hp)], query, bias[hp], self_mask(ex)).astype(BF)
            o1[rows, lanes(hp)] = merge(tm(p, v1[rows, lanes(hp)]))
        return carry

    lax.fori_loop(0, 6, self_forward, 0, unroll=2)
    ga.z_finish(5)
    ga.b_got(0, 1)
    z_starts(6)
    z_passes(14)
    ga.mid(4)
    x1[...] = x_in[...].astype(F32) + mm(o1[...], weight(3))
    h2[...] = (x1[...] * rms(x1[...]) * gain[1]).astype(BF)
    ga.done(2)

    def encode(r, carry):
        rows = pl.ds(pl.multiple_of(r * 256, 256), 256)
        for n in range(3):
            cols = slice(256 * n, 256 * n + 256)
            k2[rows, cols] = mm(enc[rows, :], columns(4, n)).astype(BF)
            v2[rows, cols] = mm(enc[rows, :], columns(5, n)).astype(BF)
        return carry

    fetch(2).wait()
    lax.fori_loop(0, 4, encode, 0)
    z_starts(7)
    ga.early_finish()
    ga.mid(5)
    z_passes(6)
    z_starts(8)
    ga.done(3)
    for n in range(3):
        cols = slice(256 * n, 256 * n + 256)
        q2[:, cols] = mm(h2[...], columns(6, n)).astype(BF)

    beyond = [jnp.where(iota((1, 512), 1) < slen[ex], 0.0, -1e30) for ex in range(2)]

    def cross_forward(hp, carry):
        for ex in range(2):
            rows = slice(128 * ex, 128 * ex + 128)
            keys = slice(512 * ex, 512 * ex + 512)
            query = both(q2[rows, lanes(hp)])
            scores = mt(query, k2[keys, lanes(hp)]) + beyond[ex]
            expo = jnp.exp(scores - jnp.max(scores, axis=1, keepdims=True))
            scale = 1.0 / jnp.sum(expo, axis=1, keepdims=True)
            o2[rows, lanes(hp)] = merge(mm(expo.astype(BF), v2[keys, lanes(hp)]) * scale)
        return carry

    def cross_step(i, carry):
        cross_forward(2 * i, carry)
        cross_forward(2 * i + 1, carry)

        @pl.when(i == 0)
        def _():
            ga.z_finish(6)
            ga.z_start(9)
            ga.z_pass(7)

        @pl.when(i == 1)
        def _():
            ga.core(4)
            ga.z_pass(8)
            ga.z_start(10)

        return carry

    lax.fori_loop(0, 3, cross_step, 0)
    ga.core(5)
    ga.mid(6)
    x2[...] = x1[...] + mm(o2[...], weight(7))
    h3[...] = (x2[...] * rms(x2[...]) * gain[2]).astype(BF)
    ga.done(4)

    def hidden(n, carry):
        for part in range(3):
            lo = 256 * part
            a = mm(h3[...], up[n, :, :, :, :, :, lo : lo + 256].reshape(768, 256))
            cols = pl.ds(pl.multiple_of(768 * n + lo, 256), 256)
            g[:, cols] = gelu(a).astype(BF)
            gp[:, cols] = a.astype(BF)
        return carry

    def keep_gain(i, term):
        for j in range(6):
            small2[0, 6 * i + j : 6 * i + j + 1, :] = term[:, 128 * j : 128 * j + 128]

    fetch(1).wait()

    def df(cols=slice(None)):
        return (cot[:, cols].astype(F32) * live).astype(BF)

    def wide(e):
        return pl.ds(pl.multiple_of(768 * e, 256), 768)

    def grad_down(e, carry):
        turned = g[:, wide(e)].T
        for n in range(3):
            cols = slice(256 * n, 256 * n + 256)
            grad = mm(turned, df(cols)).astype(BF)
            gdown[lax.div(e, 2), lax.rem(e, 2), :, :, :, cols] = grad.reshape(2, 4, 96, 256)
        return carry

    def hidden_step(i, carry):
        for e in (2 * i, 2 * i + 1):
            hidden(e, carry)
        for e in (2 * i, 2 * i + 1):
            grad_down(e, carry)

        @pl.when(i == 0)
        def _():
            ga.z_pass(9)
            ga.z_pass(10)
            ga.done(5)

        return carry

    lax.fori_loop(0, 2, hidden_step, 0)
    rs.start(6)
    ga.b_core(0)
    ga.core(6)
    rs.one(6)
    rs.start(7)
    ga.b_core(1)

    def slopes(n, carry):
        for part in range(3):
            cols = pl.ds(pl.multiple_of(768 * n + 256 * part, 256), 256)
            gp[:, cols] = gelu_slope(gp[:, cols].astype(F32)).astype(BF)
        return carry

    lax.fori_loop(0, 4, slopes, 0)
    rs.b_one()
    ga.done(6)
    ga.b_done()

    def down_block(e):
        return down[lax.div(e, 2), lax.rem(e, 2)].reshape(768, 768)

    def inner_grad(e, carry):
        dg = mt(df(), down_block(e))
        gp[:, wide(e)] = (dg * gp[:, wide(e)].astype(F32)).astype(BF)
        return carry

    def grad_up(n, carry):
        turned = h3[...].T
        for part in range(3):
            cols = slice(256 * part, 256 * part + 256)
            source = pl.ds(pl.multiple_of(768 * n + 256 * part, 256), 256)
            grad = mm(turned, gp[:, source]).astype(BF)
            gup[n, :, :, :, :, :, cols] = grad.reshape(2, 2, 2, 2, 48, 256)
        return carry

    def inner_step(i, carry):
        for e in (2 * i, 2 * i + 1):
            inner_grad(e, carry)
        for e in (2 * i, 2 * i + 1):
            grad_up(e, carry)

        @pl.when(i == 0)
        def _():
            rs.start(4)

        return carry

    lax.fori_loop(0, 2, inner_step, 0)
    rs.start(5)
    rs.one(4)
    rs.two(6)
    stage[0] = jnp.zeros((256, 768), F32)
    stage[1] = x2[...]

    def inner_back(n, carry):
        stage[0] += mt(gp[:, wide(n)], up[n].reshape(768, 768))
        return carry

    lax.fori_loop(0, 4, inner_back, 0, unroll=2)
    rs.one(5)
    pl.semaphore_signal(credit, inc=1, device_id=here.core, device_id_type=MESH)
    d_norm, gain_three = norm_back(x2[...], gain[2], stage[0])
    keep_gain(2, gain_three)
    x2[...] = cot[...].astype(F32) * live + d_norm
    ga.drain()

    def put_grads(value, rows, pairs):
        def half_rows(y, carry):
            turned = value[:, pl.ds(pl.multiple_of(384 * y, 128), 384)].T
            for u, ref in pairs:
                for n in range(3):
                    cols = slice(256 * n, 256 * n + 256)
                    rs.put(u, y, cols, mm(turned, ref[:, cols]))
            return carry

        lax.fori_loop(0, 2, half_rows, 0)

    h3[...] = x2[...].astype(BF)
    put_grads(o2, 256, ((7, h3),))
    o2[...] = mt(h3[...], weight(7)).astype(BF)

    beyond_rows = [jnp.where(iota((512, 1), 0) < slen[ex], 0.0, -1e30) for ex in range(2)]

    def cross_backward(hp, carry):
        for ex in range(2):
            rows = slice(128 * ex, 128 * ex + 128)
            keys = slice(512 * ex, 512 * ex + 512)
            query, d_out = both(q2[rows, lanes(hp)]), both(o2[rows, lanes(hp)])
            key, value = k2[keys, lanes(hp)], v2[keys, lanes(hp)]
            scores = mt(key, query) + beyond_rows[ex]
            expo = jnp.exp(scores - jnp.max(scores, axis=0, keepdims=True))
            scale = 1.0 / jnp.sum(expo, axis=0, keepdims=True)
            dp = mt(value, d_out)
            delta = jnp.sum(dp * expo, axis=0, keepdims=True) * scale
            p = expo * scale
            ds = (p * (dp - delta)).astype(BF)
            turned = mm(key.T, ds).T
            q2[rows, lanes(hp)] = merge(turned)
            k2[keys, lanes(hp)] = mm(ds, query).astype(BF)
            v2[keys, lanes(hp)] = mm(p.astype(BF), d_out).astype(BF)
        return carry

    def cross_back_step(i, carry):
        cross_backward(2 * i, carry)
        cross_backward(2 * i + 1, carry)

        @pl.when(i == 1)
        def _():
            rs.two(4)

        return carry

    lax.fori_loop(0, 3, cross_back_step, 0)
    rs.three(6)
    put_grads(h2, 256, ((6, q2),))
    pl.semaphore_wait(credit, 1)
    rs.start(3)

    def result(e, carry):
        stage[1] += mm(g[:, wide(e)], down_block(e))
        return carry

    lax.fori_loop(0, 4, result, 0, unroll=2)
    layer_out[...] = (stage[1] * live).astype(BF)
    hand(0).start()
    rs.two(5)
    rs.one(3)
    put_grads(enc, 1024, ((4, k2), (5, v2)))
    rs.start(2)

    def finish(k):
        total = rs.last(k)
        if k < 4:
            g_sq[2 * k][...] = total[:24]
            g_sq[2 * k + 1][...] = total[24:]
            hand(2 + 2 * k).start()
            hand(3 + 2 * k).start()
        elif k < 6:
            g_up[:, 1536 * (k - 4) : 1536 * (k - 4) + 768] = total[:24]
            g_up[:, 1536 * (k - 4) + 768 : 1536 * (k - 4) + 1536] = total[24:]
        else:
            g_down[0:32, :] = total

    d_norm, gain_two = norm_back(x1[...], gain[1], mt(q2[...], weight(6)))
    keep_gain(1, gain_two)
    x2[...] = x2[...] + d_norm
    rs.one(2)
    rs.three(4)

    h3[...] = x2[...].astype(BF)
    put_grads(o1, 256, ((3, h3),))
    o1[...] = mt(h3[...], weight(3)).astype(BF)
    rs.three(5)
    turn = (iota((128, 256), 0) + (iota((128, 256), 1) & 127) == 127).astype(BF)

    def self_backward(hp, carry):
        scores = []
        for ex in range(2):
            rows = slice(128 * ex, 128 * ex + 128)
            query, d_out = both(q1[rows, lanes(hp)]), both(o1[rows, lanes(hp)])
            key, value = k1[rows, lanes(hp)], v1[rows, lanes(hp)]
            p = probs(key, query, bias[hp], self_mask(ex))
            dp = mt(value, d_out)
            delta = jnp.sum(dp * p, axis=0, keepdims=True)
            ds = (p * (dp - delta)).astype(BF)
            q1[rows, lanes(hp)] = merge(tm(ds, key))
            k1[rows, lanes(hp)] = mm(ds, query).astype(BF)
            v1[rows, lanes(hp)] = mm(p.astype(BF), d_out).astype(BF)
            scores.append(ds)
        pair = mm(turn, jnp.concatenate(scores, axis=0))
        for head in range(2):
            skew = pltpu.roll(pair[:, 128 * head : 128 * head + 128], 0, 1, stride=1, stride_axis=0)
            small2[0, pl.ds(18 + 2 * hp + head, 1), :] = jnp.sum(skew, axis=0, keepdims=True)
        return carry

    lax.fori_loop(0, 6, self_backward, 0, unroll=2)
    h3[...] = normed_input()
    put_grads(h3, 256, ((2, v1), (0, q1), (1, k1)))
    rs.start(1)
    rs.two(3)
    rs.start(0)
    stage[0] = jnp.zeros((256, 768), F32)

    def first_back(y, carry):
        cols = pl.ds(pl.multiple_of(384 * y, 128), 384)
        for u, ref in ((0, q1), (1, k1), (2, v1)):
            stage[0, :, cols] += mt(ref[...], sq[u, y].reshape(384, 768))
        return carry

    lax.fori_loop(0, 2, first_back, 0, unroll=2)
    d_norm, gain_one = norm_back(x_in[...].astype(F32), gain[0], stage[0])
    g_dec[...] = x2[...] + d_norm
    hand(1).start()
    keep_gain(0, gain_one)
    small2[0, 30:32, :] = jnp.zeros((2, 128), F32)
    m2.start(0)
    rs.one(1)
    m2.finish(0)
    m2.start(1)
    rs.two(2)
    rs.three(3)
    rs.b_two()

    def out_copy(r):
        return pltpu.make_async_copy(
            stage.at[lax.rem(r, 2)],
            g_enc.at[pl.ds(pl.multiple_of(256 * r, 256), 256)],
            out_sem.at[r],
        )

    def encoder_grad(r, carry):
        @pl.when(r >= 2)
        def _():
            out_copy(r - 2).wait()

        rows = pl.ds(pl.multiple_of(256 * r, 256), 256)
        slot = lax.rem(r, 2)
        for y in range(2):
            cols = slice(384 * y, 384 * y + 384)
            stage[slot, :, cols] = mt(k2[rows, :], sq[4, y].reshape(384, 768))
            stage[slot, :, cols] += mt(v2[rows, :], sq[5, y].reshape(384, 768))
        out_copy(r).start()
        return carry

    lax.fori_loop(0, 4, encoder_grad, 0)
    rs.two(1)
    m2.finish(1)
    m2.start(2)
    rs.tail_one()
    rs.three(2)
    rs.tail_rest()
    finish(6)
    finish(4)
    finish(5)
    hand(10).start()
    rs.three(1)
    rs.b_three()
    rs.tail_two(0)
    finish(3)
    rs.tail_two(1)
    rs.tail_three(0)
    rs.tail_three(1)
    for w in (0, 1):
        g_down[32:96, 384 * w : 384 * w + 384] = rs.b_last(w)
    hand(11).start()
    m2.finish(2)
    reduced = m2.total()
    sums = jnp.concatenate(
        [
            jnp.concatenate([reduced[6 * i + j : 6 * i + j + 1, :] for j in range(6)], axis=1)
            for i in range(3)
        ],
        axis=0,
    )
    pick = (iota((768, 24), 0) == iota((768, 24), 1) + 24 * index).astype(F32)
    g_gain[...] = lax.dot_general(
        sums, pick, (((1,), (0,)), ((), ())), preferred_element_type=F32,
        precision=lax.Precision.HIGHEST,
    )
    distance = (iota((32, 128), 1) + 1) & 127
    level = jnp.minimum(distance, 16)
    for edge in thresholds:
        level = level + (distance >= edge).astype(jnp.int32)
    hot = (level == iota((32, 128), 0)).astype(F32)
    g_table[...] = lax.dot_general(
        reduced[18:30, :], hot, (((1,), (1,)), ((), ())), preferred_element_type=F32,
        precision=lax.Precision.HIGHEST,
    )
    finish(2)
    finish(1)
    for w in (0, 1):
        total = rs.tail_last(w)
        g_sq[0][:, 384 * w : 384 * w + 384] = total[:24]
        g_sq[1][:, 384 * w : 384 * w + 384] = total[24:]
    hand(2).start()
    hand(3).start()
    rs.drain(sq)
    out_copy(2).wait()
    out_copy(3).wait()
    for i in range(12):
        hand(i).wait()


VM = pl.BlockSpec(memory_space=pltpu.VMEM)
SM = pl.BlockSpec(memory_space=pltpu.SMEM)
ANY = pl.BlockSpec(memory_space=pl.ANY)


def layer_call(*args):
    shape = jax.ShapeDtypeStruct
    dims = (3, 45, 4, 56, 2, 12, 1, 2, 7, 7, 2, 21, 5, 48, 1, 3, 2, 4, 3, 14, 7, 7)
    half = lambda *dims: pltpu.VMEM(dims, BF)
    results = (
        ((256, 768), BF),
        ((256, 768), F32),
        *[((24, 768), F32)] * 8,
        ((24, 3072), F32),
        ((96, 768), F32),
        ((3, 24), F32),
        ((12, 32), F32),
    )
    return pl.pallas_call(
        layer_kernel,
        out_shape=(
            shape((1024, 768), F32),
            *[shape(*each) for each in results],
        ),
        in_specs=[VM] * 12 + [ANY] * 3 + [SM] * 3,
        out_specs=(ANY,) * 13 + (VM,) * 2,
        scratch_shapes=[
            half(8, 2, 2, 2, 2, 48, 768),
            half(4, 2, 2, 2, 2, 48, 768),
            half(2, 2, 2, 4, 2, 48, 768),
            half(4, 2, 2, 2, 2, 48, 768),
            half(2, 2, 2, 4, 96, 768),
            half(8, 2, 2, 2, 48, 768),
            half(14, 2, 2, 48, 768),
            half(14, 2, 48, 768),
            half(7, 4, 48, 768),
            half(7, 3, 48, 768),
            half(2, 2, 64, 768),
            half(3, 2, 2, 64, 768),
            half(2, 2, 64, 384),
            half(2, 64, 384),
            pltpu.VMEM((10, 8, 768), F32),
            pltpu.VMEM((10, 32, 128), F32),
            half(6, 128, 256),
            *[half(256, 768)] * 2,
            *[half(256, 768)] * 4,
            *[half(256, 768)] * 2,
            *[half(1024, 768)] * 2,
            *[half(256, 3072)] * 2,
            *[pltpu.VMEM((256, 768), F32)] * 2,
            pltpu.VMEM((2, 256, 768), F32),
            *[pltpu.SemaphoreType.DMA((each,)) for each in dims],
            pltpu.SemaphoreType.DMA((4,)),
            pltpu.SemaphoreType.DMA((12,)),
            pltpu.SemaphoreType.DMA((3,)),
            pltpu.SemaphoreType.REGULAR,
            *[pltpu.VMEM(*each) for each in results[2:12]],
            *[pltpu.VMEM(each.shape, each.dtype) for each in args[12:15]],
        ],
        compiler_params=pltpu.CompilerParams(
            collective_id=0, has_side_effects=True, vmem_limit_bytes=64 * 2**20 - 2**16
        ),
        name="layer",
    )(*args)


def hand_out_kernel(*refs):
    count = (len(refs) - 2) // 3
    source, target, held = refs[:count], refs[count : 2 * count], refs[2 * count : 3 * count]
    got, put = refs[3 * count :]
    pieces = []
    for i in range(count):
        rows = source[i].shape[0]
        parts = 4 if rows % 256 == 0 else 1
        for part in range(parts):
            at = pl.ds(part * (rows // parts), rows // parts)
            pieces.append((source[i].at[at], held[i].at[at], target[i].at[at]))
    ins = [pltpu.make_async_copy(p[0], p[1], got.at[i]) for i, p in enumerate(pieces)]
    outs = [pltpu.make_async_copy(p[1], p[2], put.at[i]) for i, p in enumerate(pieces)]
    for copy in ins:
        copy.start()
    for copy, out in zip(ins, outs):
        copy.wait()
        out.start()
    for copy in outs:
        copy.wait()


def hand_out(arrays):
    return pl.pallas_call(
        hand_out_kernel,
        out_shape=tuple(jax.ShapeDtypeStruct(item.shape, item.dtype) for item in arrays),
        in_specs=[ANY] * len(arrays),
        out_specs=(ANY,) * len(arrays),
        scratch_shapes=[pltpu.VMEM(item.shape, item.dtype) for item in arrays]
        + [pltpu.SemaphoreType.DMA((len(arrays) + 9,))] * 2,
        name="hand_out",
    )(*arrays)


def by_kernel(
    decoder_in,
    encoder_out,
    self_query,
    self_key,
    self_value,
    self_output,
    cross_query,
    cross_key,
    cross_value,
    cross_output,
    hidden_in,
    hidden_out,
    norm_gains,
    bias_table,
    target_lengths,
    source_lengths,
    example_counts,
    cotangent,
):
    results = layer_call(
        self_query,
        self_key,
        self_value,
        self_output,
        cross_key,
        cross_value,
        cross_query,
        cross_output,
        hidden_in,
        hidden_out,
        norm_gains,
        bias_table.T,
        decoder_in.reshape(256, 768),
        cotangent.reshape(256, 768),
        encoder_out.reshape(1024, 768),
        target_lengths,
        source_lengths,
        example_counts,
    )
    g_enc, out, g_dec, *g_sq, g_up, g_down, g_gain, g_table = hand_out(results)
    return (
        out.reshape(decoder_in.shape),
        g_dec.reshape(decoder_in.shape),
        g_enc.reshape(encoder_out.shape),
        *g_sq[:4],
        g_sq[6],
        g_sq[4],
        g_sq[5],
        g_sq[7],
        g_up,
        g_down,
        g_gain,
        g_table.T,
    )


def plain(
    decoder_in,
    encoder_out,
    self_query,
    self_key,
    self_value,
    self_output,
    cross_query,
    cross_key,
    cross_value,
    cross_output,
    hidden_in,
    hidden_out,
    norm_gains,
    bias_table,
    target_lengths,
    source_lengths,
    example_counts,
    cotangent,
):
    gathered = (
        lax.all_gather(self_query, AXES, axis=0, tiled=True),
        lax.all_gather(self_key, AXES, axis=0, tiled=True),
        lax.all_gather(self_value, AXES, axis=0, tiled=True),
        lax.all_gather(self_output, AXES, axis=0, tiled=True),
        lax.all_gather(cross_query, AXES, axis=0, tiled=True),
        lax.all_gather(cross_key, AXES, axis=0, tiled=True),
        lax.all_gather(cross_value, AXES, axis=0, tiled=True),
        lax.all_gather(cross_output, AXES, axis=0, tiled=True),
        lax.all_gather(hidden_in, AXES, axis=0, tiled=True),
        lax.all_gather(hidden_out, AXES, axis=0, tiled=True),
        lax.all_gather(norm_gains, AXES, axis=1, tiled=True),
    )
    w_query, w_key, w_value, w_out, x_query, x_key, x_value, x_out, w_up, w_down, gain_all = (
        gathered
    )
    slots = jnp.arange(decoder_in.shape[0], dtype=jnp.int32)
    length = decoder_in.shape[1]
    source = encoder_out.shape[1]
    width = decoder_in.shape[2]
    hidden_width = hidden_in.shape[1]
    place = jnp.arange(length, dtype=jnp.int32)
    source_place = jnp.arange(source, dtype=jnp.int32)
    live = (
        (slots < example_counts[0])[:, None] & (place[None, :] < target_lengths[:, None])
    ).astype(jnp.float32)[:, :, None]
    self_mask = (place[None, :] <= place[:, None])[None, None] & (
        place[None, None, None, :] < target_lengths[:, None, None, None]
    )
    cross_mask = source_place[None, None, None, :] < source_lengths[:, None, None, None]
    onehot = (
        buckets(length)[:, :, None] == jnp.arange(bias_table.shape[0], dtype=jnp.int32)
    ).astype(jnp.bfloat16)
    bias = jnp.einsum("lsn,nh->hls", onehot, bias_table, preferred_element_type=jnp.float32)
    gains = gain_all.astype(jnp.float32)
    inputs = decoder_in.astype(jnp.float32)
    first = normalize(inputs, gains[0]).astype(jnp.bfloat16)
    query = project(first, w_query).astype(jnp.bfloat16)
    key = project(first, w_key).astype(jnp.bfloat16)
    value = project(first, w_value).astype(jnp.bfloat16)
    mixed, logsum_self = attention_forward(
        split_heads(query), split_heads(key), split_heads(value), bias, self_mask
    )
    after_self = inputs + project(mixed, w_out)
    second = normalize(after_self, gains[1]).astype(jnp.bfloat16)
    cross_q = project(second, x_query).astype(jnp.bfloat16)
    cross_k = project(encoder_out, x_key).astype(jnp.bfloat16)
    cross_v = project(encoder_out, x_value).astype(jnp.bfloat16)
    crossed, logsum_cross = attention_forward(
        split_heads(cross_q), split_heads(cross_k), split_heads(cross_v), 0.0, cross_mask
    )
    after_cross = after_self + project(crossed, x_out)
    third = normalize(after_cross, gains[2]).astype(jnp.bfloat16)
    inner = project(third, w_up)
    active = jax.nn.gelu(inner).astype(jnp.bfloat16)
    result = after_cross + project(active, w_down)
    layer_out = (result * live).astype(jnp.bfloat16)
    regathered = (
        lax.all_gather(self_query, AXES, axis=0, tiled=True),
        lax.all_gather(self_key, AXES, axis=0, tiled=True),
        lax.all_gather(self_value, AXES, axis=0, tiled=True),
        lax.all_gather(self_output, AXES, axis=0, tiled=True),
        lax.all_gather(cross_query, AXES, axis=0, tiled=True),
        lax.all_gather(cross_key, AXES, axis=0, tiled=True),
        lax.all_gather(cross_value, AXES, axis=0, tiled=True),
        lax.all_gather(cross_output, AXES, axis=0, tiled=True),
        lax.all_gather(hidden_in, AXES, axis=0, tiled=True),
        lax.all_gather(hidden_out, AXES, axis=0, tiled=True),
        lax.all_gather(norm_gains, AXES, axis=1, tiled=True),
    )
    w_query, w_key, w_value, w_out, x_query, x_key, x_value, x_out, w_up, w_down, gain_all = (
        regathered
    )
    gains = gain_all.astype(jnp.float32)
    d_result = cotangent.astype(jnp.float32) * live
    d_branch = d_result.astype(jnp.bfloat16)
    grad_down = outer_sum(active, d_branch)
    d_inner = gelu_grad(inner, project_back(d_branch, w_down)).astype(jnp.bfloat16)
    grad_up = outer_sum(third, d_inner)
    d_cross, gain_three = norm_grad(after_cross, gains[2], project_back(d_inner, w_up))
    d_cross = d_cross + d_result
    d_branch = d_cross.astype(jnp.bfloat16)
    grad_x_out = outer_sum(crossed, d_branch)
    d_crossed = project_back(d_branch, x_out).astype(jnp.bfloat16)
    dq_cross, dk_cross, dv_cross, unused = attention_backward(
        split_heads(cross_q),
        split_heads(cross_k),
        split_heads(cross_v),
        0.0,
        cross_mask,
        logsum_cross,
        split_heads(d_crossed),
    )
    grad_x_query = outer_sum(second, dq_cross)
    grad_x_key = outer_sum(encoder_out, dk_cross)
    grad_x_value = outer_sum(encoder_out, dv_cross)
    grad_encoder = project_back(dk_cross, x_key) + project_back(dv_cross, x_value)
    d_self, gain_two = norm_grad(after_self, gains[1], project_back(dq_cross, x_query))
    d_self = d_self + d_cross
    d_branch = d_self.astype(jnp.bfloat16)
    grad_w_out = outer_sum(mixed, d_branch)
    d_mixed = project_back(d_branch, w_out).astype(jnp.bfloat16)
    dq_self, dk_self, dv_self, d_scores = attention_backward(
        split_heads(query),
        split_heads(key),
        split_heads(value),
        bias,
        self_mask,
        logsum_self,
        split_heads(d_mixed),
    )
    d_bias = jnp.sum(d_scores, axis=0, dtype=jnp.float32)
    table_term = jnp.einsum(
        "hls,lsn->nh", d_bias, onehot.astype(jnp.float32), precision=lax.Precision.HIGHEST
    )
    grad_w_query = outer_sum(first, dq_self)
    grad_w_key = outer_sum(first, dk_self)
    grad_w_value = outer_sum(first, dv_self)
    d_first = (
        project_back(dq_self, w_query)
        + project_back(dk_self, w_key)
        + project_back(dv_self, w_value)
    )
    d_inputs, gain_one = norm_grad(inputs, gains[0], d_first)
    grad_decoder = d_inputs + d_self
    gain_terms = jnp.stack([gain_one, gain_two, gain_three], axis=1)
    flats = flat_rows(
        (
            grad_w_query,
            grad_w_key,
            grad_w_value,
            grad_w_out,
            grad_x_query,
            grad_x_key,
            grad_x_value,
            grad_x_out,
            grad_up,
            grad_down,
            gain_terms,
        )
    )
    summed = (
        lax.psum_scatter(flats[0], AXES, scatter_dimension=0, tiled=True),
        lax.psum_scatter(flats[1], AXES, scatter_dimension=0, tiled=True),
        lax.psum_scatter(flats[2], AXES, scatter_dimension=0, tiled=True),
        lax.psum_scatter(flats[3], AXES, scatter_dimension=0, tiled=True),
        lax.psum_scatter(flats[4], AXES, scatter_dimension=0, tiled=True),
        lax.psum_scatter(flats[5], AXES, scatter_dimension=0, tiled=True),
        lax.psum_scatter(flats[6], AXES, scatter_dimension=0, tiled=True),
        lax.psum_scatter(flats[7], AXES, scatter_dimension=0, tiled=True),
        lax.psum_scatter(flats[8], AXES, scatter_dimension=0, tiled=True),
        lax.psum_scatter(flats[9], AXES, scatter_dimension=0, tiled=True),
        lax.psum_scatter(flats[10], AXES, scatter_dimension=0, tiled=True),
    )
    shaped = unflat_rows(
        summed, (width, width, width, width, width, width, width, width, hidden_width, width, 3)
    )
    sums = shaped[:10] + (jnp.transpose(shaped[10]),)
    grad_table = lax.psum(table_term, AXES)
    return (
        layer_out,
        grad_decoder,
        grad_encoder,
        sums[0],
        sums[1],
        sums[2],
        sums[3],
        sums[4],
        sums[5],
        sums[6],
        sums[7],
        sums[8],
        sums[9],
        sums[10],
        grad_table,
    )


def solution(mesh):
    rows = P(AXES, None)
    slots = P(AXES, None, None)
    flat = P(AXES)
    gains = P(None, AXES)
    small = mesh.shape["dp"] == 8 and mesh.shape["fsdp"] == 4
    return jax.shard_map(
        by_kernel if small else plain,
        mesh=mesh,
        in_specs=(slots, slots) + (rows,) * 10 + (gains, P(), flat, flat, flat, slots),
        out_specs=(slots, slots, slots) + (rows,) * 10 + (gains, P()),
        check_vma=False,
    )
```
